32 devices in a mesh: seq: 4 (over z), fsdp: 8 (over y, x, core).
Axes of the slice: x: 2, y: 2, z: 4, core: 2. Of those that a mesh axis runs over, the one named last changes fastest.
Arguments:
- inputs: bfloat16 [8, 2048, 1024], P('fsdp', 'seq'), may hold values from -6 to 6
- positions: int32 [8, 2048], P('fsdp', 'seq'), may hold values from 0 to 2047, as said below
- cotangent: bfloat16 [8, 2048, 1024], P('fsdp', 'seq'), may hold values from -6 to 6
- query_weight: bfloat16 [1024, 1024], P('fsdp'), may hold values from -0.1875 to 0.1875
- key_weight: bfloat16 [1024, 512], P('fsdp'), may hold values from -0.1875 to 0.1875
- value_weight: bfloat16 [1024, 512], P('fsdp'), may hold values from -0.1875 to 0.1875
- out_weight: bfloat16 [1024, 1024], P('fsdp'), may hold values from -0.75 to 0.75
- attention_gain: bfloat16 [1024], P('fsdp'), may hold values from 0.099609375 to 1.8984375
- query_gain: bfloat16 [64], P('fsdp'), may hold values from 0.099609375 to 1.8984375
- key_gain: bfloat16 [64], P('fsdp'), may hold values from 0.099609375 to 1.8984375
- feedforward_gain: bfloat16 [1024], P('fsdp'), may hold values from 0.099609375 to 1.8984375
- gate_weight: bfloat16 [1024, 4608], P('fsdp'), may hold values from -0.1875 to 0.1875
- up_weight: bfloat16 [1024, 4608], P('fsdp'), may hold values from -0.1875 to 0.1875
- down_weight: bfloat16 [4608, 1024], P('fsdp'), may hold values from -0.09375 to 0.09375
Outputs:
- output: bfloat16 [8, 2048, 1024], P('fsdp', 'seq')
- input_grad: bfloat16 [8, 2048, 1024], P('fsdp', 'seq')
- query_weight_grad: float32 [1024, 1024], P('fsdp')
- key_weight_grad: float32 [1024, 512], P('fsdp')
- value_weight_grad: float32 [1024, 512], P('fsdp')
- out_weight_grad: float32 [1024, 1024], P('fsdp')
- attention_gain_grad: float32 [1024], P('fsdp')
- query_gain_grad: float32 [64], P('fsdp')
- key_gain_grad: float32 [64], P('fsdp')
- feedforward_gain_grad: float32 [1024], P('fsdp')
- gate_weight_grad: float32 [1024, 4608], P('fsdp')
- up_weight_grad: float32 [1024, 4608], P('fsdp')
- down_weight_grad: float32 [4608, 1024], P('fsdp')
The draws below stay inside these ranges and needn't reach their ends.
Inputs may be any that keep to these rules, and one draw needn't show every extreme that they name: `positions`: each sequence is a pack of documents; a token's position counts from the first token of its document. In every draw at least one sequence is a single document.
All inputs are finite; a program needn't handle non-finite values.
Results may differ from the reference program's by a relative error of at most 0.018.
Values may be sent and summed in bfloat16 or wider, within the bound.
A program may use at most 192 MiB of HBM per device.

```python
import jax
import jax.numpy as jnp
from jax import lax

D = 1024
H = 16
KV = 8
HD = 64
FF = 4608
SEQ_LEN = 2048
SEQS = 8


def draw_positions(key, part):
    key = jax.random.fold_in(key, 7)
    cut_key, whole_key = jax.random.split(key)
    cuts = jax.random.randint(cut_key, (SEQS, SEQ_LEN), 0, SEQ_LEN // 4) == 0
    single = jax.random.randint(whole_key, (), 0, SEQS)
    others = jnp.arange(SEQS, dtype=jnp.int32)[:, None] != single
    index = jnp.broadcast_to(jnp.arange(SEQ_LEN, dtype=jnp.int32)[None, :], (SEQS, SEQ_LEN))
    starts = jnp.where(cuts & others, index, 0)
    last_start = lax.cummax(starts, axis=1)
    return (index - last_start).astype(jnp.int32)


def block_levels(stream_key, dims, cuts, low, top_value):
    def one(axis_at, blocks):
        steps = jax.random.uniform(jax.random.fold_in(jax.random.fold_in(stream_key, 6), axis_at), (blocks,), jnp.float32, low / len(cuts), top_value / len(cuts))
        return jnp.repeat(jnp.exp(steps), dims[axis_at] // blocks).reshape((-1,) + (1,) * (len(dims) - axis_at - 1))

    level = one(*cuts[0])
    for cut in cuts[1:]:
        level = level * one(*cut)
    return level


def centred(own_key, shape, scale, bound, cuts=(), kind=jnp.bfloat16):
    values = scale * jax.random.normal(own_key, shape, jnp.float32)
    if cuts:
        values = values * block_levels(own_key, shape, cuts, -0.22, 0.18)
    return jnp.clip(values, -bound, bound).astype(kind)


def setup_inputs(seed: int = 0) -> dict:
    key_of = jax.random.split(jax.random.key(seed), 15)
    inputs = centred(key_of[0], (SEQS, SEQ_LEN, D), 1.0, 6.0, ((0, 8), (1, 4)))
    positions = draw_positions(jax.random.fold_in(key_of[14], 71), 0)
    cotangent = centred(key_of[2], (SEQS, SEQ_LEN, D), 1.0, 6.0, ((0, 8), (1, 4)))
    query_weight = centred(key_of[3], (D, H * HD), D ** -0.5, 0.1875, ((0, 8),))
    key_weight = centred(key_of[4], (D, KV * HD), D ** -0.5, 0.1875, ((0, 8),))
    value_weight = centred(key_of[5], (D, KV * HD), D ** -0.5, 0.1875, ((0, 8),))
    out_weight = centred(key_of[6], (H * HD, D), (H * HD // 16) ** -0.5, 0.75, ((0, 8),))
    attention_gain = jnp.clip(1.0 + 0.18 * jax.random.normal(key_of[7], (D,), jnp.float32), 0.099609375, 1.8984375).astype(jnp.bfloat16)
    query_gain = jnp.clip(1.0 + 0.18 * jax.random.normal(key_of[8], (HD,), jnp.float32), 0.099609375, 1.8984375).astype(jnp.bfloat16)
    key_gain = jnp.clip(1.0 + 0.18 * jax.random.normal(key_of[9], (HD,), jnp.float32), 0.099609375, 1.8984375).astype(jnp.bfloat16)
    feedforward_gain = jnp.clip(1.0 + 0.18 * jax.random.normal(key_of[10], (D,), jnp.float32), 0.099609375, 1.8984375).astype(jnp.bfloat16)
    gate_weight = centred(key_of[11], (D, FF), D ** -0.5, 0.1875, ((0, 8),))
    up_weight = centred(key_of[12], (D, FF), D ** -0.5, 0.1875, ((0, 8),))
    down_weight = centred(key_of[13], (FF, D), FF ** -0.5, 0.09375, ((0, 8),))
    return {"inputs": inputs, "positions": positions, "cotangent": cotangent, "query_weight": query_weight, "key_weight": key_weight, "value_weight": value_weight, "out_weight": out_weight, "attention_gain": attention_gain, "query_gain": query_gain, "key_gain": key_gain, "feedforward_gain": feedforward_gain, "gate_weight": gate_weight, "up_weight": up_weight, "down_weight": down_weight}


EPSILON = 1e-05
ROPE_BASE = 1000000.0

@jax.custom_vjp
def low(v):
    return lax.optimization_barrier(v.astype(jnp.bfloat16)).astype(jnp.float32)

@jax.custom_vjp
def low_back(v):
    return v

def low_keep(v):
    return (low(v), None)

def low_pass(kept, grad):
    return (grad,)

def back_keep(v):
    return (v, None)

def back_low(kept, grad):
    return (low(grad),)
low.defvjp(low_keep, low_pass)
low_back.defvjp(back_keep, back_low)

def highest(left_side, right_side):
    return jnp.dot(left_side, right_side, precision=lax.Precision.HIGHEST)

def rms_scale(values, gain_vector):
    return values * lax.rsqrt(lax.optimization_barrier(jnp.mean(values * values, axis=-1, keepdims=True)) + EPSILON) * gain_vector

def rotate(values, token_positions):
    half_width = values.shape[-1] // 2
    freqs = ROPE_BASE ** (-jnp.arange(half_width, dtype=jnp.float32) / half_width)
    angles = token_positions.astype(jnp.float32)[:, None] * freqs[None, :]
    cosine = jnp.cos(angles)[:, None, :]
    sine = jnp.sin(angles)[:, None, :]
    first_half = values[..., :half_width]
    second_half = values[..., half_width:]
    return jnp.concatenate([first_half * cosine - second_half * sine, second_half * cosine + first_half * sine], axis=-1)

def attend(queries, key_rows, value_rows):
    seq_len = queries.shape[0]
    block_rows = min(512, seq_len)
    block_count = seq_len // block_rows
    score_scale = queries.shape[-1] ** (-0.5)
    key_index = jnp.arange(seq_len, dtype=jnp.int32)

    def one_block(pair):
        block_queries, first_row = pair
        scores = jnp.einsum('qbgd,kbd->bgqk', block_queries, key_rows, precision=lax.Precision.HIGHEST) * score_scale
        scores = low_back(scores)
        query_index = first_row + jnp.arange(block_rows, dtype=jnp.int32)
        allowed = query_index[:, None] >= key_index[None, :]
        scores = jnp.where(allowed, scores, -1e+30)
        row_peak = lax.optimization_barrier(jnp.max(scores, axis=-1, keepdims=True))
        exp_scores = jnp.exp(scores - row_peak)
        prob_low = low(exp_scores / lax.optimization_barrier(jnp.sum(exp_scores, axis=-1, keepdims=True)))
        return jnp.einsum('bgqk,kbd->qbgd', prob_low, value_rows, precision=lax.Precision.HIGHEST)
    blocks = queries.reshape((block_count, block_rows) + queries.shape[1:])
    starts = jnp.arange(block_count, dtype=jnp.int32) * block_rows
    outputs = lax.map(jax.checkpoint(one_block), (blocks, starts))
    return outputs.reshape(seq_len, -1)

def layer(params, rows, token_positions):
    query_weight, key_weight, value_weight, out_weight, attention_gain, query_gain, key_gain, feedforward_gain, gate_weight, up_weight, down_weight = params
    seq_len = rows.shape[0]
    normed = low(rms_scale(rows, attention_gain))
    query_proj = low_back(highest(normed, query_weight)).reshape(seq_len, H, HD)
    key_proj = low_back(highest(normed, key_weight)).reshape(seq_len, KV, HD)
    value_rows = low_back(low(highest(normed, value_weight))).reshape(seq_len, KV, HD)
    queries = low_back(low(rotate(rms_scale(query_proj, query_gain), token_positions)))
    key_rows = low_back(low(rotate(rms_scale(key_proj, key_gain), token_positions)))
    mixed = attend(queries.reshape(seq_len, KV, H // KV, HD), key_rows, value_rows)
    mixed = low_back(low(mixed))
    attention_out = low_back(highest(mixed, out_weight))
    middle = rows + attention_out
    normed_two = low(rms_scale(middle, feedforward_gain))
    gate_value = low_back(highest(normed_two, gate_weight))
    up_value = low_back(highest(normed_two, up_weight))
    hidden = low(jax.nn.silu(gate_value) * up_value)
    return middle + highest(hidden, down_weight)

def reference(inputs, positions, cotangent, query_weight, key_weight, value_weight, out_weight, attention_gain, query_gain, key_gain, feedforward_gain, gate_weight, up_weight, down_weight):
    params = (query_weight.astype(jnp.float32), key_weight.astype(jnp.float32), value_weight.astype(jnp.float32), out_weight.astype(jnp.float32), attention_gain.astype(jnp.float32), query_gain.astype(jnp.float32), key_gain.astype(jnp.float32), feedforward_gain.astype(jnp.float32), gate_weight.astype(jnp.float32), up_weight.astype(jnp.float32), down_weight.astype(jnp.float32))
    rows_all = inputs.astype(jnp.float32)

    def whole(param_set, rows_in):

        def one_sequence(pair):
            return jax.checkpoint(layer)(param_set, pair[0], pair[1])
        return lax.map(one_sequence, (rows_in, positions))
    result, pullback = jax.vjp(whole, params, rows_all)
    grads, input_grad = pullback(cotangent.astype(jnp.float32))
    return (result.astype(jnp.bfloat16), input_grad.astype(jnp.bfloat16), grads[0], grads[1], grads[2], grads[3], grads[4], grads[5], grads[6], grads[7], grads[8], grads[9], grads[10])
```

```python
import functools

import jax
import jax.numpy as jnp
from jax import lax
from jax.experimental import pallas as pl
from jax.experimental.pallas import tpu as pltpu
from jax.sharding import PartitionSpec as P

EPSILON = 1e-05
ROPE_BASE = 1000000.0
LOG2E = 1.4426950408889634
BF = jnp.bfloat16
F32 = jnp.float32
VMEM = pl.BlockSpec(memory_space=pltpu.VMEM)
SMEM = pl.BlockSpec(memory_space=pltpu.SMEM)
ANY = pl.BlockSpec(memory_space=pl.ANY)
VMEM_BYTES = 58 * 2**20


def dot_nn(a, b):
    return lax.dot_general(a, b, (((1,), (0,)), ((), ())), preferred_element_type=F32)


def dot_nt(a, b):
    return lax.dot_general(a, b, (((1,), (1,)), ((), ())), preferred_element_type=F32)


def dot_tn(a, b):
    return lax.dot_general(a, b, (((0,), (0,)), ((), ())), preferred_element_type=F32)


def shape_of(shape, dtype):
    return jax.ShapeDtypeStruct(shape, dtype)


def call(kernel, outs, in_specs, out_specs, scratch, flops, moved, **more):
    return pl.pallas_call(
        kernel,
        out_shape=outs,
        in_specs=in_specs,
        out_specs=out_specs,
        scratch_shapes=scratch,
        compiler_params=pltpu.CompilerParams(vmem_limit_bytes=VMEM_BYTES),
        cost_estimate=pl.CostEstimate(flops=flops, bytes_accessed=moved, transcendentals=0),
        **more,
    )


def row_norm(values):
    return lax.rsqrt(jnp.mean(values * values, axis=-1, keepdims=True) + EPSILON)


def piece_offset(me, at, count, rows):
    if count == 1:
        return 0
    return pl.multiple_of((me ^ at) * rows, rows)


def start_pieces(me, pieces, whole, sems, first, rows=None, base=0, stride=None, cols=None, to_cols=None):
    copies = []
    for at, piece in enumerate(pieces):
        count = piece.shape[0] if rows is None else rows
        if len(pieces) == 1:
            count, offset = whole.shape[0], 0
        else:
            offset = piece_offset(me, at, len(pieces), count if stride is None else stride) + base
        source = piece.at[pl.ds(0, count)] if cols is None else piece.at[pl.ds(0, count), pl.ds(*cols)]
        target = whole.at[pl.ds(offset, count)] if to_cols is None else whole.at[pl.ds(offset, count), pl.ds(*to_cols)]
        copy = pltpu.make_async_copy(source, target, sems.at[first + at])
        copy.start()
        copies.append(copy)
    return copies


def wait_all(copies):
    for copy in copies:
        copy.wait()


def head_mask(width, head_dim):
    rows = lax.broadcasted_iota(jnp.int32, (width, width), 0) // head_dim
    cols = lax.broadcasted_iota(jnp.int32, (width, width), 1) // head_dim
    return (rows == cols).astype(BF)


def head_sum(values, mask):
    high = values.astype(BF)
    rest = (values - high.astype(F32)).astype(BF)
    return dot_nn(high, mask) + dot_nn(rest, mask)


def partner(values, head_dim):
    half = head_dim // 2
    width = values.shape[-1]
    lane = lax.broadcasted_iota(jnp.int32, values.shape, 1)
    after = pltpu.roll(values, width - half, 1)
    before = pltpu.roll(values, half, 1)
    return jnp.where(lane % head_dim < half, after, before)


def pre_kernel(dims, ids, x_ref, gain_ref, head_gain_ref, cos_ref, sin_ref, *refs):
    nz, np_a, head_dim, q_cols, k_cols, v_cols = dims
    a_pieces, b_pieces = refs[:np_a], refs[np_a : 2 * np_a]
    refs = refs[2 * np_a :]
    normed_t_ref, proj_ref = refs[:2]
    blocks = refs[2 : 2 + nz]
    w_qk, w_v, qkv, sems = refs[2 + nz :]
    z, me = ids[0], ids[1]
    rows = w_qk.shape[0] // np_a
    copies = start_pieces(me, a_pieces, w_qk, sems, 0, rows=rows)
    copies += start_pieces(me, b_pieces, w_v, sems, np_a, rows=rows, cols=(0, v_cols))
    x = x_ref[...].astype(F32)
    normed = (x * row_norm(x) * gain_ref[...]).astype(BF)
    normed_t_ref[...] = normed.T
    width = 256
    mask = head_mask(width, head_dim)
    cos = jnp.concatenate([cos_ref[...]] * (width // 128), axis=1)
    sin = jnp.concatenate([sin_ref[...]] * (width // 128), axis=1)
    wait_all(copies)
    for start in range(0, q_cols + k_cols, width):
        cols = slice(start, start + width)
        proj = dot_nn(normed, w_qk[:, cols])
        proj_ref[:, cols] = proj
        scale = lax.rsqrt(head_sum(proj * proj, mask) * (1.0 / head_dim) + EPSILON)
        values = proj * scale * head_gain_ref[:, cols]
        qkv[:, cols] = (values * cos + partner(values, head_dim) * sin).astype(BF)
    qkv[:, q_cols + k_cols :] = dot_nn(normed, w_v[...]).astype(BF)
    pack_blocks(z, nz, qkv, blocks, (q_cols, k_cols, v_cols))


def pack_blocks(z, nz, source, blocks, widths):
    for j, block in enumerate(blocks):
        owner = z ^ j
        base, at = 0, 0
        for width in widths:
            part = width // nz
            block[:, at : at + part] = source[:, pl.ds(pl.multiple_of(base + owner * part, part), part)]
            base, at = base + width, at + part


def load_heads(z, nz, blocks, scratch, sems, first):
    copies = []
    tokens = blocks[0].shape[0]
    for j in range(nz):
        copy = pltpu.make_async_copy(
            blocks[j], scratch.at[pl.ds(pl.multiple_of((z ^ j) * tokens, tokens), tokens)], sems.at[first + j]
        )
        copy.start()
        copies.append(copy)
    return copies


def split_heads(scratch, first, heads):
    head_dim = heads.shape[-1]
    for h in range(heads.shape[0]):
        heads[h] = scratch[:, first + h * head_dim : first + (h + 1) * head_dim]


def attend_kernel(dims, ids, *refs):
    nz, rows = dims
    blocks, outs = refs[:nz], refs[nz : 2 * nz]
    full_ref, log_ref, scratch, queries, keys, values, sems = refs[2 * nz :]
    z = ids[0]
    wait_all(load_heads(z, nz, blocks, scratch, sems, 0))
    heads, seq_len, head_dim = queries.shape
    kv_heads = keys.shape[0]
    group = heads // kv_heads
    split_heads(scratch, 0, queries)
    split_heads(scratch, heads * head_dim, keys)
    split_heads(scratch, (heads + kv_heads) * head_dim, values)
    scale = head_dim**-0.5 * LOG2E
    for r in range(seq_len // rows):
        span = slice(r * rows, (r + 1) * rows)
        reach = (r + 1) * rows

        def one_head(h, _):
            b = lax.div(h, group)
            scores = dot_nt(queries[h, span], keys[b, :reach]) * scale
            row = lax.broadcasted_iota(jnp.int32, scores.shape, 0) + r * rows
            col = lax.broadcasted_iota(jnp.int32, scores.shape, 1)
            probs = jnp.exp2(jnp.where(row >= col, scores, -1e30))
            total = jnp.sum(probs, axis=1, keepdims=True)
            full_ref[h, span] = dot_nn(probs.astype(BF), values[b, :reach]) * (1.0 / total)
            log_ref[h, :, span] = jnp.broadcast_to(jnp.log2(total), (rows, 128)).T[0:8]
            return 0

        lax.fori_loop(0, heads, one_head, 0)
    tokens = outs[0].shape[0]
    for j in range(nz):
        first = pl.multiple_of((z ^ j) * tokens, tokens)
        for h in range(heads):
            outs[j][:, h * head_dim : (h + 1) * head_dim] = full_ref[h, pl.ds(first, tokens)].astype(BF)


def attend_back_kernel(dims, ids, *refs):
    nz, rows, chunk = dims
    blocks, grads = refs[:nz], refs[nz : 2 * nz]
    full_ref, log_ref = refs[2 * nz : 2 * nz + 2]
    outs = refs[2 * nz + 2 : 3 * nz + 2]
    scratch, grad_scratch, queries, keys, values, grad, delta, q_grad, k_grad, v_grad, sems = refs[3 * nz + 2 :]
    z = ids[0]
    copies = load_heads(z, nz, blocks, scratch, sems, 0)
    copies += load_heads(z, nz, grads, grad_scratch, sems, nz)
    wait_all(copies)
    heads, seq_len, head_dim = queries.shape
    kv_heads = keys.shape[0]
    group = heads // kv_heads
    split_heads(scratch, 0, queries)
    split_heads(scratch, heads * head_dim, keys)
    split_heads(scratch, (heads + kv_heads) * head_dim, values)
    split_heads(grad_scratch, 0, grad)
    factor = head_dim**-0.5
    scale = factor * LOG2E
    ones = jnp.ones((8, head_dim), F32)
    for h in range(heads):
        product = grad[h].astype(F32) * full_ref[h]
        delta[h] = lax.dot_general(
            ones, product, (((1,), (1,)), ((), ())), preferred_element_type=F32, precision=lax.Precision.HIGHEST
        )
        q_grad[h] = jnp.zeros((seq_len, head_dim), F32)
    for at in range(seq_len // rows):
        span = slice(at * rows, (at + 1) * rows)

        def one_head(b, _):
            key, value = keys[b, span], values[b, span]
            key_total = jnp.zeros((rows, head_dim), F32)
            value_total = jnp.zeros((rows, head_dim), F32)
            for g in range(group):
                h = b * group + g
                for first in range(at * rows, seq_len, chunk):
                    last = min(first + chunk, seq_len)
                    part = slice(first, last)
                    query, out_grad = queries[h, part], grad[h, part]
                    scores = dot_nt(key, query) * scale - log_ref[h, 0:1, part]
                    if first == at * rows:
                        key_at = lax.broadcasted_iota(jnp.int32, scores.shape, 0) + at * rows
                        query_at = lax.broadcasted_iota(jnp.int32, scores.shape, 1) + first
                        scores = jnp.where(query_at >= key_at, scores, -1e30)
                    probs = jnp.exp2(scores)
                    prob_grad = dot_nt(value, out_grad)
                    score_grad = (probs * (prob_grad - delta[h, 0:1, part])).astype(BF)
                    value_total = value_total + dot_nn(probs.astype(BF), out_grad)
                    key_total = key_total + dot_nn(score_grad, query)
                    q_grad[h, part] = q_grad[h, part] + dot_tn(score_grad, key)
            k_grad[b, span] = (key_total * factor).astype(BF)
            v_grad[b, span] = value_total.astype(BF)
            return 0

        lax.fori_loop(0, kv_heads, one_head, 0)
    tokens = outs[0].shape[0]
    for j in range(nz):
        here = pl.ds(pl.multiple_of((z ^ j) * tokens, tokens), tokens)
        parts = [(q_grad[h, here] * factor).astype(BF) for h in range(heads)]
        parts += [k_grad[b, here] for b in range(kv_heads)] + [v_grad[b, here] for b in range(kv_heads)]
        outs[j][...] = jnp.concatenate(parts, axis=1)


def load_columns(z, nz, blocks, whole, sems, first):
    copies = []
    width = blocks[0].shape[1]
    for j in range(nz):
        copy = pltpu.make_async_copy(
            blocks[j], whole.at[:, pl.ds(pl.multiple_of((z ^ j) * width, width), width)], sems.at[first + j]
        )
        copy.start()
        copies.append(copy)
    return copies


def norm_back(rows, gain, gradient):
    q = row_norm(rows)
    n = rows * q
    u = gradient * gain
    return q * (u - n * jnp.mean(u * n, axis=-1, keepdims=True)), jnp.sum(gradient * n, axis=0, keepdims=True)


def feed_kernel(dims, ids, x_ref, dy_ref, gain_ref, *refs):
    nz, n_out, n_ff, n_down, out_cols, width, groups = dims
    mixed_blocks, refs = refs[:nz], refs[nz:]
    out_pieces, refs = refs[:n_out], refs[n_out:]
    gate_pieces, refs = refs[:n_ff], refs[n_ff:]
    up_pieces, refs = refs[:n_ff], refs[n_ff:]
    down_pieces, refs = refs[:n_down], refs[n_down:]
    output_ref, middle_grad_ref, middle_low_ref, mixed_t_ref, normed_t_ref, gain_grad_ref = refs[:6]
    grad_blocks, refs = refs[6 : 6 + nz], refs[6 + nz :]
    hidden_hbm, gate_grad_hbm, up_grad_hbm = refs[:3]
    w_out, w_gate, w_up, w_down, mixed, middle, normed, back = refs[3:11]
    hidden_slot, gate_slot, up_slot, sems, slot_sems = refs[11:]
    z, me = ids[0], ids[1]
    at = 0
    early = load_columns(z, nz, mixed_blocks, mixed, sems, at)
    at += nz
    early += start_pieces(me, out_pieces, w_out, sems, at, rows=w_out.shape[0] // n_out, cols=out_cols)
    at += n_out
    if n_down == 1:
        down_copies = start_pieces(me, down_pieces, w_down, sems, at)
    else:
        half = n_down // 2
        rows = down_pieces[0].shape[0]
        down_copies = start_pieces(me, down_pieces[:half], w_down, sems, at, stride=2 * rows)
        down_copies += start_pieces(me, down_pieces[half:], w_down, sems, at + half, stride=2 * rows, base=rows)
    at += n_down
    hidden_cols = w_gate.shape[1]
    group_cols = hidden_cols // groups
    group_copies = []
    for g in range(groups):
        cols = (g * group_cols, group_cols)
        copies = start_pieces(me, gate_pieces, w_gate, sems, at, cols=cols, to_cols=cols)
        copies += start_pieces(me, up_pieces, w_up, sems, at + n_ff, cols=cols, to_cols=cols)
        at += 2 * n_ff
        group_copies.append(copies)
    wait_all(early)
    x = x_ref[...].astype(F32)
    mixed_rows = mixed[...]
    mixed_t_ref[...] = mixed_rows.T
    middle_rows = x + dot_nn(mixed_rows, w_out[...])
    normed_rows = (middle_rows * row_norm(middle_rows) * gain_ref[...]).astype(BF)
    normed[...] = normed_rows
    normed_t_ref[...] = normed_rows.T
    middle[...] = middle_rows
    back[...] = jnp.zeros(back.shape, F32)
    wait_all(down_copies)

    def slot_copies(slot, f):
        here = pl.ds(pl.multiple_of(f * width, width), width)
        return (
            pltpu.make_async_copy(hidden_slot.at[slot], hidden_hbm.at[here], slot_sems.at[slot, 0]),
            pltpu.make_async_copy(gate_slot.at[slot], gate_grad_hbm.at[:, here], slot_sems.at[slot, 1]),
            pltpu.make_async_copy(up_slot.at[slot], up_grad_hbm.at[:, here], slot_sems.at[slot, 2]),
        )

    def one_block(f, _):
        slot = lax.rem(f, 2)
        here = pl.ds(pl.multiple_of(f * width, width), width)

        @pl.when(f >= 2)
        def _():
            wait_all(slot_copies(slot, f - 2))

        gate = dot_nn(normed[...], w_gate[:, here])
        up = dot_nn(normed[...], w_up[:, here])
        hidden_grad = dot_nt(dy_ref[...], w_down[here])
        s = 1.0 / (1.0 + jnp.exp(-gate))
        silu = gate * s
        hidden = (silu * up).astype(BF)
        gate_grad = (hidden_grad * up * (s * (1.0 + gate * (1.0 - s)))).astype(BF)
        up_grad = (hidden_grad * silu).astype(BF)
        hidden_slot[slot] = hidden.T
        gate_slot[slot] = gate_grad
        up_slot[slot] = up_grad
        for copy in slot_copies(slot, f):
            copy.start()
        middle[...] = middle[...] + dot_nn(hidden, w_down[here])
        back[...] = back[...] + (dot_nt(gate_grad, w_gate[:, here]) + dot_nt(up_grad, w_up[:, here]))
        return 0

    blocks = hidden_cols // width
    per_group = blocks // groups
    for g in range(groups):
        wait_all(group_copies[g])
        lax.fori_loop(g * per_group, (g + 1) * per_group, one_block, 0)
    output_ref[...] = middle[...].astype(BF)
    middle_rows = x_ref[...].astype(F32) + dot_nn(mixed[...], w_out[...])
    part, gain_sum = norm_back(middle_rows, gain_ref[...], back[...])
    gain_grad_ref[...] = gain_sum
    middle_grad = dy_ref[...].astype(F32) + part
    middle_grad_ref[...] = middle_grad
    middle_low = middle_grad.astype(BF)
    middle_low_ref[...] = middle_low
    mixed[...] = dot_nt(middle_low, w_out[...]).astype(BF)
    pack_blocks(z, nz, mixed, grad_blocks, (mixed.shape[1],))
    for f in (blocks - 2, blocks - 1):
        wait_all(slot_copies(f % 2, f))


def weight_grad_kernel(dims, ids, left_ref, right_ref, *refs):
    chips, parts = dims
    if chips == 0:
        refs[0][...] = dot_nn(left_ref[...], right_ref[...]).astype(BF)
        return
    outs, (ordered,) = refs[:-1], refs[-1:]
    me = ids[1]
    chip, core = lax.div(me, 2), lax.rem(me, 2)
    rows = left_ref.shape[0] // (2 * chips)

    @pl.when(pl.program_id(0) == 0)
    def _():
        for side in range(2):
            owner_core = 1 - core if side == 0 else core
            for r in range(chips):
                owner = (chip ^ r) * 2 + owner_core
                to = (side * chips + r) * rows
                ordered[to : to + rows] = left_ref[pl.ds(pl.multiple_of(owner * rows, rows), rows)]

    right = right_ref[...]
    part = rows // parts
    for side in range(2):
        got = dot_nn(ordered[side * chips * rows : (side + 1) * chips * rows], right).astype(BF)
        for r in range(chips):
            for p in range(parts):
                first = r * rows + p * part
                outs[side * parts + p][r] = got[first : first + part]


def weight_grad(ids, left, right, chips, parts=1, width=512):
    rows, tokens = left.shape
    cols = right.shape[1]
    width = min(width, cols)
    if chips:
        part = rows // (2 * chips * parts)
        outs = [shape_of((chips, part, cols), BF)] * (2 * parts)
        out_specs = [pl.BlockSpec((chips, part, width), lambda n: (0, 0, n))] * (2 * parts)
        scratch = [pltpu.VMEM((rows, tokens), BF)]
    else:
        outs = [shape_of((rows, cols), BF)]
        out_specs = [pl.BlockSpec((rows, width), lambda n: (0, n))]
        scratch = []
    return call(
        functools.partial(weight_grad_kernel, (chips, parts)),
        outs,
        [SMEM, pl.BlockSpec((rows, tokens), lambda n: (0, 0)), pl.BlockSpec((tokens, width), lambda n: (0, n))],
        out_specs,
        scratch,
        2 * rows * tokens * cols,
        2 * (rows * tokens + tokens * cols + rows * cols),
        grid=(cols // width,),
    )(ids, left, right)


def post_kernel(dims, ids, x_ref, middle_grad_ref, gain_ref, head_gain_ref, cos_ref, sin_ref, proj_ref, *refs):
    nz, np_a, head_dim, q_cols, k_cols, v_cols = dims
    blocks, refs = refs[:nz], refs[nz:]
    a_pieces, b_pieces, refs = refs[:np_a], refs[np_a : 2 * np_a], refs[2 * np_a :]
    input_grad_ref, first_ref, second_ref, gain_grad_ref, head_gain_grad_ref = refs[:5]
    w_qk, w_v, qkv, sems = refs[5:]
    z, me = ids[0], ids[1]
    rows = w_qk.shape[0] // np_a
    copies = start_pieces(me, a_pieces, w_qk, sems, 0, rows=rows)
    copies += start_pieces(me, b_pieces, w_v, sems, np_a, rows=rows, cols=(0, v_cols))
    block_copies = []
    for j in range(nz):
        base, at = 0, 0
        for i, width in enumerate((q_cols, k_cols, v_cols)):
            part = width // nz
            to = pl.multiple_of(base + (z ^ j) * part, part)
            copy = pltpu.make_async_copy(
                blocks[j].at[:, pl.ds(at, part)], qkv.at[:, pl.ds(to, part)], sems.at[2 * np_a + 3 * j + i]
            )
            copy.start()
            block_copies.append(copy)
            base, at = base + width, at + part
    wait_all(block_copies)
    width = 256
    mask = head_mask(width, head_dim)
    cos = jnp.concatenate([cos_ref[...]] * (width // 128), axis=1)
    sin = jnp.concatenate([sin_ref[...]] * (width // 128), axis=1)
    for start in range(0, q_cols + k_cols, width):
        cols = slice(start, start + width)
        rotated = qkv[:, cols].astype(F32)
        gradient = rotated * cos - partner(rotated, head_dim) * sin
        proj = proj_ref[:, cols]
        scale = lax.rsqrt(head_sum(proj * proj, mask) * (1.0 / head_dim) + EPSILON)
        n = proj * scale
        u = gradient * head_gain_ref[:, cols]
        head_gain_grad_ref[:, cols] = jnp.sum(gradient * n, axis=0, keepdims=True)
        low = (scale * (u - n * (head_sum(u * n, mask) * (1.0 / head_dim)))).astype(BF)
        qkv[:, cols] = low
    first_ref[...] = qkv[:, :q_cols]
    second_ref[...] = qkv[:, q_cols:]
    wait_all(copies)
    normed_grad = dot_nt(qkv[:, : q_cols + k_cols], w_qk[...]) + dot_nt(qkv[:, q_cols + k_cols :], w_v[...])
    part, gain_sum = norm_back(x_ref[...].astype(F32), gain_ref[...], normed_grad)
    gain_grad_ref[...] = gain_sum
    input_grad_ref[...] = (middle_grad_ref[...] + part).astype(BF)


def add(a, b):
    return (a.astype(F32) + b.astype(F32)).astype(a.dtype)


def swap(values, axis, size, bit):
    return lax.ppermute(values, axis, [(i, i ^ bit) for i in range(size)])


def gather_plane(first, second):
    near = {0: first, 2: swap(first, "fsdp", 8, 2), 4: swap(first, "fsdp", 8, 4)}
    near[6] = swap(near[2], "fsdp", 8, 4)
    far = {0: second, 4: swap(second, "fsdp", 8, 4), 2: swap(second, "fsdp", 8, 2)}
    far[6] = swap(far[4], "fsdp", 8, 2)
    both = []
    for blocks in (near, far):
        whole = dict(blocks)
        for b in (0, 2, 4, 6):
            whole[b + 1] = swap(blocks[b], "fsdp", 8, 1)
        both.append([whole[b] for b in range(8)])
    return both


def reduce_plane(theirs, mine, x_first):
    got = swap(theirs, "fsdp", 8, 1)
    if x_first:
        away, kept, bits = (1, 3), (0, 2), (2, 4)
    else:
        away, kept, bits = (2, 3), (0, 1), (4, 2)
    send = jnp.stack([add(mine[r], got[r]) for r in away])
    keep = [add(mine[r], got[r]) for r in kept]
    back = swap(send, "fsdp", 8, bits[0])
    last = swap(add(keep[1], back[1]), "fsdp", 8, bits[1])
    return add(add(keep[0], back[0]), last)


def sum_line(values):
    size = lax.axis_size("seq")
    if size != 4:
        return lax.psum(values, "seq")
    z = lax.axis_index("seq")
    inner = add(values, lax.ppermute(values, "seq", [(0, 1), (3, 2)]))
    total = add(inner, lax.ppermute(inner, "seq", [(1, 2), (2, 1)]))
    outer = lax.ppermute(total, "seq", [(1, 0), (2, 3)])
    return jnp.where((z == 1) | (z == 2), total, outer)


def flip_to_order(values, me):
    grid = values.reshape((2, 2, 2) + values.shape[1:])
    for axis, bit in enumerate((4, 2, 1)):
        grid = jnp.where((me & bit) != 0, jnp.flip(grid, axis), grid)
    return grid.reshape(values.shape)


def per_device(
    inputs,
    positions,
    cotangent,
    query_weight,
    key_weight,
    value_weight,
    out_weight,
    attention_gain,
    query_gain,
    key_gain,
    feedforward_gain,
    gate_weight,
    up_weight,
    down_weight,
):
    seqs, tokens, model = inputs.shape
    assert seqs == 1
    fsdp, nz = lax.axis_size("fsdp"), lax.axis_size("seq")
    me, z = lax.axis_index("fsdp"), lax.axis_index("seq")
    plane = fsdp == 8
    ids = jnp.stack([z, me]).astype(jnp.int32)
    x = inputs.reshape(tokens, model)
    dy = cotangent.reshape(tokens, model)
    head_dim = query_gain.shape[0] * fsdp
    q_cols, k_cols, v_cols = query_weight.shape[1], key_weight.shape[1], value_weight.shape[1]
    heads, kv_heads = q_cols // head_dim // nz, k_cols // head_dim // nz
    hidden_cols = gate_weight.shape[1]
    seq_len = tokens * nz

    gains = jnp.concatenate([attention_gain, query_gain, key_gain, feedforward_gain])
    shard_rows = query_weight.shape[0]
    first = jnp.concatenate([query_weight, key_weight], axis=1)
    second = jnp.concatenate([value_weight, out_weight], axis=1)
    if plane:
        gain_rows = jnp.zeros((16, first.shape[1]), BF).at[0, : gains.shape[0]].set(gains)
        qk_pieces, vo_pieces = gather_plane(jnp.concatenate([first, gain_rows]), second)
        gate_pieces, up_pieces = gather_plane(gate_weight, up_weight)
        half = down_weight.shape[0] // 2
        upper, lower = gather_plane(down_weight[:half], down_weight[half:])
        down_pieces = upper + lower
        gains_all = flip_to_order(jnp.stack([p[shard_rows, : gains.shape[0]] for p in qk_pieces]), me)
    else:
        gather = functools.partial(lax.all_gather, axis_name="fsdp", axis=0, tiled=True)
        qk_pieces, vo_pieces = [gather(first)], [gather(second)]
        gate_pieces, up_pieces, down_pieces = [gather(gate_weight)], [gather(up_weight)], [gather(down_weight)]
        gains_all = lax.all_gather(gains, "fsdp", axis=0)
    gains_all = gains_all.astype(F32)
    n_a, n_h = attention_gain.shape[0], query_gain.shape[0]
    cuts = (n_a, n_a + n_h, n_a + 2 * n_h)
    attention_scale = gains_all[:, : cuts[0]].reshape(1, -1)
    query_scale = gains_all[:, cuts[0] : cuts[1]].reshape(1, -1)
    key_scale = gains_all[:, cuts[1] : cuts[2]].reshape(1, -1)
    feed_scale = gains_all[:, cuts[2] :].reshape(1, -1)
    head_scale = jnp.concatenate(
        [jnp.tile(query_scale, (1, q_cols // head_dim)), jnp.tile(key_scale, (1, k_cols // head_dim))], axis=1
    )

    half_dim = head_dim // 2
    freqs = ROPE_BASE ** (-jnp.arange(half_dim, dtype=F32) / half_dim)
    angles = positions.reshape(tokens).astype(F32)[:, None] * freqs[None, :]
    cosine, sine = jnp.cos(angles), jnp.sin(angles)
    cosine = jnp.tile(cosine, (1, 128 // half_dim))
    sine = jnp.tile(jnp.concatenate([-sine, sine], axis=1), (1, 128 // head_dim))

    np_a = len(qk_pieces)
    dims = (nz, np_a, head_dim, q_cols, k_cols, v_cols)
    block_cols = (q_cols + k_cols + v_cols) // nz
    qkv_scratch = [
        pltpu.VMEM((model, q_cols + k_cols), BF),
        pltpu.VMEM((model, v_cols), BF),
        pltpu.VMEM((tokens, q_cols + k_cols + v_cols), BF),
    ]
    proj_flops = 2 * tokens * model * (q_cols + k_cols + v_cols)
    normed_t, proj, *blocks = call(
        functools.partial(pre_kernel, dims),
        [shape_of((model, tokens), BF), shape_of((tokens, q_cols + k_cols), F32)]
        + [shape_of((tokens, block_cols), BF)] * nz,
        [SMEM] + [VMEM] * 5 + [ANY] * (2 * np_a),
        [VMEM] * (2 + nz),
        qkv_scratch + [pltpu.SemaphoreType.DMA((2 * np_a,))],
        proj_flops,
        12 * 2**20,
    )(ids, x, attention_scale, head_scale, cosine, sine, *qk_pieces, *vo_pieces)
    blocks = [blocks[0]] + [swap(blocks[j], "seq", nz, j) for j in range(1, nz)]

    mixed_cols = heads * head_dim
    head_scratch = [
        pltpu.VMEM((heads, seq_len, head_dim), BF),
        pltpu.VMEM((kv_heads, seq_len, head_dim), BF),
        pltpu.VMEM((kv_heads, seq_len, head_dim), BF),
    ]
    attend_flops = 2 * heads * seq_len * seq_len * head_dim
    *mixed, full, logs = call(
        functools.partial(attend_kernel, (nz, min(256, seq_len))),
        [shape_of((tokens, mixed_cols), BF)] * nz
        + [shape_of((heads, seq_len, head_dim), F32), shape_of((heads, 8, seq_len), F32)],
        [SMEM] + [ANY] * nz,
        [VMEM] * (nz + 2),
        [pltpu.VMEM((seq_len, block_cols), BF)] + head_scratch + [pltpu.SemaphoreType.DMA((nz,))],
        4 * attend_flops,
        8 * 2**20,
    )(ids, *blocks)
    mixed = [mixed[0]] + [swap(mixed[j], "seq", nz, j) for j in range(1, nz)]

    n_ff, n_down = len(gate_pieces), len(down_pieces)
    width = 512
    groups = 3
    rows_model = lambda kind: shape_of((tokens, model), kind)
    feed_out = call(
        functools.partial(feed_kernel, (nz, np_a, n_ff, n_down, (v_cols, model), width, groups)),
        [
            rows_model(BF),
            rows_model(F32),
            rows_model(BF),
            shape_of((model, tokens), BF),
            shape_of((model, tokens), BF),
            shape_of((1, model), F32),
        ]
        + [shape_of((tokens, mixed_cols), BF)] * nz
        + [shape_of((hidden_cols, tokens), BF)]
        + [shape_of((tokens, hidden_cols), BF)] * 2,
        [SMEM] + [VMEM] * 3 + [ANY] * (nz + np_a + 2 * n_ff + n_down),
        [VMEM] * (6 + nz) + [ANY] * 3,
        [
            pltpu.VMEM((q_cols, model), BF),
            pltpu.VMEM((model, hidden_cols), BF),
            pltpu.VMEM((model, hidden_cols), BF),
            pltpu.VMEM((hidden_cols, model), BF),
            pltpu.VMEM((tokens, q_cols), BF),
            pltpu.VMEM((tokens, model), F32),
            pltpu.VMEM((tokens, model), BF),
            pltpu.VMEM((tokens, model), F32),
            pltpu.VMEM((2, width, tokens), BF),
            pltpu.VMEM((2, tokens, width), BF),
            pltpu.VMEM((2, tokens, width), BF),
            pltpu.SemaphoreType.DMA((nz + np_a + n_down + 2 * n_ff * groups,)),
            pltpu.SemaphoreType.DMA((2, 3)),
        ],
        12 * tokens * model * hidden_cols,
        50 * 2**20,
    )(ids, x, dy, feed_scale, *mixed, *vo_pieces, *gate_pieces, *up_pieces, *down_pieces)
    output, middle_grad, middle_low, mixed_t, normed_two_t, feed_gain_part = feed_out[:6]
    mixed_grad = feed_out[6 : 6 + nz]
    hidden_t, gate_grad, up_grad = feed_out[6 + nz :]
    mixed_grad = [mixed_grad[0]] + [swap(mixed_grad[j], "seq", nz, j) for j in range(1, nz)]

    chips = 4 if plane else 0

    def scatter(values):
        return lax.psum_scatter(values, "fsdp", scatter_dimension=0, tiled=True)

    if plane:
        down_tu, down_tl, down_mu, down_ml = weight_grad(ids, hidden_t, dy, chips, parts=2, width=256)
        gate_t, gate_m = weight_grad(ids, normed_two_t, gate_grad, chips)
        up_t, up_m = weight_grad(ids, normed_two_t, up_grad, chips)
        out_t, out_m = weight_grad(ids, mixed_t, middle_low, chips)
        down_shard = jnp.concatenate(
            [sum_line(reduce_plane(down_tu, down_mu, True)), sum_line(reduce_plane(down_tl, down_ml, False))]
        )
        gate_shard = sum_line(reduce_plane(gate_t, gate_m, True))
        up_shard = sum_line(reduce_plane(up_t, up_m, False))
        out_shard = sum_line(reduce_plane(out_t, out_m, True))
    else:
        down_shard = sum_line(scatter(weight_grad(ids, hidden_t, dy, chips, width=256)[0]))
        gate_shard = sum_line(scatter(weight_grad(ids, normed_two_t, gate_grad, chips)[0]))
        up_shard = sum_line(scatter(weight_grad(ids, normed_two_t, up_grad, chips)[0]))
        out_shard = sum_line(scatter(weight_grad(ids, mixed_t, middle_low, chips)[0]))

    grads = call(
        functools.partial(attend_back_kernel, (nz, min(256, seq_len), min(1024, seq_len))),
        [shape_of((tokens, block_cols), BF)] * nz,
        [SMEM] + [ANY] * (2 * nz) + [VMEM] * 2,
        [VMEM] * nz,
        [pltpu.VMEM((seq_len, block_cols), BF), pltpu.VMEM((seq_len, mixed_cols), BF)]
        + head_scratch
        + [
            pltpu.VMEM((heads, seq_len, head_dim), BF),
            pltpu.VMEM((heads, 8, seq_len), F32),
            pltpu.VMEM((heads, seq_len, head_dim), F32),
            pltpu.VMEM((kv_heads, seq_len, head_dim), BF),
            pltpu.VMEM((kv_heads, seq_len, head_dim), BF),
            pltpu.SemaphoreType.DMA((2 * nz,)),
        ],
        10 * attend_flops,
        20 * 2**20,
    )(ids, *blocks, *mixed_grad, full, logs)
    grads = [grads[0]] + [swap(grads[j], "seq", nz, j) for j in range(1, nz)]

    input_grad, q_grad, kv_grad, attention_gain_part, head_gain_part = call(
        functools.partial(post_kernel, dims),
        [
            rows_model(BF),
            shape_of((tokens, q_cols), BF),
            shape_of((tokens, k_cols + v_cols), BF),
            shape_of((1, model), F32),
            shape_of((1, q_cols + k_cols), F32),
        ],
        [SMEM] + [VMEM] * 7 + [ANY] * (nz + 2 * np_a),
        [VMEM] * 5,
        qkv_scratch + [pltpu.SemaphoreType.DMA((2 * np_a + 3 * nz,))],
        proj_flops,
        14 * 2**20,
    )(ids, x, middle_grad, attention_scale, head_scale, cosine, sine, proj, *grads, *qk_pieces, *vo_pieces)
    if plane:
        q_t, q_m = weight_grad(ids, normed_t, q_grad, chips)
        kv_t, kv_m = weight_grad(ids, normed_t, kv_grad, chips)
        q_shard = sum_line(reduce_plane(q_t, q_m, True))
        kv_shard = sum_line(reduce_plane(kv_t, kv_m, False))
    else:
        q_shard = sum_line(scatter(weight_grad(ids, normed_t, q_grad, chips)[0]))
        kv_shard = sum_line(scatter(weight_grad(ids, normed_t, kv_grad, chips)[0]))

    q_part = head_gain_part[:, :q_cols].reshape(-1, head_dim).sum(axis=0)
    k_part = head_gain_part[:, q_cols:].reshape(-1, head_dim).sum(axis=0)
    gain_parts = jnp.concatenate(
        [v.reshape(fsdp, -1) for v in (attention_gain_part, q_part, k_part, feed_gain_part)], axis=1
    )
    if plane:
        ordered = flip_to_order(gain_parts, me).reshape(4, 2, 1, -1)
        gain_shard = sum_line(reduce_plane(ordered[:, 1], ordered[:, 0], True)).reshape(-1)
    else:
        gain_shard = sum_line(scatter(gain_parts).reshape(-1))
    wide = lambda v: v.astype(F32)
    return (
        output.reshape(inputs.shape),
        input_grad.reshape(inputs.shape),
        wide(q_shard),
        wide(kv_shard[:, :k_cols]),
        wide(kv_shard[:, k_cols:]),
        wide(out_shard),
        gain_shard[: cuts[0]],
        gain_shard[cuts[0] : cuts[1]],
        gain_shard[cuts[1] : cuts[2]],
        gain_shard[cuts[2] :],
        wide(gate_shard),
        wide(up_shard),
        wide(down_shard),
    )


def solution(mesh):
    tokens, rows, row = P("fsdp", "seq", None), P("fsdp", None), P("fsdp")
    in_specs = (tokens, P("fsdp", "seq"), tokens) + (rows,) * 4 + (row,) * 4 + (rows,) * 3
    out_specs = (tokens, tokens) + (rows,) * 4 + (row,) * 4 + (rows,) * 3
    return jax.shard_map(per_device, mesh=mesh, in_specs=in_specs, out_specs=out_specs, check_vma=False)
```

```python
import functools

import jax
import jax.numpy as jnp
from jax import lax
from jax.experimental import pallas as pl
from jax.experimental.pallas import tpu as pltpu
from jax.sharding import PartitionSpec as P

EPSILON = 1e-05
ROPE_BASE = 1000000.0
LOG2E = 1.4426950408889634
BF = jnp.bfloat16
F32 = jnp.float32
VMEM = pl.BlockSpec(memory_space=pltpu.VMEM)
SMEM = pl.BlockSpec(memory_space=pltpu.SMEM)
ANY = pl.BlockSpec(memory_space=pl.ANY)
VMEM_BYTES = 58 * 2**20


def dot_nn(a, b):
    return lax.dot_general(a, b, (((1,), (0,)), ((), ())), preferred_element_type=F32)


def dot_nt(a, b):
    return lax.dot_general(a, b, (((1,), (1,)), ((), ())), preferred_element_type=F32)


def dot_tn(a, b):
    return lax.dot_general(a, b, (((0,), (0,)), ((), ())), preferred_element_type=F32)


def shape_of(shape, dtype):
    return jax.ShapeDtypeStruct(shape, dtype)


def call(kernel, outs, in_specs, out_specs, scratch, flops, moved, collective=None, **more):
    params = {} if collective is None else {"collective_id": collective, "has_side_effects": True}
    return pl.pallas_call(
        kernel,
        out_shape=outs,
        in_specs=in_specs,
        out_specs=out_specs,
        scratch_shapes=scratch,
        compiler_params=pltpu.CompilerParams(vmem_limit_bytes=VMEM_BYTES, **params),
        cost_estimate=pl.CostEstimate(flops=flops, bytes_accessed=moved, transcendentals=0),
        **more,
    )


def row_norm(values):
    return lax.rsqrt(jnp.mean(values * values, axis=-1, keepdims=True) + EPSILON)


class Fetch:
    def __init__(self, sems):
        self.sems, self.used = sems, 0

    def start(self, source, target):
        copy = pltpu.make_async_copy(source, target, self.sems.at[self.used])
        copy.start()
        self.used += 1
        return copy


def wait_all(copies):
    for copy in copies:
        copy.wait()


def head_mask(width, head_dim):
    rows = lax.broadcasted_iota(jnp.int32, (width, width), 0) // head_dim
    cols = lax.broadcasted_iota(jnp.int32, (width, width), 1) // head_dim
    return (rows == cols).astype(BF)


def head_sum(values, mask):
    high = values.astype(BF)
    rest = (values - high.astype(F32)).astype(BF)
    return dot_nn(high, mask) + dot_nn(rest, mask)


def partner(values, head_dim):
    half = head_dim // 2
    width = values.shape[-1]
    lane = lax.broadcasted_iota(jnp.int32, values.shape, 1)
    after = pltpu.roll(values, width - half, 1)
    before = pltpu.roll(values, half, 1)
    return jnp.where(lane % head_dim < half, after, before)


def pack_blocks(z, nz, source, blocks, widths):
    for j, block in enumerate(blocks):
        owner = z ^ j
        base, at = 0, 0
        for width in widths:
            part = width // nz
            block[:, at : at + part] = source[:, pl.ds(pl.multiple_of(base + owner * part, part), part)]
            base, at = base + width, at + part


class Links:
    def __init__(self, send_sems, recv_sems):
        self.sems, self.used, self.started = (send_sems, recv_sems), 0, []

    def copy(self, source, target, device):
        copy = pltpu.make_async_remote_copy(
            src_ref=source,
            dst_ref=target,
            send_sem=self.sems[0].at[self.used],
            recv_sem=self.sems[1].at[self.used],
            device_id=device,
            device_id_type=pl.DeviceIdType.MESH,
        )
        self.used += 1
        return copy

    def start(self, source, target, device):
        copy = self.copy(source, target, device)
        copy.start()
        self.started.append(copy)
        return copy

    def wait_sends(self):
        for copy in self.started:
            copy.wait_send()


def enter(me, z, nz, plane):
    barrier = pltpu.get_barrier_semaphore()
    peers = [{"seq": z ^ j} for j in range(1, nz)]
    if plane:
        peers += [{"fsdp": me ^ bit} for bit in (1, 2, 4)]
    for peer in peers:
        pl.semaphore_signal(barrier, inc=1, device_id=peer, device_id_type=pl.DeviceIdType.MESH)
    pl.semaphore_wait(barrier, len(peers))


class Gather:
    def __init__(self, links, me, own, whole, x_first):
        self.links, self.me, self.own, self.whole = links, me, own, whole
        self.rows = own.shape[0]
        self.near, self.other = (2, 4) if x_first else (4, 2)

    def block(self, b):
        return self.whole.at[pl.ds(pl.multiple_of((self.me ^ b) * self.rows, self.rows), self.rows)]

    def pass_on(self, b, bit):
        source = self.own if b == 0 else self.block(b)
        return self.links.start(source, self.block(b), {"fsdp": self.me ^ bit})

    def begin(self):
        self.first = self.pass_on(0, self.near)
        self.second = self.pass_on(0, self.other)
        self.to_core = [self.pass_on(0, 1)]

    def forward_first(self):
        self.first.wait_recv()
        self.far = self.pass_on(self.near, self.other)
        self.to_core.append(self.pass_on(self.near, 1))

    def forward_second(self):
        self.second.wait_recv()
        self.to_core.append(self.pass_on(self.other, 1))

    def forward_far(self):
        self.far.wait_recv()
        self.to_core.append(self.pass_on(self.near + self.other, 1))

    def end(self):
        for copy in self.to_core:
            copy.wait_recv()


def forward_first(gathers):
    for gather in gathers:
        gather.forward_first()
    for gather in gathers:
        gather.forward_second()


def forward_far(gathers):
    for gather in gathers:
        gather.forward_far()


def forward_kernel(dims, x_ref, cos_ref, sin_ref, *refs):
    nz, plane, head_dim, q_cols, k_cols, v_cols, rows = dims
    n_in = 6 if plane else 3
    given, refs = refs[:n_in], refs[n_in:]
    gains_ref, normed_t_ref, proj_ref, heads_ref, mixed_ref, full_ref, log_ref = refs[:7]
    refs = refs[7:]
    if plane:
        qk_hbm, vo_hbm, gate_hbm, up_hbm, down_hbm = refs[:5]
        refs = refs[5:]
    w_qk, w_vo, normed, qkv, queries, keys, values, mix, local_sems, send_sems, recv_sems = refs
    z, me = lax.axis_index("seq"), lax.axis_index("fsdp")
    model = w_vo.shape[0]
    tokens = x_ref.shape[0]
    enter(me, z, nz, plane)
    links = Links(send_sems, recv_sems)
    local = []

    def copy_here(source, target):
        copy = pltpu.make_async_copy(source, target, local_sems.at[len(local)])
        copy.start()
        local.append(copy)
        return copy

    if plane:
        own_qk, own_vo, own_gate, own_up, own_down, _ = given
        half = own_down.shape[0] // 2
        attention = [Gather(links, me, own_qk, w_qk, True), Gather(links, me, own_vo, w_vo, False)]
        wide = [Gather(links, me, own_gate, gate_hbm, True), Gather(links, me, own_up, up_hbm, False)]
        for gather in attention:
            gather.begin()
        here = [copy_here(g.own, g.block(0)) for g in attention]
        down = []
        for side in range(2):
            g = Gather(links, me, own_down.at[pl.ds(side * half, half)], down_hbm.at[side], side == 0)
            down.append(g)
    else:
        here = [copy_here(given[0], w_qk), copy_here(given[1], w_vo)]
    x = x_ref[...].astype(F32)
    unit = x * row_norm(x)
    if plane:
        forward_first(attention)
        for gather in wide:
            gather.begin()
        for g in wide:
            copy_here(g.own, g.block(0))
        forward_far(attention)
        for g in attention:
            g.end()
        wait_all(here)
        stride = attention[0].rows
        shard = w_vo.shape[0] // 8
        gains = sum(w_qk[s * stride + shard : (s + 1) * stride].astype(F32) for s in range(8))
        for s in range(8):
            copy_here(w_qk.at[pl.ds(s * stride, shard)], qk_hbm.at[pl.ds(s * shard, shard)])
        copy_here(w_vo, vo_hbm)
    else:
        stride = shard = model
        wait_all(here)
        gains = given[2][...].astype(F32)
    gains_ref[...] = gains
    normed[...] = (unit * gains[0:1, :model]).astype(BF)
    width = 256
    mask = head_mask(width, head_dim)
    cos = jnp.concatenate([cos_ref[...]] * (width // 128), axis=1)
    sin = jnp.concatenate([sin_ref[...]] * (width // 128), axis=1)

    for start in range(0, q_cols + k_cols, width):
        cols = slice(start, start + width)
        if stride == shard:
            proj = dot_nn(normed[...], w_qk[:, cols])
        else:
            weight = jnp.concatenate([w_qk[s * stride : s * stride + shard, cols] for s in range(8)], axis=0)
            proj = dot_nn(normed[...], weight)
        proj_ref[:, cols] = proj
        scale = lax.rsqrt(head_sum(proj * proj, mask) * (1.0 / head_dim) + EPSILON)
        head = proj * scale * gains_ref[1:2, cols]
        qkv[:, cols] = (head * cos + partner(head, head_dim) * sin).astype(BF)
    qkv[:, q_cols + k_cols :] = dot_nn(normed[...], w_vo[:, :v_cols]).astype(BF)

    arrivals = []
    for j in range(nz):
        owner = z ^ j
        base, at = 0, 0
        for cols in (q_cols, k_cols, v_cols):
            part = cols // nz
            source = qkv.at[:, pl.ds(pl.multiple_of(base + owner * part, part), part)]
            target = heads_ref.at[pl.ds(pl.multiple_of(z * tokens, tokens), tokens), pl.ds(at, part)]
            if j == 0:
                arrivals.append(copy_here(source, target))
            else:
                arrivals.append(links.start(source, target, {"seq": owner}))
            base, at = base + cols, at + part
    normed_t_ref[...] = normed[...].T
    if plane:
        forward_first(wide)
        for gather in down:
            gather.begin()
        for g in down:
            copy_here(g.own, g.block(0))
    for i, copy in enumerate(arrivals):
        if i < 3:
            copy.wait()
        else:
            copy.wait_recv()

    heads, seq_len, _ = queries.shape
    kv_heads = keys.shape[0]
    group = heads // kv_heads
    split_heads(heads_ref, 0, queries)
    split_heads(heads_ref, heads * head_dim, keys)
    split_heads(heads_ref, (heads + kv_heads) * head_dim, values)
    factor = head_dim**-0.5 * LOG2E
    for r in range(seq_len // rows):
        span = slice(r * rows, (r + 1) * rows)
        reach = (r + 1) * rows

        def one_head(h, _):
            b = lax.div(h, group)
            scores = dot_nt(queries[h, span], keys[b, :reach]) * factor
            row = lax.broadcasted_iota(jnp.int32, scores.shape, 0) + r * rows
            col = lax.broadcasted_iota(jnp.int32, scores.shape, 1)
            probs = jnp.exp2(jnp.where(row >= col, scores, -1e30))
            total = jnp.sum(probs, axis=1, keepdims=True)
            full_ref[h, span] = dot_nn(probs.astype(BF), values[b, :reach]) * (1.0 / total)
            log_ref[h, :, span] = jnp.broadcast_to(jnp.log2(total), (rows, 128)).T[0:8]
            return 0

        lax.fori_loop(0, heads, one_head, 0)
    mix[...] = jnp.concatenate([full_ref[h].astype(BF) for h in range(heads)], axis=1)

    back = []
    part = mix.shape[1]
    for j in range(nz):
        owner = z ^ j
        source = mix.at[pl.ds(pl.multiple_of(owner * tokens, tokens), tokens)]
        target = mixed_ref.at[:, pl.ds(pl.multiple_of(z * part, part), part)]
        if j == 0:
            copy_here(source, target)
        else:
            back.append(links.start(source, target, {"seq": owner}))
    if plane:
        forward_far(wide)
        forward_first(down)
        forward_far(down)
        for gather in wide + down:
            gather.end()
    for copy in back:
        copy.wait_recv()
    links.wait_sends()
    for i, copy in enumerate(local):
        if not any(copy is done for done in here + arrivals[:3]):
            copy.wait()


def load_heads(z, nz, blocks, scratch, sems, first):
    copies = []
    tokens = blocks[0].shape[0]
    for j in range(nz):
        copy = pltpu.make_async_copy(
            blocks[j], scratch.at[pl.ds(pl.multiple_of((z ^ j) * tokens, tokens), tokens)], sems.at[first + j]
        )
        copy.start()
        copies.append(copy)
    return copies


def split_heads(scratch, first, heads):
    head_dim = heads.shape[-1]
    for h in range(heads.shape[0]):
        heads[h] = scratch[:, first + h * head_dim : first + (h + 1) * head_dim]


def attend_back_kernel(dims, ids, *refs):
    nz, rows, chunk = dims
    scratch, full_ref, log_ref = refs[:3]
    grads, refs = refs[3 : 3 + nz], refs[3 + nz :]
    outs, refs = refs[:nz], refs[nz:]
    grad_scratch, queries, keys, values, grad, delta, q_grad, k_grad, v_grad, sems = refs
    z = ids[0]
    wait_all(load_heads(z, nz, grads, grad_scratch, sems, 0))
    heads, seq_len, head_dim = queries.shape
    kv_heads = keys.shape[0]
    group = heads // kv_heads
    split_heads(scratch, 0, queries)
    split_heads(scratch, heads * head_dim, keys)
    split_heads(scratch, (heads + kv_heads) * head_dim, values)
    split_heads(grad_scratch, 0, grad)
    factor = head_dim**-0.5
    scale = factor * LOG2E
    ones = jnp.ones((8, head_dim), F32)
    for h in range(heads):
        product = grad[h].astype(F32) * full_ref[h]
        delta[h] = lax.dot_general(
            ones, product, (((1,), (1,)), ((), ())), preferred_element_type=F32, precision=lax.Precision.HIGHEST
        )
        q_grad[h] = jnp.zeros((seq_len, head_dim), F32)
    for at in range(seq_len // rows):
        span = slice(at * rows, (at + 1) * rows)

        def one_head(b, _):
            key, value = keys[b, span], values[b, span]
            key_total = jnp.zeros((rows, head_dim), F32)
            value_total = jnp.zeros((rows, head_dim), F32)
            for g in range(group):
                h = b * group + g
                for first in range(at * rows, seq_len, chunk):
                    last = min(first + chunk, seq_len)
                    part = slice(first, last)
                    query, out_grad = queries[h, part], grad[h, part]
                    scores = dot_nt(key, query) * scale - log_ref[h, 0:1, part]
                    if first == at * rows:
                        key_at = lax.broadcasted_iota(jnp.int32, scores.shape, 0) + at * rows
                        query_at = lax.broadcasted_iota(jnp.int32, scores.shape, 1) + first
                        scores = jnp.where(query_at >= key_at, scores, -1e30)
                    probs = jnp.exp2(scores)
                    prob_grad = dot_nt(value, out_grad)
                    score_grad = (probs * (prob_grad - delta[h, 0:1, part])).astype(BF)
                    value_total = value_total + dot_nn(probs.astype(BF), out_grad)
                    key_total = key_total + dot_nn(score_grad, query)
                    q_grad[h, part] = q_grad[h, part] + dot_tn(score_grad, key)
            k_grad[b, span] = (key_total * factor).astype(BF)
            v_grad[b, span] = value_total.astype(BF)
            return 0

        lax.fori_loop(0, kv_heads, one_head, 0)
    tokens = outs[0].shape[0]
    for j in range(nz):
        here = pl.ds(pl.multiple_of((z ^ j) * tokens, tokens), tokens)
        parts = [(q_grad[h, here] * factor).astype(BF) for h in range(heads)]
        parts += [k_grad[b, here] for b in range(kv_heads)] + [v_grad[b, here] for b in range(kv_heads)]
        outs[j][...] = jnp.concatenate(parts, axis=1)


def norm_back(rows, gain, gradient):
    q = row_norm(rows)
    n = rows * q
    u = gradient * gain
    return q * (u - n * jnp.mean(u * n, axis=-1, keepdims=True)), jnp.sum(gradient * n, axis=0, keepdims=True)


def feed_kernel(dims, ids, x_ref, dy_ref, gains_ref, mixed, *refs):
    nz, out_cols, width, groups = dims
    vo_hbm, gate_hbm, up_hbm, down_hbm = refs[:4]
    output_ref, middle_grad_ref, middle_low_ref, mixed_t_ref, normed_t_ref, gain_grad_ref = refs[4:10]
    grad_blocks, refs = refs[10 : 10 + nz], refs[10 + nz :]
    hidden_hbm, gate_grad_hbm, up_grad_hbm = refs[:3]
    w_out, w_gate, w_up, w_down, grad_low, middle, normed, back = refs[3:11]
    hidden_slot, gate_slot, up_slot, sems, slot_sems = refs[11:]
    z = ids[0]
    fetch = Fetch(sems)
    model, hidden_cols = w_gate.shape
    gain = gains_ref[2:3, :model]
    early = [fetch.start(vo_hbm.at[:, pl.ds(*out_cols)], w_out)]
    down_copies = []
    if len(down_hbm.shape) == 2:
        down_copies.append(fetch.start(down_hbm, w_down))
    else:
        half = hidden_cols // 16
        for owner in range(8):
            for side in range(2):
                target = w_down.at[pl.ds((2 * owner + side) * half, half)]
                down_copies.append(fetch.start(down_hbm.at[side, pl.ds(owner * half, half)], target))
    group_cols = hidden_cols // groups
    group_copies = []
    for g in range(groups):
        cols = pl.ds(g * group_cols, group_cols)
        group_copies.append([fetch.start(a.at[:, cols], b.at[:, cols]) for a, b in ((gate_hbm, w_gate), (up_hbm, w_up))])
    wait_all(early)
    x = x_ref[...].astype(F32)
    mixed_rows = mixed[...]
    mixed_t_ref[...] = mixed_rows.T
    middle_rows = x + dot_nn(mixed_rows, w_out[...])
    normed_rows = (middle_rows * row_norm(middle_rows) * gain).astype(BF)
    normed[...] = normed_rows
    normed_t_ref[...] = normed_rows.T
    middle[...] = middle_rows
    back[...] = jnp.zeros(back.shape, F32)
    wait_all(down_copies)

    def slot_copies(slot, f):
        here = pl.ds(pl.multiple_of(f * width, width), width)
        return (
            pltpu.make_async_copy(hidden_slot.at[slot], hidden_hbm.at[here], slot_sems.at[slot, 0]),
            pltpu.make_async_copy(gate_slot.at[slot], gate_grad_hbm.at[:, here], slot_sems.at[slot, 1]),
            pltpu.make_async_copy(up_slot.at[slot], up_grad_hbm.at[:, here], slot_sems.at[slot, 2]),
        )

    def one_block(f, _):
        slot = lax.rem(f, 2)
        here = pl.ds(pl.multiple_of(f * width, width), width)

        @pl.when(f >= 2)
        def _():
            wait_all(slot_copies(slot, f - 2))

        gate = dot_nn(normed[...], w_gate[:, here])
        up = dot_nn(normed[...], w_up[:, here])
        hidden_grad = dot_nt(dy_ref[...], w_down[here])
        s = 1.0 / (1.0 + jnp.exp(-gate))
        silu = gate * s
        hidden = (silu * up).astype(BF)
        gate_grad = (hidden_grad * up * (s * (1.0 + gate * (1.0 - s)))).astype(BF)
        up_grad = (hidden_grad * silu).astype(BF)
        hidden_slot[slot] = hidden.T
        gate_slot[slot] = gate_grad
        up_slot[slot] = up_grad
        for copy in slot_copies(slot, f):
            copy.start()
        middle[...] = middle[...] + dot_nn(hidden, w_down[here])
        back[...] = back[...] + (dot_nt(gate_grad, w_gate[:, here]) + dot_nt(up_grad, w_up[:, here]))
        return 0

    blocks = hidden_cols // width
    per_group = blocks // groups
    for g in range(groups):
        wait_all(group_copies[g])
        lax.fori_loop(g * per_group, (g + 1) * per_group, one_block, 0)
    output_ref[...] = middle[...].astype(BF)
    middle_rows = x_ref[...].astype(F32) + dot_nn(mixed[...], w_out[...])
    part, gain_sum = norm_back(middle_rows, gain, back[...])
    gain_grad_ref[...] = gain_sum
    middle_grad = dy_ref[...].astype(F32) + part
    middle_grad_ref[...] = middle_grad
    middle_low = middle_grad.astype(BF)
    middle_low_ref[...] = middle_low
    grad_low[...] = dot_nt(middle_low, w_out[...]).astype(BF)
    pack_blocks(z, nz, grad_low, grad_blocks, (grad_low.shape[1],))
    for f in (blocks - 2, blocks - 1):
        wait_all(slot_copies(f % 2, f))


def weight_grad_kernel(dims, ids, left_ref, right_ref, *refs):
    chips, parts = dims
    if chips == 0:
        refs[0][...] = dot_nn(left_ref[...], right_ref[...]).astype(BF)
        return
    outs, (ordered,) = refs[:-1], refs[-1:]
    me = ids[1]
    chip, core = lax.div(me, 2), lax.rem(me, 2)
    rows = left_ref.shape[0] // (2 * chips)

    @pl.when(pl.program_id(0) == 0)
    def _():
        for side in range(2):
            owner_core = 1 - core if side == 0 else core
            for r in range(chips):
                owner = (chip ^ r) * 2 + owner_core
                to = (side * chips + r) * rows
                ordered[to : to + rows] = left_ref[pl.ds(pl.multiple_of(owner * rows, rows), rows)]

    right = right_ref[...]
    part = rows // parts
    for side in range(2):
        got = dot_nn(ordered[side * chips * rows : (side + 1) * chips * rows], right).astype(BF)
        for r in range(chips):
            for p in range(parts):
                first = r * rows + p * part
                outs[side * parts + p][r] = got[first : first + part]


def weight_grad(ids, left, right, chips, parts=1, width=512):
    rows, tokens = left.shape
    cols = right.shape[1]
    width = min(width, cols)
    if chips:
        part = rows // (2 * chips * parts)
        outs = [shape_of((chips, part, cols), BF)] * (2 * parts)
        out_specs = [pl.BlockSpec((chips, part, width), lambda n: (0, 0, n))] * (2 * parts)
        scratch = [pltpu.VMEM((rows, tokens), BF)]
    else:
        outs = [shape_of((rows, cols), BF)]
        out_specs = [pl.BlockSpec((rows, width), lambda n: (0, n))]
        scratch = []
    return call(
        functools.partial(weight_grad_kernel, (chips, parts)),
        outs,
        [SMEM, pl.BlockSpec((rows, tokens), lambda n: (0, 0)), pl.BlockSpec((tokens, width), lambda n: (0, n))],
        out_specs,
        scratch,
        2 * rows * tokens * cols,
        2 * (rows * tokens + tokens * cols + rows * cols),
        grid=(cols // width,),
    )(ids, left, right)


def post_kernel(dims, ids, x_ref, middle_grad_ref, gains_ref, cos_ref, sin_ref, proj_ref, *refs):
    nz, head_dim, q_cols, k_cols, v_cols = dims
    blocks, refs = refs[:nz], refs[nz:]
    qk_hbm, vo_hbm = refs[:2]
    input_grad_ref, first_ref, second_ref, gain_grad_ref, head_gain_grad_ref = refs[2:7]
    w_qk, w_v, qkv, sems = refs[7:]
    z = ids[0]
    fetch = Fetch(sems)
    copies = [fetch.start(qk_hbm, w_qk), fetch.start(vo_hbm.at[:, pl.ds(0, v_cols)], w_v)]
    block_copies = []
    for j in range(nz):
        base, at = 0, 0
        for width in (q_cols, k_cols, v_cols):
            part = width // nz
            to = pl.multiple_of(base + (z ^ j) * part, part)
            block_copies.append(fetch.start(blocks[j].at[:, pl.ds(at, part)], qkv.at[:, pl.ds(to, part)]))
            base, at = base + width, at + part
    wait_all(block_copies)
    width = 256
    mask = head_mask(width, head_dim)
    cos = jnp.concatenate([cos_ref[...]] * (width // 128), axis=1)
    sin = jnp.concatenate([sin_ref[...]] * (width // 128), axis=1)
    for start in range(0, q_cols + k_cols, width):
        cols = slice(start, start + width)
        rotated = qkv[:, cols].astype(F32)
        gradient = rotated * cos - partner(rotated, head_dim) * sin
        proj = proj_ref[:, cols]
        scale = lax.rsqrt(head_sum(proj * proj, mask) * (1.0 / head_dim) + EPSILON)
        n = proj * scale
        u = gradient * gains_ref[1:2, cols]
        head_gain_grad_ref[:, cols] = jnp.sum(gradient * n, axis=0, keepdims=True)
        low = (scale * (u - n * (head_sum(u * n, mask) * (1.0 / head_dim)))).astype(BF)
        qkv[:, cols] = low
    first_ref[...] = qkv[:, :q_cols]
    second_ref[...] = qkv[:, q_cols:]
    wait_all(copies)
    normed_grad = dot_nt(qkv[:, : q_cols + k_cols], w_qk[...]) + dot_nt(qkv[:, q_cols + k_cols :], w_v[...])
    part, gain_sum = norm_back(x_ref[...].astype(F32), gains_ref[0:1, : x_ref.shape[1]], normed_grad)
    gain_grad_ref[...] = gain_sum
    input_grad_ref[...] = (middle_grad_ref[...] + part).astype(BF)


def add(a, b):
    return (a.astype(F32) + b.astype(F32)).astype(a.dtype)


def swap(values, axis, size, bit):
    return lax.ppermute(values, axis, [(i, i ^ bit) for i in range(size)])


def reduce_plane(theirs, mine, x_first):
    got = swap(theirs, "fsdp", 8, 1)
    if x_first:
        away, kept, bits = (1, 3), (0, 2), (2, 4)
    else:
        away, kept, bits = (2, 3), (0, 1), (4, 2)
    send = jnp.stack([add(mine[r], got[r]) for r in away])
    keep = [add(mine[r], got[r]) for r in kept]
    back = swap(send, "fsdp", 8, bits[0])
    last = swap(add(keep[1], back[1]), "fsdp", 8, bits[1])
    return add(add(keep[0], back[0]), last)


def sum_line(values):
    size = lax.axis_size("seq")
    if size != 4:
        return lax.psum(values, "seq")
    z = lax.axis_index("seq")
    inner = add(values, lax.ppermute(values, "seq", [(0, 1), (3, 2)]))
    total = add(inner, lax.ppermute(inner, "seq", [(1, 2), (2, 1)]))
    outer = lax.ppermute(total, "seq", [(1, 0), (2, 3)])
    return jnp.where((z == 1) | (z == 2), total, outer)


def flip_to_order(values, me):
    grid = values.reshape((2, 2, 2) + values.shape[1:])
    for axis, bit in enumerate((4, 2, 1)):
        grid = jnp.where((me & bit) != 0, jnp.flip(grid, axis), grid)
    return grid.reshape(values.shape)


def per_device(
    inputs,
    positions,
    cotangent,
    query_weight,
    key_weight,
    value_weight,
    out_weight,
    attention_gain,
    query_gain,
    key_gain,
    feedforward_gain,
    gate_weight,
    up_weight,
    down_weight,
):
    seqs, tokens, model = inputs.shape
    assert seqs == 1
    fsdp, nz = lax.axis_size("fsdp"), lax.axis_size("seq")
    me, z = lax.axis_index("fsdp"), lax.axis_index("seq")
    plane = fsdp == 8
    ids = jnp.stack([z, me]).astype(jnp.int32)
    x = inputs.reshape(tokens, model)
    dy = cotangent.reshape(tokens, model)
    head_dim = query_gain.shape[0] * fsdp
    q_cols, k_cols, v_cols = query_weight.shape[1], key_weight.shape[1], value_weight.shape[1]
    heads, kv_heads = q_cols // head_dim // nz, k_cols // head_dim // nz
    hidden_cols = gate_weight.shape[1]
    seq_len = tokens * nz

    first = jnp.concatenate([query_weight, key_weight], axis=1)
    second = jnp.concatenate([value_weight, out_weight], axis=1)
    wide_cols = q_cols + k_cols

    def spread(values, count):
        share = values.shape[0]
        row = lax.dynamic_update_slice(jnp.zeros((share * fsdp,), BF), values, (me * share,))
        return jnp.tile(row, count)

    head_row = jnp.concatenate([spread(query_gain, q_cols // head_dim), spread(key_gain, k_cols // head_dim)])
    fill = jnp.zeros((wide_cols - model,), BF)
    gain_rows = [jnp.concatenate([spread(attention_gain, 1), fill]), head_row]
    gain_rows += [jnp.concatenate([spread(feedforward_gain, 1), fill])] + [jnp.zeros((wide_cols,), BF)] * 13
    gain_rows = jnp.stack(gain_rows)
    if plane:
        given = [jnp.concatenate([first, gain_rows]), second, gate_weight, up_weight, down_weight]
        given.append(jnp.zeros((8, 128), F32))
    else:
        gather = functools.partial(lax.all_gather, axis_name="fsdp", axis=0, tiled=True)
        qk_full, vo_full, gate_full = gather(first), gather(second), gather(gate_weight)
        up_full, down_full = gather(up_weight), gather(down_weight)
        given = [qk_full, vo_full, lax.psum(gain_rows.astype(F32), "fsdp")]

    half_dim = head_dim // 2
    freqs = ROPE_BASE ** (-jnp.arange(half_dim, dtype=F32) / half_dim)
    angles = positions.reshape(tokens).astype(F32)[:, None] * freqs[None, :]
    cosine, sine = jnp.cos(angles), jnp.sin(angles)
    cosine = jnp.tile(cosine, (1, 128 // half_dim))
    sine = jnp.tile(jnp.concatenate([-sine, sine], axis=1), (1, 128 // head_dim))

    dims = (nz, plane, head_dim, q_cols, k_cols, v_cols, min(256, seq_len))
    block_cols = (q_cols + k_cols + v_cols) // nz
    mixed_cols = heads * head_dim
    head_scratch = [
        pltpu.VMEM((heads, seq_len, head_dim), BF),
        pltpu.VMEM((kv_heads, seq_len, head_dim), BF),
        pltpu.VMEM((kv_heads, seq_len, head_dim), BF),
    ]
    attend_flops = 2 * heads * seq_len * seq_len * head_dim
    proj_flops = 2 * tokens * model * (q_cols + k_cols + v_cols)
    outs = [
        shape_of((16, wide_cols), F32),
        shape_of((model, tokens), BF),
        shape_of((tokens, wide_cols), F32),
        shape_of((seq_len, block_cols), BF),
        shape_of((tokens, q_cols), BF),
        shape_of((heads, seq_len, head_dim), F32),
        shape_of((heads, 8, seq_len), F32),
    ]
    n_links = 3 * (nz - 1) + nz - 1
    qk_rows = model
    if plane:
        hidden = gate_weight.shape[1]
        outs += [shape_of((model, wide_cols), BF), shape_of((model, v_cols + model), BF)]
        outs += [shape_of((model, hidden), BF)] * 2 + [shape_of((2, hidden // 2, model), BF)]
        n_links += 6 * 7
        qk_rows += 8 * 16
    got = call(
        functools.partial(forward_kernel, dims),
        outs,
        [VMEM] * 3 + ([ANY] * 5 + [VMEM] if plane else [ANY] * 2 + [VMEM]),
        [VMEM] * 7 + [ANY] * (len(outs) - 7),
        [
            pltpu.VMEM((qk_rows, wide_cols), BF),
            pltpu.VMEM((model, v_cols + model), BF),
            pltpu.VMEM((tokens, model), BF),
            pltpu.VMEM((tokens, q_cols + k_cols + v_cols), BF),
        ]
        + head_scratch
        + [
            pltpu.VMEM((seq_len, mixed_cols), BF),
            pltpu.SemaphoreType.DMA((24,)),
            pltpu.SemaphoreType.DMA((n_links,)),
            pltpu.SemaphoreType.DMA((n_links,)),
        ],
        proj_flops + 4 * attend_flops,
        60 * 2**20,
        collective=1,
    )(x, cosine, sine, *given)
    gains, normed_t, proj, head_rows, mixed, full, logs = got[:7]
    if plane:
        qk_full, vo_full, gate_full, up_full, down_full = got[7:]

    width = 512
    groups = 3
    rows_model = lambda kind: shape_of((tokens, model), kind)
    feed_out = call(
        functools.partial(feed_kernel, (nz, (v_cols, model), width, groups)),
        [
            rows_model(BF),
            rows_model(F32),
            rows_model(BF),
            shape_of((model, tokens), BF),
            shape_of((model, tokens), BF),
            shape_of((1, model), F32),
        ]
        + [shape_of((tokens, mixed_cols), BF)] * nz
        + [shape_of((hidden_cols, tokens), BF)]
        + [shape_of((tokens, hidden_cols), BF)] * 2,
        [SMEM] + [VMEM] * 4 + [ANY] * 4,
        [VMEM] * (6 + nz) + [ANY] * 3,
        [
            pltpu.VMEM((q_cols, model), BF),
            pltpu.VMEM((model, hidden_cols), BF),
            pltpu.VMEM((model, hidden_cols), BF),
            pltpu.VMEM((hidden_cols, model), BF),
            pltpu.VMEM((tokens, q_cols), BF),
            pltpu.VMEM((tokens, model), F32),
            pltpu.VMEM((tokens, model), BF),
            pltpu.VMEM((tokens, model), F32),
            pltpu.VMEM((2, width, tokens), BF),
            pltpu.VMEM((2, tokens, width), BF),
            pltpu.VMEM((2, tokens, width), BF),
            pltpu.SemaphoreType.DMA((17 + 2 * groups,)),
            pltpu.SemaphoreType.DMA((2, 3)),
        ],
        12 * tokens * model * hidden_cols,
        50 * 2**20,
    )(ids, x, dy, gains, mixed, vo_full, gate_full, up_full, down_full)
    output, middle_grad, middle_low, mixed_t, normed_two_t, feed_gain_part = feed_out[:6]
    mixed_grad = feed_out[6 : 6 + nz]
    hidden_t, gate_grad, up_grad = feed_out[6 + nz :]
    mixed_grad = [mixed_grad[0]] + [swap(mixed_grad[j], "seq", nz, j) for j in range(1, nz)]

    chips = 4 if plane else 0

    def scatter(values):
        return lax.psum_scatter(values, "fsdp", scatter_dimension=0, tiled=True)

    if plane:
        down_tu, down_tl, down_mu, down_ml = weight_grad(ids, hidden_t, dy, chips, parts=2, width=256)
        gate_t, gate_m = weight_grad(ids, normed_two_t, gate_grad, chips)
        up_t, up_m = weight_grad(ids, normed_two_t, up_grad, chips)
        out_t, out_m = weight_grad(ids, mixed_t, middle_low, chips)
        down_shard = jnp.concatenate(
            [sum_line(reduce_plane(down_tu, down_mu, True)), sum_line(reduce_plane(down_tl, down_ml, False))]
        )
        gate_shard = sum_line(reduce_plane(gate_t, gate_m, True))
        up_shard = sum_line(reduce_plane(up_t, up_m, False))
        out_shard = sum_line(reduce_plane(out_t, out_m, True))
    else:
        down_shard = sum_line(scatter(weight_grad(ids, hidden_t, dy, chips, width=256)[0]))
        gate_shard = sum_line(scatter(weight_grad(ids, normed_two_t, gate_grad, chips)[0]))
        up_shard = sum_line(scatter(weight_grad(ids, normed_two_t, up_grad, chips)[0]))
        out_shard = sum_line(scatter(weight_grad(ids, mixed_t, middle_low, chips)[0]))

    grads = call(
        functools.partial(attend_back_kernel, (nz, min(256, seq_len), min(1024, seq_len))),
        [shape_of((tokens, block_cols), BF)] * nz,
        [SMEM] + [VMEM] * 3 + [ANY] * nz,
        [VMEM] * nz,
        [pltpu.VMEM((seq_len, mixed_cols), BF)]
        + head_scratch
        + [
            pltpu.VMEM((heads, seq_len, head_dim), BF),
            pltpu.VMEM((heads, 8, seq_len), F32),
            pltpu.VMEM((heads, seq_len, head_dim), F32),
            pltpu.VMEM((kv_heads, seq_len, head_dim), BF),
            pltpu.VMEM((kv_heads, seq_len, head_dim), BF),
            pltpu.SemaphoreType.DMA((nz,)),
        ],
        10 * attend_flops,
        20 * 2**20,
    )(ids, head_rows, full, logs, *mixed_grad)
    grads = [grads[0]] + [swap(grads[j], "seq", nz, j) for j in range(1, nz)]

    input_grad, q_grad, kv_grad, attention_gain_part, head_gain_part = call(
        functools.partial(post_kernel, (nz, head_dim, q_cols, k_cols, v_cols)),
        [
            rows_model(BF),
            shape_of((tokens, q_cols), BF),
            shape_of((tokens, k_cols + v_cols), BF),
            shape_of((1, model), F32),
            shape_of((1, q_cols + k_cols), F32),
        ],
        [SMEM] + [VMEM] * 6 + [ANY] * (nz + 2),
        [VMEM] * 5,
        [
            pltpu.VMEM((model, wide_cols), BF),
            pltpu.VMEM((model, v_cols), BF),
            pltpu.VMEM((tokens, wide_cols + v_cols), BF),
            pltpu.SemaphoreType.DMA((2 + 3 * nz,)),
        ],
        proj_flops,
        14 * 2**20,
    )(ids, x, middle_grad, gains, cosine, sine, proj, *grads, qk_full, vo_full)
    if plane:
        q_t, q_m = weight_grad(ids, normed_t, q_grad, chips)
        kv_t, kv_m = weight_grad(ids, normed_t, kv_grad, chips)
        q_shard = sum_line(reduce_plane(q_t, q_m, True))
        kv_shard = sum_line(reduce_plane(kv_t, kv_m, False))
    else:
        q_shard = sum_line(scatter(weight_grad(ids, normed_t, q_grad, chips)[0]))
        kv_shard = sum_line(scatter(weight_grad(ids, normed_t, kv_grad, chips)[0]))

    q_part = head_gain_part[:, :q_cols].reshape(-1, head_dim).sum(axis=0)
    k_part = head_gain_part[:, q_cols:].reshape(-1, head_dim).sum(axis=0)
    gain_parts = jnp.concatenate(
        [v.reshape(fsdp, -1) for v in (attention_gain_part, q_part, k_part, feed_gain_part)], axis=1
    )
    if plane:
        ordered = flip_to_order(gain_parts, me).reshape(4, 2, 1, -1)
        gain_shard = sum_line(reduce_plane(ordered[:, 1], ordered[:, 0], True)).reshape(-1)
    else:
        gain_shard = sum_line(scatter(gain_parts).reshape(-1))
    n_a, n_h = attention_gain.shape[0], query_gain.shape[0]
    cuts = (n_a, n_a + n_h, n_a + 2 * n_h)
    wide = lambda v: v.astype(F32)
    return (
        output.reshape(inputs.shape),
        input_grad.reshape(inputs.shape),
        wide(q_shard),
        wide(kv_shard[:, :k_cols]),
        wide(kv_shard[:, k_cols:]),
        wide(out_shard),
        gain_shard[: cuts[0]],
        gain_shard[cuts[0] : cuts[1]],
        gain_shard[cuts[1] : cuts[2]],
        gain_shard[cuts[2] :],
        wide(gate_shard),
        wide(up_shard),
        wide(down_shard),
    )


def solution(mesh):
    tokens, rows, row = P("fsdp", "seq", None), P("fsdp", None), P("fsdp")
    in_specs = (tokens, P("fsdp", "seq"), tokens) + (rows,) * 4 + (row,) * 4 + (rows,) * 3
    out_specs = (tokens, tokens) + (rows,) * 4 + (row,) * 4 + (rows,) * 3
    return jax.shard_map(per_device, mesh=mesh, in_specs=in_specs, out_specs=out_specs, check_vma=False)
```

```python
import functools

import jax
import jax.numpy as jnp
from jax import lax
from jax.experimental import pallas as pl
from jax.experimental.pallas import tpu as pltpu
from jax.sharding import PartitionSpec as P

EPSILON = 1e-05
ROPE_BASE = 1000000.0
LOG2E = 1.4426950408889634
BF = jnp.bfloat16
F32 = jnp.float32
VMEM = pl.BlockSpec(memory_space=pltpu.VMEM)
SMEM = pl.BlockSpec(memory_space=pltpu.SMEM)
ANY = pl.BlockSpec(memory_space=pl.ANY)
VMEM_BYTES = 62 * 2**20


def dot_nn(a, b):
    return lax.dot_general(a, b, (((1,), (0,)), ((), ())), preferred_element_type=F32)


def dot_nt(a, b):
    return lax.dot_general(a, b, (((1,), (1,)), ((), ())), preferred_element_type=F32)


def dot_tn(a, b):
    return lax.dot_general(a, b, (((0,), (0,)), ((), ())), preferred_element_type=F32)


def shape_of(shape, dtype):
    return jax.ShapeDtypeStruct(shape, dtype)


def call(kernel, outs, in_specs, out_specs, scratch, flops, moved, collective=None, **more):
    params = {} if collective is None else {"collective_id": collective, "has_side_effects": True}
    return pl.pallas_call(
        kernel,
        out_shape=outs,
        in_specs=in_specs,
        out_specs=out_specs,
        scratch_shapes=scratch,
        compiler_params=pltpu.CompilerParams(vmem_limit_bytes=VMEM_BYTES, **params),
        cost_estimate=pl.CostEstimate(flops=flops, bytes_accessed=moved, transcendentals=0),
        **more,
    )


def row_norm(values):
    return lax.rsqrt(jnp.mean(values * values, axis=-1, keepdims=True) + EPSILON)


class Fetch:
    def __init__(self, sems):
        self.sems, self.used = sems, 0

    def start(self, source, target):
        copy = pltpu.make_async_copy(source, target, self.sems.at[self.used])
        copy.start()
        self.used += 1
        return copy


def wait_all(copies):
    for copy in copies:
        copy.wait()


def head_mask(width, head_dim):
    rows = lax.broadcasted_iota(jnp.int32, (width, width), 0) // head_dim
    cols = lax.broadcasted_iota(jnp.int32, (width, width), 1) // head_dim
    return (rows == cols).astype(BF)


def head_sum(values, mask):
    high = values.astype(BF)
    rest = (values - high.astype(F32)).astype(BF)
    return dot_nn(high, mask) + dot_nn(rest, mask)


def partner(values, head_dim):
    half = head_dim // 2
    width = values.shape[-1]
    lane = lax.broadcasted_iota(jnp.int32, values.shape, 1)
    after = pltpu.roll(values, width - half, 1)
    before = pltpu.roll(values, half, 1)
    return jnp.where(lane % head_dim < half, after, before)


def pack_blocks(z, nz, source, blocks, widths):
    for j, block in enumerate(blocks):
        owner = z ^ j
        base, at = 0, 0
        for width in widths:
            part = width // nz
            block[:, at : at + part] = source[:, pl.ds(pl.multiple_of(base + owner * part, part), part)]
            base, at = base + width, at + part


class Links:
    def __init__(self, send_sems, recv_sems):
        self.sems, self.used, self.started = (send_sems, recv_sems), 0, []

    def reserve(self, count):
        self.used += count
        return self.used - count

    def copy(self, source, target, device, at=None):
        at = self.reserve(1) if at is None else at
        return pltpu.make_async_remote_copy(
            src_ref=source,
            dst_ref=target,
            send_sem=self.sems[0].at[at],
            recv_sem=self.sems[1].at[at],
            device_id=device,
            device_id_type=pl.DeviceIdType.MESH,
        )

    def start(self, source, target, device):
        copy = self.copy(source, target, device)
        copy.start()
        self.started.append(copy)
        return copy

    def wait_sends(self):
        for copy in self.started:
            copy.wait_send()


def enter(me, z, nz, plane):
    barrier = pltpu.get_barrier_semaphore()
    peers = [{"seq": z ^ j} for j in range(1, nz)]
    if plane:
        peers += [{"fsdp": me ^ bit} for bit in (1, 2, 4)]
    for peer in peers:
        pl.semaphore_signal(barrier, inc=1, device_id=peer, device_id_type=pl.DeviceIdType.MESH)
    pl.semaphore_wait(barrier, len(peers))


class Gather:
    def __init__(self, links, me, own, whole, x_first):
        self.links, self.me, self.own, self.whole = links, me, own, whole
        self.rows = own.shape[0]
        self.near, self.other = (2, 4) if x_first else (4, 2)

    def block(self, b):
        return self.whole.at[pl.ds(pl.multiple_of((self.me ^ b) * self.rows, self.rows), self.rows)]

    def pass_on(self, b, bit):
        source = self.own if b == 0 else self.block(b)
        return self.links.start(source, self.block(b), {"fsdp": self.me ^ bit})

    def begin(self):
        self.first = self.pass_on(0, self.near)
        self.second = self.pass_on(0, self.other)
        self.to_core = [self.pass_on(0, 1)]

    def forward_first(self):
        self.first.wait_recv()
        self.far = self.pass_on(self.near, self.other)
        self.to_core.append(self.pass_on(self.near, 1))

    def forward_second(self):
        self.second.wait_recv()
        self.to_core.append(self.pass_on(self.other, 1))

    def forward_far(self):
        self.far.wait_recv()
        self.to_core.append(self.pass_on(self.near + self.other, 1))

    def end(self):
        for copy in self.to_core:
            copy.wait_recv()


def forward_first(gathers):
    for gather in gathers:
        gather.forward_first()
    for gather in gathers:
        gather.forward_second()


def forward_far(gathers):
    for gather in gathers:
        gather.forward_far()


def forward_kernel(dims, x_ref, cos_ref, sin_ref, *refs):
    nz, plane, head_dim, q_cols, k_cols, v_cols, rows = dims
    n_in = 5 if plane else 3
    given, refs = refs[:n_in], refs[n_in:]
    gains_ref, proj_ref, heads_ref, mixed_ref, log_ref, normed_t_hbm = refs[:6]
    refs = refs[6:]
    if plane:
        qk_hbm, vo_hbm, gate_hbm, up_hbm, down_hbm = refs[:5]
        refs = refs[5:]
    w_qk, w_vo, normed, normed_t, qkv, queries, keys, values, full, mix, local_sems, send_sems, recv_sems = refs
    z, me = lax.axis_index("seq"), lax.axis_index("fsdp")
    model = w_vo.shape[0]
    tokens = x_ref.shape[0]
    enter(me, z, nz, plane)
    links = Links(send_sems, recv_sems)
    local = []

    def copy_here(source, target):
        copy = pltpu.make_async_copy(source, target, local_sems.at[len(local)])
        copy.start()
        local.append(copy)
        return copy

    if plane:
        own_qk, own_vo, own_gate, own_up, own_down = given
        half = own_down.shape[0] // 2
        attention = [Gather(links, me, own_qk, w_qk, True), Gather(links, me, own_vo, w_vo, False)]
        wide = [Gather(links, me, own_gate, gate_hbm, True), Gather(links, me, own_up, up_hbm, False)]
        for gather in attention:
            gather.begin()
        here = [copy_here(g.own, g.block(0)) for g in attention]
        down = []
        for side in range(2):
            g = Gather(links, me, own_down.at[pl.ds(side * half, half)], down_hbm.at[side], side == 0)
            down.append(g)
    else:
        here = [copy_here(given[0], w_qk), copy_here(given[1], w_vo)]
    x = x_ref[...].astype(F32)
    unit = x * row_norm(x)
    if plane:
        forward_first(attention)
        for gather in wide:
            gather.begin()
        for g in wide:
            copy_here(g.own, g.block(0))
        forward_far(attention)
        for g in attention:
            g.end()
        wait_all(here)
        stride = attention[0].rows
        shard = w_vo.shape[0] // 8
        gains = sum(w_qk[s * stride + shard : (s + 1) * stride].astype(F32) for s in range(8))
        for s in range(8):
            copy_here(w_qk.at[pl.ds(s * stride, shard)], qk_hbm.at[pl.ds(s * shard, shard)])
        copy_here(w_vo, vo_hbm)
    else:
        stride = shard = model
        wait_all(here)
        gains = given[2][...].astype(F32)
    gains_ref[...] = gains
    normed[...] = (unit * gains[0:1, :model]).astype(BF)
    width = 256
    mask = head_mask(width, head_dim)
    cos = jnp.concatenate([cos_ref[...]] * (width // 128), axis=1)
    sin = jnp.concatenate([sin_ref[...]] * (width // 128), axis=1)

    for start in range(0, q_cols + k_cols, width):
        cols = slice(start, start + width)
        if stride == shard:
            proj = dot_nn(normed[...], w_qk[:, cols])
        else:
            weight = jnp.concatenate([w_qk[s * stride : s * stride + shard, cols] for s in range(8)], axis=0)
            proj = dot_nn(normed[...], weight)
        proj_ref[:, cols] = proj
        scale = lax.rsqrt(head_sum(proj * proj, mask) * (1.0 / head_dim) + EPSILON)
        head = proj * scale * gains_ref[1:2, cols]
        qkv[:, cols] = (head * cos + partner(head, head_dim) * sin).astype(BF)
    qkv[:, q_cols + k_cols :] = dot_nn(normed[...], w_vo[:, :v_cols]).astype(BF)

    arrivals = []
    for j in range(nz):
        owner = z ^ j
        base, at = 0, 0
        for cols in (q_cols, k_cols, v_cols):
            part = cols // nz
            source = qkv.at[:, pl.ds(pl.multiple_of(base + owner * part, part), part)]
            target = heads_ref.at[pl.ds(pl.multiple_of(z * tokens, tokens), tokens), pl.ds(at, part)]
            if j == 0:
                arrivals.append(copy_here(source, target))
            else:
                arrivals.append(links.start(source, target, {"seq": owner}))
            base, at = base + cols, at + part
    normed_t[...] = normed[...].T
    if plane:
        to_core = both_cores(links, copy_here, me, normed_t, normed_t_hbm, 1)
        forward_first(wide)
        for gather in down:
            gather.begin()
        for g in down:
            copy_here(g.own, g.block(0))
    else:
        copy_here(normed_t, normed_t_hbm)
    for i, copy in enumerate(arrivals):
        if i < 3:
            copy.wait()
        else:
            copy.wait_recv()

    heads, seq_len, _ = queries.shape
    kv_heads = keys.shape[0]
    group = heads // kv_heads
    split_heads(heads_ref, 0, queries)
    split_heads(heads_ref, heads * head_dim, keys)
    split_heads(heads_ref, (heads + kv_heads) * head_dim, values)
    factor = head_dim**-0.5 * LOG2E
    part = mix.shape[1]
    first_back = links.reserve(nz)
    own_mix = local_sems.shape[0] - 1
    for r in range(seq_len // rows):
        span = slice(r * rows, (r + 1) * rows)
        reach = (r + 1) * rows

        def one_head(h, _):
            b = lax.div(h, group)
            scores = dot_nt(queries[h, span], keys[b, :reach]) * factor
            row = lax.broadcasted_iota(jnp.int32, scores.shape, 0) + r * rows
            col = lax.broadcasted_iota(jnp.int32, scores.shape, 1)
            probs = jnp.exp2(jnp.where(row >= col, scores, -1e30))
            total = jnp.sum(probs, axis=1, keepdims=True)
            full[h, span] = (dot_nn(probs.astype(BF), values[b, :reach]) * (1.0 / total)).astype(BF)
            log_ref[h, :, span] = jnp.broadcast_to(jnp.log2(total), (rows, 128)).T[0:8]
            return 0

        lax.fori_loop(0, heads, one_head, 0)
        if reach % tokens == 0:
            t = reach // tokens - 1
            mine = slice(t * tokens, reach)
            mix[mine] = jnp.concatenate([full[h, mine] for h in range(heads)], axis=1)
            target = mixed_ref.at[:, pl.ds(pl.multiple_of(z * part, part), part)]

            @pl.when(z == t)
            def _():
                pltpu.make_async_copy(mix.at[mine], target, local_sems.at[own_mix]).start()

            @pl.when(z != t)
            def _():
                links.copy(mix.at[mine], target, {"seq": t}, at=first_back + (z ^ t)).start()

    if plane:
        forward_far(wide)
        forward_first(down)
        forward_far(down)
        for gather in wide + down:
            gather.end()
        to_core.wait_recv()
    here_rows = mix.at[pl.ds(0, tokens)]
    here_cols = mixed_ref.at[:, pl.ds(0, part)]
    pltpu.make_async_copy(here_rows, here_cols, local_sems.at[own_mix]).wait()
    for j in range(1, nz):
        copy = links.copy(here_rows, here_cols, {"seq": z ^ j}, at=first_back + j)
        copy.wait_recv()
        copy.wait_send()
    links.wait_sends()
    for copy in local:
        if not any(copy is done for done in here + arrivals[:3]):
            copy.wait()


def both_cores(links, copy_here, me, source, target, axis):
    size = source.shape[axis]
    here = pl.ds(pl.multiple_of(lax.rem(me, 2) * size, size), size)
    place = target.at[here] if axis == 0 else target.at[:, here]
    copy_here(source, place)
    return links.start(source, place, {"fsdp": me ^ 1})


def split_heads(scratch, first, heads):
    head_dim = heads.shape[-1]
    for h in range(heads.shape[0]):
        heads[h] = scratch[:, first + h * head_dim : first + (h + 1) * head_dim]


def attend_back(dims, heads_ref, grads_ref, log_ref, delta_ref, packed, scratch, after):
    rows, chunk = dims
    queries, keys, values, grad, q_grad, k_grad, v_grad = scratch
    heads, seq_len, head_dim = queries.shape
    kv_heads = keys.shape[0]
    group = heads // kv_heads
    split_heads(heads_ref, 0, queries)
    split_heads(heads_ref, heads * head_dim, keys)
    split_heads(heads_ref, (heads + kv_heads) * head_dim, values)
    split_heads(grads_ref, 0, grad)
    factor = head_dim**-0.5
    scale = factor * LOG2E
    for h in range(heads):
        q_grad[h] = jnp.zeros((seq_len, head_dim), F32)
    for at in range(seq_len // rows):
        span = slice(at * rows, (at + 1) * rows)

        def one_head(b, _):
            key, value = keys[b, span], values[b, span]
            key_total = jnp.zeros((rows, head_dim), F32)
            value_total = jnp.zeros((rows, head_dim), F32)
            for g in range(group):
                h = b * group + g
                for first in range(at * rows, seq_len, chunk):
                    last = min(first + chunk, seq_len)
                    part = slice(first, last)
                    query, out_grad = queries[h, part], grad[h, part]
                    scores = dot_nt(key, query) * scale - log_ref[h, 0:1, part]
                    if first == at * rows:
                        key_at = lax.broadcasted_iota(jnp.int32, scores.shape, 0) + at * rows
                        query_at = lax.broadcasted_iota(jnp.int32, scores.shape, 1) + first
                        scores = jnp.where(query_at >= key_at, scores, -1e30)
                    probs = jnp.exp2(scores)
                    prob_grad = dot_nt(value, out_grad)
                    score_grad = (probs * (prob_grad - delta_ref[h, 0:1, part])).astype(BF)
                    value_total = value_total + dot_nn(probs.astype(BF), out_grad)
                    key_total = key_total + dot_nn(score_grad, query)
                    q_grad[h, part] = q_grad[h, part] + dot_tn(score_grad, key)
            k_grad[b, span] = (key_total * factor).astype(BF)
            v_grad[b, span] = value_total.astype(BF)
            return 0

        lax.fori_loop(0, kv_heads, one_head, 0)
        parts = [(q_grad[h, span] * factor).astype(BF) for h in range(heads)]
        parts += [k_grad[b, span] for b in range(kv_heads)] + [v_grad[b, span] for b in range(kv_heads)]
        packed[span] = jnp.concatenate(parts, axis=1)
        after(at)


def attend_back_scratch(heads, kv_heads, seq_len, head_dim):
    rows = lambda count, kind: pltpu.VMEM((count, seq_len, head_dim), kind)
    return [rows(heads, BF), rows(kv_heads, BF), rows(kv_heads, BF), rows(heads, BF), rows(heads, F32), rows(kv_heads, BF), rows(kv_heads, BF)]


def attend_back_kernel(dims, heads_ref, grads_ref, log_ref, delta_ref, packed, *scratch):
    attend_back(dims, heads_ref, grads_ref, log_ref, delta_ref, packed, scratch, lambda at: None)


def norm_back(rows, gain, gradient):
    q = row_norm(rows)
    n = rows * q
    u = gradient * gain
    return q * (u - n * jnp.mean(u * n, axis=-1, keepdims=True)), jnp.sum(gradient * n, axis=0, keepdims=True)


def feed_kernel(dims, x_ref, dy_ref, gains_ref, mixed, *refs):
    nz, plane, head_dim, out_cols, width, groups = dims
    vo_hbm, gate_hbm, up_hbm, down_hbm = refs[:4]
    output_ref, middle_grad_ref, middle_low_ref, gain_grad_ref, grad_low, delta_ref = refs[4:10]
    mixed_t_hbm, normed_t_hbm, hidden_hbm, gate_grad_hbm, up_grad_hbm, dy_hbm = refs[10:16]
    w_out, w_gate, w_up, w_down, transposed, middle, normed, back = refs[16:24]
    hidden_slot, gate_slot, up_slot, sems, slot_sems, send_sems, recv_sems, slot_sends, block_recvs = refs[24:]
    me = lax.axis_index("fsdp")
    tokens = x_ref.shape[0]
    core = lax.rem(me, 2) if plane else 0
    place = pl.ds(pl.multiple_of(core * tokens, tokens), tokens)
    sibling = {"fsdp": me ^ 1}
    links = Links(send_sems, recv_sems)
    if plane:
        barrier = pltpu.get_barrier_semaphore()
        pl.semaphore_signal(barrier, inc=1, device_id=sibling, device_id_type=pl.DeviceIdType.MESH)
        pl.semaphore_wait(barrier, 1)
    local, to_core = [], []

    def share(source, target):
        local.append(fetch.start(source, target))
        if plane:
            to_core.append(links.start(source, target, sibling))

    fetch = Fetch(sems)
    model, hidden_cols = w_gate.shape
    gain = gains_ref[2:3, :model]
    early = [fetch.start(vo_hbm.at[:, pl.ds(*out_cols)], w_out)]
    down_copies = []
    if len(down_hbm.shape) == 2:
        down_copies.append(fetch.start(down_hbm, w_down))
    else:
        half = hidden_cols // 16
        for owner in range(8):
            for side in range(2):
                target = w_down.at[pl.ds((2 * owner + side) * half, half)]
                down_copies.append(fetch.start(down_hbm.at[side, pl.ds(owner * half, half)], target))
    group_cols = hidden_cols // groups
    group_copies = []
    for g in range(groups):
        cols = pl.ds(g * group_cols, group_cols)
        group_copies.append([fetch.start(a.at[:, cols], b.at[:, cols]) for a, b in ((gate_hbm, w_gate), (up_hbm, w_up))])
    wait_all(early)
    x = x_ref[...].astype(F32)
    mixed_rows = mixed[...]
    transposed[0] = mixed_rows.T
    share(transposed.at[0], mixed_t_hbm.at[:, place])
    share(dy_ref, dy_hbm.at[place])
    middle_rows = x + dot_nn(mixed_rows, w_out[...])
    normed_rows = (middle_rows * row_norm(middle_rows) * gain).astype(BF)
    normed[...] = normed_rows
    transposed[1] = normed_rows.T
    share(transposed.at[1], normed_t_hbm.at[:, place])
    middle[...] = middle_rows
    back[...] = jnp.zeros(back.shape, F32)
    wait_all(down_copies)

    def slot_places(f):
        here = pl.ds(pl.multiple_of(f * width, width), width)
        return (
            (hidden_slot, hidden_hbm.at[here, place]),
            (gate_slot, gate_grad_hbm.at[place, here]),
            (up_slot, up_grad_hbm.at[place, here]),
        )

    def slot_copies(slot, f):
        return [
            pltpu.make_async_copy(s.at[slot], target, slot_sems.at[slot, i]) for i, (s, target) in enumerate(slot_places(f))
        ]

    def slot_links(slot, f):
        if not plane:
            return []
        return [
            pltpu.make_async_remote_copy(
                src_ref=s.at[slot],
                dst_ref=target,
                send_sem=slot_sends.at[slot, i],
                recv_sem=block_recvs.at[f, i],
                device_id=sibling,
                device_id_type=pl.DeviceIdType.MESH,
            )
            for i, (s, target) in enumerate(slot_places(f))
        ]

    def wait_slot(slot, f):
        wait_all(slot_copies(slot, f))
        for copy in slot_links(slot, f):
            copy.wait_send()

    def one_block(f, _):
        slot = lax.rem(f, 2)
        here = pl.ds(pl.multiple_of(f * width, width), width)

        @pl.when(f >= 2)
        def _():
            wait_slot(slot, f - 2)

        gate = dot_nn(normed[...], w_gate[:, here])
        up = dot_nn(normed[...], w_up[:, here])
        hidden_grad = dot_nt(dy_ref[...], w_down[here])
        s = 1.0 / (1.0 + jnp.exp(-gate))
        silu = gate * s
        hidden = (silu * up).astype(BF)
        gate_grad = (hidden_grad * up * (s * (1.0 + gate * (1.0 - s)))).astype(BF)
        up_grad = (hidden_grad * silu).astype(BF)
        hidden_slot[slot] = hidden.T
        gate_slot[slot] = gate_grad
        up_slot[slot] = up_grad
        for copy in slot_copies(slot, f) + slot_links(slot, f):
            copy.start()
        middle[...] = middle[...] + dot_nn(hidden, w_down[here])
        back[...] = back[...] + (dot_nt(gate_grad, w_gate[:, here]) + dot_nt(up_grad, w_up[:, here]))
        return 0

    blocks = hidden_cols // width
    per_group = blocks // groups
    for g in range(groups):
        wait_all(group_copies[g])
        lax.fori_loop(g * per_group, (g + 1) * per_group, one_block, 0)
    output_ref[...] = middle[...].astype(BF)
    middle_rows = x_ref[...].astype(F32) + dot_nn(mixed[...], w_out[...])
    part, gain_sum = norm_back(middle_rows, gain, back[...])
    gain_grad_ref[...] = gain_sum
    middle_grad = dy_ref[...].astype(F32) + part
    middle_grad_ref[...] = middle_grad
    middle_low = middle_grad.astype(BF)
    middle_low_ref[...] = middle_low
    mixed_grad = dot_nt(middle_low, w_out[...]).astype(BF)
    grad_low[...] = mixed_grad
    product = mixed_grad.astype(F32) * mixed[...].astype(F32)
    heads = mixed.shape[1] // head_dim // nz
    row = lax.broadcasted_iota(jnp.int32, (8 * nz, mixed.shape[1]), 0)
    col = lax.broadcasted_iota(jnp.int32, (8 * nz, mixed.shape[1]), 1)
    pick = ((col // head_dim == (row // 8) * heads + row % 8) & (row % 8 < heads)).astype(BF)
    high = product.astype(BF)
    delta_ref[...] = dot_nt(pick, high) + dot_nt(pick, (product - high.astype(F32)).astype(BF))
    for f in (blocks - 2, blocks - 1):
        wait_slot(f % 2, f)
    if plane:
        for f in range(blocks):
            for copy in slot_links(f % 2, f):
                copy.wait_recv()
        for copy in to_core:
            copy.wait_recv()
        links.wait_sends()
    wait_all(local)


def weight_grad_kernel(left_ref, right_ref, out_ref):
    out_ref[...] = dot_nn(left_ref[...], right_ref[...]).astype(BF)


def weight_grad(left, right, width=256):
    rows, tokens = left.shape
    cols = right.shape[1]
    return call(
        weight_grad_kernel,
        shape_of((rows, cols), BF),
        [pl.BlockSpec((rows, tokens), lambda n: (0, 0)), pl.BlockSpec((tokens, width), lambda n: (0, n))],
        pl.BlockSpec((rows, width), lambda n: (0, n)),
        [],
        2 * rows * tokens * cols,
        2 * (rows * tokens + tokens * cols + rows * cols),
        grid=(cols // width,),
    )(left, right)


def project_back(dims, x, middle_grad, gains_ref, cos_ref, sin_ref, proj_ref, qkv, weights, outs):
    head_dim, wide_cols = dims
    w_qk, w_v = weights
    input_grad_ref, gain_grad_ref, head_gain_grad_ref = outs
    width = 256
    mask = head_mask(width, head_dim)
    cos = jnp.concatenate([cos_ref[...]] * (width // 128), axis=1)
    sin = jnp.concatenate([sin_ref[...]] * (width // 128), axis=1)
    for start in range(0, wide_cols, width):
        cols = slice(start, start + width)
        rotated = qkv[:, cols].astype(F32)
        gradient = rotated * cos - partner(rotated, head_dim) * sin
        proj = proj_ref[:, cols]
        scale = lax.rsqrt(head_sum(proj * proj, mask) * (1.0 / head_dim) + EPSILON)
        n = proj * scale
        u = gradient * gains_ref[1:2, cols]
        head_gain_grad_ref[:, cols] = jnp.sum(gradient * n, axis=0, keepdims=True)
        qkv[:, cols] = (scale * (u - n * (head_sum(u * n, mask) * (1.0 / head_dim)))).astype(BF)

    def finish():
        normed_grad = dot_nt(qkv[:, :wide_cols], w_qk[...]) + dot_nt(qkv[:, wide_cols:], w_v[...])
        part, gain_sum = norm_back(x[...].astype(F32), gains_ref[0:1, : x.shape[1]], normed_grad)
        gain_grad_ref[...] = gain_sum
        input_grad_ref[...] = (middle_grad[...] + part).astype(BF)

    return finish


def post_kernel(dims, x_ref, middle_grad_ref, gains_ref, cos_ref, sin_ref, proj_ref, grads_ref, qk_ref, v_ref, *refs):
    input_grad_ref, qkv, gain_grad_ref, head_gain_grad_ref = refs
    qkv[...] = grads_ref[...]
    outs = (input_grad_ref, gain_grad_ref, head_gain_grad_ref)
    project_back(
        dims, x_ref, middle_grad_ref, gains_ref, cos_ref, sin_ref, proj_ref, qkv, (qk_ref, v_ref), outs
    )()


class Reduce:
    def __init__(self, links, fetch, me, z, x_first, away, kept, first, second, inward, across, out):
        self.links, self.fetch, self.me, self.z = links, fetch, me, z
        self.away, self.kept, self.out = away, kept, out
        self.bits = (2, 4) if x_first else (4, 2)
        order = (1, 3, 0, 2) if x_first else (2, 3, 0, 1)
        self.slots = {r: (away if i < 2 else kept, i % 2) for i, r in enumerate(order)}
        self.arrived, self.second, self.inward, self.across = first, second, inward, across
        self.outer, self.inner = (z == 0) | (z == 3), (z == 1) | (z == 2)
        self.one = links.copy(away, first, {"fsdp": me ^ self.bits[0]})
        self.two = links.copy(kept.at[1], second, {"fsdp": me ^ self.bits[1]})
        self.three = links.copy(kept.at[0], inward, {"seq": z ^ 1})
        self.four = links.copy(kept.at[0], across, {"seq": z ^ 3})
        self.five = links.copy(kept.at[1], out, {"seq": z ^ 1})

    def put(self, r, cols, values):
        ref, i = self.slots[r]
        ref[i, :, cols] = values

    def rows_of(self):
        rows = self.kept.shape[1]
        step = 32 if rows % 32 == 0 else 16
        return rows // step, step

    def by_rows(self, work):
        count, step = self.rows_of()

        def body(i, _):
            work(pl.ds(pl.multiple_of(i * step, step), step))
            return 0

        lax.fori_loop(0, count, body, 0)

    def begin(self):
        self.one.start()

    def fold_one(self):
        self.one.wait_recv()
        self.one.wait_send()
        load = self.fetch.start(self.arrived, self.away)
        load.wait()

        def work(rows):
            for i in range(2):
                self.kept[i, rows] = self.kept[i, rows] + self.away[i, rows]

        self.by_rows(work)
        self.two.start()

    def fold_two(self):
        self.two.wait_recv()

        def work(rows):
            self.kept[0, rows] = self.kept[0, rows] + self.second[rows]

        self.by_rows(work)

        @pl.when(self.outer)
        def _():
            self.three.start()

    def fold_three(self):
        @pl.when(self.inner)
        def _():
            self.three.wait_recv()

            def work(rows):
                self.kept[0, rows] = self.kept[0, rows] + self.inward[rows]

            self.by_rows(work)
            self.four.start()

    def fold_four(self):
        self.two.wait_send()
        here = pltpu.make_async_copy(self.kept.at[1], self.out, self.fetch.sems.at[self.fetch.used])
        self.fetch.used += 1

        @pl.when(self.inner)
        def _():
            self.four.wait_recv()

            def work(rows):
                self.kept[1, rows] = self.kept[0, rows] + self.across[rows]

            self.by_rows(work)
            self.five.start()
            here.start()

        self.here = here

    def end(self):
        @pl.when(self.inner)
        def _():
            self.four.wait_send()
            self.five.wait_send()
            self.here.wait()

        @pl.when(self.outer)
        def _():
            self.three.wait_send()
            self.five.wait_recv()


def each(reduces, step):
    for reduce in reduces:
        getattr(reduce, step)()


class Total:
    def __init__(self, links, me, z, sums, arrived):
        self.sums, self.arrived = sums, arrived
        peers = [{"fsdp": me ^ 1}, {"fsdp": me ^ 2}, {"fsdp": me ^ 4}, {"seq": z ^ 1}, {"seq": z ^ 2}]
        self.copies = [links.copy(sums.at[i], arrived.at[i], peer) for i, peer in enumerate(peers)]

    def begin(self, at):
        self.copies[at].start()

    def fold(self, at):
        self.copies[at].wait_recv()
        self.sums[at + 1] = self.sums[at] + self.arrived[at]

    def end(self):
        for copy in self.copies:
            copy.wait_send()


def backward_kernel(dims, gains_ref, cos_ref, sin_ref, heads_ref, log_ref, grad_low, delta_own, low_ref, feed_gain_ref, *refs):
    nz, head_dim, cols, attend_dims, names = dims
    q_cols, k_cols, v_cols = cols
    given, refs = refs[:12], refs[12:]
    x_hbm, middle_grad_hbm, proj_hbm, hidden_hbm, dy_hbm, normed_two_hbm = given[:6]
    gate_hbm, up_hbm, mixed_hbm, normed_hbm, qk_hbm, vo_hbm = given[6:]
    input_grad_ref, totals_ref = refs[:2]
    n = len(names)
    finals, refs = dict(zip(names, refs[2 : 2 + n])), refs[2 + n :]
    firsts, refs = dict(zip(names, refs[:n])), refs[n:]
    low_hbm, refs = refs[0], refs[1:]
    aways, refs = dict(zip(names, refs[:n])), refs[n:]
    kepts, refs = dict(zip(names, refs[:n])), refs[n:]
    seconds, refs = dict(zip(names, refs[:n])), refs[n:]
    inwards, refs = dict(zip(names, refs[:n])), refs[n:]
    acrosses, refs = dict(zip(names, refs[:n])), refs[n:]
    grads, delta, qkv, other_qkv, sums, sum_arrived, gain_grad, head_gain_grad, sems, send_sems, recv_sems = refs
    z, me = lax.axis_index("seq"), lax.axis_index("fsdp")
    chip, core = lax.div(me, 2), lax.rem(me, 2)
    enter(me, z, nz, True)
    links, fetch = Links(send_sems, recv_sems), Fetch(sems)
    tokens = grad_low.shape[0]
    late = []

    def copy_here(source, target):
        copy = fetch.start(source, target)
        late.append(copy)
        return copy

    part = grad_low.shape[1] // nz
    my_rows = pl.ds(pl.multiple_of(z * tokens, tokens), tokens)
    arrivals = []
    for j in range(nz):
        owner = z ^ j
        pairs = [(grad_low.at[:, pl.ds(pl.multiple_of(owner * part, part), part)], grads.at[my_rows])]
        pairs.append((delta_own.at[pl.ds(pl.multiple_of(owner * 8, 8), 8)], delta.at[:, my_rows]))
        for source, target in pairs:
            if j == 0:
                copy_here(source, target)
            else:
                arrivals.append(links.start(source, target, {"seq": owner}))
    low_arrival = both_cores(links, copy_here, me, low_ref, low_hbm, 0)
    reduces = {}
    for name in names:
        x_first = name in ("down0", "gate0", "up0", "out0", "q")
        reduces[name] = Reduce(
            links, fetch, me, z, x_first, aways[name], kepts[name], firsts[name], seconds[name], inwards[name],
            acrosses[name], finals[name],
        )
    down, gate, up, out = ([reduces[kind + str(i)] for i in range(2)] for kind in ("down", "gate", "up", "out"))
    last = [reduces["q"], reduces["kv"]]
    total = Total(links, me, z, sums, sum_arrived)
    qkv_link = links.copy(qkv, other_qkv, {"fsdp": me ^ 1})
    chips = 4
    step = 256

    def my_blocks(source, target, rows):
        copies = []
        for r in range(chips):
            owner = (chip ^ r) * 2 + core
            copies.append(fetch.start(source.at[pl.ds(pl.multiple_of(owner * rows, rows), rows)], target.at[pl.ds(r * rows, rows)]))
        return copies

    def weight_grads(hidden, dy, normed_two, right, mixed, low):
        half = down[0].kept.shape[1]
        shard = gate[0].kept.shape[1]
        width = right.shape[2]
        ready = my_blocks(hidden_hbm, hidden, 2 * half) + [fetch.start(dy_hbm, dy)]
        ready_two = my_blocks(normed_two_hbm, normed_two, shard)
        chunks = [
            (source, units, c) for source, units in ((gate_hbm, gate), (up_hbm, up)) for c in range(source.shape[1] // width)
        ]
        loads = {}

        def load(i):
            if i < len(chunks):
                source, _, c = chunks[i]
                loads[i] = fetch.start(source.at[:, pl.ds(c * width, width)], right.at[i % 2])

        load(0)
        load(1)
        ready_out = my_blocks(mixed_hbm, mixed, shard)
        wait_all(ready)

        def down_block(i, _):
            here = pl.ds(pl.multiple_of(i * step, step), step)
            for r in range(chips):
                got = dot_nn(hidden[2 * r * half : 2 * (r + 1) * half], dy[:, here]).astype(BF)
                for side in range(2):
                    down[side].put(r, here, got[side * half : (side + 1) * half])
            return 0

        lax.fori_loop(0, dy.shape[1] // step, down_block, 0)
        each(down, "begin")
        wait_all(ready_two)
        per_unit = gate[0].kept.shape[2] // width
        for i, (source, units, c) in enumerate(chunks):
            loads[i].wait()
            unit = units[c // per_unit]
            base = (c % per_unit) * width

            def wide_block(k, _):
                here = pl.ds(pl.multiple_of(k * step, step), step)
                to = pl.ds(pl.multiple_of(base + k * step, step), step)
                got = dot_nn(normed_two[...], right[i % 2, :, here]).astype(BF)
                for r in range(chips):
                    unit.put(r, to, got[r * shard : (r + 1) * shard])
                return 0

            lax.fori_loop(0, width // step, wide_block, 0)
            load(i + 2)
            if source is gate_hbm and (c + 1) % per_unit == 0:
                unit.begin()
        low_arrival.wait_recv()
        late[-1].wait()
        late.pop()
        fetch.start(low_hbm, low).wait()
        wait_all(ready_out)
        cols_out = out[0].kept.shape[2]
        for start in range(0, low.shape[1], step):
            got = dot_nn(mixed[...], low[:, start : start + step]).astype(BF)
            to = slice(start % cols_out, start % cols_out + step)
            for r in range(chips):
                out[start // cols_out].put(r, to, got[r * shard : (r + 1) * shard])

    half = kepts["down0"].shape[1]
    shard = kepts["gate0"].shape[1]
    both = 2 * tokens
    model = low_ref.shape[1]
    wide_part = kepts["gate0"].shape[2] // 3
    pl.run_scoped(
        weight_grads,
        pltpu.VMEM((2 * chips * half, both), BF),
        pltpu.VMEM((both, model), BF),
        pltpu.VMEM((chips * shard, both), BF),
        pltpu.VMEM((2, both, wide_part), BF),
        pltpu.VMEM((chips * shard, both), BF),
        pltpu.VMEM((both, model), BF),
    )
    for copy in arrivals:
        copy.wait_recv()
    wait_all(late)
    del late[:]

    seq_len, block_cols = heads_ref.shape
    rows, _ = attend_dims
    first_back = links.reserve(3 * nz)
    own_back = fetch.used
    fetch.used += 3
    widths = [c // nz for c in cols]
    bases = [0, q_cols, q_cols + k_cols]

    def pieces(source_rows, packed):
        at = 0
        for i in range(3):
            yield i, packed.at[source_rows, pl.ds(at, widths[i])], qkv.at[
                :, pl.ds(pl.multiple_of(bases[i] + z * widths[i], widths[i]), widths[i])
            ]
            at += widths[i]

    def attention(packed, delta_rows, *scratch):
        for h in range(delta_rows.shape[0]):
            delta_rows[h] = jnp.broadcast_to(delta[h : h + 1], (8, seq_len))

        def after(at):
            reach = (at + 1) * rows
            if reach % tokens == 0:
                t = reach // tokens - 1
                mine = pl.ds(t * tokens, tokens)

                @pl.when(z == t)
                def _():
                    for i, source, target in pieces(mine, packed):
                        pltpu.make_async_copy(source, target, sems.at[own_back + i]).start()

                @pl.when(z != t)
                def _():
                    for i, source, target in pieces(mine, packed):
                        links.copy(source, target, {"seq": t}, at=first_back + 3 * (z ^ t) + i).start()

            if at == 0:
                each(down, "fold_one")
                each(up, "begin")
                each(out, "begin")
            if at == 3:
                each(gate, "fold_one")

        attend_back(attend_dims, heads_ref, grads, log_ref, delta_rows, packed, scratch, after)
        each(down, "fold_two")
        for i, source, target in pieces(pl.ds(0, tokens), packed):
            pltpu.make_async_copy(source, target, sems.at[own_back + i]).wait()
            for j in range(1, nz):
                copy = links.copy(source, target, {"seq": z ^ j}, at=first_back + 3 * j + i)
                copy.wait_recv()
                copy.wait_send()

    heads = log_ref.shape[0]
    kv_heads = k_cols // head_dim // nz
    pl.run_scoped(
        attention,
        pltpu.VMEM((seq_len, block_cols), BF),
        pltpu.VMEM((heads, 8, seq_len), F32),
        *attend_back_scratch(heads, kv_heads, seq_len, head_dim),
    )

    def projections(w_qk, w_v, proj, x, middle_grad, normed, grads_out):
        ready = [fetch.start(proj_hbm, proj)]
        ready_two = [
            fetch.start(a, b)
            for a, b in ((qk_hbm, w_qk), (vo_hbm.at[:, pl.ds(0, v_cols)], w_v), (x_hbm, x), (middle_grad_hbm, middle_grad))
        ]
        ready_three = my_blocks(normed_hbm, normed, shard)
        wait_all(ready)
        outs = (input_grad_ref, gain_grad, head_gain_grad)
        finish = project_back(
            (head_dim, q_cols + k_cols), x, middle_grad, gains_ref, cos_ref, sin_ref, proj, qkv, (w_qk, w_v), outs
        )
        qkv_link.start()
        each(up, "fold_one")
        each(out, "fold_one")
        each(down, "fold_three")
        wait_all(ready_two)
        finish()
        row = jnp.concatenate([gain_grad[...], head_gain_grad[...], feed_gain_ref[...]], axis=1)
        sums[0] = jnp.broadcast_to(row, sums.shape[1:])
        total.begin(0)
        qkv_link.wait()
        wait_all(ready_three)
        mine = normed[:, pl.ds(pl.multiple_of(core * tokens, tokens), tokens)]
        theirs = normed[:, pl.ds(pl.multiple_of((1 - core) * tokens, tokens), tokens)]
        cols_out = last[0].kept.shape[2]
        for start in range(0, qkv.shape[1], step):
            here = slice(start, start + step)
            got = (dot_nn(mine, qkv[:, here]) + dot_nn(theirs, other_qkv[:, here])).astype(BF)
            to = slice(start % cols_out, start % cols_out + step)
            for r in range(chips):
                last[start // cols_out].put(r, to, got[r * shard : (r + 1) * shard])

    pl.run_scoped(
        projections,
        pltpu.VMEM((model, q_cols + k_cols), BF),
        pltpu.VMEM((model, v_cols), BF),
        pltpu.VMEM((tokens, q_cols + k_cols), F32),
        pltpu.VMEM((tokens, model), BF),
        pltpu.VMEM((tokens, model), F32),
        pltpu.VMEM((chips * shard, both), BF),
        pltpu.VMEM((8, 128), F32),
    )
    each(last, "begin")
    total.fold(0)
    total.begin(1)
    each(gate, "fold_two")
    total.fold(1)
    total.begin(2)
    each(out, "fold_two")
    each(last, "fold_one")
    total.fold(2)
    total.begin(3)
    each(up, "fold_two")
    each(down, "fold_four")
    each(gate, "fold_three")
    each(last, "fold_two")
    each(out, "fold_three")
    total.fold(3)
    total.begin(4)
    each(up, "fold_three")
    each(last, "fold_three")
    each(gate, "fold_four")
    each(out, "fold_four")
    total.fold(4)
    each(up, "fold_four")
    each(last, "fold_four")
    totals_ref[...] = sums[5]
    total.end()
    for name in names:
        reduces[name].end()
    links.wait_sends()


def add(a, b):
    return (a.astype(F32) + b.astype(F32)).astype(a.dtype)


def sum_line(values):
    size = lax.axis_size("seq")
    if size != 4:
        return lax.psum(values, "seq")
    z = lax.axis_index("seq")
    inner = add(values, lax.ppermute(values, "seq", [(0, 1), (3, 2)]))
    total = add(inner, lax.ppermute(inner, "seq", [(1, 2), (2, 1)]))
    outer = lax.ppermute(total, "seq", [(1, 0), (2, 3)])
    return jnp.where((z == 1) | (z == 2), total, outer)


def per_device(
    inputs,
    positions,
    cotangent,
    query_weight,
    key_weight,
    value_weight,
    out_weight,
    attention_gain,
    query_gain,
    key_gain,
    feedforward_gain,
    gate_weight,
    up_weight,
    down_weight,
):
    seqs, tokens, model = inputs.shape
    assert seqs == 1
    fsdp, nz = lax.axis_size("fsdp"), lax.axis_size("seq")
    me, z = lax.axis_index("fsdp"), lax.axis_index("seq")
    plane = fsdp == 8 and nz == 4
    both = 2 * tokens if plane else tokens
    x = inputs.reshape(tokens, model)
    dy = cotangent.reshape(tokens, model)
    head_dim = query_gain.shape[0] * fsdp
    q_cols, k_cols, v_cols = query_weight.shape[1], key_weight.shape[1], value_weight.shape[1]
    heads, kv_heads = q_cols // head_dim // nz, k_cols // head_dim // nz
    hidden_cols = gate_weight.shape[1]
    seq_len = tokens * nz

    first = jnp.concatenate([query_weight, key_weight], axis=1)
    second = jnp.concatenate([value_weight, out_weight], axis=1)
    wide_cols = q_cols + k_cols

    def spread(values, count):
        share = values.shape[0]
        row = lax.dynamic_update_slice(jnp.zeros((share * fsdp,), BF), values, (me * share,))
        return jnp.tile(row, count)

    head_row = jnp.concatenate([spread(query_gain, q_cols // head_dim), spread(key_gain, k_cols // head_dim)])
    fill = jnp.zeros((wide_cols - model,), BF)
    gain_rows = [jnp.concatenate([spread(attention_gain, 1), fill]), head_row]
    gain_rows += [jnp.concatenate([spread(feedforward_gain, 1), fill])] + [jnp.zeros((wide_cols,), BF)] * 13
    gain_rows = jnp.stack(gain_rows)
    if plane:
        given = [jnp.concatenate([first, gain_rows]), second, gate_weight, up_weight, down_weight]
    else:
        gather = functools.partial(lax.all_gather, axis_name="fsdp", axis=0, tiled=True)
        qk_full, vo_full, gate_full = gather(first), gather(second), gather(gate_weight)
        up_full, down_full = gather(up_weight), gather(down_weight)
        given = [qk_full, vo_full, lax.psum(gain_rows.astype(F32), "fsdp")]

    half_dim = head_dim // 2
    freqs = ROPE_BASE ** (-jnp.arange(half_dim, dtype=F32) / half_dim)
    angles = positions.reshape(tokens).astype(F32)[:, None] * freqs[None, :]
    cosine, sine = jnp.cos(angles), jnp.sin(angles)
    cosine = jnp.tile(cosine, (1, 128 // half_dim))
    sine = jnp.tile(jnp.concatenate([-sine, sine], axis=1), (1, 128 // head_dim))

    dims = (nz, plane, head_dim, q_cols, k_cols, v_cols, min(256, seq_len))
    block_cols = (q_cols + k_cols + v_cols) // nz
    mixed_cols = heads * head_dim
    head_scratch = [
        pltpu.VMEM((heads, seq_len, head_dim), BF),
        pltpu.VMEM((kv_heads, seq_len, head_dim), BF),
        pltpu.VMEM((kv_heads, seq_len, head_dim), BF),
    ]
    attend_flops = 2 * heads * seq_len * seq_len * head_dim
    proj_flops = 2 * tokens * model * (q_cols + k_cols + v_cols)
    outs = [
        shape_of((16, wide_cols), F32),
        shape_of((tokens, wide_cols), F32),
        shape_of((seq_len, block_cols), BF),
        shape_of((tokens, q_cols), BF),
        shape_of((heads, 8, seq_len), F32),
        shape_of((model, both), BF),
    ]
    n_links = 3 * (nz - 1) + nz + 1
    qk_rows = model
    if plane:
        hidden = gate_weight.shape[1]
        outs += [shape_of((model, wide_cols), BF), shape_of((model, v_cols + model), BF)]
        outs += [shape_of((model, hidden), BF)] * 2 + [shape_of((2, hidden // 2, model), BF)]
        n_links += 6 * 7
        qk_rows += 8 * 16
    got = call(
        functools.partial(forward_kernel, dims),
        outs,
        [VMEM] * 3 + ([ANY] * 5 if plane else [ANY] * 2 + [VMEM]),
        [VMEM] * 5 + [ANY] * (len(outs) - 5),
        [
            pltpu.VMEM((qk_rows, wide_cols), BF),
            pltpu.VMEM((model, v_cols + model), BF),
            pltpu.VMEM((tokens, model), BF),
            pltpu.VMEM((model, tokens), BF),
            pltpu.VMEM((tokens, q_cols + k_cols + v_cols), BF),
        ]
        + head_scratch
        + [
            pltpu.VMEM((heads, seq_len, head_dim), BF),
            pltpu.VMEM((seq_len, mixed_cols), BF),
            pltpu.SemaphoreType.DMA((24,)),
            pltpu.SemaphoreType.DMA((n_links,)),
            pltpu.SemaphoreType.DMA((n_links,)),
        ],
        proj_flops + 4 * attend_flops,
        60 * 2**20,
        collective=1,
    )(x, cosine, sine, *given)
    gains, proj, head_rows, mixed, logs, normed_t = got[:6]
    if plane:
        qk_full, vo_full, gate_full, up_full, down_full = got[6:]

    width = 512
    groups = 3
    rows_model = lambda kind: shape_of((tokens, model), kind)
    feed_out = call(
        functools.partial(feed_kernel, (nz, plane, head_dim, (v_cols, model), width, groups)),
        [
            rows_model(BF),
            rows_model(F32),
            rows_model(BF),
            shape_of((1, model), F32),
            shape_of((tokens, q_cols), BF),
            shape_of((8 * nz, tokens), F32),
            shape_of((q_cols, both), BF),
            shape_of((model, both), BF),
            shape_of((hidden_cols, both), BF),
            shape_of((both, hidden_cols), BF),
            shape_of((both, hidden_cols), BF),
            shape_of((both, model), BF),
        ],
        [VMEM] * 4 + [ANY] * 4,
        [VMEM] * 6 + [ANY] * 6,
        [
            pltpu.VMEM((q_cols, model), BF),
            pltpu.VMEM((model, hidden_cols), BF),
            pltpu.VMEM((model, hidden_cols), BF),
            pltpu.VMEM((hidden_cols, model), BF),
            pltpu.VMEM((2, model, tokens), BF),
            pltpu.VMEM((tokens, model), F32),
            pltpu.VMEM((tokens, model), BF),
            pltpu.VMEM((tokens, model), F32),
            pltpu.VMEM((2, width, tokens), BF),
            pltpu.VMEM((2, tokens, width), BF),
            pltpu.VMEM((2, tokens, width), BF),
            pltpu.SemaphoreType.DMA((20 + 2 * groups,)),
            pltpu.SemaphoreType.DMA((2, 3)),
            pltpu.SemaphoreType.DMA((3,)),
            pltpu.SemaphoreType.DMA((3,)),
            pltpu.SemaphoreType.DMA((2, 3)),
            pltpu.SemaphoreType.DMA((hidden_cols // width, 3)),
        ],
        12 * tokens * model * hidden_cols,
        50 * 2**20,
        collective=2 if plane else None,
    )(x, dy, gains, mixed, vo_full, gate_full, up_full, down_full)
    output, middle_grad, middle_low, feed_gain_part, mixed_grad, delta = feed_out[:6]
    mixed_t, normed_two_t, hidden_t, gate_grad, up_grad, dy_both = feed_out[6:]

    attend_dims = (min(256, seq_len), min(1024, seq_len))
    attend_scratch = attend_back_scratch(heads, kv_heads, seq_len, head_dim)
    if plane:
        down_rows, down_cols = down_weight.shape
        blocks = {"down0": (down_rows // 2, down_cols), "down1": (down_rows // 2, down_cols)}
        for name in ("gate0", "gate1", "up0", "up1"):
            blocks[name] = (gate_weight.shape[0], hidden_cols // 2)
        blocks["out0"] = blocks["out1"] = (out_weight.shape[0], model // 2)
        blocks["q"] = blocks["kv"] = (query_weight.shape[0], q_cols)
        assert k_cols + v_cols == q_cols
        names = tuple(blocks)
        pairs = [(2,) + shape for shape in blocks.values()]
        total_cols = model + wide_cols + model
        n_links = 2 * (nz - 1) + 3 * nz + 2 + 5 * len(names) + 5
        n_copies = 2 + 1 + 4 * 4 + 16 + 3 + 6 + 4 + 2 * len(names)
        got = call(
            functools.partial(backward_kernel, (nz, head_dim, (q_cols, k_cols, v_cols), attend_dims, names)),
            [rows_model(BF), shape_of((8, total_cols), F32)]
            + [shape_of(shape, BF) for shape in blocks.values()]
            + [shape_of(shape, BF) for shape in pairs]
            + [shape_of((both, model), BF)],
            [VMEM] * 9 + [ANY] * 12,
            [VMEM] * 2 + [ANY] * (2 * len(names) + 1),
            [pltpu.VMEM(shape, BF) for shape in pairs] * 2
            + [pltpu.VMEM(shape, BF) for shape in blocks.values()] * 3
            + [
                pltpu.VMEM((seq_len, mixed_cols), BF),
                pltpu.VMEM((8, seq_len), F32),
                pltpu.VMEM((tokens, q_cols + k_cols + v_cols), BF),
                pltpu.VMEM((tokens, q_cols + k_cols + v_cols), BF),
                pltpu.VMEM((6, 8, total_cols), F32),
                pltpu.VMEM((5, 8, total_cols), F32),
                pltpu.VMEM((1, model), F32),
                pltpu.VMEM((1, wide_cols), F32),
                pltpu.SemaphoreType.DMA((n_copies,)),
                pltpu.SemaphoreType.DMA((n_links,)),
                pltpu.SemaphoreType.DMA((n_links,)),
            ],
            10 * attend_flops + 2 * tokens * model * (3 * hidden_cols + 3 * (q_cols + k_cols)),
            100 * 2**20,
            collective=3,
        )(
            gains, cosine, sine, head_rows, logs, mixed_grad, delta, middle_low, feed_gain_part, x, middle_grad, proj,
            hidden_t, dy_both, normed_two_t, gate_grad, up_grad, mixed_t, normed_t, qk_full, vo_full,
        )
        input_grad, totals = got[:2]
        shards = {name: value.astype(F32) for name, value in zip(names, got[2:])}
        down_shard = jnp.concatenate([shards["down0"], shards["down1"]])
        gate_shard, up_shard, out_shard = (
            jnp.concatenate([shards[kind + "0"], shards[kind + "1"]], axis=1) for kind in ("gate", "up", "out")
        )
        q_shard, kv_shard = shards["q"], shards["kv"]
        totals = totals[0]
    else:
        exchange = functools.partial(lax.all_to_all, axis_name="seq", tiled=True)
        grad_rows = exchange(mixed_grad, split_axis=1, concat_axis=0)
        delta_rows = exchange(delta, split_axis=0, concat_axis=1)
        packed = call(
            functools.partial(attend_back_kernel, attend_dims),
            shape_of((seq_len, block_cols), BF),
            [VMEM] * 4,
            VMEM,
            attend_scratch,
            10 * attend_flops,
            20 * 2**20,
        )(head_rows, grad_rows, logs, jnp.broadcast_to(delta_rows[:heads, None], (heads, 8, seq_len)))
        cuts = (mixed_cols, mixed_cols + k_cols // nz)
        parts = (packed[:, : cuts[0]], packed[:, cuts[0] : cuts[1]], packed[:, cuts[1] :])
        qkv = jnp.concatenate([exchange(part, split_axis=0, concat_axis=1) for part in parts], axis=1)
        input_grad, qkv, gain_part, head_gain_part = call(
            functools.partial(post_kernel, (head_dim, wide_cols)),
            [
                rows_model(BF),
                shape_of((tokens, wide_cols + v_cols), BF),
                shape_of((1, model), F32),
                shape_of((1, wide_cols), F32),
            ],
            [VMEM] * 9,
            [VMEM] * 4,
            [],
            proj_flops,
            14 * 2**20,
        )(x, middle_grad, gains, cosine, sine, proj, qkv, qk_full, vo_full[:, :v_cols])

        def reduce(left, right):
            return sum_line(lax.psum_scatter(weight_grad(left, right), "fsdp", scatter_dimension=0, tiled=True)).astype(F32)

        down_shard, gate_shard = reduce(hidden_t, dy), reduce(normed_two_t, gate_grad)
        up_shard, out_shard = reduce(normed_two_t, up_grad), reduce(mixed_t, middle_low)
        qkv_shard = reduce(normed_t, qkv)
        q_shard, kv_shard = qkv_shard[:, :q_cols], qkv_shard[:, q_cols:]
        totals = lax.psum(jnp.concatenate([gain_part, head_gain_part, feed_gain_part], axis=1)[0], ("seq", "fsdp"))

    q_total = totals[model : model + q_cols].reshape(-1, head_dim).sum(axis=0)
    k_total = totals[model + q_cols : model + wide_cols].reshape(-1, head_dim).sum(axis=0)

    def share(values):
        size = values.shape[0] // fsdp
        return lax.dynamic_slice(values, (me * size,), (size,))

    return (
        output.reshape(inputs.shape),
        input_grad.reshape(inputs.shape),
        q_shard,
        kv_shard[:, :k_cols],
        kv_shard[:, k_cols:],
        out_shard,
        share(totals[:model]),
        share(q_total),
        share(k_total),
        share(totals[model + wide_cols :]),
        gate_shard,
        up_shard,
        down_shard,
    )


def solution(mesh):
    tokens, rows, row = P("fsdp", "seq", None), P("fsdp", None), P("fsdp")
    in_specs = (tokens, P("fsdp", "seq"), tokens) + (rows,) * 4 + (row,) * 4 + (rows,) * 3
    out_specs = (tokens, tokens) + (rows,) * 4 + (row,) * 4 + (rows,) * 3
    return jax.shard_map(per_device, mesh=mesh, in_specs=in_specs, out_specs=out_specs, check_vma=False)
```

```python
import functools

import jax
import jax.numpy as jnp
from jax import lax
from jax.experimental import pallas as pl
from jax.experimental.pallas import tpu as pltpu
from jax.sharding import PartitionSpec as P

EPSILON = 1e-05
ROPE_BASE = 1000000.0
LOG2E = 1.4426950408889634
BF = jnp.bfloat16
F32 = jnp.float32
VMEM = pl.BlockSpec(memory_space=pltpu.VMEM)
SMEM = pl.BlockSpec(memory_space=pltpu.SMEM)
ANY = pl.BlockSpec(memory_space=pl.ANY)
VMEM_BYTES = 62 * 2**20


def dot_nn(a, b):
    return lax.dot_general(a, b, (((1,), (0,)), ((), ())), preferred_element_type=F32)


def dot_nt(a, b):
    return lax.dot_general(a, b, (((1,), (1,)), ((), ())), preferred_element_type=F32)


def dot_tn(a, b):
    return lax.dot_general(a, b, (((0,), (0,)), ((), ())), preferred_element_type=F32)


def shape_of(shape, dtype):
    return jax.ShapeDtypeStruct(shape, dtype)


def call(kernel, outs, in_specs, out_specs, scratch, flops, moved, collective=None, **more):
    params = {} if collective is None else {"collective_id": collective, "has_side_effects": True}
    return pl.pallas_call(
        kernel,
        out_shape=outs,
        in_specs=in_specs,
        out_specs=out_specs,
        scratch_shapes=scratch,
        compiler_params=pltpu.CompilerParams(vmem_limit_bytes=VMEM_BYTES, **params),
        cost_estimate=pl.CostEstimate(flops=flops, bytes_accessed=moved, transcendentals=0),
        **more,
    )


def row_norm(values):
    return lax.rsqrt(jnp.mean(values * values, axis=-1, keepdims=True) + EPSILON)


class Fetch:
    def __init__(self, sems):
        self.sems, self.used = sems, 0

    def copy(self, source, target):
        self.used += 1
        return pltpu.make_async_copy(source, target, self.sems.at[self.used - 1])

    def start(self, source, target):
        copy = self.copy(source, target)
        copy.start()
        return copy


def wait_all(copies):
    for copy in copies:
        copy.wait()


def head_mask(width, head_dim):
    rows = lax.broadcasted_iota(jnp.int32, (width, width), 0) // head_dim
    cols = lax.broadcasted_iota(jnp.int32, (width, width), 1) // head_dim
    return (rows == cols).astype(BF)


def head_sum(values, mask):
    high = values.astype(BF)
    rest = (values - high.astype(F32)).astype(BF)
    return dot_nn(high, mask) + dot_nn(rest, mask)


def key_lanes(shape, head_dim):
    return lax.broadcasted_iota(jnp.int32, shape, 1) % (2 * head_dim) < head_dim


def partner(values, head_dim):
    half = head_dim // 2
    width = values.shape[-1]
    lane = lax.broadcasted_iota(jnp.int32, values.shape, 1)
    after = pltpu.roll(values, width - half, 1)
    before = pltpu.roll(values, half, 1)
    return jnp.where(lane % head_dim < half, after, before)


class Links:
    def __init__(self, send_sems, recv_sems):
        self.sems, self.used, self.started = (send_sems, recv_sems), 0, []

    def reserve(self, count):
        self.used += count
        return self.used - count

    def copy(self, source, target, device, at=None):
        at = self.reserve(1) if at is None else at
        return pltpu.make_async_remote_copy(
            src_ref=source,
            dst_ref=target,
            send_sem=self.sems[0].at[at],
            recv_sem=self.sems[1].at[at],
            device_id=device,
            device_id_type=pl.DeviceIdType.MESH,
        )

    def start(self, source, target, device):
        copy = self.copy(source, target, device)
        copy.start()
        self.started.append(copy)
        return copy

    def wait_sends(self):
        for copy in self.started:
            copy.wait_send()


def enter(me, z, nz, plane):
    barrier = pltpu.get_barrier_semaphore()
    peers = [{"seq": z ^ j} for j in range(1, nz)]
    if plane:
        peers += [{"fsdp": me ^ bit} for bit in (1, 2, 4)]
    for peer in peers:
        pl.semaphore_signal(barrier, inc=1, device_id=peer, device_id_type=pl.DeviceIdType.MESH)
    pl.semaphore_wait(barrier, len(peers))


class Gather:
    def __init__(self, links, me, own, whole, x_first, stride=None, base=0):
        self.links, self.me, self.own, self.whole = links, me, own, whole
        self.rows = own.shape[0]
        self.stride, self.base = self.rows if stride is None else stride, base
        self.near, self.other = (2, 4) if x_first else (4, 2)

    def block(self, b):
        return self.whole.at[pl.ds(pl.multiple_of((self.me ^ b) * self.stride + self.base, 16), self.rows)]

    def pass_on(self, b, bit):
        source = self.own if b == 0 else self.block(b)
        return self.links.start(source, self.block(b), {"fsdp": self.me ^ bit})

    def begin(self):
        self.first = self.pass_on(0, self.near)
        self.second = self.pass_on(0, self.other)
        self.to_core = [self.pass_on(0, 1)]

    def forward_first(self):
        self.first.wait_recv()
        self.far = self.pass_on(self.near, self.other)
        self.to_core.append(self.pass_on(self.near, 1))

    def forward_second(self):
        self.second.wait_recv()
        self.to_core.append(self.pass_on(self.other, 1))

    def forward_far(self):
        self.far.wait_recv()
        self.to_core.append(self.pass_on(self.near + self.other, 1))

    def end(self):
        for copy in self.to_core:
            copy.wait_recv()


def begin(gathers, copy_here=None):
    for gather in gathers:
        gather.begin()
    return [copy_here(gather.own, gather.block(0)) for gather in gathers]


def forward_first(gathers):
    for gather in gathers:
        gather.forward_first()
    for gather in gathers:
        gather.forward_second()


def forward_far(gathers):
    for gather in gathers:
        gather.forward_far()


def end(gathers):
    for gather in gathers:
        gather.end()


def forward_kernel(dims, x_ref, dy_ref, cos_ref, sin_ref, *refs):
    nz, plane, head_dim, widths, rows, width, groups = dims
    n_in = 5 if plane else 6
    given, refs = refs[:n_in], refs[n_in:]
    gains_ref, heads_ref, log_ref, output_ref, middle_grad_ref, middle_low_ref, gain_grad_ref, grad_low, delta_ref = refs[:9]
    refs = refs[9:]
    proj_hbm, normed_t_hbm, mixed_t_hbm, normed_two_hbm, hidden_hbm, gate_grad_hbm, up_grad_hbm, dy_hbm = refs[:8]
    refs = refs[8:]
    if plane:
        first_hbm, second_hbm, gate_hbm, up_hbm, down_hbm = refs[:5]
        refs = refs[5:]
    else:
        gate_hbm, up_hbm, down_hbm = given[3:]
    w_first, w_second, w_out, normed, transposed, proj, qkv, queries, keys, values, full, mix, mixed = refs[:13]
    w_gate, w_up, w_down, middle, total, back, hidden_slot, gate_slot, up_slot = refs[13:22]
    local_sems, weight_sems, slot_sems, send_sems, recv_sems, slot_sends, block_recvs = refs[22:]
    z, me = lax.axis_index("seq"), lax.axis_index("fsdp")
    model = w_second.shape[0]
    hidden_cols = gate_hbm.shape[1]
    tokens = x_ref.shape[0]
    enter(me, z, nz, plane)
    links = Links(send_sems, recv_sems)
    local = []
    to_core = []
    core = lax.rem(me, 2) if plane else 0
    place = pl.ds(pl.multiple_of(core * tokens, tokens), tokens)
    sibling = {"fsdp": me ^ 1}

    def copy_here(source, target):
        copy = pltpu.make_async_copy(source, target, local_sems.at[len(local)])
        copy.start()
        local.append(copy)
        return copy

    def share(source, target):
        copy_here(source, target)
        if plane:
            to_core.append(links.start(source, target, sibling))

    if plane:
        own_first, own_second, own_gate, own_up, own_down = given
        half = own_down.shape[0] // 2
        attention = [Gather(links, me, own_first, w_first, True), Gather(links, me, own_second, w_second, False)]
        here = begin(attention, copy_here)
        down = [
            Gather(links, me, own_down.at[pl.ds(side * half, half)], down_hbm, side == 0, 2 * half, side * half)
            for side in range(2)
        ]
        wide, at = [], 0
        for count in groups:
            cols = pl.ds(at * width, count * width)
            pair = ((own_gate, gate_hbm, True), (own_up, up_hbm, False))
            wide.append([Gather(links, me, own.at[:, cols], whole.at[:, cols], first) for own, whole, first in pair])
            at += count
    else:
        here = [copy_here(given[0], w_first), copy_here(given[1], w_second)]
    x = x_ref[...].astype(F32)
    unit = x * row_norm(x)
    if plane:
        forward_first(attention)
        here_down = begin(down, copy_here)
        forward_far(attention)
        end(attention)
        wait_all(here)
        stride = attention[0].rows
        shard = model // 8
        gains = sum(w_first[s * stride + shard : (s + 1) * stride].astype(F32) for s in range(8))
        for s in range(8):
            copy_here(w_first.at[pl.ds(s * stride, shard)], first_hbm.at[pl.ds(s * shard, shard)])
        copy_here(w_second, second_hbm)
    else:
        stride = shard = model
        wait_all(here)
        gains = given[2][...].astype(F32)
    out_half = model // 2
    for s in range(model // shard):
        source = w_first.at[pl.ds(s * stride, shard), pl.ds(w_first.shape[1] - out_half, out_half)]
        copy_here(source, w_out.at[pl.ds(s * shard, shard), pl.ds(0, out_half)])
    copy_here(w_second.at[:, pl.ds(w_second.shape[1] - out_half, out_half)], w_out.at[:, pl.ds(out_half, out_half)])
    out_copies = local[-model // shard - 1 :]
    gains_ref[...] = gains
    normed[...] = (unit * gains[0:1, :model]).astype(BF)
    chunk = 256
    mask = head_mask(chunk, head_dim)
    cos = jnp.concatenate([cos_ref[...]] * (chunk // 128), axis=1)
    sin = jnp.concatenate([sin_ref[...]] * (chunk // 128), axis=1)
    part_cols = nz * sum(widths)
    parts = qkv.shape[1] // part_cols
    my_rows = pl.ds(pl.multiple_of(z * tokens, tokens), tokens)
    arrivals = []
    for b in range(parts):
        for start in range(0, part_cols, chunk):
            cols = slice(start, start + chunk)
            if b == 1 or stride == shard:
                weight = (w_first, w_second)[b][:, cols]
            else:
                weight = jnp.concatenate([w_first[s * stride : s * stride + shard, cols] for s in range(8)], axis=0)
            got = dot_nn(normed[...], weight)
            here_cols = slice(b * part_cols + start, b * part_cols + start + chunk)
            proj[:, here_cols] = got
            scale = lax.rsqrt(head_sum(got * got, mask) * (1.0 / head_dim) + EPSILON)
            head = got * scale * gains_ref[1:2, cols]
            head = head * cos + partner(head, head_dim) * sin
            if start >= nz * widths[0]:
                head = jnp.where(key_lanes(head.shape, head_dim), head, got)
            qkv[:, here_cols] = head.astype(BF)
        arrived = []
        for j in range(nz):
            owner = z ^ j
            for i, size in enumerate(widths):
                base = b * part_cols + i * nz * widths[0]
                source = qkv.at[:, pl.ds(pl.multiple_of(base + owner * size, size), size)]
                target = heads_ref.at[my_rows, pl.ds(b * sum(widths) + i * widths[0], size)]
                if j == 0:
                    arrived.append(copy_here(source, target))
                else:
                    arrived.append(links.start(source, target, {"seq": owner}))
        arrivals.append(arrived)
    copy_here(proj, proj_hbm)
    transposed[0] = normed[...].T
    share(transposed.at[0], normed_t_hbm.at[:, place])
    share(dy_ref, dy_hbm.at[place])
    if plane:
        here_wide = [begin(wide[0], copy_here)]
        forward_first(down)
        here_wide.append(begin(wide[1], copy_here))
    group, seq_len, _ = queries.shape
    factor = head_dim**-0.5 * LOG2E
    arriving, here_mixed = [], []
    for b in range(parts):
        for i, copy in enumerate(arrivals[b]):
            if i < 2:
                copy.wait()
            else:
                copy.wait_recv()
        first = b * sum(widths)
        for g in range(group):
            queries[g] = heads_ref[:, first + g * head_dim : first + (g + 1) * head_dim]
        first += widths[0]
        keys[...] = heads_ref[:, first : first + head_dim]
        values[...] = heads_ref[:, first + head_dim : first + 2 * head_dim]
        for r in range(seq_len // rows):
            span = slice(r * rows, (r + 1) * rows)
            reach = (r + 1) * rows

            def one_head(g, _):
                scores = dot_nt(queries[g, span], keys[:reach]) * factor
                row = lax.broadcasted_iota(jnp.int32, scores.shape, 0) + r * rows
                col = lax.broadcasted_iota(jnp.int32, scores.shape, 1)
                probs = jnp.exp2(jnp.where(row >= col, scores, -1e30))
                total = jnp.sum(probs, axis=1, keepdims=True)
                full[g, span] = (dot_nn(probs.astype(BF), values[:reach]) * (1.0 / total)).astype(BF)
                log_ref[b * group + g, :, span] = jnp.broadcast_to(jnp.log2(total), (rows, 128)).T[0:8]
                return 0

            lax.fori_loop(0, group, one_head, 0)
        mix[b] = jnp.concatenate([full[g] for g in range(group)], axis=1)
        for j in range(nz):
            owner = z ^ j
            source = mix.at[b, pl.ds(pl.multiple_of(owner * tokens, tokens), tokens)]
            to = pl.multiple_of((z * parts + b) * widths[0], widths[0])
            target = mixed.at[:, pl.ds(to, widths[0])]
            if j == 0:
                here_mixed.append(copy_here(source, target))
            else:
                arriving.append(links.start(source, target, {"seq": owner}))
        if plane and b == 0:
            forward_first(wide[0])
            here_wide.append(begin(wide[2], copy_here))
    if plane:
        forward_far(down)
        forward_first(wide[1])
        here_wide.append(begin(wide[3], copy_here))
        forward_far(wide[0])
    for copy in arriving:
        copy.wait_recv()
    wait_all(here_mixed + out_copies)

    gain = gains_ref[2:3, :model]
    middle_rows = x_ref[...].astype(F32) + dot_nn(mixed[...], w_out[...])
    middle[...] = middle_rows
    total[...] = middle_rows
    normed_rows = (middle_rows * row_norm(middle_rows) * gain).astype(BF)
    normed[...] = normed_rows
    transposed[1] = normed_rows.T
    share(transposed.at[1], normed_two_hbm.at[:, place])
    transposed[2] = mixed[...].T
    share(transposed.at[2], mixed_t_hbm.at[:, place])
    back[...] = jnp.zeros(back.shape, F32)

    def slot_places(f):
        here = pl.ds(pl.multiple_of(f * width, width), width)
        return (
            (hidden_slot, hidden_hbm.at[here, place]),
            (gate_slot, gate_grad_hbm.at[place, here]),
            (up_slot, up_grad_hbm.at[place, here]),
        )

    def slot_copies(slot, f):
        return [
            pltpu.make_async_copy(s.at[slot], target, slot_sems.at[slot, i]) for i, (s, target) in enumerate(slot_places(f))
        ]

    def slot_links(slot, f):
        if not plane:
            return []
        return [
            pltpu.make_async_remote_copy(
                src_ref=s.at[slot],
                dst_ref=target,
                send_sem=slot_sends.at[slot, i],
                recv_sem=block_recvs.at[f, i],
                device_id=sibling,
                device_id_type=pl.DeviceIdType.MESH,
            )
            for i, (s, target) in enumerate(slot_places(f))
        ]

    def wait_slot(slot, f):
        wait_all(slot_copies(slot, f))
        for copy in slot_links(slot, f):
            copy.wait_send()

    def weight_copies(f):
        here = pl.ds(pl.multiple_of(f * width, width), width)
        slot = lax.rem(f, 2)
        pairs = ((gate_hbm.at[:, here], w_gate), (up_hbm.at[:, here], w_up), (down_hbm.at[here], w_down))
        return [
            pltpu.make_async_copy(source, target.at[slot], weight_sems.at[slot, i])
            for i, (source, target) in enumerate(pairs)
        ]

    def one_block(last, f, _):
        slot = lax.rem(f, 2)

        @pl.when(f + 1 < last)
        def _():
            for copy in weight_copies(f + 1):
                copy.start()

        wait_all(weight_copies(f))

        @pl.when(f >= 2)
        def _():
            wait_slot(slot, f - 2)

        gate = dot_nn(normed[...], w_gate[slot])
        up = dot_nn(normed[...], w_up[slot])
        hidden_grad = dot_nt(dy_ref[...], w_down[slot])
        s = 1.0 / (1.0 + jnp.exp(-gate))
        silu = gate * s
        hidden = (silu * up).astype(BF)
        gate_grad = (hidden_grad * up * (s * (1.0 + gate * (1.0 - s)))).astype(BF)
        up_grad = (hidden_grad * silu).astype(BF)
        hidden_slot[slot] = hidden.T
        gate_slot[slot] = gate_grad
        up_slot[slot] = up_grad
        for copy in slot_copies(slot, f) + slot_links(slot, f):
            copy.start()
        total[...] = total[...] + dot_nn(hidden, w_down[slot])
        back[...] = back[...] + (dot_nt(gate_grad, w_gate[slot]) + dot_nt(up_grad, w_up[slot]))
        return 0

    blocks = hidden_cols // width
    at = 0
    if plane:
        end(down)
        wait_all(here_down)
    for g, count in enumerate(groups):
        if plane:
            if g + 1 < len(groups):
                if g > 0:
                    forward_first(wide[g + 1])
            if g > 0:
                forward_far(wide[g])
            end(wide[g])
            wait_all(here_wide[g])
        for copy in weight_copies(at):
            copy.start()
        lax.fori_loop(at, at + count, functools.partial(one_block, at + count), 0)
        at += count
    output_ref[...] = total[...].astype(BF)
    part, gain_sum = norm_back(middle[...], gain, back[...])
    gain_grad_ref[...] = gain_sum
    middle_grad = dy_ref[...].astype(F32) + part
    middle_grad_ref[...] = middle_grad
    middle_low = middle_grad.astype(BF)
    middle_low_ref[...] = middle_low
    mixed_grad = dot_nt(middle_low, w_out[...]).astype(BF)
    grad_low[...] = mixed_grad
    product = mixed_grad.astype(F32) * mixed[...].astype(F32)
    heads = mixed.shape[1] // head_dim // nz
    row = lax.broadcasted_iota(jnp.int32, (8 * nz, mixed.shape[1]), 0)
    col = lax.broadcasted_iota(jnp.int32, (8 * nz, mixed.shape[1]), 1)
    pick = ((col // head_dim == (row // 8) * heads + row % 8) & (row % 8 < heads)).astype(BF)
    high = product.astype(BF)
    delta_ref[...] = dot_nt(pick, high) + dot_nt(pick, (product - high.astype(F32)).astype(BF))
    for f in (blocks - 2, blocks - 1):
        wait_slot(f % 2, f)
    if plane:
        for f in range(blocks):
            for copy in slot_links(f % 2, f):
                copy.wait_recv()
        for copy in to_core:
            copy.wait_recv()
        links.wait_sends()
    done = here + out_copies + here_mixed + [c for arrived in arrivals for c in arrived[:2]]
    if plane:
        done += here_down + [c for copies in here_wide for c in copies]
    for copy in local:
        if not any(copy is other for other in done):
            copy.wait()


def both_cores(links, copy_here, me, source, target, axis):
    size = source.shape[axis]
    here = pl.ds(pl.multiple_of(lax.rem(me, 2) * size, size), size)
    place = target.at[here] if axis == 0 else target.at[:, here]
    copy_here(source, place)
    return links.start(source, place, {"fsdp": me ^ 1})


def attend_back(dims, b, heads_ref, grads_ref, log_ref, delta_ref, packed, scratch, after):
    rows, chunk = dims
    queries, keys, values, grad, q_grad, k_grad, v_grad = scratch
    group, seq_len, head_dim = queries.shape
    first = b * (group + 2) * head_dim
    for g in range(group):
        queries[g] = heads_ref[:, first + g * head_dim : first + (g + 1) * head_dim]
        at = (b * group + g) * head_dim
        grad[g] = grads_ref[:, at : at + head_dim]
        q_grad[g] = jnp.zeros((seq_len, head_dim), F32)
    first += group * head_dim
    keys[...] = heads_ref[:, first : first + head_dim]
    values[...] = heads_ref[:, first + head_dim : first + 2 * head_dim]
    factor = head_dim**-0.5
    scale = factor * LOG2E
    for at in range(seq_len // rows):
        span = slice(at * rows, (at + 1) * rows)
        key, value = keys[span], values[span]
        k_grad[span] = jnp.zeros((rows, head_dim), F32)
        v_grad[span] = jnp.zeros((rows, head_dim), F32)

        def one_head(g, _):
            key_total = jnp.zeros((rows, head_dim), F32)
            value_total = jnp.zeros((rows, head_dim), F32)
            for start in range(at * rows, seq_len, chunk):
                part = slice(start, min(start + chunk, seq_len))
                query, out_grad = queries[g, part], grad[g, part]
                scores = dot_nt(key, query) * scale - log_ref[b * group + g, 0:1, part]
                if start == at * rows:
                    key_at = lax.broadcasted_iota(jnp.int32, scores.shape, 0) + at * rows
                    query_at = lax.broadcasted_iota(jnp.int32, scores.shape, 1) + start
                    scores = jnp.where(query_at >= key_at, scores, -1e30)
                probs = jnp.exp2(scores)
                prob_grad = dot_nt(value, out_grad)
                score_grad = (probs * (prob_grad - delta_ref[b * group + g, 0:1, part])).astype(BF)
                value_total = value_total + dot_nn(probs.astype(BF), out_grad)
                key_total = key_total + dot_nn(score_grad, query)
                q_grad[g, part] = q_grad[g, part] + dot_tn(score_grad, key)
            k_grad[span] = k_grad[span] + key_total
            v_grad[span] = v_grad[span] + value_total
            return 0

        lax.fori_loop(0, group, one_head, 0)
        parts = [(q_grad[g, span] * factor).astype(BF) for g in range(group)]
        parts += [(k_grad[span] * factor).astype(BF), v_grad[span].astype(BF)]
        packed[span] = jnp.concatenate(parts, axis=1)
        after(at)


def attend_back_scratch(group, seq_len, head_dim):
    many = lambda kind: pltpu.VMEM((group, seq_len, head_dim), kind)
    one = lambda kind: pltpu.VMEM((seq_len, head_dim), kind)
    return [many(BF), one(BF), one(BF), many(BF), many(F32), one(F32), one(F32)]


def attend_back_kernel(dims, heads_ref, grads_ref, log_ref, delta_ref, packed, *scratch):
    for b in range(packed.shape[0]):
        attend_back(dims, b, heads_ref, grads_ref, log_ref, delta_ref, packed.at[b], scratch, lambda at: None)


def norm_back(rows, gain, gradient):
    q = row_norm(rows)
    n = rows * q
    u = gradient * gain
    return q * (u - n * jnp.mean(u * n, axis=-1, keepdims=True)), jnp.sum(gradient * n, axis=0, keepdims=True)


def weight_grad_kernel(left_ref, right_ref, out_ref):
    out_ref[...] = dot_nn(left_ref[...], right_ref[...]).astype(BF)


def weight_grad(left, right, width=256):
    rows, tokens = left.shape
    cols = right.shape[1]
    return call(
        weight_grad_kernel,
        shape_of((rows, cols), BF),
        [pl.BlockSpec((rows, tokens), lambda n: (0, 0)), pl.BlockSpec((tokens, width), lambda n: (0, n))],
        pl.BlockSpec((rows, width), lambda n: (0, n)),
        [],
        2 * rows * tokens * cols,
        2 * (rows * tokens + tokens * cols + rows * cols),
        grid=(cols // width,),
    )(left, right)


def project_back(dims, b, gains_ref, cos_ref, sin_ref, proj_ref, qkv, head_gain_grad_ref):
    nz, head_dim, widths = dims
    part_cols = nz * sum(widths)
    width = 256
    mask = head_mask(width, head_dim)
    cos = jnp.concatenate([cos_ref[...]] * (width // 128), axis=1)
    sin = jnp.concatenate([sin_ref[...]] * (width // 128), axis=1)
    for start in range(0, part_cols, width):
        cols = slice(b * part_cols + start, b * part_cols + start + width)
        rotated = qkv[:, cols].astype(F32)
        gradient = rotated * cos - partner(rotated, head_dim) * sin
        proj = proj_ref[:, cols]
        scale = lax.rsqrt(head_sum(proj * proj, mask) * (1.0 / head_dim) + EPSILON)
        n = proj * scale
        u = gradient * gains_ref[1:2, start : start + width]
        head_gain_grad_ref[:, cols] = jnp.sum(gradient * n, axis=0, keepdims=True)
        back = scale * (u - n * (head_sum(u * n, mask) * (1.0 / head_dim)))
        if start >= nz * widths[0]:
            back = jnp.where(key_lanes(back.shape, head_dim), back, rotated)
        qkv[:, cols] = back.astype(BF)


def input_back(x_ref, middle_grad_ref, gains_ref, qkv, weight, input_grad_ref, gain_grad_ref):
    normed_grad = dot_nt(qkv[...], weight[...])
    part, gain_sum = norm_back(x_ref[...].astype(F32), gains_ref[0:1, : x_ref.shape[1]], normed_grad)
    gain_grad_ref[...] = gain_sum
    input_grad_ref[...] = (middle_grad_ref[...] + part).astype(BF)


def post_kernel(dims, x_ref, middle_grad_ref, gains_ref, cos_ref, sin_ref, proj_ref, grads_ref, weight_ref, *refs):
    input_grad_ref, qkv, gain_grad_ref, head_gain_grad_ref = refs
    nz, _, widths = dims
    qkv[...] = grads_ref[...]
    for b in range(qkv.shape[1] // (nz * sum(widths))):
        project_back(dims, b, gains_ref, cos_ref, sin_ref, proj_ref, qkv, head_gain_grad_ref)
    input_back(x_ref, middle_grad_ref, gains_ref, qkv, weight_ref, input_grad_ref, gain_grad_ref)


class Reduce:
    def __init__(self, links, fetch, me, z, x_first, away, kept, first, second, inward, across, out):
        self.links, self.fetch, self.me, self.z = links, fetch, me, z
        self.away, self.kept, self.out = away, kept, out
        self.bits = (2, 4) if x_first else (4, 2)
        order = (1, 3, 0, 2) if x_first else (2, 3, 0, 1)
        self.slots = {r: (away if i < 2 else kept, i % 2) for i, r in enumerate(order)}
        self.arrived, self.second, self.inward, self.across = first, second, inward, across
        self.outer, self.inner = (z == 0) | (z == 3), (z == 1) | (z == 2)
        self.one = links.copy(away, first, {"fsdp": me ^ self.bits[0]})
        self.two = links.copy(kept.at[1], second, {"fsdp": me ^ self.bits[1]})
        self.three = links.copy(kept.at[0], inward, {"seq": z ^ 1})
        self.four = links.copy(kept.at[0], across, {"seq": z ^ 3})
        self.five = links.copy(kept.at[1], out, {"seq": z ^ 1})
        self.here = fetch.copy(kept.at[1], out)
        self.load = fetch.copy(first, away)

    def put(self, r, cols, values):
        ref, i = self.slots[r]
        ref[i, :, cols] = values

    def rows_of(self):
        rows = self.kept.shape[1]
        step = 32 if rows % 32 == 0 else 16
        return rows // step, step

    def by_rows(self, work):
        count, step = self.rows_of()

        def body(i, _):
            work(pl.ds(pl.multiple_of(i * step, step), step))
            return 0

        lax.fori_loop(0, count, body, 0)

    def begin(self):
        self.one.start()

    def load_one(self):
        self.one.wait_recv()
        self.one.wait_send()
        self.load.start()

    def fold_one(self):
        self.load.wait()

        def work(rows):
            for i in range(2):
                self.kept[i, rows] = self.kept[i, rows] + self.away[i, rows]

        self.by_rows(work)
        self.two.start()

    def fold_two(self):
        self.two.wait_recv()

        def work(rows):
            self.kept[0, rows] = self.kept[0, rows] + self.second[rows]

        self.by_rows(work)

        @pl.when(self.outer)
        def _():
            self.three.start()

    def fold_three(self):
        @pl.when(self.inner)
        def _():
            self.three.wait_recv()

            def work(rows):
                self.kept[0, rows] = self.kept[0, rows] + self.inward[rows]

            self.by_rows(work)
            self.four.start()

    def fold_four(self):
        self.two.wait_send()

        @pl.when(self.inner)
        def _():
            self.four.wait_recv()

            def work(rows):
                self.kept[1, rows] = self.kept[0, rows] + self.across[rows]

            self.by_rows(work)
            self.five.start()
            self.here.start()

    def end(self):
        @pl.when(self.inner)
        def _():
            self.four.wait_send()
            self.five.wait_send()
            self.here.wait()

        @pl.when(self.outer)
        def _():
            self.three.wait_send()
            self.five.wait_recv()


def each(reduces, step):
    if step == "fold_one":
        each(reduces, "load_one")
    for reduce in reduces:
        getattr(reduce, step)()


class Total:
    def __init__(self, links, me, z, sums, arrived):
        self.sums, self.arrived = sums, arrived
        peers = [{"fsdp": me ^ 1}, {"fsdp": me ^ 2}, {"fsdp": me ^ 4}, {"seq": z ^ 1}, {"seq": z ^ 2}]
        self.copies = [links.copy(sums.at[i], arrived.at[i], peer) for i, peer in enumerate(peers)]

    def begin(self, at):
        self.copies[at].start()

    def fold(self, at):
        self.copies[at].wait_recv()
        self.sums[at + 1] = self.sums[at] + self.arrived[at]

    def end(self):
        for copy in self.copies:
            copy.wait_send()


def backward_kernel(dims, gains_ref, cos_ref, sin_ref, heads_ref, log_ref, grad_low, delta_own, low_ref, feed_gain_ref, *refs):
    nz, head_dim, widths, attend_dims, names = dims
    given, refs = refs[:12], refs[12:]
    x_hbm, middle_grad_hbm, proj_hbm, hidden_hbm, dy_hbm, normed_two_hbm = given[:6]
    gate_hbm, up_hbm, mixed_hbm, normed_hbm, first_hbm, second_hbm = given[6:]
    input_grad_ref, totals_ref = refs[:2]
    n = len(names)
    finals, refs = dict(zip(names, refs[2 : 2 + n])), refs[2 + n :]
    firsts, refs = dict(zip(names, refs[:n])), refs[n:]
    low_hbm, refs = refs[0], refs[1:]
    aways, refs = dict(zip(names, refs[:n])), refs[n:]
    kepts, refs = dict(zip(names, refs[:n])), refs[n:]
    seconds, refs = dict(zip(names, refs[:n])), refs[n:]
    inwards, refs = dict(zip(names, refs[:n])), refs[n:]
    acrosses, refs = dict(zip(names, refs[:n])), refs[n:]
    grads, delta, qkv, other_qkv, sums, sum_arrived, gain_grad, head_gain_grad, sems, send_sems, recv_sems = refs
    z, me = lax.axis_index("seq"), lax.axis_index("fsdp")
    chip, core = lax.div(me, 2), lax.rem(me, 2)
    enter(me, z, nz, True)
    links, fetch = Links(send_sems, recv_sems), Fetch(sems)
    tokens = grad_low.shape[0]
    seq_len, block_cols = heads_ref.shape
    part_cols = nz * sum(widths)
    parts = qkv.shape[1] // part_cols
    late = []

    def copy_here(source, target):
        copy = fetch.start(source, target)
        late.append(copy)
        return copy

    my_rows = pl.ds(pl.multiple_of(z * tokens, tokens), tokens)
    arrivals = []
    for b in range(parts):
        arrived = []
        for j in range(nz):
            owner = z ^ j
            from_cols = pl.ds(pl.multiple_of((owner * parts + b) * widths[0], widths[0]), widths[0])
            pairs = [(grad_low.at[:, from_cols], grads.at[my_rows, pl.ds(b * widths[0], widths[0])])]
            if b == 0:
                pairs.append((delta_own.at[pl.ds(pl.multiple_of(owner * 8, 8), 8)], delta.at[:, my_rows]))
            for source, target in pairs:
                if j == 0:
                    copy_here(source, target)
                else:
                    arrived.append(links.start(source, target, {"seq": owner}))
        arrivals.append(arrived)
    low_arrival = both_cores(links, copy_here, me, low_ref, low_hbm, 0)
    reduces = {}
    for name in names:
        reduces[name] = Reduce(
            links, fetch, me, z, name[-1] == "x", aways[name], kepts[name], firsts[name], seconds[name], inwards[name],
            acrosses[name], finals[name],
        )
    down = [[reduces[f"down{c}{way}"] for way in "xy"] for c in range(2)]
    gate, up = [reduces["gate0x"], reduces["gate1y"], reduces["gate2x"]], [reduces["up0y"], reduces["up1x"], reduces["up2y"]]
    wide = [gate[:2], [gate[2], up[0]], up[1:]]
    out = [reduces["outx"], reduces["outy"]]
    last = [[reduces[f"last{b}{way}"] for way in "xy"] for b in range(parts)]
    total = Total(links, me, z, sums, sum_arrived)
    part_cols_of = lambda b: pl.ds(b * part_cols, part_cols)
    qkv_links = [
        links.copy(qkv.at[:, part_cols_of(b)], other_qkv.at[:, part_cols_of(b)], {"fsdp": me ^ 1}) for b in range(parts)
    ]
    chips = 4
    step = 256
    half = down[0][0].kept.shape[1]
    shard = gate[0].kept.shape[1]
    both = 2 * tokens
    model = low_ref.shape[1]

    def my_blocks(source, target, rows):
        copies = []
        for r in range(chips):
            owner = (chip ^ r) * 2 + core
            copies.append(fetch.start(source.at[pl.ds(pl.multiple_of(owner * rows, rows), rows)], target.at[pl.ds(r * rows, rows)]))
        return copies

    def wide_grads(places, left, right):
        width = right.shape[2]
        chunks = [
            (source, (first + c) * width, unit, c * width)
            for source, first, unit in places
            for c in range(unit.kept.shape[2] // width)
        ]
        count = len(chunks)
        loads = [
            fetch.copy(source.at[:, pl.ds(at, width)], right.at[c % 2]) for c, (source, at, _, _) in enumerate(chunks)
        ]
        loads[0].start()
        loads[1].start()
        for c in range(count):
            loads[c].wait()
            _, _, unit, base = chunks[c]

            def block(k, _):
                here = pl.ds(pl.multiple_of(k * step, step), step)
                to = pl.ds(pl.multiple_of(base + k * step, step), step)
                got = dot_nn(left[...], right[c % 2, :, here]).astype(BF)
                for r in range(chips):
                    unit.put(r, to, got[r * shard : (r + 1) * shard])
                return 0

            lax.fori_loop(0, width // step, block, 0)
            if c + 2 < count:
                loads[c + 2].start()

    def early_grads(hidden, dy, normed_two, right, mixed, low):
        ready = my_blocks(hidden_hbm, hidden, 2 * half) + [fetch.start(dy_hbm, dy)]
        ready_two = my_blocks(normed_two_hbm, normed_two, shard)
        ready_three = my_blocks(mixed_hbm, mixed, shard)
        wait_all(ready)
        cols = down[0][0].kept.shape[2]
        for c in range(2):

            def down_block(i, _):
                to = pl.ds(pl.multiple_of(i * step, step), step)
                here = pl.ds(pl.multiple_of(c * cols + i * step, step), step)
                for r in range(chips):
                    got = dot_nn(hidden[2 * r * half : 2 * (r + 1) * half], dy[:, here]).astype(BF)
                    for side in range(2):
                        down[c][side].put(r, to, got[side * half : (side + 1) * half])
                return 0

            lax.fori_loop(0, cols // step, down_block, 0)
            each(down[c], "begin")
        wait_all(ready_two)
        per_unit = gate[0].kept.shape[2] // right.shape[2]
        wide_grads([(gate_hbm, i * per_unit, gate[i]) for i in range(3)] + [(up_hbm, 0, up[0])], normed_two, right)
        low_arrival.wait_recv()
        wait_all(late)
        del late[:]
        ready_three.append(fetch.start(low_hbm, low))
        wait_all(ready_three)
        cols = out[0].kept.shape[2]
        for start in range(0, low.shape[1], step):
            got = dot_nn(mixed[...], low[:, start : start + step]).astype(BF)
            for r in range(chips):
                out[start // cols].put(r, slice(start % cols, start % cols + step), got[r * shard : (r + 1) * shard])
        each(down[0], "fold_one")

    def late_grads(normed_two, right):
        wait_all(my_blocks(normed_two_hbm, normed_two, shard))
        per_unit = up[0].kept.shape[2] // right.shape[2]
        wide_grads([(up_hbm, i * per_unit, up[i]) for i in (1, 2)], normed_two, right)

    wide_part = gate[0].kept.shape[2] // 2
    pl.run_scoped(
        early_grads,
        pltpu.VMEM((2 * chips * half, both), BF),
        pltpu.VMEM((both, model), BF),
        pltpu.VMEM((chips * shard, both), BF),
        pltpu.VMEM((2, both, wide_part), BF),
        pltpu.VMEM((chips * shard, both), BF),
        pltpu.VMEM((both, model), BF),
    )

    heads = log_ref.shape[0]
    group = heads // parts
    first_back = links.reserve(parts * 2 * nz)
    own_back = fetch.used
    fetch.used += parts * 2

    def back_copies(b, packed):
        for i, width in enumerate(widths):
            base = b * part_cols + i * nz * widths[0]
            target = qkv.at[:, pl.ds(pl.multiple_of(base + z * width, width), width)]
            for j in range(nz):
                owner = z ^ j
                rows = pl.ds(pl.multiple_of(owner * tokens, tokens), tokens)
                source = packed.at[b, rows, pl.ds(i * widths[0], width)]
                if j == 0:
                    yield j, pltpu.make_async_copy(source, target, sems.at[own_back + 2 * b + i])
                else:
                    yield j, links.copy(source, target, {"seq": owner}, at=first_back + (2 * b + i) * nz + j)

    def attention(packed, delta_rows, *scratch):
        def after_first(at):
            if at == 3:
                each(down[1], "fold_one")
                each(wide[0], "begin")

        def after_second(at):
            if at == 1:
                each(down[0], "fold_two")
            if at == 3:
                each(down[1], "fold_two")

        for b, after in enumerate((after_first, after_second)):
            for copy in arrivals[b]:
                copy.wait_recv()
            if b == 0:
                for h in range(heads):
                    delta_rows[h] = jnp.broadcast_to(delta[h : h + 1], (8, seq_len))
            attend_back(attend_dims, b, heads_ref, grads, log_ref, delta_rows, packed.at[b], scratch, after)
            for _, copy in back_copies(b, packed):
                copy.start()
        pl.run_scoped(
            late_grads,
            pltpu.VMEM((chips * shard, both), BF),
            pltpu.VMEM((2, both, wide_part), BF),
        )
        each(wide[0], "fold_one")
        each(wide[1], "begin")
        each(wide[2], "begin")
        each(down[0], "fold_three")
        for b in range(parts):
            for j, copy in back_copies(b, packed):
                if j == 0:
                    copy.wait()
                else:
                    copy.wait_recv()
            project(b)
            if b == 0:
                each(down[1], "fold_three")
                each(wide[0], "fold_two")
        each(wide[1], "fold_one")
        for b in range(parts):
            for j, copy in back_copies(b, packed):
                if j:
                    copy.wait_send()

    def project(b):
        def inner(proj):
            cols = part_cols_of(b)
            fetch.start(proj_hbm.at[:, cols], proj.at[:, cols]).wait()
            project_back((nz, head_dim, widths), b, gains_ref, cos_ref, sin_ref, proj, qkv, head_gain_grad)
            qkv_links[b].start()

        pl.run_scoped(inner, pltpu.VMEM((tokens, parts * part_cols), F32))

    pl.run_scoped(
        attention,
        pltpu.VMEM((parts, seq_len, sum(widths)), BF),
        pltpu.VMEM((heads, 8, seq_len), F32),
        *attend_back_scratch(group, seq_len, head_dim),
    )

    def projections(weight, x, middle_grad, normed):
        ready = my_blocks(normed_hbm, normed, shard)
        ready_two = [fetch.start(x_hbm, x), fetch.start(middle_grad_hbm, middle_grad)]
        for b, source in enumerate((first_hbm, second_hbm)):
            ready_two.append(fetch.start(source.at[:, pl.ds(0, part_cols)], weight.at[:, part_cols_of(b)]))
        wait_all(ready)
        mine = normed[:, pl.ds(pl.multiple_of(core * tokens, tokens), tokens)]
        theirs = normed[:, pl.ds(pl.multiple_of((1 - core) * tokens, tokens), tokens)]
        for b in range(parts):
            qkv_links[b].wait()
            cols = last[b][0].kept.shape[2]
            for start in range(0, part_cols, step):
                here = slice(b * part_cols + start, b * part_cols + start + step)
                got = (dot_nn(mine, qkv[:, here]) + dot_nn(theirs, other_qkv[:, here])).astype(BF)
                for r in range(chips):
                    last[b][start // cols].put(r, slice(start % cols, start % cols + step), got[r * shard : (r + 1) * shard])
            each(last[b], "begin")
        each(out, "begin")
        wait_all(ready_two)
        input_back(x, middle_grad, gains_ref, qkv, weight, input_grad_ref, gain_grad)
        row = jnp.concatenate([gain_grad[...], head_gain_grad[...], feed_gain_ref[...]], axis=1)
        sums[0] = jnp.broadcast_to(row, sums.shape[1:])
        total.begin(0)

    pl.run_scoped(
        projections,
        pltpu.VMEM((model, parts * part_cols), BF),
        pltpu.VMEM((tokens, model), BF),
        pltpu.VMEM((tokens, model), F32),
        pltpu.VMEM((chips * shard, both), BF),
    )
    each(down[0], "fold_four")
    each(down[1], "fold_four")
    total.fold(0)
    total.begin(1)
    each(wide[0], "fold_three")
    each(wide[2], "fold_one")
    each(wide[1], "fold_two")
    total.fold(1)
    total.begin(2)
    each(last[0], "fold_one")
    each(last[1], "fold_one")
    each(out, "fold_one")
    each(wide[2], "fold_two")
    total.fold(2)
    total.begin(3)
    each(wide[0], "fold_four")
    each(last[0], "fold_two")
    each(last[1], "fold_two")
    each(out, "fold_two")
    total.fold(3)
    total.begin(4)
    each(wide[1], "fold_three")
    each(wide[2], "fold_three")
    each(wide[1], "fold_four")
    each(last[0], "fold_three")
    each(last[1], "fold_three")
    each(out, "fold_three")
    total.fold(4)
    each(wide[2], "fold_four")
    each(last[0], "fold_four")
    each(last[1], "fold_four")
    each(out, "fold_four")
    totals_ref[...] = sums[5]
    total.end()
    for name in names:
        reduces[name].end()
    links.wait_sends()


def add(a, b):
    return (a.astype(F32) + b.astype(F32)).astype(a.dtype)


def sum_line(values):
    size = lax.axis_size("seq")
    if size != 4:
        return lax.psum(values, "seq")
    z = lax.axis_index("seq")
    inner = add(values, lax.ppermute(values, "seq", [(0, 1), (3, 2)]))
    total = add(inner, lax.ppermute(inner, "seq", [(1, 2), (2, 1)]))
    outer = lax.ppermute(total, "seq", [(1, 0), (2, 3)])
    return jnp.where((z == 1) | (z == 2), total, outer)


def per_device(
    inputs,
    positions,
    cotangent,
    query_weight,
    key_weight,
    value_weight,
    out_weight,
    attention_gain,
    query_gain,
    key_gain,
    feedforward_gain,
    gate_weight,
    up_weight,
    down_weight,
):
    seqs, tokens, model = inputs.shape
    assert seqs == 1
    fsdp, nz = lax.axis_size("fsdp"), lax.axis_size("seq")
    me, z = lax.axis_index("fsdp"), lax.axis_index("seq")
    plane = fsdp == 8 and nz == 4
    both = 2 * tokens if plane else tokens
    x = inputs.reshape(tokens, model)
    dy = cotangent.reshape(tokens, model)
    head_dim = query_gain.shape[0] * fsdp
    q_cols, k_cols, v_cols = query_weight.shape[1], key_weight.shape[1], value_weight.shape[1]
    heads, kv_heads = q_cols // head_dim // nz, k_cols // head_dim // nz
    hidden_cols = gate_weight.shape[1]
    seq_len = tokens * nz

    group, parts = heads // kv_heads, kv_heads
    widths = (group * head_dim, 2 * head_dim)
    part_cols = nz * sum(widths)
    assert parts == 2

    def by_parts(query, key, value):
        rows = query.shape[0]
        q = query.reshape(rows, nz, parts, widths[0])
        kv = jnp.stack([v.reshape(rows, nz, parts, head_dim) for v in (key, value)], axis=3).reshape(rows, nz, parts, widths[1])
        return [jnp.concatenate([v[:, :, b].reshape(rows, -1) for v in (q, kv)], axis=1) for b in range(parts)]

    first, second = by_parts(query_weight, key_weight, value_weight)
    half_out = model // 2
    first = jnp.concatenate([first, out_weight[:, :half_out]], axis=1)
    second = jnp.concatenate([second, out_weight[:, half_out:]], axis=1)
    first_cols = first.shape[1]

    def spread(values):
        share = values.shape[0]
        return lax.dynamic_update_slice(jnp.zeros((share * fsdp,), BF), values, (me * share,))

    def gain_row(values):
        return jnp.concatenate([values, jnp.zeros((first_cols - values.shape[0],), BF)])

    key_row = jnp.concatenate([spread(key_gain), jnp.zeros((head_dim,), BF)])
    head_row = jnp.concatenate([jnp.tile(spread(query_gain), nz * group), jnp.tile(key_row, nz)])
    gain_rows = [gain_row(spread(attention_gain)), gain_row(head_row), gain_row(spread(feedforward_gain))]
    gain_rows = jnp.stack(gain_rows + [jnp.zeros((first_cols,), BF)] * 13)
    if plane:
        given = [jnp.concatenate([first, gain_rows]), second, gate_weight, up_weight, down_weight]
    else:
        gather = functools.partial(lax.all_gather, axis_name="fsdp", axis=0, tiled=True)
        first_full, second_full, gate_full = gather(first), gather(second), gather(gate_weight)
        up_full, down_full = gather(up_weight), gather(down_weight)
        given = [first_full, second_full, lax.psum(gain_rows.astype(F32), "fsdp"), gate_full, up_full, down_full]

    half_dim = head_dim // 2
    freqs = ROPE_BASE ** (-jnp.arange(half_dim, dtype=F32) / half_dim)
    angles = positions.reshape(tokens).astype(F32)[:, None] * freqs[None, :]
    cosine, sine = jnp.cos(angles), jnp.sin(angles)
    cosine = jnp.tile(cosine, (1, 128 // half_dim))
    sine = jnp.tile(jnp.concatenate([-sine, sine], axis=1), (1, 128 // head_dim))

    width = 512
    blocks = hidden_cols // width
    sizes = (blocks - 6, 3, 2, 1)
    block_cols = parts * sum(widths)
    mixed_cols = heads * head_dim
    attend_flops = 2 * heads * seq_len * seq_len * head_dim
    proj_flops = 2 * tokens * model * parts * part_cols
    rows_model = lambda kind: shape_of((tokens, model), kind)
    outs = [
        shape_of((16, first_cols), F32),
        shape_of((seq_len, block_cols), BF),
        shape_of((heads, 8, seq_len), F32),
        rows_model(BF),
        rows_model(F32),
        rows_model(BF),
        shape_of((1, model), F32),
        shape_of((tokens, q_cols), BF),
        shape_of((8 * nz, tokens), F32),
        shape_of((tokens, parts * part_cols), F32),
        shape_of((model, both), BF),
        shape_of((q_cols, both), BF),
        shape_of((model, both), BF),
        shape_of((hidden_cols, both), BF),
        shape_of((both, hidden_cols), BF),
        shape_of((both, hidden_cols), BF),
        shape_of((both, model), BF),
    ]
    n_links = parts * 3 * (nz - 1)
    first_rows = model
    if plane:
        outs += [shape_of((model, first_cols), BF)] * 2
        outs += [shape_of((model, hidden_cols), BF)] * 2 + [shape_of((hidden_cols, model), BF)]
        n_links += (4 + 2 * len(sizes)) * 7 + 4
        first_rows += 8 * 16
    many = lambda count: pltpu.VMEM((count, seq_len, head_dim), BF)
    one = pltpu.VMEM((seq_len, head_dim), BF)
    got = call(
        functools.partial(forward_kernel, (nz, plane, head_dim, widths, min(256, seq_len), width, sizes)),
        outs,
        [VMEM] * 4 + ([ANY] * 5 if plane else [ANY] * 2 + [VMEM] + [ANY] * 3),
        [VMEM] * 9 + [ANY] * (len(outs) - 9),
        [
            pltpu.VMEM((first_rows, first_cols), BF),
            pltpu.VMEM((model, first_cols), BF),
            pltpu.VMEM((q_cols, model), BF),
            pltpu.VMEM((tokens, model), BF),
            pltpu.VMEM((3, model, tokens), BF),
            pltpu.VMEM((tokens, parts * part_cols), F32),
            pltpu.VMEM((tokens, parts * part_cols), BF),
            many(group),
            one,
            one,
            many(group),
            pltpu.VMEM((parts, seq_len, widths[0]), BF),
            pltpu.VMEM((tokens, q_cols), BF),
            pltpu.VMEM((2, model, width), BF),
            pltpu.VMEM((2, model, width), BF),
            pltpu.VMEM((2, width, model), BF),
            pltpu.VMEM((tokens, model), F32),
            pltpu.VMEM((tokens, model), F32),
            pltpu.VMEM((tokens, model), F32),
            pltpu.VMEM((2, width, tokens), BF),
            pltpu.VMEM((2, tokens, width), BF),
            pltpu.VMEM((2, tokens, width), BF),
            pltpu.SemaphoreType.DMA((48,)),
            pltpu.SemaphoreType.DMA((2, 3)),
            pltpu.SemaphoreType.DMA((2, 3)),
            pltpu.SemaphoreType.DMA((n_links,)),
            pltpu.SemaphoreType.DMA((n_links,)),
            pltpu.SemaphoreType.DMA((2, 3)),
            pltpu.SemaphoreType.DMA((blocks, 3)),
        ],
        proj_flops + 4 * attend_flops + 12 * tokens * model * hidden_cols,
        100 * 2**20,
        collective=1,
    )(x, dy, cosine, sine, *given)
    gains, head_rows, logs, output, middle_grad, middle_low, feed_gain_part, mixed_grad, delta = got[:9]
    proj, normed_t, mixed_t, normed_two_t, hidden_t, gate_grad, up_grad, dy_both = got[9:17]
    if plane:
        first_full, second_full = got[17:19]

    attend_dims = (min(256, seq_len), min(1024, seq_len))
    attend_scratch = attend_back_scratch(group, seq_len, head_dim)
    if plane:
        down_rows, down_cols = down_weight.shape
        blocks = {f"down{c}{way}": (down_rows // 2, down_cols // 2) for c in range(2) for way in "xy"}
        wide_names = ("gate0x", "gate1y", "gate2x", "up0y", "up1x", "up2y")
        blocks |= {name: (gate_weight.shape[0], hidden_cols // 3) for name in wide_names}
        blocks |= {"out" + way: (out_weight.shape[0], model // 2) for way in "xy"}
        blocks |= {f"last{b}{way}": (query_weight.shape[0], part_cols // 2) for b in range(parts) for way in "xy"}
        names = tuple(blocks)
        pairs = [(2,) + shape for shape in blocks.values()]
        total_cols = model + parts * part_cols + model
        n_links = 3 * (nz - 1) + 2 * parts * nz + 1 + parts + 5 * len(names) + 5
        n_copies = 64 + 2 * len(names)
        got = call(
            functools.partial(backward_kernel, (nz, head_dim, widths, attend_dims, names)),
            [rows_model(BF), shape_of((8, total_cols), F32)]
            + [shape_of(shape, BF) for shape in blocks.values()]
            + [shape_of(shape, BF) for shape in pairs]
            + [shape_of((both, model), BF)],
            [VMEM] * 9 + [ANY] * 12,
            [VMEM] * 2 + [ANY] * (2 * len(names) + 1),
            [pltpu.VMEM(shape, BF) for shape in pairs] * 2
            + [pltpu.VMEM(shape, BF) for shape in blocks.values()] * 3
            + [
                pltpu.VMEM((seq_len, mixed_cols), BF),
                pltpu.VMEM((8, seq_len), F32),
                pltpu.VMEM((tokens, parts * part_cols), BF),
                pltpu.VMEM((tokens, parts * part_cols), BF),
                pltpu.VMEM((6, 8, total_cols), F32),
                pltpu.VMEM((5, 8, total_cols), F32),
                pltpu.VMEM((1, model), F32),
                pltpu.VMEM((1, parts * part_cols), F32),
                pltpu.SemaphoreType.DMA((n_copies,)),
                pltpu.SemaphoreType.DMA((n_links,)),
                pltpu.SemaphoreType.DMA((n_links,)),
            ],
            10 * attend_flops + 2 * tokens * model * (3 * hidden_cols + 3 * (q_cols + k_cols)),
            100 * 2**20,
            collective=3,
        )(
            gains, cosine, sine, head_rows, logs, mixed_grad, delta, middle_low, feed_gain_part, x, middle_grad, proj,
            hidden_t, dy_both, normed_two_t, gate_grad, up_grad, mixed_t, normed_t, first_full, second_full,
        )
        input_grad, totals = got[:2]
        shards = {name: value.astype(F32) for name, value in zip(names, got[2:])}
        down_shard = jnp.concatenate(
            [jnp.concatenate([shards["down0" + way], shards["down1" + way]], axis=1) for way in "xy"]
        )
        gate_shard, up_shard, out_shard = (
            jnp.concatenate([shards[name] for name in names if name.startswith(kind)], axis=1)
            for kind in ("gate", "up", "out")
        )
        part_shards = [(shards[f"last{b}x"], shards[f"last{b}y"]) for b in range(parts)]
        totals = totals[0]
    else:
        exchange = functools.partial(lax.all_to_all, axis_name="seq", tiled=True)
        grad_rows = exchange(mixed_grad, split_axis=1, concat_axis=0)
        delta_rows = exchange(delta, split_axis=0, concat_axis=1)
        packed = call(
            functools.partial(attend_back_kernel, attend_dims),
            shape_of((parts, seq_len, sum(widths)), BF),
            [VMEM] * 4,
            VMEM,
            attend_scratch,
            10 * attend_flops,
            20 * 2**20,
        )(head_rows, grad_rows, logs, jnp.broadcast_to(delta_rows[:heads, None], (heads, 8, seq_len)))
        pieces = [piece for b in range(parts) for piece in (packed[b, :, : widths[0]], packed[b, :, widths[0] :])]
        qkv = jnp.concatenate([exchange(piece, split_axis=0, concat_axis=1) for piece in pieces], axis=1)
        weight = jnp.concatenate([first_full[:, :part_cols], second_full[:, :part_cols]], axis=1)
        input_grad, qkv, gain_part, head_gain_part = call(
            functools.partial(post_kernel, (nz, head_dim, widths)),
            [
                rows_model(BF),
                shape_of((tokens, parts * part_cols), BF),
                shape_of((1, model), F32),
                shape_of((1, parts * part_cols), F32),
            ],
            [VMEM] * 8,
            [VMEM] * 4,
            [],
            proj_flops,
            14 * 2**20,
        )(x, middle_grad, gains, cosine, sine, proj, qkv, weight)

        def reduce(left, right):
            return sum_line(lax.psum_scatter(weight_grad(left, right), "fsdp", scatter_dimension=0, tiled=True)).astype(F32)

        down_shard, gate_shard = reduce(hidden_t, dy), reduce(normed_two_t, gate_grad)
        up_shard, out_shard = reduce(normed_two_t, up_grad), reduce(mixed_t, middle_low)
        qkv_shard = reduce(normed_t, qkv)
        section = nz * widths[0]
        part_shards = [
            (qkv_shard[:, b * part_cols : b * part_cols + section], qkv_shard[:, b * part_cols + section : (b + 1) * part_cols])
            for b in range(parts)
        ]
        totals = lax.psum(jnp.concatenate([gain_part, head_gain_part, feed_gain_part], axis=1)[0], ("seq", "fsdp"))

    shard_rows = query_weight.shape[0]
    q_shard = jnp.stack([q.reshape(shard_rows, nz, widths[0]) for q, _ in part_shards], axis=2).reshape(shard_rows, -1)
    kv_shard = jnp.stack([kv.reshape(shard_rows, nz, 2, head_dim) for _, kv in part_shards], axis=2)
    k_shard, v_shard = (kv_shard[:, :, :, i].reshape(shard_rows, -1) for i in range(2))

    head_totals = totals[model : model + parts * part_cols].reshape(parts, part_cols)
    q_total = head_totals[:, : nz * widths[0]].reshape(-1, head_dim).sum(axis=0)
    k_total = head_totals[:, nz * widths[0] :].reshape(-1, 2, head_dim)[:, 0].sum(axis=0)

    def share(values):
        size = values.shape[0] // fsdp
        return lax.dynamic_slice(values, (me * size,), (size,))

    return (
        output.reshape(inputs.shape),
        input_grad.reshape(inputs.shape),
        q_shard,
        k_shard,
        v_shard,
        out_shard,
        share(totals[:model]),
        share(q_total),
        share(k_total),
        share(totals[model + parts * part_cols :]),
        gate_shard,
        up_shard,
        down_shard,
    )


def solution(mesh):
    tokens, rows, row = P("fsdp", "seq", None), P("fsdp", None), P("fsdp")
    in_specs = (tokens, P("fsdp", "seq"), tokens) + (rows,) * 4 + (row,) * 4 + (rows,) * 3
    out_specs = (tokens, tokens) + (rows,) * 4 + (row,) * 4 + (rows,) * 3
    return jax.shard_map(per_device, mesh=mesh, in_specs=in_specs, out_specs=out_specs, check_vma=False)
```

```python
import functools

import jax
import jax.numpy as jnp
from jax import lax
from jax.experimental import pallas as pl
from jax.experimental.pallas import tpu as pltpu
from jax.sharding import PartitionSpec as P

EPSILON = 1e-05
ROPE_BASE = 1000000.0
LOG2E = 1.4426950408889634
BF = jnp.bfloat16
F32 = jnp.float32
VMEM = pl.BlockSpec(memory_space=pltpu.VMEM)
SMEM = pl.BlockSpec(memory_space=pltpu.SMEM)
ANY = pl.BlockSpec(memory_space=pl.ANY)
VMEM_BYTES = 62 * 2**20


def dot_nn(a, b):
    return lax.dot_general(a, b, (((1,), (0,)), ((), ())), preferred_element_type=F32)


def dot_nt(a, b):
    return lax.dot_general(a, b, (((1,), (1,)), ((), ())), preferred_element_type=F32)


def dot_tn(a, b):
    return lax.dot_general(a, b, (((0,), (0,)), ((), ())), preferred_element_type=F32)


def shape_of(shape, dtype):
    return jax.ShapeDtypeStruct(shape, dtype)


def call(kernel, outs, in_specs, out_specs, scratch, flops, moved, collective=None, **more):
    params = {} if collective is None else {"collective_id": collective, "has_side_effects": True}
    return pl.pallas_call(
        kernel,
        out_shape=outs,
        in_specs=in_specs,
        out_specs=out_specs,
        scratch_shapes=scratch,
        compiler_params=pltpu.CompilerParams(vmem_limit_bytes=VMEM_BYTES, **params),
        cost_estimate=pl.CostEstimate(flops=flops, bytes_accessed=moved, transcendentals=0),
        **more,
    )


def row_norm(values):
    return lax.rsqrt(jnp.mean(values * values, axis=-1, keepdims=True) + EPSILON)


class Fetch:
    def __init__(self, sems):
        self.sems, self.used = sems, 0

    def copy(self, source, target):
        self.used += 1
        return pltpu.make_async_copy(source, target, self.sems.at[self.used - 1])

    def start(self, source, target):
        copy = self.copy(source, target)
        copy.start()
        return copy


def wait_all(copies):
    for copy in copies:
        copy.wait()


def head_mask(width, head_dim):
    rows = lax.broadcasted_iota(jnp.int32, (width, width), 0) // head_dim
    cols = lax.broadcasted_iota(jnp.int32, (width, width), 1) // head_dim
    return (rows == cols).astype(BF)


def head_sum(values, mask):
    high = values.astype(BF)
    rest = (values - high.astype(F32)).astype(BF)
    return dot_nn(high, mask) + dot_nn(rest, mask)


def key_lanes(shape, head_dim):
    return lax.broadcasted_iota(jnp.int32, shape, 1) % (2 * head_dim) < head_dim


def partner(values, head_dim):
    half = head_dim // 2
    width = values.shape[-1]
    lane = lax.broadcasted_iota(jnp.int32, values.shape, 1)
    after = pltpu.roll(values, width - half, 1)
    before = pltpu.roll(values, half, 1)
    return jnp.where(lane % head_dim < half, after, before)


class Links:
    def __init__(self, send_sems, recv_sems):
        self.sems, self.used, self.started = (send_sems, recv_sems), 0, []

    def reserve(self, count):
        self.used += count
        return self.used - count

    def copy(self, source, target, device, at=None):
        at = self.reserve(1) if at is None else at
        return pltpu.make_async_remote_copy(
            src_ref=source,
            dst_ref=target,
            send_sem=self.sems[0].at[at],
            recv_sem=self.sems[1].at[at],
            device_id=device,
            device_id_type=pl.DeviceIdType.MESH,
        )

    def plan(self, source, target, device):
        self.started.append(self.copy(source, target, device))
        return self.started[-1]

    def start(self, source, target, device):
        copy = self.plan(source, target, device)
        copy.start()
        return copy

    def wait_sends(self):
        for copy in self.started:
            copy.wait_send()


def enter(me, z, nz, plane):
    barrier = pltpu.get_barrier_semaphore()
    peers = [{"seq": z ^ j} for j in range(1, nz)]
    if plane:
        peers += [{"fsdp": me ^ bit} for bit in (1, 2, 4)]
    for peer in peers:
        pl.semaphore_signal(barrier, inc=1, device_id=peer, device_id_type=pl.DeviceIdType.MESH)
    pl.semaphore_wait(barrier, len(peers))


class Gather:
    def __init__(self, links, me, own, whole, x_first, stride=None, base=0):
        self.links, self.me, self.own, self.whole = links, me, own, whole
        self.rows = own.shape[0]
        self.stride, self.base = self.rows if stride is None else stride, base
        near, other = (2, 4) if x_first else (4, 2)
        self.first, self.second = self.pass_on(0, near), self.pass_on(0, other)
        self.far = self.pass_on(near, other)
        self.to_core = [self.pass_on(b, 1) for b in (0, near, other, near + other)]

    def block(self, b):
        return self.whole.at[pl.ds(pl.multiple_of((self.me ^ b) * self.stride + self.base, 16), self.rows)]

    def pass_on(self, b, bit):
        source = self.own if b == 0 else self.block(b)
        return self.links.plan(source, self.block(b), {"fsdp": self.me ^ bit})

    def begin(self):
        for copy in (self.first, self.second, self.to_core[0]):
            copy.start()

    def forward_first(self):
        self.first.wait_recv()
        self.far.start()
        self.to_core[1].start()

    def forward_second(self):
        self.second.wait_recv()
        self.to_core[2].start()

    def forward_far(self):
        self.far.wait_recv()
        self.to_core[3].start()

    def end(self):
        for copy in self.to_core:
            copy.wait_recv()


def begin(gathers):
    for gather in gathers:
        gather.begin()


def forward_first(gathers):
    for gather in gathers:
        gather.forward_first()
    for gather in gathers:
        gather.forward_second()


def forward_far(gathers):
    for gather in gathers:
        gather.forward_far()


def end(gathers):
    for gather in gathers:
        gather.end()


def forward_kernel(dims, x_ref, dy_ref, cos_ref, sin_ref, *refs):
    nz, plane, head_dim, widths, rows, width, groups = dims
    n_in = 5 if plane else 6
    given, refs = refs[:n_in], refs[n_in:]
    gains_ref, heads_ref, log_ref, output_ref, middle_grad_ref, middle_low_ref, gain_grad_ref, grad_low, delta_ref = refs[:9]
    refs = refs[9:]
    proj_hbm, normed_t_hbm, mixed_t_hbm, normed_two_hbm, hidden_hbm, gate_grad_hbm, up_grad_hbm, dy_hbm = refs[:8]
    refs = refs[8:]
    if plane:
        first_hbm, second_hbm, gate_hbm, up_hbm, down_hbm = refs[:5]
        refs = refs[5:]
    else:
        gate_hbm, up_hbm, down_hbm = given[3:]
    w_first, w_second, w_out, normed, transposed, proj, qkv, queries, keys, values, full, mix, mixed = refs[:13]
    w_gate, w_up, w_down, middle, total, back, hidden_slot, gate_slot, up_slot = refs[13:22]
    local_sems, weight_sems, slot_sems, send_sems, recv_sems, slot_sends, block_recvs = refs[22:29]
    own_slots = refs[29:]
    z, me = lax.axis_index("seq"), lax.axis_index("fsdp")
    model = w_second.shape[0]
    hidden_cols = gate_hbm.shape[1]
    tokens = x_ref.shape[0]
    enter(me, z, nz, plane)
    links = Links(send_sems, recv_sems)
    local = []
    to_core = []
    core = lax.rem(me, 2) if plane else 0
    place = pl.ds(pl.multiple_of(core * tokens, tokens), tokens)
    sibling = {"fsdp": me ^ 1}

    def copy_here(source, target):
        copy = pltpu.make_async_copy(source, target, local_sems.at[len(local)])
        copy.start()
        local.append(copy)
        return copy

    def share(source, target):
        copy_here(source, target)
        if plane:
            to_core.append(links.start(source, target, sibling))

    if plane:
        own_first, own_second, own_gate, own_up, own_down = given
        half = own_down.shape[0] // 2
        part_cols = nz * sum(widths)
        both = ((own_first, w_first, True), (own_second, w_second, False))

        def columns(pairs, start, size):
            cols = pl.ds(start, size)
            return [Gather(links, me, own.at[:, cols], whole.at[:, cols], x_first) for own, whole, x_first in pairs]

        attention = columns(both, 0, part_cols)
        outward = columns(both, part_cols, own_first.shape[1] - part_cols)
        begin(attention)
        here = [copy_here(gather.own, gather.block(0)) for gather in attention + outward]
        own_places = [(own_gate, own_slots[0], gate_hbm), (own_up, own_slots[1], up_hbm), (own_down, own_slots[2], down_hbm)]
        own_loads = [copy_here(own, slot) for own, slot, _ in own_places]
        down = [
            Gather(links, me, own_down.at[pl.ds(side * half, half)], down_hbm, side == 0, 2 * half, side * half)
            for side in range(2)
        ]
        wide, at = [], 0
        for count in groups:
            wide.append(columns(((own_gate, gate_hbm, True), (own_up, up_hbm, False)), at * width, count * width))
            at += count
    else:
        here = [copy_here(given[0], w_first), copy_here(given[1], w_second)]
    x = x_ref[...].astype(F32)
    unit = x * row_norm(x)
    if plane:
        forward_first(attention)
        begin(outward)
        begin(down)
        forward_far(attention)
        end(attention)
        wait_all(here)
        stride = attention[0].rows
        shard = model // 8
        gains = sum(w_first[s * stride + shard : (s + 1) * stride, :part_cols].astype(F32) for s in range(8))
    else:
        stride = shard = model
        wait_all(here)
        gains = given[2][:, : nz * sum(widths)].astype(F32)
    if plane:
        wait_all(own_loads)
        own_stores = []
        for own, slot, whole in own_places:
            count = own.shape[0]
            own_stores.append(copy_here(slot, whole.at[pl.ds(pl.multiple_of(me * count, count), count)]))
    gains_ref[...] = gains
    normed[...] = (unit * gains[0:1, :model]).astype(BF)
    chunk = 256
    mask = head_mask(chunk, head_dim)
    cos = jnp.concatenate([cos_ref[...]] * (chunk // 128), axis=1)
    sin = jnp.concatenate([sin_ref[...]] * (chunk // 128), axis=1)
    part_cols = nz * sum(widths)
    parts = qkv.shape[1] // part_cols
    out_half = model // 2
    my_rows = pl.ds(pl.multiple_of(z * tokens, tokens), tokens)
    arrivals = []
    for b in range(parts):
        for start in range(0, part_cols, chunk):
            cols = slice(start, start + chunk)
            if b == 1 or stride == shard:
                weight = (w_first, w_second)[b][:, cols]
            else:
                weight = jnp.concatenate([w_first[s * stride : s * stride + shard, cols] for s in range(8)], axis=0)
            got = dot_nn(normed[...], weight)
            here_cols = slice(b * part_cols + start, b * part_cols + start + chunk)
            proj[:, here_cols] = got
            scale = lax.rsqrt(head_sum(got * got, mask) * (1.0 / head_dim) + EPSILON)
            head = got * scale * gains_ref[1:2, cols]
            head = head * cos + partner(head, head_dim) * sin
            if start >= nz * widths[0]:
                head = jnp.where(key_lanes(head.shape, head_dim), head, got)
            qkv[:, here_cols] = head.astype(BF)
        arrived = []
        for j in range(nz):
            owner = z ^ j
            for i, size in enumerate(widths):
                base = b * part_cols + i * nz * widths[0]
                source = qkv.at[:, pl.ds(pl.multiple_of(base + owner * size, size), size)]
                target = heads_ref.at[my_rows, pl.ds(b * sum(widths) + i * widths[0], size)]
                if j == 0:
                    arrived.append(copy_here(source, target))
                else:
                    arrived.append(links.start(source, target, {"seq": owner}))
        arrivals.append(arrived)
    copy_here(proj, proj_hbm)
    transposed[0] = normed[...].T
    share(transposed.at[0], normed_t_hbm.at[:, place])
    share(dy_ref, dy_hbm.at[place])
    if plane:
        forward_first(outward)
        begin(wide[0])
    group, seq_len, _ = queries.shape
    factor = head_dim**-0.5 * LOG2E
    arriving, here_mixed = [], []
    for b in range(parts):
        for i, copy in enumerate(arrivals[b]):
            if i < 2:
                copy.wait()
            else:
                copy.wait_recv()
        first = b * sum(widths)
        for g in range(group):
            queries[g] = heads_ref[:, first + g * head_dim : first + (g + 1) * head_dim]
        first += widths[0]
        keys[...] = heads_ref[:, first : first + head_dim]
        values[...] = heads_ref[:, first + head_dim : first + 2 * head_dim]
        for r in range(seq_len // rows):
            span = slice(r * rows, (r + 1) * rows)
            reach = (r + 1) * rows

            def one_head(g, _):
                scores = dot_nt(queries[g, span], keys[:reach]) * factor
                row = lax.broadcasted_iota(jnp.int32, scores.shape, 0) + r * rows
                col = lax.broadcasted_iota(jnp.int32, scores.shape, 1)
                probs = jnp.exp2(jnp.where(row >= col, scores, -1e30))
                total = jnp.sum(probs, axis=1, keepdims=True)
                full[g, span] = (dot_nn(probs.astype(BF), values[:reach]) * (1.0 / total)).astype(BF)
                log_ref[b * group + g, :, span] = jnp.broadcast_to(jnp.log2(total), (rows, 128)).T[0:8]
                return 0

            lax.fori_loop(0, group, one_head, 0)
        mix[b] = jnp.concatenate([full[g] for g in range(group)], axis=1)
        for j in range(nz):
            owner = z ^ j
            source = mix.at[b, pl.ds(pl.multiple_of(owner * tokens, tokens), tokens)]
            to = pl.multiple_of((z * parts + b) * widths[0], widths[0])
            target = mixed.at[:, pl.ds(to, widths[0])]
            if j == 0:
                here_mixed.append(copy_here(source, target))
            else:
                arriving.append(links.start(source, target, {"seq": owner}))
        if plane and b == 0:
            forward_far(outward)
            forward_first(down)
            end(outward)
            for s in range(8):
                copy_here(w_first.at[pl.ds(s * stride, shard)], first_hbm.at[pl.ds(s * shard, shard)])
            copy_here(w_second, second_hbm)
            forward_first(wide[0])
            begin(wide[1])
            begin(wide[2])
        if b == 0:
            out_copies = [
                copy_here(
                    w_first.at[pl.ds(s * stride, shard), pl.ds(part_cols, out_half)],
                    w_out.at[pl.ds(s * shard, shard), pl.ds(0, out_half)],
                )
                for s in range(model // shard)
            ]
            out_copies.append(copy_here(w_second.at[:, pl.ds(part_cols, out_half)], w_out.at[:, pl.ds(out_half, out_half)]))
    if plane:
        forward_far(down)
        end(down)
        wait_all(own_stores)
        forward_far(wide[0])
    for copy in arriving:
        copy.wait_recv()
    wait_all(here_mixed + out_copies)

    gain = gains_ref[2:3, :model]
    middle_rows = x_ref[...].astype(F32) + dot_nn(mixed[...], w_out[...])
    middle[...] = middle_rows
    total[...] = middle_rows
    normed_rows = (middle_rows * row_norm(middle_rows) * gain).astype(BF)
    normed[...] = normed_rows
    transposed[1] = normed_rows.T
    share(transposed.at[1], normed_two_hbm.at[:, place])
    transposed[2] = mixed[...].T
    share(transposed.at[2], mixed_t_hbm.at[:, place])
    back[...] = jnp.zeros(back.shape, F32)

    def slot_places(f):
        here = pl.ds(pl.multiple_of(f * width, width), width)
        return (
            (hidden_slot, hidden_hbm.at[here, place]),
            (gate_slot, gate_grad_hbm.at[place, here]),
            (up_slot, up_grad_hbm.at[place, here]),
        )

    def slot_copies(slot, f):
        return [
            pltpu.make_async_copy(s.at[slot], target, slot_sems.at[slot, i]) for i, (s, target) in enumerate(slot_places(f))
        ]

    def slot_links(slot, f):
        if not plane:
            return []
        return [
            pltpu.make_async_remote_copy(
                src_ref=s.at[slot],
                dst_ref=target,
                send_sem=slot_sends.at[slot, i],
                recv_sem=block_recvs.at[f, i],
                device_id=sibling,
                device_id_type=pl.DeviceIdType.MESH,
            )
            for i, (s, target) in enumerate(slot_places(f))
        ]

    def wait_slot(slot, f):
        wait_all(slot_copies(slot, f))
        for copy in slot_links(slot, f):
            copy.wait_send()

    def weight_copies(f):
        here = pl.ds(pl.multiple_of(f * width, width), width)
        slot = lax.rem(f, 2)
        pairs = ((gate_hbm.at[:, here], w_gate), (up_hbm.at[:, here], w_up), (down_hbm.at[here], w_down))
        return [
            pltpu.make_async_copy(source, target.at[slot], weight_sems.at[slot, i])
            for i, (source, target) in enumerate(pairs)
        ]

    blocks = hidden_cols // width
    firsts = [sum(groups[:g]) for g in range(len(groups))]

    ahead = [0, 0, firsts[min(1, len(firsts) - 1)] - 1] + firsts[2:]

    def arrive(f):
        for g in range(1, len(groups)):

            @pl.when(f == ahead[g])
            def _():
                forward_first(wide[g])
                if g + 2 < len(groups):
                    begin(wide[g + 2])

        for g in range(len(groups)):

            @pl.when(f == firsts[g])
            def _():
                if g:
                    forward_far(wide[g])
                end(wide[g])

    def one_block(f, _):
        slot = lax.rem(f, 2)
        if plane:
            arrive(f)

        def fetch(block):
            for copy in weight_copies(block):
                copy.start()

        in_first = f < (firsts[1] if plane else blocks)
        pl.when((f == 0) | ~in_first)(lambda: fetch(f))
        pl.when(in_first & (f + 1 < (firsts[1] if plane else blocks)))(lambda: fetch(f + 1))
        wait_all(weight_copies(f))

        @pl.when(f >= 2)
        def _():
            wait_slot(slot, f - 2)

        gate = dot_nn(normed[...], w_gate[slot])
        up = dot_nn(normed[...], w_up[slot])
        hidden_grad = dot_nt(dy_ref[...], w_down[slot])
        s = 1.0 / (1.0 + jnp.exp(-gate))
        silu = gate * s
        hidden = (silu * up).astype(BF)
        gate_grad = (hidden_grad * up * (s * (1.0 + gate * (1.0 - s)))).astype(BF)
        up_grad = (hidden_grad * silu).astype(BF)
        hidden_slot[slot] = hidden.T
        gate_slot[slot] = gate_grad
        up_slot[slot] = up_grad
        for copy in slot_copies(slot, f) + slot_links(slot, f):
            copy.start()
        total[...] = total[...] + dot_nn(hidden, w_down[slot])
        back[...] = back[...] + (dot_nt(gate_grad, w_gate[slot]) + dot_nt(up_grad, w_up[slot]))
        return 0

    lax.fori_loop(0, blocks, one_block, 0)
    output_ref[...] = total[...].astype(BF)
    part, gain_sum = norm_back(middle[...], gain, back[...])
    gain_grad_ref[...] = gain_sum
    middle_grad = dy_ref[...].astype(F32) + part
    middle_grad_ref[...] = middle_grad
    middle_low = middle_grad.astype(BF)
    middle_low_ref[...] = middle_low
    mixed_grad = dot_nt(middle_low, w_out[...]).astype(BF)
    grad_low[...] = mixed_grad
    product = mixed_grad.astype(F32) * mixed[...].astype(F32)
    heads = mixed.shape[1] // head_dim // nz
    row = lax.broadcasted_iota(jnp.int32, (8 * nz, mixed.shape[1]), 0)
    col = lax.broadcasted_iota(jnp.int32, (8 * nz, mixed.shape[1]), 1)
    pick = ((col // head_dim == (row // 8) * heads + row % 8) & (row % 8 < heads)).astype(BF)
    high = product.astype(BF)
    delta_ref[...] = dot_nt(pick, high) + dot_nt(pick, (product - high.astype(F32)).astype(BF))
    for f in (blocks - 2, blocks - 1):
        wait_slot(f % 2, f)
    if plane:
        for f in range(blocks):
            for copy in slot_links(f % 2, f):
                copy.wait_recv()
        for copy in to_core:
            copy.wait_recv()
        links.wait_sends()
    done = here + out_copies + here_mixed + [c for arrived in arrivals for c in arrived[:2]]
    if plane:
        done += own_loads + own_stores
    for copy in local:
        if not any(copy is other for other in done):
            copy.wait()


def both_cores(links, copy_here, me, source, target, axis):
    size = source.shape[axis]
    here = pl.ds(pl.multiple_of(lax.rem(me, 2) * size, size), size)
    place = target.at[here] if axis == 0 else target.at[:, here]
    copy_here(source, place)
    return links.start(source, place, {"fsdp": me ^ 1})


def attend_back(dims, b, heads_ref, grads_ref, log_ref, delta_ref, packed, scratch):
    rows, chunk = dims
    queries, keys, values, grad, q_grad, k_grad, v_grad = scratch
    group, seq_len, head_dim = queries.shape
    first = b * (group + 2) * head_dim
    for g in range(group):
        queries[g] = heads_ref[:, first + g * head_dim : first + (g + 1) * head_dim]
        at = (b * group + g) * head_dim
        grad[g] = grads_ref[:, at : at + head_dim]
        q_grad[g] = jnp.zeros((seq_len, head_dim), F32)
    first += group * head_dim
    keys[...] = heads_ref[:, first : first + head_dim]
    values[...] = heads_ref[:, first + head_dim : first + 2 * head_dim]
    factor = head_dim**-0.5
    scale = factor * LOG2E
    for at in range(seq_len // rows):
        span = slice(at * rows, (at + 1) * rows)
        key, value = keys[span], values[span]
        k_grad[span] = jnp.zeros((rows, head_dim), F32)
        v_grad[span] = jnp.zeros((rows, head_dim), F32)

        def one_head(g, _):
            key_total = jnp.zeros((rows, head_dim), F32)
            value_total = jnp.zeros((rows, head_dim), F32)
            for start in range(at * rows, seq_len, chunk):
                part = slice(start, min(start + chunk, seq_len))
                query, out_grad = queries[g, part], grad[g, part]
                scores = dot_nt(key, query) * scale - log_ref[b * group + g, 0:1, part]
                if start == at * rows:
                    key_at = lax.broadcasted_iota(jnp.int32, scores.shape, 0) + at * rows
                    query_at = lax.broadcasted_iota(jnp.int32, scores.shape, 1) + start
                    scores = jnp.where(query_at >= key_at, scores, -1e30)
                probs = jnp.exp2(scores)
                prob_grad = dot_nt(value, out_grad)
                score_grad = (probs * (prob_grad - delta_ref[b * group + g, 0:1, part])).astype(BF)
                value_total = value_total + dot_nn(probs.astype(BF), out_grad)
                key_total = key_total + dot_nn(score_grad, query)
                q_grad[g, part] = q_grad[g, part] + dot_tn(score_grad, key)
            k_grad[span] = k_grad[span] + key_total
            v_grad[span] = v_grad[span] + value_total
            return 0

        lax.fori_loop(0, group, one_head, 0)
        parts = [(q_grad[g, span] * factor).astype(BF) for g in range(group)]
        parts += [(k_grad[span] * factor).astype(BF), v_grad[span].astype(BF)]
        packed[span] = jnp.concatenate(parts, axis=1)
        yield at


def attend_back_scratch(group, seq_len, head_dim):
    many = lambda kind: pltpu.VMEM((group, seq_len, head_dim), kind)
    one = lambda kind: pltpu.VMEM((seq_len, head_dim), kind)
    return [many(BF), one(BF), one(BF), many(BF), many(F32), one(F32), one(F32)]


def attend_back_kernel(dims, heads_ref, grads_ref, log_ref, delta_ref, packed, *scratch):
    for b in range(packed.shape[0]):
        for _ in attend_back(dims, b, heads_ref, grads_ref, log_ref, delta_ref, packed.at[b], scratch):
            pass


def norm_back(rows, gain, gradient):
    q = row_norm(rows)
    n = rows * q
    u = gradient * gain
    return q * (u - n * jnp.mean(u * n, axis=-1, keepdims=True)), jnp.sum(gradient * n, axis=0, keepdims=True)


def weight_grad_kernel(left_ref, right_ref, out_ref):
    out_ref[...] = dot_nn(left_ref[...], right_ref[...]).astype(BF)


def weight_grad(left, right, width=256):
    rows, tokens = left.shape
    cols = right.shape[1]
    return call(
        weight_grad_kernel,
        shape_of((rows, cols), BF),
        [pl.BlockSpec((rows, tokens), lambda n: (0, 0)), pl.BlockSpec((tokens, width), lambda n: (0, n))],
        pl.BlockSpec((rows, width), lambda n: (0, n)),
        [],
        2 * rows * tokens * cols,
        2 * (rows * tokens + tokens * cols + rows * cols),
        grid=(cols // width,),
    )(left, right)


def project_back(dims, b, gains_ref, cos_ref, sin_ref, proj_ref, qkv, head_gain_grad_ref):
    nz, head_dim, widths = dims
    part_cols = nz * sum(widths)
    width = 256
    mask = head_mask(width, head_dim)
    cos = jnp.concatenate([cos_ref[...]] * (width // 128), axis=1)
    sin = jnp.concatenate([sin_ref[...]] * (width // 128), axis=1)
    for start in range(0, part_cols, width):
        cols = slice(b * part_cols + start, b * part_cols + start + width)
        rotated = qkv[:, cols].astype(F32)
        gradient = rotated * cos - partner(rotated, head_dim) * sin
        proj = proj_ref[:, start : start + width]
        scale = lax.rsqrt(head_sum(proj * proj, mask) * (1.0 / head_dim) + EPSILON)
        n = proj * scale
        u = gradient * gains_ref[1:2, start : start + width]
        head_gain_grad_ref[:, cols] = jnp.sum(gradient * n, axis=0, keepdims=True)
        back = scale * (u - n * (head_sum(u * n, mask) * (1.0 / head_dim)))
        if start >= nz * widths[0]:
            back = jnp.where(key_lanes(back.shape, head_dim), back, rotated)
        qkv[:, cols] = back.astype(BF)


def input_back(x_ref, middle_grad_ref, gains_ref, qkv, weight, input_grad_ref, gain_grad_ref):
    normed_grad = dot_nt(qkv[...], weight[...])
    part, gain_sum = norm_back(x_ref[...].astype(F32), gains_ref[0:1, : x_ref.shape[1]], normed_grad)
    gain_grad_ref[...] = gain_sum
    input_grad_ref[...] = (middle_grad_ref[...] + part).astype(BF)


def post_kernel(dims, x_ref, middle_grad_ref, gains_ref, cos_ref, sin_ref, proj_ref, grads_ref, weight_ref, *refs):
    input_grad_ref, qkv, gain_grad_ref, head_gain_grad_ref = refs
    nz, _, widths = dims
    qkv[...] = grads_ref[...]
    for b in range(qkv.shape[1] // (nz * sum(widths))):
        part_cols = nz * sum(widths)
        part = proj_ref.at[:, pl.ds(b * part_cols, part_cols)]
        project_back(dims, b, gains_ref, cos_ref, sin_ref, part, qkv, head_gain_grad_ref)
    input_back(x_ref, middle_grad_ref, gains_ref, qkv, weight_ref, input_grad_ref, gain_grad_ref)


class Reduce:
    def __init__(self, links, fetch, me, z, x_first, away, kept, first, second, inward, across, out):
        self.links, self.fetch, self.me, self.z = links, fetch, me, z
        self.away, self.kept, self.out = away, kept, out
        self.bits = (2, 4) if x_first else (4, 2)
        order = (1, 3, 0, 2) if x_first else (2, 3, 0, 1)
        self.slots = {r: (away if i < 2 else kept, i % 2) for i, r in enumerate(order)}
        self.arrived, self.second, self.inward, self.across = first, second, inward, across
        self.outer, self.inner = (z == 0) | (z == 3), (z == 1) | (z == 2)
        self.one = links.copy(away, first, {"fsdp": me ^ self.bits[0]})
        self.two = links.copy(kept.at[1], second, {"fsdp": me ^ self.bits[1]})
        self.three = links.copy(kept.at[0], inward, {"seq": z ^ 1})
        self.four = links.copy(kept.at[0], across, {"seq": z ^ 3})
        self.five = links.copy(kept.at[1], out, {"seq": z ^ 1})
        self.here = fetch.copy(kept.at[1], out)
        self.load = fetch.copy(first, away)

    def put(self, r, cols, values):
        ref, i = self.slots[r]
        ref[i, :, cols] = values

    def rows_of(self):
        rows = self.kept.shape[1]
        step = 32 if rows % 32 == 0 else 16
        return rows // step, step

    def by_rows(self, work):
        count, step = self.rows_of()

        def body(i, _):
            work(pl.ds(pl.multiple_of(i * step, step), step))
            return 0

        lax.fori_loop(0, count, body, 0)

    def begin(self):
        self.one.start()

    def load_one(self):
        self.one.wait_recv()
        self.one.wait_send()
        self.load.start()

    def fold_one(self):
        self.load.wait()

        def work(rows):
            for i in range(2):
                self.kept[i, rows] = self.kept[i, rows] + self.away[i, rows]

        self.by_rows(work)
        self.two.start()

    def fold_two(self):
        self.two.wait_recv()

        def work(rows):
            self.kept[0, rows] = self.kept[0, rows] + self.second[rows]

        self.by_rows(work)

        @pl.when(self.outer)
        def _():
            self.three.start()

    def fold_three(self):
        @pl.when(self.inner)
        def _():
            self.three.wait_recv()

            def work(rows):
                self.kept[0, rows] = self.kept[0, rows] + self.inward[rows]

            self.by_rows(work)
            self.four.start()

    def fold_four(self):
        self.two.wait_send()

        @pl.when(self.inner)
        def _():
            self.four.wait_recv()

            def work(rows):
                self.kept[1, rows] = self.kept[0, rows] + self.across[rows]

            self.by_rows(work)
            self.five.start()
            self.here.start()

    def end(self):
        @pl.when(self.inner)
        def _():
            self.four.wait_send()
            self.five.wait_send()
            self.here.wait()

        @pl.when(self.outer)
        def _():
            self.three.wait_send()
            self.five.wait_recv()


def each(reduces, step):
    if step == "fold_one":
        each(reduces, "load_one")
    for reduce in reduces:
        getattr(reduce, step)()


class Total:
    def __init__(self, links, me, z, sums, arrived):
        self.sums, self.arrived = sums, arrived
        peers = [{"fsdp": me ^ 1}, {"fsdp": me ^ 2}, {"fsdp": me ^ 4}, {"seq": z ^ 1}, {"seq": z ^ 2}]
        self.copies = [links.copy(sums.at[i], arrived.at[i], peer) for i, peer in enumerate(peers)]

    def begin(self, at):
        self.copies[at].start()

    def fold(self, at):
        self.copies[at].wait_recv()
        self.sums[at + 1] = self.sums[at] + self.arrived[at]

    def end(self):
        for copy in self.copies:
            copy.wait_send()


EARLY = (
    ("down0", "matmul"), ("down0", "begin"), ("out", "matmul"), ("out", "begin"), ("down1", "matmul"),
    ("wide0", "matmul"), ("wide1", "matmul"),
)
MIDDLE = (
    ("keys", 0, 0), ("down0", "fold_one"), ("keys", 0, 1), ("keys", 0, 2), ("down1", "begin"), ("keys", 0, 3),
    ("down0", "fold_two"), ("wide1", "begin"), ("keys", 0, 4), ("keys", 0, 5), ("keys", 0, 6), ("keys", 0, 7),
    ("keys", 1, 0), ("keys", 1, 1), ("keys", 1, 2), ("down1", "fold_one"), ("keys", 1, 3), ("keys", 1, 4),
    ("keys", 1, 5), ("out", "fold_one"), ("keys", 1, 6), ("keys", 1, 7), ("wide1", "fold_one"), ("wide2", "matmul"),
    ("wide2", "begin"), ("down1", "fold_two"), ("project", 0), ("down0", "fold_three"), ("wide1", "fold_two"),
    ("last0", "matmul"), ("project", 1),
)
LATE = (
    ("last0", "begin"), ("down1", "fold_three"), ("wide2", "fold_one"), ("down0", "fold_four"), ("last1", "matmul"),
    ("last0", "fold_one"), ("wide1", "fold_three"), ("last1", "begin"), ("down1", "fold_four"), ("out", "fold_two"),
    ("wide0", "begin"), ("out", "fold_three"), ("input",), ("wide2", "fold_two"), ("wide1", "fold_four"), ("total", 0),
    ("wide2", "fold_three"), ("last0", "fold_two"), ("last1", "fold_one"), ("wide0", "fold_one"), ("total", 1),
    ("out", "fold_four"), ("last1", "fold_two"), ("last0", "fold_three"), ("wide2", "fold_four"),
    ("last1", "fold_three"), ("wide0", "fold_two"), ("last0", "fold_four"), ("total", 2), ("wide0", "fold_three"),
    ("last1", "fold_four"), ("total", 3), ("wide0", "fold_four"), ("total", 4),
)


def backward_kernel(dims, gains_ref, cos_ref, sin_ref, heads_ref, log_ref, grad_low, delta_own, low_ref, feed_gain_ref, *refs):
    nz, head_dim, widths, attend_dims, names = dims
    given, refs = refs[:12], refs[12:]
    x_hbm, middle_grad_hbm, proj_hbm, hidden_hbm, dy_hbm, normed_two_hbm = given[:6]
    gate_hbm, up_hbm, mixed_hbm, normed_hbm, first_hbm, second_hbm = given[6:]
    input_grad_ref, totals_ref = refs[:2]
    n = len(names)
    finals, refs = dict(zip(names, refs[2 : 2 + n])), refs[2 + n :]
    firsts, refs = dict(zip(names, refs[:n])), refs[n:]
    low_hbm, refs = refs[0], refs[1:]
    aways, refs = dict(zip(names, refs[:n])), refs[n:]
    kepts, refs = dict(zip(names, refs[:n])), refs[n:]
    seconds, refs = dict(zip(names, refs[:n])), refs[n:]
    inwards, refs = dict(zip(names, refs[:n])), refs[n:]
    acrosses, refs = dict(zip(names, refs[:n])), refs[n:]
    grads, delta, qkv, other_qkv, normed_two, normed, sums, sum_arrived, gain_grad, head_gain_grad = refs[:10]
    sems, send_sems, recv_sems = refs[10:]
    z, me = lax.axis_index("seq"), lax.axis_index("fsdp")
    chip, core = lax.div(me, 2), lax.rem(me, 2)
    enter(me, z, nz, True)
    links, fetch = Links(send_sems, recv_sems), Fetch(sems)
    tokens = grad_low.shape[0]
    seq_len, block_cols = heads_ref.shape
    part_cols = nz * sum(widths)
    parts = qkv.shape[1] // part_cols
    late = []

    def copy_here(source, target):
        copy = fetch.start(source, target)
        late.append(copy)
        return copy

    my_rows = pl.ds(pl.multiple_of(z * tokens, tokens), tokens)
    arrivals = []
    for b in range(parts):
        arrived = []
        for j in range(nz):
            owner = z ^ j
            from_cols = pl.ds(pl.multiple_of((owner * parts + b) * widths[0], widths[0]), widths[0])
            pairs = [(grad_low.at[:, from_cols], grads.at[my_rows, pl.ds(b * widths[0], widths[0])])]
            if b == 0:
                pairs.append((delta_own.at[pl.ds(pl.multiple_of(owner * 8, 8), 8)], delta.at[:, my_rows]))
            for source, target in pairs:
                if j == 0:
                    copy_here(source, target)
                else:
                    arrived.append(links.start(source, target, {"seq": owner}))
        arrivals.append(arrived)
    low_arrival = both_cores(links, copy_here, me, low_ref, low_hbm, 0)
    reduces = {}
    for name in names:
        reduces[name] = Reduce(
            links, fetch, me, z, name[-1] == "x", aways[name], kepts[name], firsts[name], seconds[name], inwards[name],
            acrosses[name], finals[name],
        )
    down = [[reduces[f"down{c}{way}"] for way in "xy"] for c in range(2)]
    gate, up = [reduces["gate0x"], reduces["gate1y"], reduces["gate2x"]], [reduces["up0y"], reduces["up1x"], reduces["up2y"]]
    wide = [gate[:2], [gate[2], up[0]], up[1:]]
    out = [reduces["outx"], reduces["outy"]]
    last = [[reduces[f"last{b}{way}"] for way in "xy"] for b in range(parts)]
    total = Total(links, me, z, sums, sum_arrived)
    part_cols_of = lambda b: pl.ds(b * part_cols, part_cols)
    qkv_links = [
        links.copy(qkv.at[:, part_cols_of(b)], other_qkv.at[:, part_cols_of(b)], {"fsdp": me ^ 1}) for b in range(parts)
    ]
    chips = 4
    step = 256
    half = down[0][0].kept.shape[1]
    shard = gate[0].kept.shape[1]
    both = 2 * tokens
    model = low_ref.shape[1]

    def my_blocks(source, target, rows):
        copies = []
        for r in range(chips):
            owner = (chip ^ r) * 2 + core
            copies.append(fetch.start(source.at[pl.ds(pl.multiple_of(owner * rows, rows), rows)], target.at[pl.ds(r * rows, rows)]))
        return copies

    def wide_grads(places, left, right):
        width = right.shape[2]
        chunks = [
            (source, (first + c) * width, unit, c * width)
            for source, first, unit in places
            for c in range(unit.kept.shape[2] // width)
        ]
        count = len(chunks)
        loads = [
            fetch.copy(source.at[:, pl.ds(at, width)], right.at[c % 2]) for c, (source, at, _, _) in enumerate(chunks)
        ]
        loads[0].start()
        loads[1].start()
        for c in range(count):
            loads[c].wait()
            _, _, unit, base = chunks[c]

            def block(k, _):
                here = pl.ds(pl.multiple_of(k * step, step), step)
                to = pl.ds(pl.multiple_of(base + k * step, step), step)
                got = dot_nn(left[...], right[c % 2, :, here]).astype(BF)
                for r in range(chips):
                    unit.put(r, to, got[r * shard : (r + 1) * shard])
                return 0

            lax.fori_loop(0, width // step, block, 0)
            if c + 2 < count:
                loads[c + 2].start()

    ready = {"two": my_blocks(normed_two_hbm, normed_two, shard), "one": my_blocks(normed_hbm, normed, shard)}

    def ready_now(name):
        wait_all(ready.pop(name, ()))

    per_unit = 2
    wide_part = gate[0].kept.shape[2] // per_unit
    sides = {"gate": gate_hbm, "up": up_hbm}
    wide_names = (("gate", 0), ("gate", 1), ("gate", 2), ("up", 0), ("up", 1), ("up", 2))

    def wide_matmul(i, right):
        ready_now("two")
        pair = zip(wide_names[2 * i : 2 * i + 2], wide[i])
        wide_grads([(sides[kind], at * per_unit, unit) for (kind, at), unit in pair], normed_two, right)

    def out_matmul(mixed, low):
        cols = out[0].kept.shape[2]
        for start in range(0, low.shape[1], step):
            got = dot_nn(mixed[...], low[:, start : start + step]).astype(BF)
            for r in range(chips):
                out[start // cols].put(r, slice(start % cols, start % cols + step), got[r * shard : (r + 1) * shard])

    def down_matmul(c, hidden, dy):
        cols = down[0][0].kept.shape[2]

        def block(i, _):
            to = pl.ds(pl.multiple_of(i * step, step), step)
            here = pl.ds(pl.multiple_of(c * cols + i * step, step), step)
            for r in range(chips):
                got = dot_nn(hidden[2 * r * half : 2 * (r + 1) * half], dy[:, here]).astype(BF)
                for side in range(2):
                    down[c][side].put(r, to, got[side * half : (side + 1) * half])
            return 0

        lax.fori_loop(0, cols // step, block, 0)

    def last_matmul(b):
        ready_now("one")
        mine = normed[:, pl.ds(pl.multiple_of(core * tokens, tokens), tokens)]
        theirs = normed[:, pl.ds(pl.multiple_of((1 - core) * tokens, tokens), tokens)]
        qkv_links[b].wait()
        cols = last[b][0].kept.shape[2]
        for start in range(0, part_cols, step):
            here = slice(b * part_cols + start, b * part_cols + start + step)
            got = (dot_nn(mine, qkv[:, here]) + dot_nn(theirs, other_qkv[:, here])).astype(BF)
            for r in range(chips):
                last[b][start // cols].put(r, slice(start % cols, start % cols + step), got[r * shard : (r + 1) * shard])

    pairs = {"out": out}
    pairs |= {f"down{c}": down[c] for c in range(2)}
    pairs |= {f"wide{i}": wide[i] for i in range(3)}
    pairs |= {f"last{b}": last[b] for b in range(parts)}
    right_shape = pltpu.VMEM((2, both, wide_part), BF)

    def sum_step(name, what):
        if what != "matmul":
            each(pairs[name], what)
        elif name[:4] == "last":
            last_matmul(int(name[4]))
        else:
            pl.run_scoped(functools.partial(wide_matmul, int(name[4])), right_shape)

    def early(hidden, dy, right, mixed, low):
        ready["down"] = my_blocks(hidden_hbm, hidden, 2 * half) + [fetch.start(dy_hbm, dy)]
        ready["out"] = my_blocks(mixed_hbm, mixed, shard)
        for name, what in EARLY:
            if what != "matmul":
                each(pairs[name], what)
            elif name[:4] == "down":
                ready_now("down")
                down_matmul(int(name[4]), hidden, dy)
            elif name == "out":
                low_arrival.wait_recv()
                wait_all(late)
                del late[:]
                ready["out"].append(fetch.start(low_hbm, low))
                ready_now("out")
                out_matmul(mixed, low)
            else:
                wide_matmul(int(name[4]), right)

    pl.run_scoped(
        early,
        pltpu.VMEM((2 * chips * half, both), BF),
        pltpu.VMEM((both, model), BF),
        right_shape,
        pltpu.VMEM((chips * shard, both), BF),
        pltpu.VMEM((both, model), BF),
    )

    heads = log_ref.shape[0]
    group = heads // parts
    first_back = links.reserve(parts * 2 * nz)
    own_back = fetch.used
    fetch.used += parts * 2

    def back_copies(b, packed):
        for i, width in enumerate(widths):
            base = b * part_cols + i * nz * widths[0]
            target = qkv.at[:, pl.ds(pl.multiple_of(base + z * width, width), width)]
            for j in range(nz):
                owner = z ^ j
                rows = pl.ds(pl.multiple_of(owner * tokens, tokens), tokens)
                source = packed.at[b, rows, pl.ds(i * widths[0], width)]
                if j == 0:
                    yield j, pltpu.make_async_copy(source, target, sems.at[own_back + 2 * b + i])
                else:
                    yield j, links.copy(source, target, {"seq": owner}, at=first_back + (2 * b + i) * nz + j)

    def middle(packed, delta_rows, *scratch):
        blocks = {}

        def keys_step(b, at):
            if at == 0:
                for copy in arrivals[b]:
                    copy.wait_recv()
                if b == 0:
                    for h in range(heads):
                        delta_rows[h] = jnp.broadcast_to(delta[h : h + 1], (8, seq_len))
                blocks[b] = attend_back(attend_dims, b, heads_ref, grads, log_ref, delta_rows, packed.at[b], scratch)
            next(blocks[b])
            if (at + 1) * attend_dims[0] == seq_len:
                for _, copy in back_copies(b, packed):
                    copy.start()

        def project_step(b):
            for j, copy in back_copies(b, packed):
                if j == 0:
                    copy.wait()
                else:
                    copy.wait_recv()

            def inner(proj):
                fetch.start(proj_hbm.at[:, part_cols_of(b)], proj).wait()
                project_back((nz, head_dim, widths), b, gains_ref, cos_ref, sin_ref, proj, qkv, head_gain_grad)

            pl.run_scoped(inner, pltpu.VMEM((tokens, part_cols), F32))
            qkv_links[b].start()

        for token in MIDDLE:
            if token[0] == "keys":
                keys_step(*token[1:])
            elif token[0] == "project":
                project_step(token[1])
            else:
                sum_step(*token)
        for b in range(parts):
            for j, copy in back_copies(b, packed):
                if j:
                    copy.wait_send()

    pl.run_scoped(
        middle,
        pltpu.VMEM((parts, seq_len, sum(widths)), BF),
        pltpu.VMEM((heads, 8, seq_len), F32),
        *attend_back_scratch(group, seq_len, head_dim),
    )

    def input_step(weight, x, middle_grad):
        copies = [fetch.start(x_hbm, x), fetch.start(middle_grad_hbm, middle_grad)]
        for b, source in enumerate((first_hbm, second_hbm)):
            copies.append(fetch.start(source.at[:, pl.ds(0, part_cols)], weight.at[:, part_cols_of(b)]))
        wait_all(copies)
        input_back(x, middle_grad, gains_ref, qkv, weight, input_grad_ref, gain_grad)
        row = jnp.concatenate([gain_grad[...], head_gain_grad[...], feed_gain_ref[...]], axis=1)
        sums[0] = jnp.broadcast_to(row, sums.shape[1:])

    for token in LATE:
        if token[0] == "input":
            pl.run_scoped(
                input_step,
                pltpu.VMEM((model, parts * part_cols), BF),
                pltpu.VMEM((tokens, model), BF),
                pltpu.VMEM((tokens, model), F32),
            )
            total.begin(0)
        elif token[0] == "total":
            total.fold(token[1])
            if token[1] < 4:
                total.begin(token[1] + 1)
        else:
            sum_step(*token)
    totals_ref[...] = sums[5]
    total.end()
    for name in names:
        reduces[name].end()
    links.wait_sends()


def finish_kernel(dims, *refs):
    names, nz, head_dim = dims
    n = len(names)
    output_in, input_grad_in = refs[:2]
    shards, refs = dict(zip(names, refs[2 : 2 + n])), refs[2 + n :]
    output, input_grad, q_out, k_out, v_out, out_out, gate_out, up_out, down_out = refs[:9]
    slots, refs = dict(zip(names, refs[9 : 9 + n])), refs[9 + n :]
    passing, q, k, v, out, gate, up, down, load_sems, store_sems = refs
    fetch, store = Fetch(load_sems), Fetch(store_sems)
    wide = [name for name in names if name[:4] in ("gate", "up0y", "up1x", "up2y")]
    order = wide + [name for name in names if name not in wide]
    loads = {name: fetch.start(shards[name], slots[name]) for name in order}
    moves = [fetch.start(source, passing.at[i]) for i, source in enumerate((output_in, input_grad_in))]
    stores = []

    def place(name, target, row, col):
        loads[name].wait()
        rows, cols = slots[name].shape
        target[row : row + rows, col : col + cols] = slots[name][...].astype(F32)

    cols = slots["gate0x"].shape[1]
    for target, done, pieces in (
        (gate, gate_out, ("gate0x", "gate1y", "gate2x")),
        (up, up_out, ("up0y", "up1x", "up2y")),
    ):
        for i, name in enumerate(pieces):
            place(name, target, 0, i * cols)
        stores.append(store.start(target, done))
    rows, cols = slots["down0x"].shape
    for c in range(2):
        for i, way in enumerate("xy"):
            place(f"down{c}{way}", down, i * rows, c * cols)
    stores.append(store.start(down, down_out))
    cols = slots["outx"].shape[1]
    for i, way in enumerate("xy"):
        place("out" + way, out, 0, i * cols)
    stores.append(store.start(out, out_out))
    parts = 2
    width = q.shape[1] // (nz * parts)
    for b in range(parts):
        loads[f"last{b}x"].wait()
        for i in range(nz):
            to = (i * parts + b) * width
            q[:, to : to + width] = slots[f"last{b}x"][:, i * width : (i + 1) * width].astype(F32)
    stores.append(store.start(q, q_out))
    for b in range(parts):
        loads[f"last{b}y"].wait()
    for i, target in enumerate((k, v)):
        pieces = [
            slots[f"last{b}y"][:, (2 * at + i) * head_dim : (2 * at + i + 1) * head_dim]
            for at in range(nz)
            for b in range(parts)
        ]
        target[...] = jnp.concatenate(pieces, axis=1).astype(F32)
    stores += [store.start(k, k_out), store.start(v, v_out)]
    for i, target in enumerate((output, input_grad)):
        moves[i].wait()
        stores.append(store.start(passing.at[i], target))
    wait_all(stores)


def add(a, b):
    return (a.astype(F32) + b.astype(F32)).astype(a.dtype)


def sum_line(values):
    size = lax.axis_size("seq")
    if size != 4:
        return lax.psum(values, "seq")
    z = lax.axis_index("seq")
    inner = add(values, lax.ppermute(values, "seq", [(0, 1), (3, 2)]))
    total = add(inner, lax.ppermute(inner, "seq", [(1, 2), (2, 1)]))
    outer = lax.ppermute(total, "seq", [(1, 0), (2, 3)])
    return jnp.where((z == 1) | (z == 2), total, outer)


def per_device(
    inputs,
    positions,
    cotangent,
    query_weight,
    key_weight,
    value_weight,
    out_weight,
    attention_gain,
    query_gain,
    key_gain,
    feedforward_gain,
    gate_weight,
    up_weight,
    down_weight,
):
    seqs, tokens, model = inputs.shape
    assert seqs == 1
    fsdp, nz = lax.axis_size("fsdp"), lax.axis_size("seq")
    me, z = lax.axis_index("fsdp"), lax.axis_index("seq")
    plane = fsdp == 8 and nz == 4
    both = 2 * tokens if plane else tokens
    x = inputs.reshape(tokens, model)
    dy = cotangent.reshape(tokens, model)
    head_dim = query_gain.shape[0] * fsdp
    q_cols, k_cols, v_cols = query_weight.shape[1], key_weight.shape[1], value_weight.shape[1]
    heads, kv_heads = q_cols // head_dim // nz, k_cols // head_dim // nz
    hidden_cols = gate_weight.shape[1]
    seq_len = tokens * nz

    group, parts = heads // kv_heads, kv_heads
    widths = (group * head_dim, 2 * head_dim)
    part_cols = nz * sum(widths)
    assert parts == 2

    def by_parts(query, key, value):
        rows = query.shape[0]
        q = query.reshape(rows, nz, parts, widths[0])
        kv = jnp.stack([v.reshape(rows, nz, parts, head_dim) for v in (key, value)], axis=3).reshape(rows, nz, parts, widths[1])
        return [jnp.concatenate([v[:, :, b].reshape(rows, -1) for v in (q, kv)], axis=1) for b in range(parts)]

    first, second = by_parts(query_weight, key_weight, value_weight)
    half_out = model // 2
    first = jnp.concatenate([first, out_weight[:, :half_out]], axis=1)
    second = jnp.concatenate([second, out_weight[:, half_out:]], axis=1)
    first_cols = first.shape[1]

    def spread(values, count=1):
        share = values.shape[0]
        own = (jnp.arange(share * fsdp * count) % (share * fsdp)) // share == me
        return jnp.where(own, jnp.tile(values, fsdp * count), jnp.zeros((), BF))

    def gain_row(values):
        return jnp.concatenate([values, jnp.zeros((first_cols - values.shape[0],), BF)])

    key_row = jnp.concatenate([spread(key_gain), jnp.zeros((head_dim,), BF)])
    head_row = jnp.concatenate([spread(query_gain, nz * group), jnp.tile(key_row, nz)])
    gain_rows = [gain_row(spread(attention_gain)), gain_row(head_row), gain_row(spread(feedforward_gain))]
    gain_rows = jnp.stack(gain_rows + [jnp.zeros((first_cols,), BF)] * 13)
    if plane:
        given = [jnp.concatenate([first, gain_rows]), second, gate_weight, up_weight, down_weight]
    else:
        gather = functools.partial(lax.all_gather, axis_name="fsdp", axis=0, tiled=True)
        first_full, second_full, gate_full = gather(first), gather(second), gather(gate_weight)
        up_full, down_full = gather(up_weight), gather(down_weight)
        given = [first_full, second_full, lax.psum(gain_rows.astype(F32), "fsdp"), gate_full, up_full, down_full]

    half_dim = head_dim // 2
    lane = jnp.arange(128)
    freqs = ROPE_BASE ** (-(lane % half_dim).astype(F32) / half_dim)
    angles = positions.reshape(tokens).astype(F32)[:, None] * freqs[None, :]
    cosine = jnp.cos(angles)
    sine = jnp.sin(angles) * jnp.where(lane % head_dim < half_dim, -1.0, 1.0)[None, :]

    width = 512
    blocks = hidden_cols // width
    sizes = (blocks - 6,) + (1,) * 6
    block_cols = parts * sum(widths)
    mixed_cols = heads * head_dim
    attend_flops = 2 * heads * seq_len * seq_len * head_dim
    proj_flops = 2 * tokens * model * parts * part_cols
    rows_model = lambda kind: shape_of((tokens, model), kind)
    outs = [
        shape_of((16, part_cols), F32),
        shape_of((seq_len, block_cols), BF),
        shape_of((heads, 8, seq_len), F32),
        rows_model(BF),
        rows_model(F32),
        rows_model(BF),
        shape_of((1, model), F32),
        shape_of((tokens, q_cols), BF),
        shape_of((8 * nz, tokens), F32),
        shape_of((tokens, parts * part_cols), F32),
        shape_of((model, both), BF),
        shape_of((q_cols, both), BF),
        shape_of((model, both), BF),
        shape_of((hidden_cols, both), BF),
        shape_of((both, hidden_cols), BF),
        shape_of((both, hidden_cols), BF),
        shape_of((both, model), BF),
    ]
    n_links = parts * 3 * (nz - 1)
    first_rows = model
    if plane:
        outs += [shape_of((model, first_cols), BF)] * 2
        outs += [shape_of((model, hidden_cols), BF)] * 2 + [shape_of((hidden_cols, model), BF)]
        n_links += (6 + 2 * len(sizes)) * 7 + 4
        first_rows += 8 * 16
    many = lambda count: pltpu.VMEM((count, seq_len, head_dim), BF)
    one = pltpu.VMEM((seq_len, head_dim), BF)
    got = call(
        functools.partial(forward_kernel, (nz, plane, head_dim, widths, min(256, seq_len), width, sizes)),
        outs,
        [VMEM] * 4 + ([ANY] * 5 if plane else [ANY] * 2 + [VMEM] + [ANY] * 3),
        [VMEM] * 9 + [ANY] * (len(outs) - 9),
        [
            pltpu.VMEM((first_rows, first_cols), BF),
            pltpu.VMEM((model, first_cols), BF),
            pltpu.VMEM((q_cols, model), BF),
            pltpu.VMEM((tokens, model), BF),
            pltpu.VMEM((3, model, tokens), BF),
            pltpu.VMEM((tokens, parts * part_cols), F32),
            pltpu.VMEM((tokens, parts * part_cols), BF),
            many(group),
            one,
            one,
            many(group),
            pltpu.VMEM((parts, seq_len, widths[0]), BF),
            pltpu.VMEM((tokens, q_cols), BF),
            pltpu.VMEM((2, model, width), BF),
            pltpu.VMEM((2, model, width), BF),
            pltpu.VMEM((2, width, model), BF),
            pltpu.VMEM((tokens, model), F32),
            pltpu.VMEM((tokens, model), F32),
            pltpu.VMEM((tokens, model), F32),
            pltpu.VMEM((2, width, tokens), BF),
            pltpu.VMEM((2, tokens, width), BF),
            pltpu.VMEM((2, tokens, width), BF),
            pltpu.SemaphoreType.DMA((48,)),
            pltpu.SemaphoreType.DMA((2, 3)),
            pltpu.SemaphoreType.DMA((2, 3)),
            pltpu.SemaphoreType.DMA((n_links,)),
            pltpu.SemaphoreType.DMA((n_links,)),
            pltpu.SemaphoreType.DMA((2, 3)),
            pltpu.SemaphoreType.DMA((blocks, 3)),
        ]
        + [pltpu.VMEM(w.shape, BF) for w in (gate_weight, up_weight, down_weight) if plane],
        proj_flops + 4 * attend_flops + 12 * tokens * model * hidden_cols,
        100 * 2**20,
        collective=1,
    )(x, dy, cosine, sine, *given)
    gains, head_rows, logs, output, middle_grad, middle_low, feed_gain_part, mixed_grad, delta = got[:9]
    proj, normed_t, mixed_t, normed_two_t, hidden_t, gate_grad, up_grad, dy_both = got[9:17]
    if plane:
        first_full, second_full = got[17:19]

    attend_dims = (min(256, seq_len), min(1024, seq_len))
    attend_scratch = attend_back_scratch(group, seq_len, head_dim)
    if plane:
        down_rows, down_cols = down_weight.shape
        blocks = {f"down{c}{way}": (down_rows // 2, down_cols // 2) for c in range(2) for way in "xy"}
        wide_names = ("gate0x", "gate1y", "gate2x", "up0y", "up1x", "up2y")
        blocks |= {name: (gate_weight.shape[0], hidden_cols // 3) for name in wide_names}
        blocks |= {"out" + way: (out_weight.shape[0], model // 2) for way in "xy"}
        blocks |= {f"last{b}{way}": (query_weight.shape[0], part_cols // 2) for b in range(parts) for way in "xy"}
        names = tuple(blocks)
        pairs = [(2,) + shape for shape in blocks.values()]
        total_cols = model + parts * part_cols + model
        n_links = 3 * (nz - 1) + 2 * parts * nz + 1 + parts + 5 * len(names) + 5
        n_copies = 64 + 2 * len(names)
        got = call(
            functools.partial(backward_kernel, (nz, head_dim, widths, attend_dims, names)),
            [rows_model(BF), shape_of((8, total_cols), F32)]
            + [shape_of(shape, BF) for shape in blocks.values()]
            + [shape_of(shape, BF) for shape in pairs]
            + [shape_of((both, model), BF)],
            [VMEM] * 9 + [ANY] * 12,
            [VMEM] * 2 + [ANY] * (2 * len(names) + 1),
            [pltpu.VMEM(shape, BF) for shape in pairs] * 2
            + [pltpu.VMEM(shape, BF) for shape in blocks.values()] * 3
            + [
                pltpu.VMEM((seq_len, mixed_cols), BF),
                pltpu.VMEM((8, seq_len), F32),
                pltpu.VMEM((tokens, parts * part_cols), BF),
                pltpu.VMEM((tokens, parts * part_cols), BF),
                pltpu.VMEM((model // 2, both), BF),
                pltpu.VMEM((model // 2, both), BF),
                pltpu.VMEM((6, 8, total_cols), F32),
                pltpu.VMEM((5, 8, total_cols), F32),
                pltpu.VMEM((1, model), F32),
                pltpu.VMEM((1, parts * part_cols), F32),
                pltpu.SemaphoreType.DMA((n_copies,)),
                pltpu.SemaphoreType.DMA((n_links,)),
                pltpu.SemaphoreType.DMA((n_links,)),
            ],
            10 * attend_flops + 2 * tokens * model * (3 * hidden_cols + 3 * (q_cols + k_cols)),
            100 * 2**20,
            collective=3,
        )(
            gains, cosine, sine, head_rows, logs, mixed_grad, delta, middle_low, feed_gain_part, x, middle_grad, proj,
            hidden_t, dy_both, normed_two_t, gate_grad, up_grad, mixed_t, normed_t, first_full, second_full,
        )
        input_grad, totals = got[:2]
        slots = [pltpu.VMEM(shape, BF) for shape in blocks.values()]
        out_shapes = [w.shape for w in (query_weight, key_weight, value_weight, out_weight, gate_weight, up_weight, down_weight)]
        output, input_grad, q_shard, k_shard, v_shard, out_shard, gate_shard, up_shard, down_shard = call(
            functools.partial(finish_kernel, (names, nz, head_dim)),
            [rows_model(BF)] * 2 + [shape_of(shape, F32) for shape in out_shapes],
            [ANY] * (2 + len(names)),
            [ANY] * 9,
            slots
            + [pltpu.VMEM((2, tokens, model), BF)]
            + [pltpu.VMEM(shape, F32) for shape in out_shapes]
            + [pltpu.SemaphoreType.DMA((2 + len(names),)), pltpu.SemaphoreType.DMA((9,))],
            0,
            18 * 2**20,
        )(output, input_grad, *got[2 : 2 + len(names)])
        totals = totals[0]
    else:
        exchange = functools.partial(lax.all_to_all, axis_name="seq", tiled=True)
        grad_rows = exchange(mixed_grad, split_axis=1, concat_axis=0)
        delta_rows = exchange(delta, split_axis=0, concat_axis=1)
        packed = call(
            functools.partial(attend_back_kernel, attend_dims),
            shape_of((parts, seq_len, sum(widths)), BF),
            [VMEM] * 4,
            VMEM,
            attend_scratch,
            10 * attend_flops,
            20 * 2**20,
        )(head_rows, grad_rows, logs, jnp.broadcast_to(delta_rows[:heads, None], (heads, 8, seq_len)))
        pieces = [piece for b in range(parts) for piece in (packed[b, :, : widths[0]], packed[b, :, widths[0] :])]
        qkv = jnp.concatenate([exchange(piece, split_axis=0, concat_axis=1) for piece in pieces], axis=1)
        weight = jnp.concatenate([first_full[:, :part_cols], second_full[:, :part_cols]], axis=1)
        input_grad, qkv, gain_part, head_gain_part = call(
            functools.partial(post_kernel, (nz, head_dim, widths)),
            [
                rows_model(BF),
                shape_of((tokens, parts * part_cols), BF),
                shape_of((1, model), F32),
                shape_of((1, parts * part_cols), F32),
            ],
            [VMEM] * 8,
            [VMEM] * 4,
            [],
            proj_flops,
            14 * 2**20,
        )(x, middle_grad, gains, cosine, sine, proj, qkv, weight)

        def reduce(left, right):
            return sum_line(lax.psum_scatter(weight_grad(left, right), "fsdp", scatter_dimension=0, tiled=True)).astype(F32)

        down_shard, gate_shard = reduce(hidden_t, dy), reduce(normed_two_t, gate_grad)
        up_shard, out_shard = reduce(normed_two_t, up_grad), reduce(mixed_t, middle_low)
        qkv_shard = reduce(normed_t, qkv)
        section = nz * widths[0]
        part_shards = [
            (qkv_shard[:, b * part_cols : b * part_cols + section], qkv_shard[:, b * part_cols + section : (b + 1) * part_cols])
            for b in range(parts)
        ]
        shard_rows = query_weight.shape[0]
        q_shard = jnp.stack([q.reshape(shard_rows, nz, widths[0]) for q, _ in part_shards], axis=2).reshape(shard_rows, -1)
        kv_shard = jnp.stack([kv.reshape(shard_rows, nz, 2, head_dim) for _, kv in part_shards], axis=2)
        k_shard, v_shard = (kv_shard[:, :, :, i].reshape(shard_rows, -1) for i in range(2))
        totals = lax.psum(jnp.concatenate([gain_part, head_gain_part, feed_gain_part], axis=1)[0], ("seq", "fsdp"))

    head_totals = totals[model : model + parts * part_cols].reshape(parts, part_cols)
    q_total = head_totals[:, : nz * widths[0]].reshape(-1, head_dim).sum(axis=0)
    k_total = head_totals[:, nz * widths[0] :].reshape(-1, 2, head_dim)[:, 0].sum(axis=0)

    def share(values):
        own = jnp.arange(fsdp)[:, None] == me
        return jnp.sum(jnp.where(own, values.reshape(fsdp, -1), 0.0), axis=0)

    return (
        output.reshape(inputs.shape),
        input_grad.reshape(inputs.shape),
        q_shard,
        k_shard,
        v_shard,
        out_shard,
        share(totals[:model]),
        share(q_total),
        share(k_total),
        share(totals[model + parts * part_cols :]),
        gate_shard,
        up_shard,
        down_shard,
    )


def solution(mesh):
    tokens, rows, row = P("fsdp", "seq", None), P("fsdp", None), P("fsdp")
    in_specs = (tokens, P("fsdp", "seq"), tokens) + (rows,) * 4 + (row,) * 4 + (rows,) * 3
    out_specs = (tokens, tokens) + (rows,) * 4 + (row,) * 4 + (rows,) * 3
    return jax.shard_map(per_device, mesh=mesh, in_specs=in_specs, out_specs=out_specs, check_vma=False)
```

```python
import functools

import jax
import jax.numpy as jnp
from jax import lax
from jax.experimental import pallas as pl
from jax.experimental.pallas import tpu as pltpu
from jax.sharding import PartitionSpec as P

EPSILON = 1e-05
ROPE_BASE = 1000000.0
LOG2E = 1.4426950408889634
BF = jnp.bfloat16
F32 = jnp.float32
VMEM = pl.BlockSpec(memory_space=pltpu.VMEM)
SMEM = pl.BlockSpec(memory_space=pltpu.SMEM)
ANY = pl.BlockSpec(memory_space=pl.ANY)
VMEM_BYTES = 62 * 2**20


def dot_nn(a, b):
    return lax.dot_general(a, b, (((1,), (0,)), ((), ())), preferred_element_type=F32)


def dot_nt(a, b):
    return lax.dot_general(a, b, (((1,), (1,)), ((), ())), preferred_element_type=F32)


def dot_tn(a, b):
    return lax.dot_general(a, b, (((0,), (0,)), ((), ())), preferred_element_type=F32)


def shape_of(shape, dtype):
    return jax.ShapeDtypeStruct(shape, dtype)


def call(kernel, outs, in_specs, out_specs, scratch, flops, moved, collective=None, **more):
    params = {} if collective is None else {"collective_id": collective, "has_side_effects": True}
    return pl.pallas_call(
        kernel,
        out_shape=outs,
        in_specs=in_specs,
        out_specs=out_specs,
        scratch_shapes=scratch,
        compiler_params=pltpu.CompilerParams(vmem_limit_bytes=VMEM_BYTES, **params),
        cost_estimate=pl.CostEstimate(flops=flops, bytes_accessed=moved, transcendentals=0),
        **more,
    )


def row_norm(values):
    return lax.rsqrt(jnp.mean(values * values, axis=-1, keepdims=True) + EPSILON)


class Fetch:
    def __init__(self, sems):
        self.sems, self.used = sems, 0

    def copy(self, source, target):
        self.used += 1
        return pltpu.make_async_copy(source, target, self.sems.at[self.used - 1])

    def start(self, source, target):
        copy = self.copy(source, target)
        copy.start()
        return copy


def wait_all(copies):
    for copy in copies:
        copy.wait()


def head_mask(width, head_dim):
    rows = lax.broadcasted_iota(jnp.int32, (width, width), 0) // head_dim
    cols = lax.broadcasted_iota(jnp.int32, (width, width), 1) // head_dim
    return (rows == cols).astype(BF)


def head_sum(values, mask):
    high = values.astype(BF)
    rest = (values - high.astype(F32)).astype(BF)
    return dot_nn(high, mask) + dot_nn(rest, mask)


def head_gain(gains, start, width):
    section = gains.shape[1]
    row, first = (2, start) if start < section else (3, start - section)
    return gains[row : row + 1, first : first + width]


def model_gain(gains, row):
    return jnp.concatenate([gains[row : row + 1, :], gains[row + 1 : row + 2, :]], axis=1)


def key_lanes(shape, head_dim):
    return lax.broadcasted_iota(jnp.int32, shape, 1) % (2 * head_dim) < head_dim


def partner(values, head_dim):
    half = head_dim // 2
    width = values.shape[-1]
    lane = lax.broadcasted_iota(jnp.int32, values.shape, 1)
    after = pltpu.roll(values, width - half, 1)
    before = pltpu.roll(values, half, 1)
    return jnp.where(lane % head_dim < half, after, before)


class Links:
    def __init__(self, send_sems, recv_sems):
        self.sems, self.used, self.started = (send_sems, recv_sems), 0, []

    def reserve(self, count):
        self.used += count
        return self.used - count

    def copy(self, source, target, device, at=None):
        at = self.reserve(1) if at is None else at
        return pltpu.make_async_remote_copy(
            src_ref=source,
            dst_ref=target,
            send_sem=self.sems[0].at[at],
            recv_sem=self.sems[1].at[at],
            device_id=device,
            device_id_type=pl.DeviceIdType.MESH,
        )

    def plan(self, source, target, device):
        self.started.append(self.copy(source, target, device))
        return self.started[-1]

    def start(self, source, target, device):
        copy = self.plan(source, target, device)
        copy.start()
        return copy

    def wait_sends(self):
        for copy in self.started:
            copy.wait_send()


def enter(me, z, nz, plane):
    barrier = pltpu.get_barrier_semaphore()
    peers = [{"seq": z ^ j} for j in range(1, nz)]
    if plane:
        peers += [{"fsdp": me ^ bit} for bit in (1, 2, 4)]
    for peer in peers:
        pl.semaphore_signal(barrier, inc=1, device_id=peer, device_id_type=pl.DeviceIdType.MESH)
    pl.semaphore_wait(barrier, len(peers))


class Gather:
    def __init__(self, links, me, own, whole, x_first, stride=None, base=0):
        self.links, self.me, self.own, self.whole = links, me, own, whole
        self.rows = own.shape[0]
        self.stride, self.base = self.rows if stride is None else stride, base
        near, other = (2, 4) if x_first else (4, 2)
        self.first, self.second = self.pass_on(0, near), self.pass_on(0, other)
        self.far = self.pass_on(near, other)
        self.to_core = [self.pass_on(b, 1) for b in (0, near, other, near + other)]

    def block(self, b):
        return self.whole.at[pl.ds(pl.multiple_of((self.me ^ b) * self.stride + self.base, 16), self.rows)]

    def pass_on(self, b, bit):
        source = self.own if b == 0 else self.block(b)
        return self.links.plan(source, self.block(b), {"fsdp": self.me ^ bit})

    def begin(self):
        for copy in (self.first, self.second, self.to_core[0]):
            copy.start()

    def forward_first(self):
        self.first.wait_recv()
        self.far.start()
        self.to_core[1].start()

    def forward_second(self):
        self.second.wait_recv()
        self.to_core[2].start()

    def forward_far(self):
        self.far.wait_recv()
        self.to_core[3].start()

    def end(self):
        for copy in self.to_core:
            copy.wait_recv()


def begin(gathers):
    for gather in gathers:
        gather.begin()


def forward_first(gathers):
    for gather in gathers:
        gather.forward_first()
    for gather in gathers:
        gather.forward_second()


def forward_far(gathers):
    for gather in gathers:
        gather.forward_far()


def end(gathers):
    for gather in gathers:
        gather.end()


def rotation(position_ref, freq_ref, head_dim):
    tokens = position_ref.shape[1]
    at = jnp.broadcast_to(position_ref[...].astype(F32), (8, tokens)).T[:, 0:1]
    angles = at * freq_ref[...]
    lane = lax.broadcasted_iota(jnp.int32, (1, 128), 1)
    return jnp.cos(angles), jnp.sin(angles) * jnp.where(lane % head_dim < head_dim // 2, -1.0, 1.0)


def forward_kernel(dims, x_ref, dy_ref, position_ref, freq_ref, *refs):
    nz, plane, head_dim, widths, rows, width, groups = dims
    n_in = 11 if plane else 6
    given, refs = refs[:n_in], refs[n_in:]
    gains_ref, tables_ref, gain_grad_ref, delta_ref = refs[:4]
    heads_hbm, log_hbm, output_hbm, middle_grad_hbm, middle_low_hbm, grad_low_hbm = refs[4:10]
    refs = refs[10:]
    proj_hbm, normed_t_hbm, mixed_t_hbm, normed_two_hbm, hidden_hbm, gate_grad_hbm, up_grad_hbm, dy_hbm = refs[:8]
    refs = refs[8:]
    if plane:
        first_hbm, second_hbm, gate_hbm, up_hbm, down_hbm = refs[:5]
        refs = refs[5:]
    else:
        gate_hbm, up_hbm, down_hbm = given[3:]
    w_first, w_second, w_out, normed, transposed, proj, qkv, queries, keys, values, full, mix, mixed = refs[:13]
    heads_ref, log_ref, output_slot, low_slot, grad_low, refs = *refs[13:18], refs[:13] + refs[18:]
    w_gate, w_up, w_down, middle, total, back, hidden_slot, gate_slot, up_slot = refs[13:22]
    local_sems, weight_sems, slot_sems, send_sems, recv_sems, slot_sends, block_recvs = refs[22:29]
    own_slots = refs[29:]
    z, me = lax.axis_index("seq"), lax.axis_index("fsdp")
    model = w_second.shape[0]
    hidden_cols = gate_hbm.shape[1]
    tokens = x_ref.shape[0]
    enter(me, z, nz, plane)
    links = Links(send_sems, recv_sems)
    local = []
    to_core = []
    core = lax.rem(me, 2) if plane else 0
    place = pl.ds(pl.multiple_of(core * tokens, tokens), tokens)
    sibling = {"fsdp": me ^ 1}

    def copy_here(source, target):
        copy = pltpu.make_async_copy(source, target, local_sems.at[len(local)])
        copy.start()
        local.append(copy)
        return copy

    def share(source, target):
        copy_here(source, target)
        if plane:
            to_core.append(links.start(source, target, sibling))

    part_cols = nz * sum(widths)
    section = nz * widths[0]
    parts = qkv.shape[1] // part_cols
    if plane:
        own_q, own_k, own_v, own_out, own_gate, own_up, own_down = given[:7]
        own_first, own_second, own_keys, own_values = own_slots[3:]
        packing = [copy_here(own_k, own_keys), copy_here(own_v, own_values)]
        for at in range(nz * parts):
            to = pl.ds(at % parts * section + at // parts * widths[0], widths[0])
            source = own_q.at[:, pl.ds(at * widths[0], widths[0])]
            packing.append(copy_here(source, own_first.at[pl.ds(0, own_q.shape[0]), to]))
        lane = lax.broadcasted_iota(jnp.int32, (8, section), 1)
        head_rows = []
        for gain, period in zip(given[7:9], (head_dim, 2 * head_dim)):
            size = gain.shape[1]
            row = jnp.zeros((1, section), F32)
            for i in range(size):
                row = jnp.where(lane[:1] % period == me * size + i, gain[:, i : i + 1].astype(F32), row)
            head_rows.append(row)
        model_rows = []
        for gain in given[9:]:
            size = gain.shape[1]
            tiled = jnp.concatenate([gain[...].astype(F32)] * (section // size), axis=1)
            for row in range(2):
                model_rows.append(jnp.where((row * section + lane[:1]) // size == me, tiled, 0.0))
        rows_16 = model_rows[:2] + head_rows + model_rows[2:] + [jnp.zeros((10, section), F32)]
        own_first[own_q.shape[0] :, :section] = jnp.concatenate(rows_16, axis=0).astype(BF)
        wait_all(packing)
        pieces = []
        for b in range(parts):
            for at in range(nz):
                cols = slice((at * parts + b) * head_dim, (at * parts + b + 1) * head_dim)
                pieces += [own_keys[:, cols], own_values[:, cols]]
        own_second[...] = jnp.concatenate(pieces, axis=1)
        half = own_down.shape[0] // 2
        shard = own_q.shape[0]
        stride = own_first.shape[0]

        def columns(pairs, start, size):
            cols = pl.ds(start, size)
            return [Gather(links, me, own.at[:, cols], whole.at[:, cols], x_first) for own, whole, x_first in pairs]

        by_part = [columns(((own_first, w_first, True), (own_second, w_second, False)), 0, section)]
        later = pl.ds(section, section)
        by_part.append(
            [
                Gather(links, me, own_first.at[pl.ds(0, shard), later], w_first.at[:, later], True, stride),
                Gather(links, me, own_second.at[:, later], w_second.at[:, later], False),
            ]
        )
        out_half = own_out.shape[1] // 2
        to = pl.ds(2 * section, out_half)
        outward = [
            Gather(links, me, own_out.at[:, pl.ds(0, out_half)], w_first.at[:, to], True, stride),
            Gather(links, me, own_out.at[:, pl.ds(out_half, out_half)], w_second.at[:, to], False),
        ]
        begin(by_part[0])
        here = [copy_here(gather.own, gather.block(0)) for gather in by_part[0] + by_part[1] + outward]
        own_places = [(own_gate, own_slots[0], gate_hbm), (own_up, own_slots[1], up_hbm), (own_down, own_slots[2], down_hbm)]
        own_loads = [copy_here(own, slot) for own, slot, _ in own_places]
        down = [
            Gather(links, me, own_down.at[pl.ds(side * half, half)], down_hbm, side == 0, 2 * half, side * half)
            for side in range(2)
        ]
        wide, at = [], 0
        for count in groups:
            wide.append(columns(((own_gate, gate_hbm, True), (own_up, up_hbm, False)), at * width, count * width))
            at += count
    else:
        here = [copy_here(given[0], w_first), copy_here(given[1], w_second)]
    x = x_ref[...].astype(F32)
    unit = x * row_norm(x)
    cosine, sine = rotation(position_ref, freq_ref, head_dim)
    tables_ref[0] = cosine
    tables_ref[1] = sine
    if plane:
        forward_first(by_part[0])
        begin(by_part[1])
        begin(outward)
        forward_far(by_part[0])
        end(by_part[0])
        wait_all(here + own_loads)
        own_stores = []
        for own, slot, whole in own_places:
            count = own.shape[0]
            own_stores.append(copy_here(slot, whole.at[pl.ds(pl.multiple_of(me * count, count), count)]))
        gains = sum(w_first[s * stride + shard : (s + 1) * stride, :section].astype(F32) for s in range(8))
    else:
        stride = shard = model
        wait_all(here)
        gains = given[2][:, :section].astype(F32)
    gains_ref[...] = gains
    normed[...] = (unit * model_gain(gains, 0)).astype(BF)
    chunk = 256
    mask = head_mask(chunk, head_dim)
    cos = jnp.concatenate([tables_ref[0]] * (chunk // 128), axis=1)
    sin = jnp.concatenate([tables_ref[1]] * (chunk // 128), axis=1)
    out_half = model // 2
    my_rows = pl.ds(pl.multiple_of(z * tokens, tokens), tokens)
    arrivals = []
    for b in range(parts):
        if plane and b == 1:
            forward_first(by_part[1])
            begin(down)
            forward_far(by_part[1])
            end(by_part[1])
        for start in range(0, part_cols, chunk):
            at = b * section + start % section
            cols = slice(at, at + chunk)
            if start >= section:
                weight = w_second[:, cols]
            elif stride == shard:
                weight = w_first[:, cols]
            else:
                weight = jnp.concatenate([w_first[s * stride : s * stride + shard, cols] for s in range(8)], axis=0)
            got = dot_nn(normed[...], weight)
            here_cols = slice(b * part_cols + start, b * part_cols + start + chunk)
            proj[:, here_cols] = got
            scale = lax.rsqrt(head_sum(got * got, mask) * (1.0 / head_dim) + EPSILON)
            head = got * scale * head_gain(gains_ref, start, chunk)
            head = head * cos + partner(head, head_dim) * sin
            if start >= nz * widths[0]:
                head = jnp.where(key_lanes(head.shape, head_dim), head, got)
            qkv[:, here_cols] = head.astype(BF)
        arrived = []
        for j in range(nz):
            owner = z ^ j
            for i, size in enumerate(widths):
                base = b * part_cols + i * nz * widths[0]
                source = qkv.at[:, pl.ds(pl.multiple_of(base + owner * size, size), size)]
                target = heads_ref.at[my_rows, pl.ds(b * sum(widths) + i * widths[0], size)]
                if j == 0:
                    arrived.append(copy_here(source, target))
                else:
                    arrived.append(links.start(source, target, {"seq": owner}))
        arrivals.append(arrived)
    copy_here(proj, proj_hbm)
    transposed[0] = normed[...].T
    share(transposed.at[0], normed_t_hbm.at[:, place])
    share(dy_ref, dy_hbm.at[place])
    if plane:
        forward_first(outward)
        begin(wide[0])
    group, seq_len, _ = queries.shape
    factor = head_dim**-0.5 * LOG2E
    arriving, here_mixed = [], []
    for b in range(parts):
        for i, copy in enumerate(arrivals[b]):
            if i < 2:
                copy.wait()
            else:
                copy.wait_recv()
        first = b * sum(widths)
        for g in range(group):
            queries[g] = heads_ref[:, first + g * head_dim : first + (g + 1) * head_dim]
        first += widths[0]
        keys[...] = heads_ref[:, first : first + head_dim]
        values[...] = heads_ref[:, first + head_dim : first + 2 * head_dim]
        for r in range(seq_len // rows):
            span = slice(r * rows, (r + 1) * rows)
            reach = (r + 1) * rows

            def one_head(g, _):
                scores = dot_nt(queries[g, span], keys[:reach]) * factor
                row = lax.broadcasted_iota(jnp.int32, scores.shape, 0) + r * rows
                col = lax.broadcasted_iota(jnp.int32, scores.shape, 1)
                probs = jnp.exp2(jnp.where(row >= col, scores, -1e30))
                total = jnp.sum(probs, axis=1, keepdims=True)
                full[g, span] = (dot_nn(probs.astype(BF), values[:reach]) * (1.0 / total)).astype(BF)
                log_ref[b * group + g, :, span] = jnp.broadcast_to(jnp.log2(total), (rows, 128)).T[0:8]
                return 0

            lax.fori_loop(0, group, one_head, 0)
        mix[b] = jnp.concatenate([full[g] for g in range(group)], axis=1)
        for j in range(nz):
            owner = z ^ j
            source = mix.at[b, pl.ds(pl.multiple_of(owner * tokens, tokens), tokens)]
            to = pl.multiple_of((z * parts + b) * widths[0], widths[0])
            target = mixed.at[:, pl.ds(to, widths[0])]
            if j == 0:
                here_mixed.append(copy_here(source, target))
            else:
                arriving.append(links.start(source, target, {"seq": owner}))
        if plane and b == 0:
            forward_far(outward)
            forward_first(down)
            end(outward)
            for s in range(8):
                copy_here(w_first.at[pl.ds(s * stride, shard)], first_hbm.at[pl.ds(s * shard, shard)])
            copy_here(w_second, second_hbm)
            forward_first(wide[0])
            begin(wide[1])
            begin(wide[2])
        if b == 0:
            out_copies = [
                copy_here(
                    w_first.at[pl.ds(s * stride, shard), pl.ds(2 * section, out_half)],
                    w_out.at[pl.ds(s * shard, shard), pl.ds(0, out_half)],
                )
                for s in range(model // shard)
            ]
            out_copies.append(copy_here(w_second.at[:, pl.ds(2 * section, out_half)], w_out.at[:, pl.ds(out_half, out_half)]))
    if plane:
        forward_far(down)
        end(down)
        wait_all(own_stores)
        forward_far(wide[0])
    for copy in arriving:
        copy.wait_recv()
    wait_all(here_mixed + out_copies)

    copy_here(heads_ref, heads_hbm)
    copy_here(log_ref, log_hbm)

    gain = model_gain(gains_ref, 4)
    middle_rows = x_ref[...].astype(F32) + dot_nn(mixed[...], w_out[...])
    middle[...] = middle_rows
    total[...] = middle_rows
    normed_rows = (middle_rows * row_norm(middle_rows) * gain).astype(BF)
    normed[...] = normed_rows
    transposed[1] = normed_rows.T
    share(transposed.at[1], normed_two_hbm.at[:, place])
    transposed[2] = mixed[...].T
    share(transposed.at[2], mixed_t_hbm.at[:, place])
    back[...] = jnp.zeros(back.shape, F32)

    def slot_places(f):
        here = pl.ds(pl.multiple_of(f * width, width), width)
        return (
            (hidden_slot, hidden_hbm.at[here, place]),
            (gate_slot, gate_grad_hbm.at[place, here]),
            (up_slot, up_grad_hbm.at[place, here]),
        )

    def slot_copies(slot, f):
        return [
            pltpu.make_async_copy(s.at[slot], target, slot_sems.at[slot, i]) for i, (s, target) in enumerate(slot_places(f))
        ]

    def slot_links(slot, f):
        if not plane:
            return []
        return [
            pltpu.make_async_remote_copy(
                src_ref=s.at[slot],
                dst_ref=target,
                send_sem=slot_sends.at[slot, i],
                recv_sem=block_recvs.at[f, i],
                device_id=sibling,
                device_id_type=pl.DeviceIdType.MESH,
            )
            for i, (s, target) in enumerate(slot_places(f))
        ]

    def wait_slot(slot, f):
        wait_all(slot_copies(slot, f))
        for copy in slot_links(slot, f):
            copy.wait_send()

    def weight_copies(f):
        here = pl.ds(pl.multiple_of(f * width, width), width)
        slot = lax.rem(f, 2)
        pairs = ((gate_hbm.at[:, here], w_gate), (up_hbm.at[:, here], w_up), (down_hbm.at[here], w_down))
        return [
            pltpu.make_async_copy(source, target.at[slot], weight_sems.at[slot, i])
            for i, (source, target) in enumerate(pairs)
        ]

    blocks = hidden_cols // width
    firsts = [sum(groups[:g]) for g in range(len(groups))]

    ahead = [0, 0, firsts[min(1, len(firsts) - 1)] - 1] + firsts[2:]

    def arrive(f):
        for g in range(1, len(groups)):

            @pl.when(f == ahead[g])
            def _():
                forward_first(wide[g])
                if g + 2 < len(groups):
                    begin(wide[g + 2])

        for g in range(len(groups)):

            @pl.when(f == firsts[g])
            def _():
                if g:
                    forward_far(wide[g])
                end(wide[g])

    def one_block(f, _):
        slot = lax.rem(f, 2)
        if plane:
            arrive(f)

        def fetch(block):
            for copy in weight_copies(block):
                copy.start()

        in_first = f < (firsts[1] if plane else blocks)
        pl.when((f == 0) | ~in_first)(lambda: fetch(f))
        pl.when(in_first & (f + 1 < (firsts[1] if plane else blocks)))(lambda: fetch(f + 1))
        wait_all(weight_copies(f))

        @pl.when(f >= 2)
        def _():
            wait_slot(slot, f - 2)

        gate = dot_nn(normed[...], w_gate[slot])
        up = dot_nn(normed[...], w_up[slot])
        hidden_grad = dot_nt(dy_ref[...], w_down[slot])
        s = 1.0 / (1.0 + jnp.exp(-gate))
        silu = gate * s
        hidden = (silu * up).astype(BF)
        gate_grad = (hidden_grad * up * (s * (1.0 + gate * (1.0 - s)))).astype(BF)
        up_grad = (hidden_grad * silu).astype(BF)
        hidden_slot[slot] = hidden.T
        gate_slot[slot] = gate_grad
        up_slot[slot] = up_grad
        for copy in slot_copies(slot, f) + slot_links(slot, f):
            copy.start()
        total[...] = total[...] + dot_nn(hidden, w_down[slot])
        back[...] = back[...] + (dot_nt(gate_grad, w_gate[slot]) + dot_nt(up_grad, w_up[slot]))
        return 0

    lax.fori_loop(0, blocks, one_block, 0)
    output_slot[...] = total[...].astype(BF)
    copy_here(output_slot, output_hbm)
    part, gain_sum = norm_back(middle[...], gain, back[...])
    gain_grad_ref[...] = gain_sum
    middle_grad = dy_ref[...].astype(F32) + part
    back[...] = middle_grad
    copy_here(back, middle_grad_hbm)
    middle_low = middle_grad.astype(BF)
    low_slot[...] = middle_low
    copy_here(low_slot, middle_low_hbm)
    mixed_grad = dot_nt(middle_low, w_out[...]).astype(BF)
    grad_low[...] = mixed_grad
    copy_here(grad_low, grad_low_hbm)
    product = mixed_grad.astype(F32) * mixed[...].astype(F32)
    heads = mixed.shape[1] // head_dim // nz
    row = lax.broadcasted_iota(jnp.int32, (8 * nz, mixed.shape[1]), 0)
    col = lax.broadcasted_iota(jnp.int32, (8 * nz, mixed.shape[1]), 1)
    pick = ((col // head_dim == (row // 8) * heads + row % 8) & (row % 8 < heads)).astype(BF)
    high = product.astype(BF)
    delta_ref[...] = dot_nt(pick, high) + dot_nt(pick, (product - high.astype(F32)).astype(BF))
    for f in (blocks - 2, blocks - 1):
        wait_slot(f % 2, f)
    if plane:
        for f in range(blocks):
            for copy in slot_links(f % 2, f):
                copy.wait_recv()
        for copy in to_core:
            copy.wait_recv()
        links.wait_sends()
    done = here + out_copies + here_mixed + [c for arrived in arrivals for c in arrived[:2]]
    if plane:
        done += packing + own_loads + own_stores
    for copy in local:
        if not any(copy is other for other in done):
            copy.wait()


def both_cores(links, copy_here, me, source, target, axis):
    size = source.shape[axis]
    here = pl.ds(pl.multiple_of(lax.rem(me, 2) * size, size), size)
    place = target.at[here] if axis == 0 else target.at[:, here]
    copy_here(source, place)
    return links.start(source, place, {"fsdp": me ^ 1})


def attend_back(dims, b, heads_ref, grads_ref, log_ref, delta_ref, packed, scratch):
    rows, chunk = dims
    queries, keys, values, grad, q_grad, k_grad, v_grad = scratch
    group, seq_len, head_dim = queries.shape
    first = b * (group + 2) * head_dim
    for g in range(group):
        queries[g] = heads_ref[:, first + g * head_dim : first + (g + 1) * head_dim]
        at = (b * group + g) * head_dim
        grad[g] = grads_ref[:, at : at + head_dim]
        q_grad[g] = jnp.zeros((seq_len, head_dim), F32)
    first += group * head_dim
    keys[...] = heads_ref[:, first : first + head_dim]
    values[...] = heads_ref[:, first + head_dim : first + 2 * head_dim]
    factor = head_dim**-0.5
    scale = factor * LOG2E
    for at in range(seq_len // rows):
        span = slice(at * rows, (at + 1) * rows)
        key, value = keys[span], values[span]
        k_grad[span] = jnp.zeros((rows, head_dim), F32)
        v_grad[span] = jnp.zeros((rows, head_dim), F32)

        def one_head(g, _):
            key_total = jnp.zeros((rows, head_dim), F32)
            value_total = jnp.zeros((rows, head_dim), F32)
            for start in range(at * rows, seq_len, chunk):
                part = slice(start, min(start + chunk, seq_len))
                query, out_grad = queries[g, part], grad[g, part]
                scores = dot_nt(key, query) * scale - log_ref[b * group + g, 0:1, part]
                if start == at * rows:
                    key_at = lax.broadcasted_iota(jnp.int32, scores.shape, 0) + at * rows
                    query_at = lax.broadcasted_iota(jnp.int32, scores.shape, 1) + start
                    scores = jnp.where(query_at >= key_at, scores, -1e30)
                probs = jnp.exp2(scores)
                prob_grad = dot_nt(value, out_grad)
                score_grad = (probs * (prob_grad - delta_ref[b * group + g, 0:1, part])).astype(BF)
                value_total = value_total + dot_nn(probs.astype(BF), out_grad)
                key_total = key_total + dot_nn(score_grad, query)
                q_grad[g, part] = q_grad[g, part] + dot_tn(score_grad, key)
            k_grad[span] = k_grad[span] + key_total
            v_grad[span] = v_grad[span] + value_total
            return 0

        lax.fori_loop(0, group, one_head, 0)
        parts = [(q_grad[g, span] * factor).astype(BF) for g in range(group)]
        parts += [(k_grad[span] * factor).astype(BF), v_grad[span].astype(BF)]
        packed[span] = jnp.concatenate(parts, axis=1)
        yield at


def attend_back_scratch(group, seq_len, head_dim):
    many = lambda kind: pltpu.VMEM((group, seq_len, head_dim), kind)
    one = lambda kind: pltpu.VMEM((seq_len, head_dim), kind)
    return [many(BF), one(BF), one(BF), many(BF), many(F32), one(F32), one(F32)]


def attend_back_kernel(dims, heads_ref, grads_ref, log_ref, delta_ref, packed, *scratch):
    for b in range(packed.shape[0]):
        for _ in attend_back(dims, b, heads_ref, grads_ref, log_ref, delta_ref, packed.at[b], scratch):
            pass


def norm_back(rows, gain, gradient):
    q = row_norm(rows)
    n = rows * q
    u = gradient * gain
    return q * (u - n * jnp.mean(u * n, axis=-1, keepdims=True)), jnp.sum(gradient * n, axis=0, keepdims=True)


def weight_grad_kernel(left_ref, right_ref, out_ref):
    out_ref[...] = dot_nn(left_ref[...], right_ref[...]).astype(BF)


def weight_grad(left, right, width=256):
    rows, tokens = left.shape
    cols = right.shape[1]
    return call(
        weight_grad_kernel,
        shape_of((rows, cols), BF),
        [pl.BlockSpec((rows, tokens), lambda n: (0, 0)), pl.BlockSpec((tokens, width), lambda n: (0, n))],
        pl.BlockSpec((rows, width), lambda n: (0, n)),
        [],
        2 * rows * tokens * cols,
        2 * (rows * tokens + tokens * cols + rows * cols),
        grid=(cols // width,),
    )(left, right)


def project_back(dims, b, gains_ref, tables_ref, proj_ref, qkv, head_gain_grad_ref):
    nz, head_dim, widths = dims
    part_cols = nz * sum(widths)
    width = 256
    mask = head_mask(width, head_dim)
    cos = jnp.concatenate([tables_ref[0]] * (width // 128), axis=1)
    sin = jnp.concatenate([tables_ref[1]] * (width // 128), axis=1)
    for start in range(0, part_cols, width):
        cols = slice(b * part_cols + start, b * part_cols + start + width)
        rotated = qkv[:, cols].astype(F32)
        gradient = rotated * cos - partner(rotated, head_dim) * sin
        proj = proj_ref[:, start : start + width]
        scale = lax.rsqrt(head_sum(proj * proj, mask) * (1.0 / head_dim) + EPSILON)
        n = proj * scale
        u = gradient * head_gain(gains_ref, start, width)
        head_gain_grad_ref[:, cols] = jnp.sum(gradient * n, axis=0, keepdims=True)
        back = scale * (u - n * (head_sum(u * n, mask) * (1.0 / head_dim)))
        if start >= nz * widths[0]:
            back = jnp.where(key_lanes(back.shape, head_dim), back, rotated)
        qkv[:, cols] = back.astype(BF)


def input_back(x_ref, middle_grad_ref, gains_ref, qkv, weight, input_grad_ref, gain_grad_ref):
    normed_grad = dot_nt(qkv[...], weight[...])
    part, gain_sum = norm_back(x_ref[...].astype(F32), model_gain(gains_ref, 0), normed_grad)
    gain_grad_ref[...] = gain_sum
    input_grad_ref[...] = (middle_grad_ref[...] + part).astype(BF)


def post_kernel(dims, x_ref, middle_grad_ref, gains_ref, tables_ref, proj_ref, grads_ref, weight_ref, *refs):
    input_grad_ref, qkv, gain_grad_ref, head_gain_grad_ref = refs
    nz, _, widths = dims
    qkv[...] = grads_ref[...]
    for b in range(qkv.shape[1] // (nz * sum(widths))):
        part_cols = nz * sum(widths)
        part = proj_ref.at[:, pl.ds(b * part_cols, part_cols)]
        project_back(dims, b, gains_ref, tables_ref, part, qkv, head_gain_grad_ref)
    input_back(x_ref, middle_grad_ref, gains_ref, qkv, weight_ref, input_grad_ref, gain_grad_ref)


class Reduce:
    def __init__(self, links, fetch, me, z, x_first, away, kept, first, second, inward, across, out):
        self.links, self.fetch, self.me, self.z = links, fetch, me, z
        self.away, self.kept, self.out = away, kept, out
        self.bits = (2, 4) if x_first else (4, 2)
        order = (1, 3, 0, 2) if x_first else (2, 3, 0, 1)
        self.slots = {r: (away if i < 2 else kept, i % 2) for i, r in enumerate(order)}
        self.arrived, self.second, self.inward, self.across = first, second, inward, across
        self.outer, self.inner = (z == 0) | (z == 3), (z == 1) | (z == 2)
        self.one = links.copy(away, first, {"fsdp": me ^ self.bits[0]})
        self.two = links.copy(kept.at[1], second, {"fsdp": me ^ self.bits[1]})
        self.three = links.copy(kept.at[0], inward, {"seq": z ^ 1})
        self.four = links.copy(kept.at[0], across, {"seq": z ^ 3})
        self.five = links.copy(kept.at[1], out, {"seq": z ^ 1})
        self.here = fetch.copy(kept.at[1], out)
        self.load = fetch.copy(first, away)

    def put(self, r, cols, values):
        ref, i = self.slots[r]
        ref[i, :, cols] = values

    def rows_of(self):
        rows = self.kept.shape[1]
        step = 32 if rows % 32 == 0 else 16
        return rows // step, step

    def by_rows(self, work):
        count, step = self.rows_of()

        def body(i, _):
            work(pl.ds(pl.multiple_of(i * step, step), step))
            return 0

        lax.fori_loop(0, count, body, 0)

    def begin(self):
        self.one.start()

    def load_one(self):
        self.one.wait_recv()
        self.one.wait_send()
        self.load.start()

    def fold_one(self):
        self.load.wait()

        def work(rows):
            for i in range(2):
                self.kept[i, rows] = self.kept[i, rows] + self.away[i, rows]

        self.by_rows(work)
        self.two.start()

    def fold_two(self):
        self.two.wait_recv()

        def work(rows):
            self.kept[0, rows] = self.kept[0, rows] + self.second[rows]

        self.by_rows(work)

        @pl.when(self.outer)
        def _():
            self.three.start()

    def fold_three(self):
        @pl.when(self.inner)
        def _():
            self.three.wait_recv()

            def work(rows):
                self.kept[0, rows] = self.kept[0, rows] + self.inward[rows]

            self.by_rows(work)
            self.four.start()

    def fold_four(self):
        self.two.wait_send()

        @pl.when(self.inner)
        def _():
            self.four.wait_recv()

            def work(rows):
                self.kept[1, rows] = self.kept[0, rows] + self.across[rows]

            self.by_rows(work)
            self.five.start()
            self.here.start()

    def end(self):
        @pl.when(self.inner)
        def _():
            self.four.wait_send()
            self.five.wait_send()
            self.here.wait()

        @pl.when(self.outer)
        def _():
            self.three.wait_send()
            self.five.wait_recv()


def each(reduces, step):
    if step == "fold_one":
        each(reduces, "load_one")
    for reduce in reduces:
        getattr(reduce, step)()


class Total:
    def __init__(self, links, me, z, sums, arrived):
        self.sums, self.arrived = sums, arrived
        peers = [{"fsdp": me ^ 1}, {"fsdp": me ^ 2}, {"fsdp": me ^ 4}, {"seq": z ^ 1}, {"seq": z ^ 2}]
        self.copies = [links.copy(sums.at[i], arrived.at[i], peer) for i, peer in enumerate(peers)]

    def begin(self, at):
        self.copies[at].start()

    def fold(self, at):
        self.copies[at].wait_recv()
        self.sums[at + 1] = self.sums[at] + self.arrived[at]

    def end(self):
        for copy in self.copies:
            copy.wait_send()


EARLY = (
    ("down1", "matmul"), ("down1", "begin"), ("out", "matmul"), ("wide2", "matmul"), ("wide2", "begin"),
    ("down0", "matmul"),
)
MIDDLE = (
    ("keys", 0, 0), ("keys", 0, 1), ("keys", 0, 2), ("keys", 0, 3), ("keys", 0, 4), ("keys", 0, 5), ("keys", 0, 6),
    ("keys", 0, 7), ("down1", "fold_one"), ("down0", "begin"), ("wide1", "matmul"), ("wide2", "fold_one"),
    ("keys", 1, 0), ("down1", "fold_two"), ("keys", 1, 1), ("keys", 1, 2), ("keys", 1, 3), ("keys", 1, 4),
    ("down1", "fold_three"), ("keys", 1, 5), ("out", "begin"), ("keys", 1, 6), ("keys", 1, 7), ("wide0", "matmul"),
    ("wide2", "fold_two"), ("wide0", "begin"), ("down0", "fold_one"), ("project", 0), ("out", "fold_one"),
    ("last0", "matmul"), ("down1", "fold_four"), ("wide0", "fold_one"), ("last0", "begin"), ("wide2", "fold_three"),
    ("down0", "fold_two"), ("project", 1),
)
LATE = (
    ("wide1", "begin"), ("down0", "fold_three"), ("wide2", "fold_four"), ("wide0", "fold_two"), ("last0", "fold_one"),
    ("input",), ("wide0", "fold_three"), ("down0", "fold_four"), ("total", 0), ("last1", "matmul"),
    ("wide1", "fold_one"), ("last1", "begin"), ("out", "fold_two"), ("out", "fold_three"), ("wide0", "fold_four"),
    ("last0", "fold_two"), ("wide1", "fold_two"), ("last0", "fold_three"), ("total", 1), ("out", "fold_four"),
    ("last1", "fold_one"), ("wide1", "fold_three"), ("total", 2), ("last1", "fold_two"), ("last0", "fold_four"),
    ("last1", "fold_three"), ("wide1", "fold_four"), ("total", 3), ("total", 4), ("last1", "fold_four"),
)


def backward_kernel(dims, gains_ref, tables_ref, delta_own, feed_gain_ref, heads_hbm, log_hbm, grad_low, low_own, *refs):
    nz, head_dim, widths, attend_dims, names = dims
    given, refs = refs[:12], refs[12:]
    x_hbm, middle_grad_hbm, proj_hbm, hidden_hbm, dy_hbm, normed_two_hbm = given[:6]
    gate_hbm, up_hbm, mixed_hbm, normed_hbm, first_hbm, second_hbm = given[6:]
    input_grad_ref, totals_ref = refs[:2]
    n = len(names)
    finals, refs = dict(zip(names, refs[2 : 2 + n])), refs[2 + n :]
    firsts, refs = dict(zip(names, refs[:n])), refs[n:]
    low_hbm, refs = refs[0], refs[1:]
    aways, refs = dict(zip(names, refs[:n])), refs[n:]
    kepts, refs = dict(zip(names, refs[:n])), refs[n:]
    seconds, refs = dict(zip(names, refs[:n])), refs[n:]
    inwards, refs = dict(zip(names, refs[:n])), refs[n:]
    acrosses, refs = dict(zip(names, refs[:n])), refs[n:]
    grads, delta, qkv, other_qkv, normed_two, normed, sums, sum_arrived, gain_grad, head_gain_grad = refs[:10]
    heads_ref, log_ref, low_ref, sems, send_sems, recv_sems = refs[10:]
    z, me = lax.axis_index("seq"), lax.axis_index("fsdp")
    chip, core = lax.div(me, 2), lax.rem(me, 2)
    links, fetch = Links(send_sems, recv_sems), Fetch(sems)
    low_load = fetch.start(low_own, low_ref)
    head_loads = [fetch.start(heads_hbm, heads_ref), fetch.start(log_hbm, log_ref)]
    enter(me, z, nz, True)
    tokens = grad_low.shape[0]
    seq_len, block_cols = heads_ref.shape
    part_cols = nz * sum(widths)
    parts = qkv.shape[1] // part_cols
    late = []

    def copy_here(source, target):
        copy = fetch.start(source, target)
        late.append(copy)
        return copy

    my_rows = pl.ds(pl.multiple_of(z * tokens, tokens), tokens)
    arrivals = []
    for b in range(parts):
        arrived = []
        for j in range(nz):
            owner = z ^ j
            from_cols = pl.ds(pl.multiple_of((owner * parts + b) * widths[0], widths[0]), widths[0])
            pairs = [(grad_low.at[:, from_cols], grads.at[my_rows, pl.ds(b * widths[0], widths[0])])]
            if b == 0:
                pairs.append((delta_own.at[pl.ds(pl.multiple_of(owner * 8, 8), 8)], delta.at[:, my_rows]))
            for source, target in pairs:
                if j == 0:
                    copy_here(source, target)
                else:
                    arrived.append(links.start(source, target, {"seq": owner}))
        arrivals.append(arrived)
    low_load.wait()
    low_arrival = both_cores(links, copy_here, me, low_ref, low_hbm, 0)
    reduces = {}
    for name in names:
        reduces[name] = Reduce(
            links, fetch, me, z, name[-1] == "x", aways[name], kepts[name], firsts[name], seconds[name], inwards[name],
            acrosses[name], finals[name],
        )
    down = [[reduces[f"down{c}{way}"] for way in "xy"] for c in range(2)]
    gate, up = [reduces["gate0x"], reduces["gate1y"], reduces["gate2x"]], [reduces["up0y"], reduces["up1x"], reduces["up2y"]]
    wide = [gate[:2], [gate[2], up[0]], up[1:]]
    out = [reduces["outx"], reduces["outy"]]
    last = [[reduces[f"last{b}{way}"] for way in "xy"] for b in range(parts)]
    total = Total(links, me, z, sums, sum_arrived)
    part_cols_of = lambda b: pl.ds(b * part_cols, part_cols)
    qkv_links = [
        links.copy(qkv.at[:, part_cols_of(b)], other_qkv.at[:, part_cols_of(b)], {"fsdp": me ^ 1}) for b in range(parts)
    ]
    chips = 4
    step = 256
    half = down[0][0].kept.shape[1]
    shard = gate[0].kept.shape[1]
    both = 2 * tokens
    model = low_ref.shape[1]

    def my_blocks(source, target, rows):
        copies = []
        for r in range(chips):
            owner = (chip ^ r) * 2 + core
            copies.append(fetch.start(source.at[pl.ds(pl.multiple_of(owner * rows, rows), rows)], target.at[pl.ds(r * rows, rows)]))
        return copies

    def wide_grads(places, left, right):
        width = right.shape[2]
        chunks = [
            (source, (first + c) * width, unit, c * width)
            for source, first, unit in places
            for c in range(unit.kept.shape[2] // width)
        ]
        count = len(chunks)
        loads = [
            fetch.copy(source.at[:, pl.ds(at, width)], right.at[c % 2]) for c, (source, at, _, _) in enumerate(chunks)
        ]
        loads[0].start()
        loads[1].start()
        for c in range(count):
            loads[c].wait()
            _, _, unit, base = chunks[c]

            def block(k, _):
                here = pl.ds(pl.multiple_of(k * step, step), step)
                to = pl.ds(pl.multiple_of(base + k * step, step), step)
                got = dot_nn(left[...], right[c % 2, :, here]).astype(BF)
                for r in range(chips):
                    unit.put(r, to, got[r * shard : (r + 1) * shard])
                return 0

            lax.fori_loop(0, width // step, block, 0)
            if c + 2 < count:
                loads[c + 2].start()

    ready = {"two": my_blocks(normed_two_hbm, normed_two, shard), "one": my_blocks(normed_hbm, normed, shard)}

    def ready_now(name):
        wait_all(ready.pop(name, ()))

    per_unit = 2
    wide_part = gate[0].kept.shape[2] // per_unit
    sides = {"gate": gate_hbm, "up": up_hbm}
    wide_names = (("gate", 0), ("gate", 1), ("gate", 2), ("up", 0), ("up", 1), ("up", 2))

    def wide_matmul(i, right):
        ready_now("two")
        pair = zip(wide_names[2 * i : 2 * i + 2], wide[i])
        wide_grads([(sides[kind], at * per_unit, unit) for (kind, at), unit in pair], normed_two, right)

    def out_matmul(mixed, low):
        cols = out[0].kept.shape[2]
        for start in range(0, low.shape[1], step):
            got = dot_nn(mixed[...], low[:, start : start + step]).astype(BF)
            for r in range(chips):
                out[start // cols].put(r, slice(start % cols, start % cols + step), got[r * shard : (r + 1) * shard])

    def down_matmul(c, hidden, dy):
        cols = down[0][0].kept.shape[2]

        def block(i, _):
            to = pl.ds(pl.multiple_of(i * step, step), step)
            here = pl.ds(pl.multiple_of(c * cols + i * step, step), step)
            for r in range(chips):
                got = dot_nn(hidden[2 * r * half : 2 * (r + 1) * half], dy[:, here]).astype(BF)
                for side in range(2):
                    down[c][side].put(r, to, got[side * half : (side + 1) * half])
            return 0

        lax.fori_loop(0, cols // step, block, 0)

    def last_matmul(b):
        ready_now("one")
        mine = normed[:, pl.ds(pl.multiple_of(core * tokens, tokens), tokens)]
        theirs = normed[:, pl.ds(pl.multiple_of((1 - core) * tokens, tokens), tokens)]
        qkv_links[b].wait()
        cols = last[b][0].kept.shape[2]
        for start in range(0, part_cols, step):
            here = slice(b * part_cols + start, b * part_cols + start + step)
            got = (dot_nn(mine, qkv[:, here]) + dot_nn(theirs, other_qkv[:, here])).astype(BF)
            for r in range(chips):
                last[b][start // cols].put(r, slice(start % cols, start % cols + step), got[r * shard : (r + 1) * shard])

    pairs = {"out": out}
    pairs |= {f"down{c}": down[c] for c in range(2)}
    pairs |= {f"wide{i}": wide[i] for i in range(3)}
    pairs |= {f"last{b}": last[b] for b in range(parts)}
    right_shape = pltpu.VMEM((2, both, wide_part), BF)

    def sum_step(name, what):
        if what != "matmul":
            each(pairs[name], what)
        elif name[:4] == "last":
            last_matmul(int(name[4]))
        else:
            pl.run_scoped(functools.partial(wide_matmul, int(name[4])), right_shape)

    def early(hidden, dy, right, mixed, low):
        ready["down"] = my_blocks(hidden_hbm, hidden, 2 * half) + [fetch.start(dy_hbm, dy)]
        ready["out"] = my_blocks(mixed_hbm, mixed, shard)
        for name, what in EARLY:
            if what != "matmul":
                each(pairs[name], what)
            elif name[:4] == "down":
                ready_now("down")
                down_matmul(int(name[4]), hidden, dy)
            elif name == "out":
                low_arrival.wait_recv()
                wait_all(late)
                del late[:]
                ready["out"].append(fetch.start(low_hbm, low))
                ready_now("out")
                out_matmul(mixed, low)
            else:
                wide_matmul(int(name[4]), right)

    pl.run_scoped(
        early,
        pltpu.VMEM((2 * chips * half, both), BF),
        pltpu.VMEM((both, model), BF),
        right_shape,
        pltpu.VMEM((chips * shard, both), BF),
        pltpu.VMEM((both, model), BF),
    )

    wait_all(head_loads)
    heads = log_ref.shape[0]
    group = heads // parts
    first_back = links.reserve(parts * 2 * nz)
    own_back = fetch.used
    fetch.used += parts * 2

    def back_copies(b, packed):
        for i, width in enumerate(widths):
            base = b * part_cols + i * nz * widths[0]
            target = qkv.at[:, pl.ds(pl.multiple_of(base + z * width, width), width)]
            for j in range(nz):
                owner = z ^ j
                rows = pl.ds(pl.multiple_of(owner * tokens, tokens), tokens)
                source = packed.at[b, rows, pl.ds(i * widths[0], width)]
                if j == 0:
                    yield j, pltpu.make_async_copy(source, target, sems.at[own_back + 2 * b + i])
                else:
                    yield j, links.copy(source, target, {"seq": owner}, at=first_back + (2 * b + i) * nz + j)

    def middle(packed, delta_rows, *scratch):
        blocks = {}

        def keys_step(b, at):
            if at == 0:
                for copy in arrivals[b]:
                    copy.wait_recv()
                if b == 0:
                    for h in range(heads):
                        delta_rows[h] = jnp.broadcast_to(delta[h : h + 1], (8, seq_len))
                blocks[b] = attend_back(attend_dims, b, heads_ref, grads, log_ref, delta_rows, packed.at[b], scratch)
            next(blocks[b])
            if (at + 1) * attend_dims[0] == seq_len:
                for _, copy in back_copies(b, packed):
                    copy.start()

        def project_step(b):
            for j, copy in back_copies(b, packed):
                if j == 0:
                    copy.wait()
                else:
                    copy.wait_recv()

            def inner(proj):
                fetch.start(proj_hbm.at[:, part_cols_of(b)], proj).wait()
                project_back((nz, head_dim, widths), b, gains_ref, tables_ref, proj, qkv, head_gain_grad)

            pl.run_scoped(inner, pltpu.VMEM((tokens, part_cols), F32))
            qkv_links[b].start()

        for token in MIDDLE:
            if token[0] == "keys":
                keys_step(*token[1:])
            elif token[0] == "project":
                project_step(token[1])
            else:
                sum_step(*token)
        for b in range(parts):
            for j, copy in back_copies(b, packed):
                if j:
                    copy.wait_send()

    pl.run_scoped(
        middle,
        pltpu.VMEM((parts, seq_len, sum(widths)), BF),
        pltpu.VMEM((heads, 8, seq_len), F32),
        *attend_back_scratch(group, seq_len, head_dim),
    )

    def input_step(weight, x, middle_grad):
        copies = [fetch.start(x_hbm, x), fetch.start(middle_grad_hbm, middle_grad)]
        section = part_cols // 2
        for b in range(parts):
            for i, source in enumerate((first_hbm, second_hbm)):
                to = pl.ds(b * part_cols + i * section, section)
                copies.append(fetch.start(source.at[:, pl.ds(b * section, section)], weight.at[:, to]))
        wait_all(copies)
        input_back(x, middle_grad, gains_ref, qkv, weight, input_grad_ref, gain_grad)
        row = jnp.concatenate([gain_grad[...], head_gain_grad[...], feed_gain_ref[...]], axis=1)
        sums[0] = jnp.broadcast_to(row, sums.shape[1:])

    for token in LATE:
        if token[0] == "input":
            pl.run_scoped(
                input_step,
                pltpu.VMEM((model, parts * part_cols), BF),
                pltpu.VMEM((tokens, model), BF),
                pltpu.VMEM((tokens, model), F32),
            )
            total.begin(0)
        elif token[0] == "total":
            total.fold(token[1])
            if token[1] < 4:
                total.begin(token[1] + 1)
        else:
            sum_step(*token)
    totals_ref[...] = sums[5]
    total.end()
    for name in names:
        reduces[name].end()
    links.wait_sends()


def finish_kernel(dims, *refs):
    names, nz, head_dim = dims
    n = len(names)
    output_in, input_grad_in = refs[:2]
    shards, refs = dict(zip(names, refs[2 : 2 + n])), refs[2 + n :]
    output, input_grad, q_out, k_out, v_out, out_out, gate_out, up_out, down_out = refs[:9]
    slots, refs = dict(zip(names, refs[9 : 9 + n])), refs[9 + n :]
    passing, q, k, v, out, gate, up, down, load_sems, store_sems = refs
    fetch, store = Fetch(load_sems), Fetch(store_sems)
    wide = [name for name in names if name[:4] in ("gate", "up0y", "up1x", "up2y")]
    order = wide + [name for name in names if name not in wide]
    loads = {name: fetch.start(shards[name], slots[name]) for name in order}
    moves = [fetch.start(source, passing.at[i]) for i, source in enumerate((output_in, input_grad_in))]
    stores = []

    def place(name, target, row, col):
        loads[name].wait()
        rows, cols = slots[name].shape
        target[row : row + rows, col : col + cols] = slots[name][...].astype(F32)

    cols = slots["gate0x"].shape[1]
    for target, done, pieces in (
        (gate, gate_out, ("gate0x", "gate1y", "gate2x")),
        (up, up_out, ("up0y", "up1x", "up2y")),
    ):
        for i, name in enumerate(pieces):
            place(name, target, 0, i * cols)
        stores.append(store.start(target, done))
    rows, cols = slots["down0x"].shape
    for c in range(2):
        for i, way in enumerate("xy"):
            place(f"down{c}{way}", down, i * rows, c * cols)
    stores.append(store.start(down, down_out))
    cols = slots["outx"].shape[1]
    for i, way in enumerate("xy"):
        place("out" + way, out, 0, i * cols)
    stores.append(store.start(out, out_out))
    parts = 2
    width = q.shape[1] // (nz * parts)
    for b in range(parts):
        loads[f"last{b}x"].wait()
        for i in range(nz):
            to = (i * parts + b) * width
            q[:, to : to + width] = slots[f"last{b}x"][:, i * width : (i + 1) * width].astype(F32)
    stores.append(store.start(q, q_out))
    for b in range(parts):
        loads[f"last{b}y"].wait()
    for i, target in enumerate((k, v)):
        pieces = [
            slots[f"last{b}y"][:, (2 * at + i) * head_dim : (2 * at + i + 1) * head_dim]
            for at in range(nz)
            for b in range(parts)
        ]
        target[...] = jnp.concatenate(pieces, axis=1).astype(F32)
    stores += [store.start(k, k_out), store.start(v, v_out)]
    for i, target in enumerate((output, input_grad)):
        moves[i].wait()
        stores.append(store.start(passing.at[i], target))
    wait_all(stores)


def add(a, b):
    return (a.astype(F32) + b.astype(F32)).astype(a.dtype)


def sum_line(values):
    size = lax.axis_size("seq")
    if size != 4:
        return lax.psum(values, "seq")
    z = lax.axis_index("seq")
    inner = add(values, lax.ppermute(values, "seq", [(0, 1), (3, 2)]))
    total = add(inner, lax.ppermute(inner, "seq", [(1, 2), (2, 1)]))
    outer = lax.ppermute(total, "seq", [(1, 0), (2, 3)])
    return jnp.where((z == 1) | (z == 2), total, outer)


def per_device(
    inputs,
    positions,
    cotangent,
    query_weight,
    key_weight,
    value_weight,
    out_weight,
    attention_gain,
    query_gain,
    key_gain,
    feedforward_gain,
    gate_weight,
    up_weight,
    down_weight,
):
    seqs, tokens, model = inputs.shape
    assert seqs == 1
    fsdp, nz = lax.axis_size("fsdp"), lax.axis_size("seq")
    me, z = lax.axis_index("fsdp"), lax.axis_index("seq")
    plane = fsdp == 8 and nz == 4
    both = 2 * tokens if plane else tokens
    x = inputs.reshape(tokens, model)
    dy = cotangent.reshape(tokens, model)
    head_dim = query_gain.shape[0] * fsdp
    q_cols, k_cols, v_cols = query_weight.shape[1], key_weight.shape[1], value_weight.shape[1]
    heads, kv_heads = q_cols // head_dim // nz, k_cols // head_dim // nz
    hidden_cols = gate_weight.shape[1]
    seq_len = tokens * nz

    group, parts = heads // kv_heads, kv_heads
    widths = (group * head_dim, 2 * head_dim)
    part_cols = nz * sum(widths)
    assert parts == 2

    section = nz * widths[0]
    assert model == 2 * section and part_cols == 2 * section
    half_out = model // 2
    first_cols = 2 * section + half_out
    if plane:
        given = [query_weight, key_weight, value_weight, out_weight, gate_weight, up_weight, down_weight]
        given += [query_gain[None], key_gain[None], attention_gain[None], feedforward_gain[None]]
    else:
        shard_rows = query_weight.shape[0]
        q = query_weight.reshape(shard_rows, nz, parts, widths[0])
        kv = jnp.stack([v.reshape(shard_rows, nz, parts, head_dim) for v in (key_weight, value_weight)], axis=3)
        first, second = (
            jnp.concatenate([v[:, :, b].reshape(shard_rows, section) for b in range(parts)] + [rest], axis=1)
            for v, rest in ((q, out_weight[:, :half_out]), (kv, out_weight[:, half_out:]))
        )
        gather = functools.partial(lax.all_gather, axis_name="fsdp", axis=0, tiled=True)
        first_full, second_full, gate_full = gather(first), gather(second), gather(gate_weight)
        up_full, down_full = gather(up_weight), gather(down_weight)
        key_row = jnp.concatenate([gather(key_gain), jnp.zeros((head_dim,), BF)])
        gain_rows = [gather(attention_gain).reshape(2, section), jnp.tile(gather(query_gain), nz * group)[None]]
        gain_rows += [jnp.tile(key_row, nz)[None], gather(feedforward_gain).reshape(2, section)]
        gain_rows = jnp.concatenate(gain_rows + [jnp.zeros((10, section), BF)]).astype(F32)
        given = [first_full, second_full, gain_rows, gate_full, up_full, down_full]

    half_dim = head_dim // 2
    freqs = ROPE_BASE ** (-(jnp.arange(128) % half_dim).astype(F32) / half_dim)

    rows_model = lambda kind: shape_of((tokens, model), kind)
    width = 512
    blocks = hidden_cols // width
    sizes = (blocks - 6,) + (1,) * 6
    block_cols = parts * sum(widths)
    mixed_cols = heads * head_dim
    attend_flops = 2 * heads * seq_len * seq_len * head_dim
    proj_flops = 2 * tokens * model * parts * part_cols
    outs = [
        shape_of((16, section), F32),
        shape_of((2, tokens, 128), F32),
        shape_of((1, model), F32),
        shape_of((8 * nz, tokens), F32),
        shape_of((seq_len, block_cols), BF),
        shape_of((heads, 8, seq_len), F32),
        rows_model(BF),
        rows_model(F32),
        rows_model(BF),
        shape_of((tokens, q_cols), BF),
        shape_of((tokens, parts * part_cols), F32),
        shape_of((model, both), BF),
        shape_of((q_cols, both), BF),
        shape_of((model, both), BF),
        shape_of((hidden_cols, both), BF),
        shape_of((both, hidden_cols), BF),
        shape_of((both, hidden_cols), BF),
        shape_of((both, model), BF),
    ]
    n_links = parts * 3 * (nz - 1)
    first_rows = model
    if plane:
        outs += [shape_of((model, first_cols), BF)] * 2
        outs += [shape_of((model, hidden_cols), BF)] * 2 + [shape_of((hidden_cols, model), BF)]
        n_links += (8 + 2 * len(sizes)) * 7 + 4
        first_rows += 8 * 16
    many = lambda count: pltpu.VMEM((count, seq_len, head_dim), BF)
    one = pltpu.VMEM((seq_len, head_dim), BF)
    got = call(
        functools.partial(forward_kernel, (nz, plane, head_dim, widths, min(256, seq_len), width, sizes)),
        outs,
        [VMEM] * 4 + ([ANY] * 7 + [VMEM] * 4 if plane else [ANY] * 2 + [VMEM] + [ANY] * 3),
        [VMEM] * 4 + [ANY] * (len(outs) - 4),
        [
            pltpu.VMEM((first_rows, first_cols), BF),
            pltpu.VMEM((model, first_cols), BF),
            pltpu.VMEM((q_cols, model), BF),
            pltpu.VMEM((tokens, model), BF),
            pltpu.VMEM((3, model, tokens), BF),
            pltpu.VMEM((tokens, parts * part_cols), F32),
            pltpu.VMEM((tokens, parts * part_cols), BF),
            many(group),
            one,
            one,
            many(group),
            pltpu.VMEM((parts, seq_len, widths[0]), BF),
            pltpu.VMEM((tokens, q_cols), BF),
            pltpu.VMEM((seq_len, block_cols), BF),
            pltpu.VMEM((heads, 8, seq_len), F32),
            pltpu.VMEM((tokens, model), BF),
            pltpu.VMEM((tokens, model), BF),
            pltpu.VMEM((tokens, q_cols), BF),
            pltpu.VMEM((2, model, width), BF),
            pltpu.VMEM((2, model, width), BF),
            pltpu.VMEM((2, width, model), BF),
            pltpu.VMEM((tokens, model), F32),
            pltpu.VMEM((tokens, model), F32),
            pltpu.VMEM((tokens, model), F32),
            pltpu.VMEM((2, width, tokens), BF),
            pltpu.VMEM((2, tokens, width), BF),
            pltpu.VMEM((2, tokens, width), BF),
            pltpu.SemaphoreType.DMA((64,)),
            pltpu.SemaphoreType.DMA((2, 3)),
            pltpu.SemaphoreType.DMA((2, 3)),
            pltpu.SemaphoreType.DMA((n_links,)),
            pltpu.SemaphoreType.DMA((n_links,)),
            pltpu.SemaphoreType.DMA((2, 3)),
            pltpu.SemaphoreType.DMA((blocks, 3)),
        ]
        + [pltpu.VMEM(w.shape, BF) for w in (gate_weight, up_weight, down_weight) if plane]
        + [pltpu.VMEM((query_weight.shape[0] + extra, 2 * section), BF) for extra in (16, 0) if plane]
        + [pltpu.VMEM(key_weight.shape, BF) for _ in range(2) if plane],
        proj_flops + 4 * attend_flops + 12 * tokens * model * hidden_cols,
        100 * 2**20,
        collective=1,
    )(x, dy, positions.reshape(1, tokens), freqs[None], *given)
    gains, tables, feed_gain_part, delta = got[:4]
    head_rows, logs, output, middle_grad, middle_low, mixed_grad = got[4:10]
    proj, normed_t, mixed_t, normed_two_t, hidden_t, gate_grad, up_grad, dy_both = got[10:18]
    if plane:
        first_full, second_full = got[18:20]

    attend_dims = (min(256, seq_len), min(1024, seq_len))
    attend_scratch = attend_back_scratch(group, seq_len, head_dim)
    if plane:
        down_rows, down_cols = down_weight.shape
        blocks = {f"down{c}{way}": (down_rows // 2, down_cols // 2) for c in range(2) for way in "xy"}
        wide_names = ("gate0x", "gate1y", "gate2x", "up0y", "up1x", "up2y")
        blocks |= {name: (gate_weight.shape[0], hidden_cols // 3) for name in wide_names}
        blocks |= {"out" + way: (out_weight.shape[0], model // 2) for way in "xy"}
        blocks |= {f"last{b}{way}": (query_weight.shape[0], part_cols // 2) for b in range(parts) for way in "xy"}
        names = tuple(blocks)
        pairs = [(2,) + shape for shape in blocks.values()]
        total_cols = model + parts * part_cols + model
        n_links = 3 * (nz - 1) + 2 * parts * nz + 1 + parts + 5 * len(names) + 5
        n_copies = 64 + 2 * len(names)
        got = call(
            functools.partial(backward_kernel, (nz, head_dim, widths, attend_dims, names)),
            [rows_model(BF), shape_of((8, total_cols), F32)]
            + [shape_of(shape, BF) for shape in blocks.values()]
            + [shape_of(shape, BF) for shape in pairs]
            + [shape_of((both, model), BF)],
            [VMEM] * 4 + [ANY] * 16,
            [VMEM] * 2 + [ANY] * (2 * len(names) + 1),
            [pltpu.VMEM(shape, BF) for shape in pairs] * 2
            + [pltpu.VMEM(shape, BF) for shape in blocks.values()] * 3
            + [
                pltpu.VMEM((seq_len, mixed_cols), BF),
                pltpu.VMEM((8, seq_len), F32),
                pltpu.VMEM((tokens, parts * part_cols), BF),
                pltpu.VMEM((tokens, parts * part_cols), BF),
                pltpu.VMEM((model // 2, both), BF),
                pltpu.VMEM((model // 2, both), BF),
                pltpu.VMEM((6, 8, total_cols), F32),
                pltpu.VMEM((5, 8, total_cols), F32),
                pltpu.VMEM((1, model), F32),
                pltpu.VMEM((1, parts * part_cols), F32),
                pltpu.VMEM((seq_len, block_cols), BF),
                pltpu.VMEM((heads, 8, seq_len), F32),
                pltpu.VMEM((tokens, model), BF),
                pltpu.SemaphoreType.DMA((n_copies,)),
                pltpu.SemaphoreType.DMA((n_links,)),
                pltpu.SemaphoreType.DMA((n_links,)),
            ],
            10 * attend_flops + 2 * tokens * model * (3 * hidden_cols + 3 * (q_cols + k_cols)),
            100 * 2**20,
            collective=3,
        )(
            gains, tables, delta, feed_gain_part, head_rows, logs, mixed_grad, middle_low, x, middle_grad, proj,
            hidden_t, dy_both, normed_two_t, gate_grad, up_grad, mixed_t, normed_t, first_full, second_full,
        )
        input_grad, totals = got[:2]
        slots = [pltpu.VMEM(shape, BF) for shape in blocks.values()]
        out_shapes = [w.shape for w in (query_weight, key_weight, value_weight, out_weight, gate_weight, up_weight, down_weight)]
        output, input_grad, q_shard, k_shard, v_shard, out_shard, gate_shard, up_shard, down_shard = call(
            functools.partial(finish_kernel, (names, nz, head_dim)),
            [rows_model(BF)] * 2 + [shape_of(shape, F32) for shape in out_shapes],
            [ANY] * (2 + len(names)),
            [ANY] * 9,
            slots
            + [pltpu.VMEM((2, tokens, model), BF)]
            + [pltpu.VMEM(shape, F32) for shape in out_shapes]
            + [pltpu.SemaphoreType.DMA((2 + len(names),)), pltpu.SemaphoreType.DMA((9,))],
            0,
            18 * 2**20,
        )(output, input_grad, *got[2 : 2 + len(names)])
        totals = totals[0]
    else:
        exchange = functools.partial(lax.all_to_all, axis_name="seq", tiled=True)
        grad_rows = exchange(mixed_grad, split_axis=1, concat_axis=0)
        delta_rows = exchange(delta, split_axis=0, concat_axis=1)
        packed = call(
            functools.partial(attend_back_kernel, attend_dims),
            shape_of((parts, seq_len, sum(widths)), BF),
            [VMEM] * 4,
            VMEM,
            attend_scratch,
            10 * attend_flops,
            20 * 2**20,
        )(head_rows, grad_rows, logs, jnp.broadcast_to(delta_rows[:heads, None], (heads, 8, seq_len)))
        pieces = [piece for b in range(parts) for piece in (packed[b, :, : widths[0]], packed[b, :, widths[0] :])]
        qkv = jnp.concatenate([exchange(piece, split_axis=0, concat_axis=1) for piece in pieces], axis=1)
        weight = jnp.concatenate(
            [full[:, b * section : (b + 1) * section] for b in range(parts) for full in (first_full, second_full)], axis=1
        )
        input_grad, qkv, gain_part, head_gain_part = call(
            functools.partial(post_kernel, (nz, head_dim, widths)),
            [
                rows_model(BF),
                shape_of((tokens, parts * part_cols), BF),
                shape_of((1, model), F32),
                shape_of((1, parts * part_cols), F32),
            ],
            [VMEM] * 7,
            [VMEM] * 4,
            [],
            proj_flops,
            14 * 2**20,
        )(x, middle_grad, gains, tables, proj, qkv, weight)

        def reduce(left, right):
            return sum_line(lax.psum_scatter(weight_grad(left, right), "fsdp", scatter_dimension=0, tiled=True)).astype(F32)

        down_shard, gate_shard = reduce(hidden_t, dy), reduce(normed_two_t, gate_grad)
        up_shard, out_shard = reduce(normed_two_t, up_grad), reduce(mixed_t, middle_low)
        qkv_shard = reduce(normed_t, qkv)
        part_shards = [
            (qkv_shard[:, b * part_cols : b * part_cols + section], qkv_shard[:, b * part_cols + section : (b + 1) * part_cols])
            for b in range(parts)
        ]
        q_shard = jnp.stack([q.reshape(shard_rows, nz, widths[0]) for q, _ in part_shards], axis=2).reshape(shard_rows, -1)
        kv_shard = jnp.stack([kv.reshape(shard_rows, nz, 2, head_dim) for _, kv in part_shards], axis=2)
        k_shard, v_shard = (kv_shard[:, :, :, i].reshape(shard_rows, -1) for i in range(2))
        totals = lax.psum(jnp.concatenate([gain_part, head_gain_part, feed_gain_part], axis=1)[0], ("seq", "fsdp"))

    head_totals = totals[model : model + parts * part_cols].reshape(parts, part_cols)
    q_total = head_totals[:, : nz * widths[0]].reshape(-1, head_dim).sum(axis=0)
    k_total = head_totals[:, nz * widths[0] :].reshape(-1, 2, head_dim)[:, 0].sum(axis=0)

    def share(values):
        own = jnp.arange(fsdp)[:, None] == me
        return jnp.sum(jnp.where(own, values.reshape(fsdp, -1), 0.0), axis=0)

    return (
        output.reshape(inputs.shape),
        input_grad.reshape(inputs.shape),
        q_shard,
        k_shard,
        v_shard,
        out_shard,
        share(totals[:model]),
        share(q_total),
        share(k_total),
        share(totals[model + parts * part_cols :]),
        gate_shard,
        up_shard,
        down_shard,
    )


def solution(mesh):
    tokens, rows, row = P("fsdp", "seq", None), P("fsdp", None), P("fsdp")
    in_specs = (tokens, P("fsdp", "seq"), tokens) + (rows,) * 4 + (row,) * 4 + (rows,) * 3
    out_specs = (tokens, tokens) + (rows,) * 4 + (row,) * 4 + (rows,) * 3
    return jax.shard_map(per_device, mesh=mesh, in_specs=in_specs, out_specs=out_specs, check_vma=False)
```

```python
import functools

import jax
import jax.numpy as jnp
from jax import lax
from jax.experimental import pallas as pl
from jax.experimental.pallas import tpu as pltpu
from jax.sharding import PartitionSpec as P

EPSILON = 1e-05
ROPE_BASE = 1000000.0
LOG2E = 1.4426950408889634
BF = jnp.bfloat16
F32 = jnp.float32
VMEM = pl.BlockSpec(memory_space=pltpu.VMEM)
SMEM = pl.BlockSpec(memory_space=pltpu.SMEM)
ANY = pl.BlockSpec(memory_space=pl.ANY)
VMEM_BYTES = 62 * 2**20


def dot_nn(a, b):
    return lax.dot_general(a, b, (((1,), (0,)), ((), ())), preferred_element_type=F32)


def dot_nt(a, b):
    return lax.dot_general(a, b, (((1,), (1,)), ((), ())), preferred_element_type=F32)


def dot_tn(a, b):
    return lax.dot_general(a, b, (((0,), (0,)), ((), ())), preferred_element_type=F32)


def shape_of(shape, dtype):
    return jax.ShapeDtypeStruct(shape, dtype)


def call(kernel, outs, in_specs, out_specs, scratch, flops, moved, collective=None, **more):
    params = {} if collective is None else {"collective_id": collective, "has_side_effects": True}
    return pl.pallas_call(
        kernel,
        out_shape=outs,
        in_specs=in_specs,
        out_specs=out_specs,
        scratch_shapes=scratch,
        compiler_params=pltpu.CompilerParams(vmem_limit_bytes=VMEM_BYTES, **params),
        cost_estimate=pl.CostEstimate(flops=flops, bytes_accessed=moved, transcendentals=0),
        **more,
    )


def row_norm(values):
    return lax.rsqrt(jnp.mean(values * values, axis=-1, keepdims=True) + EPSILON)


class Fetch:
    def __init__(self, sems):
        self.sems, self.used = sems, 0

    def copy(self, source, target):
        self.used += 1
        return pltpu.make_async_copy(source, target, self.sems.at[self.used - 1])

    def start(self, source, target):
        copy = self.copy(source, target)
        copy.start()
        return copy


def wait_all(copies):
    for copy in copies:
        copy.wait()


def head_mask(width, head_dim):
    rows = lax.broadcasted_iota(jnp.int32, (width, width), 0) // head_dim
    cols = lax.broadcasted_iota(jnp.int32, (width, width), 1) // head_dim
    return (rows == cols).astype(BF)


def head_sum(values, mask):
    high = values.astype(BF)
    rest = (values - high.astype(F32)).astype(BF)
    return dot_nn(high, mask) + dot_nn(rest, mask)


def head_gain(gains, start, width):
    section = gains.shape[1]
    row, first = (2, start) if start < section else (3, start - section)
    return gains[row : row + 1, first : first + width]


def model_gain(gains, row):
    return jnp.concatenate([gains[row : row + 1, :], gains[row + 1 : row + 2, :]], axis=1)


def key_lanes(shape, head_dim):
    return lax.broadcasted_iota(jnp.int32, shape, 1) % (2 * head_dim) < head_dim


def partner(values, head_dim):
    half = head_dim // 2
    width = values.shape[-1]
    lane = lax.broadcasted_iota(jnp.int32, values.shape, 1)
    after = pltpu.roll(values, width - half, 1)
    before = pltpu.roll(values, half, 1)
    return jnp.where(lane % head_dim < half, after, before)


class Links:
    def __init__(self, send_sems, recv_sems):
        self.sems, self.used, self.started = (send_sems, recv_sems), 0, []

    def reserve(self, count):
        self.used += count
        return self.used - count

    def copy(self, source, target, device, at=None):
        at = self.reserve(1) if at is None else at
        return pltpu.make_async_remote_copy(
            src_ref=source,
            dst_ref=target,
            send_sem=self.sems[0].at[at],
            recv_sem=self.sems[1].at[at],
            device_id=device,
            device_id_type=pl.DeviceIdType.MESH,
        )

    def plan(self, source, target, device):
        self.started.append(self.copy(source, target, device))
        return self.started[-1]

    def start(self, source, target, device):
        copy = self.plan(source, target, device)
        copy.start()
        return copy

    def wait_sends(self):
        for copy in self.started:
            copy.wait_send()


def enter(me, z, nz, plane):
    barrier = pltpu.get_barrier_semaphore()
    peers = [{"seq": z ^ j} for j in range(1, nz)]
    if plane:
        peers += [{"fsdp": me ^ bit} for bit in (1, 2, 4)]
    for peer in peers:
        pl.semaphore_signal(barrier, inc=1, device_id=peer, device_id_type=pl.DeviceIdType.MESH)
    pl.semaphore_wait(barrier, len(peers))


class Gather:
    def __init__(self, links, me, own, whole, x_first, stride=None, base=0):
        self.links, self.me, self.own, self.whole = links, me, own, whole
        self.rows = own.shape[0]
        self.stride, self.base = self.rows if stride is None else stride, base
        near, other = (2, 4) if x_first else (4, 2)
        self.first, self.second = self.pass_on(0, near), self.pass_on(0, other)
        self.far = self.pass_on(near, other)
        self.to_core = [self.pass_on(b, 1) for b in (0, near, other, near + other)]

    def block(self, b):
        return self.whole.at[pl.ds(pl.multiple_of((self.me ^ b) * self.stride + self.base, 16), self.rows)]

    def pass_on(self, b, bit):
        source = self.own if b == 0 else self.block(b)
        return self.links.plan(source, self.block(b), {"fsdp": self.me ^ bit})

    def begin(self):
        for copy in (self.first, self.second, self.to_core[0]):
            copy.start()

    def forward_first(self):
        self.first.wait_recv()
        self.far.start()
        self.to_core[1].start()

    def forward_second(self):
        self.second.wait_recv()
        self.to_core[2].start()

    def forward_far(self):
        self.far.wait_recv()
        self.to_core[3].start()

    def end(self):
        for copy in self.to_core:
            copy.wait_recv()


def begin(gathers):
    for gather in gathers:
        gather.begin()


def forward_first(gathers):
    for gather in gathers:
        gather.forward_first()
    for gather in gathers:
        gather.forward_second()


def forward_far(gathers):
    for gather in gathers:
        gather.forward_far()


def end(gathers):
    for gather in gathers:
        gather.end()


def rotation(position_ref, freq_ref, head_dim):
    tokens = position_ref.shape[1]
    at = jnp.broadcast_to(position_ref[...].astype(F32), (8, tokens)).T[:, 0:1]
    angles = at * freq_ref[...]
    lane = lax.broadcasted_iota(jnp.int32, (1, 128), 1)
    return jnp.cos(angles), jnp.sin(angles) * jnp.where(lane % head_dim < head_dim // 2, -1.0, 1.0)


def forward_kernel(dims, x_ref, dy_ref, position_ref, freq_ref, *refs):
    nz, plane, head_dim, widths, rows, width, groups = dims
    n_in = 11 if plane else 6
    given, refs = refs[:n_in], refs[n_in:]
    gains_ref, tables_ref, gain_grad_ref, delta_ref = refs[:4]
    heads_hbm, log_hbm, output_hbm, middle_grad_hbm, middle_low_hbm, grad_low_hbm = refs[4:10]
    refs = refs[10:]
    proj_hbm, normed_t_hbm, mixed_t_hbm, normed_two_hbm, hidden_hbm, gate_grad_hbm, up_grad_hbm, dy_hbm = refs[:8]
    refs = refs[8:]
    if plane:
        first_hbm, second_hbm, gate_hbm, up_hbm, down_hbm = refs[:5]
        refs = refs[5:]
    else:
        gate_hbm, up_hbm, down_hbm = given[3:]
    w_first, w_second, w_out, normed, transposed, proj, qkv, queries, keys, values, full, mix, mixed = refs[:13]
    heads_ref, log_ref, output_slot, low_slot, grad_low, refs = *refs[13:18], refs[:13] + refs[18:]
    w_gate, w_up, w_down, middle, total, back, hidden_slot, gate_slot, up_slot = refs[13:22]
    local_sems, weight_sems, slot_sems, send_sems, recv_sems, slot_sends, block_recvs = refs[22:29]
    own_slots = refs[29:]
    z, me = lax.axis_index("seq"), lax.axis_index("fsdp")
    model = w_second.shape[0]
    hidden_cols = gate_hbm.shape[1]
    tokens = x_ref.shape[0]
    enter(me, z, nz, plane)
    links = Links(send_sems, recv_sems)
    local = []
    to_core = []
    core = lax.rem(me, 2) if plane else 0
    place = pl.ds(pl.multiple_of(core * tokens, tokens), tokens)
    sibling = {"fsdp": me ^ 1}

    def copy_here(source, target):
        copy = pltpu.make_async_copy(source, target, local_sems.at[len(local)])
        copy.start()
        local.append(copy)
        return copy

    def share(source, target):
        copy_here(source, target)
        if plane:
            to_core.append(links.start(source, target, sibling))

    part_cols = nz * sum(widths)
    section = nz * widths[0]
    parts = qkv.shape[1] // part_cols
    if plane:
        own_q, own_k, own_v, own_out, own_gate, own_up, own_down = given[:7]
        own_first, own_second, own_keys, own_values = own_slots[3:]
        packing = [copy_here(own_k, own_keys), copy_here(own_v, own_values)]
        for at in range(nz * parts):
            to = pl.ds(at % parts * section + at // parts * widths[0], widths[0])
            source = own_q.at[:, pl.ds(at * widths[0], widths[0])]
            packing.append(copy_here(source, own_first.at[pl.ds(0, own_q.shape[0]), to]))
        lane = lax.broadcasted_iota(jnp.int32, (8, section), 1)
        head_rows = []
        for gain, period in zip(given[7:9], (head_dim, 2 * head_dim)):
            size = gain.shape[1]
            row = jnp.zeros((1, section), F32)
            for i in range(size):
                row = jnp.where(lane[:1] % period == me * size + i, gain[:, i : i + 1].astype(F32), row)
            head_rows.append(row)
        model_rows = []
        for gain in given[9:]:
            size = gain.shape[1]
            tiled = jnp.concatenate([gain[...].astype(F32)] * (section // size), axis=1)
            for row in range(2):
                model_rows.append(jnp.where((row * section + lane[:1]) // size == me, tiled, 0.0))
        rows_16 = model_rows[:2] + head_rows + model_rows[2:] + [jnp.zeros((10, section), F32)]
        own_first[own_q.shape[0] :, :section] = jnp.concatenate(rows_16, axis=0).astype(BF)
        wait_all(packing)
        pieces = []
        for b in range(parts):
            for at in range(nz):
                cols = slice((at * parts + b) * head_dim, (at * parts + b + 1) * head_dim)
                pieces += [own_keys[:, cols], own_values[:, cols]]
        own_second[...] = jnp.concatenate(pieces, axis=1)
        half = own_down.shape[0] // 2
        shard = own_q.shape[0]
        stride = own_first.shape[0]

        def columns(pairs, start, size):
            cols = pl.ds(start, size)
            return [Gather(links, me, own.at[:, cols], whole.at[:, cols], x_first) for own, whole, x_first in pairs]

        by_part = [columns(((own_first, w_first, True), (own_second, w_second, False)), 0, section)]
        later = pl.ds(section, section)
        by_part.append(
            [
                Gather(links, me, own_first.at[pl.ds(0, shard), later], w_first.at[:, later], True, stride),
                Gather(links, me, own_second.at[:, later], w_second.at[:, later], False),
            ]
        )
        out_half = own_out.shape[1] // 2
        to = pl.ds(2 * section, out_half)
        outward = [
            Gather(links, me, own_out.at[:, pl.ds(0, out_half)], w_first.at[:, to], True, stride),
            Gather(links, me, own_out.at[:, pl.ds(out_half, out_half)], w_second.at[:, to], False),
        ]
        begin(by_part[0])
        here = [copy_here(gather.own, gather.block(0)) for gather in by_part[0] + by_part[1] + outward]
        own_places = [(own_gate, own_slots[0], gate_hbm), (own_up, own_slots[1], up_hbm), (own_down, own_slots[2], down_hbm)]
        own_loads = [copy_here(own, slot) for own, slot, _ in own_places]
        down = [
            Gather(links, me, own_down.at[pl.ds(side * half, half)], down_hbm, side == 0, 2 * half, side * half)
            for side in range(2)
        ]
        wide, at = [], 0
        for count in groups:
            wide.append(columns(((own_gate, gate_hbm, True), (own_up, up_hbm, False)), at * width, count * width))
            at += count
    else:
        here = [copy_here(given[0], w_first), copy_here(given[1], w_second)]
    x = x_ref[...].astype(F32)
    unit = x * row_norm(x)
    cosine, sine = rotation(position_ref, freq_ref, head_dim)
    tables_ref[0] = cosine
    tables_ref[1] = sine
    if plane:
        forward_first(by_part[0])
        begin(by_part[1])
        begin(outward)
        forward_far(by_part[0])
        end(by_part[0])
        wait_all(here + own_loads)
        own_stores = []
        for own, slot, whole in own_places:
            count = own.shape[0]
            own_stores.append(copy_here(slot, whole.at[pl.ds(pl.multiple_of(me * count, count), count)]))
        gains = sum(w_first[s * stride + shard : (s + 1) * stride, :section].astype(F32) for s in range(8))
    else:
        stride = shard = model
        wait_all(here)
        gains = given[2][:, :section].astype(F32)
    gains_ref[...] = gains
    normed[...] = (unit * model_gain(gains, 0)).astype(BF)
    chunk = 256
    mask = head_mask(chunk, head_dim)
    cos = jnp.concatenate([tables_ref[0]] * (chunk // 128), axis=1)
    sin = jnp.concatenate([tables_ref[1]] * (chunk // 128), axis=1)
    out_half = model // 2
    my_rows = pl.ds(pl.multiple_of(z * tokens, tokens), tokens)
    arrivals = []
    for b in range(parts):
        if plane and b == 1:
            forward_first(by_part[1])
            begin(down)
            forward_far(by_part[1])
            end(by_part[1])
        for start in range(0, part_cols, chunk):
            at = b * section + start % section
            cols = slice(at, at + chunk)
            if start >= section:
                weight = w_second[:, cols]
            elif stride == shard:
                weight = w_first[:, cols]
            else:
                weight = jnp.concatenate([w_first[s * stride : s * stride + shard, cols] for s in range(8)], axis=0)
            got = dot_nn(normed[...], weight)
            here_cols = slice(b * part_cols + start, b * part_cols + start + chunk)
            proj[:, here_cols] = got
            scale = lax.rsqrt(head_sum(got * got, mask) * (1.0 / head_dim) + EPSILON)
            head = got * scale * head_gain(gains_ref, start, chunk)
            head = head * cos + partner(head, head_dim) * sin
            if start >= nz * widths[0]:
                head = jnp.where(key_lanes(head.shape, head_dim), head, got)
            qkv[:, here_cols] = head.astype(BF)
        arrived = []
        for j in range(nz):
            owner = z ^ j
            for i, size in enumerate(widths):
                base = b * part_cols + i * nz * widths[0]
                source = qkv.at[:, pl.ds(pl.multiple_of(base + owner * size, size), size)]
                target = heads_ref.at[my_rows, pl.ds(b * sum(widths) + i * widths[0], size)]
                if j == 0:
                    arrived.append(copy_here(source, target))
                else:
                    arrived.append(links.start(source, target, {"seq": owner}))
        arrivals.append(arrived)
    copy_here(proj, proj_hbm)
    transposed[0] = normed[...].T
    share(transposed.at[0], normed_t_hbm.at[:, place])
    share(dy_ref, dy_hbm.at[place])
    if plane:
        forward_first(outward)
        begin(wide[0])
    group, seq_len, _ = queries.shape
    factor = head_dim**-0.5 * LOG2E
    arriving, here_mixed = [], []
    for b in range(parts):
        for i, copy in enumerate(arrivals[b]):
            if i < 2:
                copy.wait()
            else:
                copy.wait_recv()
        first = b * sum(widths)
        for g in range(group):
            queries[g] = heads_ref[:, first + g * head_dim : first + (g + 1) * head_dim]
        first += widths[0]
        keys[...] = heads_ref[:, first : first + head_dim]
        values[...] = heads_ref[:, first + head_dim : first + 2 * head_dim]
        for r in range(seq_len // rows):
            span = slice(r * rows, (r + 1) * rows)
            reach = (r + 1) * rows

            def one_head(g, _):
                scores = dot_nt(queries[g, span], keys[:reach]) * factor
                row = lax.broadcasted_iota(jnp.int32, scores.shape, 0) + r * rows
                col = lax.broadcasted_iota(jnp.int32, scores.shape, 1)
                probs = jnp.exp2(jnp.where(row >= col, scores, -1e30))
                total = jnp.sum(probs, axis=1, keepdims=True)
                full[g, span] = (dot_nn(probs.astype(BF), values[:reach]) * (1.0 / total)).astype(BF)
                log_ref[b * group + g, :, span] = jnp.broadcast_to(jnp.log2(total), (rows, 128)).T[0:8]
                return 0

            lax.fori_loop(0, group, one_head, 0)
        mix[b] = jnp.concatenate([full[g] for g in range(group)], axis=1)
        for j in range(nz):
            owner = z ^ j
            source = mix.at[b, pl.ds(pl.multiple_of(owner * tokens, tokens), tokens)]
            to = pl.multiple_of((z * parts + b) * widths[0], widths[0])
            target = mixed.at[:, pl.ds(to, widths[0])]
            if j == 0:
                here_mixed.append(copy_here(source, target))
            else:
                arriving.append(links.start(source, target, {"seq": owner}))
        if plane and b == 0:
            forward_far(outward)
            forward_first(down)
            end(outward)
            for s in range(8):
                copy_here(w_first.at[pl.ds(s * stride, shard)], first_hbm.at[pl.ds(s * shard, shard)])
            copy_here(w_second, second_hbm)
            forward_first(wide[0])
            begin(wide[1])
            begin(wide[2])
        if b == 0:
            out_copies = [
                copy_here(
                    w_first.at[pl.ds(s * stride, shard), pl.ds(2 * section, out_half)],
                    w_out.at[pl.ds(s * shard, shard), pl.ds(0, out_half)],
                )
                for s in range(model // shard)
            ]
            out_copies.append(copy_here(w_second.at[:, pl.ds(2 * section, out_half)], w_out.at[:, pl.ds(out_half, out_half)]))
    if plane:
        forward_far(down)
        end(down)
        wait_all(own_stores)
        forward_far(wide[0])
    for copy in arriving:
        copy.wait_recv()
    wait_all(here_mixed + out_copies)

    copy_here(heads_ref, heads_hbm)
    copy_here(log_ref, log_hbm)

    gain = model_gain(gains_ref, 4)
    middle_rows = x_ref[...].astype(F32) + dot_nn(mixed[...], w_out[...])
    middle[...] = middle_rows
    total[...] = middle_rows
    normed_rows = (middle_rows * row_norm(middle_rows) * gain).astype(BF)
    normed[...] = normed_rows
    transposed[1] = normed_rows.T
    share(transposed.at[1], normed_two_hbm.at[:, place])
    transposed[2] = mixed[...].T
    share(transposed.at[2], mixed_t_hbm.at[:, place])
    back[...] = jnp.zeros(back.shape, F32)

    def slot_places(f):
        here = pl.ds(pl.multiple_of(f * width, width), width)
        return (
            (hidden_slot, hidden_hbm.at[here, place]),
            (gate_slot, gate_grad_hbm.at[place, here]),
            (up_slot, up_grad_hbm.at[place, here]),
        )

    def slot_copies(slot, f):
        return [
            pltpu.make_async_copy(s.at[slot], target, slot_sems.at[slot, i]) for i, (s, target) in enumerate(slot_places(f))
        ]

    def slot_links(slot, f):
        if not plane:
            return []
        return [
            pltpu.make_async_remote_copy(
                src_ref=s.at[slot],
                dst_ref=target,
                send_sem=slot_sends.at[slot, i],
                recv_sem=block_recvs.at[f, i],
                device_id=sibling,
                device_id_type=pl.DeviceIdType.MESH,
            )
            for i, (s, target) in enumerate(slot_places(f))
        ]

    def wait_slot(slot, f):
        wait_all(slot_copies(slot, f))
        for copy in slot_links(slot, f):
            copy.wait_send()

    def weight_copies(f):
        here = pl.ds(pl.multiple_of(f * width, width), width)
        slot = lax.rem(f, 2)
        pairs = ((gate_hbm.at[:, here], w_gate), (up_hbm.at[:, here], w_up), (down_hbm.at[here], w_down))
        return [
            pltpu.make_async_copy(source, target.at[slot], weight_sems.at[slot, i])
            for i, (source, target) in enumerate(pairs)
        ]

    blocks = hidden_cols // width
    firsts = [sum(groups[:g]) for g in range(len(groups))]

    ahead = [0, 0, firsts[min(1, len(firsts) - 1)] - 1] + firsts[2:]

    def arrive(f):
        for g in range(1, len(groups)):

            @pl.when(f == ahead[g])
            def _():
                forward_first(wide[g])
                if g + 2 < len(groups):
                    begin(wide[g + 2])

        for g in range(len(groups)):

            @pl.when(f == firsts[g])
            def _():
                if g:
                    forward_far(wide[g])
                end(wide[g])

    def one_block(f, _):
        slot = lax.rem(f, 2)
        if plane:
            arrive(f)

        def fetch(block):
            for copy in weight_copies(block):
                copy.start()

        in_first = f < (firsts[1] if plane else blocks)
        pl.when((f == 0) | ~in_first)(lambda: fetch(f))
        pl.when(in_first & (f + 1 < (firsts[1] if plane else blocks)))(lambda: fetch(f + 1))
        wait_all(weight_copies(f))

        @pl.when(f >= 2)
        def _():
            wait_slot(slot, f - 2)

        gate = dot_nn(normed[...], w_gate[slot])
        up = dot_nn(normed[...], w_up[slot])
        hidden_grad = dot_nt(dy_ref[...], w_down[slot])
        s = 1.0 / (1.0 + jnp.exp(-gate))
        silu = gate * s
        hidden = (silu * up).astype(BF)
        gate_grad = (hidden_grad * up * (s * (1.0 + gate * (1.0 - s)))).astype(BF)
        up_grad = (hidden_grad * silu).astype(BF)
        hidden_slot[slot] = hidden.T
        gate_slot[slot] = gate_grad
        up_slot[slot] = up_grad
        for copy in slot_copies(slot, f) + slot_links(slot, f):
            copy.start()
        total[...] = total[...] + dot_nn(hidden, w_down[slot])
        back[...] = back[...] + (dot_nt(gate_grad, w_gate[slot]) + dot_nt(up_grad, w_up[slot]))
        return 0

    lax.fori_loop(0, blocks, one_block, 0)
    output_slot[...] = total[...].astype(BF)
    copy_here(output_slot, output_hbm)
    part, gain_sum = norm_back(middle[...], gain, back[...])
    gain_grad_ref[...] = gain_sum
    middle_grad = dy_ref[...].astype(F32) + part
    back[...] = middle_grad
    copy_here(back, middle_grad_hbm)
    middle_low = middle_grad.astype(BF)
    low_slot[...] = middle_low
    copy_here(low_slot, middle_low_hbm)
    mixed_grad = dot_nt(middle_low, w_out[...]).astype(BF)
    grad_low[...] = mixed_grad
    copy_here(grad_low, grad_low_hbm)
    product = mixed_grad.astype(F32) * mixed[...].astype(F32)
    heads = mixed.shape[1] // head_dim // nz
    row = lax.broadcasted_iota(jnp.int32, (8 * nz, mixed.shape[1]), 0)
    col = lax.broadcasted_iota(jnp.int32, (8 * nz, mixed.shape[1]), 1)
    pick = ((col // head_dim == (row // 8) * heads + row % 8) & (row % 8 < heads)).astype(BF)
    high = product.astype(BF)
    delta_ref[...] = dot_nt(pick, high) + dot_nt(pick, (product - high.astype(F32)).astype(BF))
    for f in (blocks - 2, blocks - 1):
        wait_slot(f % 2, f)
    if plane:
        for f in range(blocks):
            for copy in slot_links(f % 2, f):
                copy.wait_recv()
        for copy in to_core:
            copy.wait_recv()
        links.wait_sends()
    done = here + out_copies + here_mixed + [c for arrived in arrivals for c in arrived[:2]]
    if plane:
        done += packing + own_loads + own_stores
    for copy in local:
        if not any(copy is other for other in done):
            copy.wait()


def both_cores(links, copy_here, me, source, target, axis):
    size = source.shape[axis]
    here = pl.ds(pl.multiple_of(lax.rem(me, 2) * size, size), size)
    place = target.at[here] if axis == 0 else target.at[:, here]
    copy_here(source, place)
    return links.start(source, place, {"fsdp": me ^ 1})


def attend_back(dims, b, heads_ref, grads_ref, log_ref, delta_ref, packed, scratch):
    rows, chunk = dims
    queries, keys, values, grad, q_grad, k_grad, v_grad = scratch
    group, seq_len, head_dim = queries.shape
    first = b * (group + 2) * head_dim
    for g in range(group):
        queries[g] = heads_ref[:, first + g * head_dim : first + (g + 1) * head_dim]
        at = (b * group + g) * head_dim
        grad[g] = grads_ref[:, at : at + head_dim]
        q_grad[g] = jnp.zeros((seq_len, head_dim), F32)
    first += group * head_dim
    keys[...] = heads_ref[:, first : first + head_dim]
    values[...] = heads_ref[:, first + head_dim : first + 2 * head_dim]
    factor = head_dim**-0.5
    scale = factor * LOG2E
    for at in range(seq_len // rows):
        span = slice(at * rows, (at + 1) * rows)
        key, value = keys[span], values[span]
        k_grad[span] = jnp.zeros((rows, head_dim), F32)
        v_grad[span] = jnp.zeros((rows, head_dim), F32)

        def one_head(g, _):
            key_total = jnp.zeros((rows, head_dim), F32)
            value_total = jnp.zeros((rows, head_dim), F32)
            for start in range(at * rows, seq_len, chunk):
                part = slice(start, min(start + chunk, seq_len))
                query, out_grad = queries[g, part], grad[g, part]
                scores = dot_nt(key, query) * scale - log_ref[b * group + g, 0:1, part]
                if start == at * rows:
                    key_at = lax.broadcasted_iota(jnp.int32, scores.shape, 0) + at * rows
                    query_at = lax.broadcasted_iota(jnp.int32, scores.shape, 1) + start
                    scores = jnp.where(query_at >= key_at, scores, -1e30)
                probs = jnp.exp2(scores)
                prob_grad = dot_nt(value, out_grad)
                score_grad = (probs * (prob_grad - delta_ref[b * group + g, 0:1, part])).astype(BF)
                value_total = value_total + dot_nn(probs.astype(BF), out_grad)
                key_total = key_total + dot_nn(score_grad, query)
                q_grad[g, part] = q_grad[g, part] + dot_tn(score_grad, key)
            k_grad[span] = k_grad[span] + key_total
            v_grad[span] = v_grad[span] + value_total
            return 0

        lax.fori_loop(0, group, one_head, 0)
        parts = [(q_grad[g, span] * factor).astype(BF) for g in range(group)]
        parts += [(k_grad[span] * factor).astype(BF), v_grad[span].astype(BF)]
        packed[span] = jnp.concatenate(parts, axis=1)
        yield at


def attend_back_scratch(group, seq_len, head_dim):
    many = lambda kind: pltpu.VMEM((group, seq_len, head_dim), kind)
    one = lambda kind: pltpu.VMEM((seq_len, head_dim), kind)
    return [many(BF), one(BF), one(BF), many(BF), many(F32), one(F32), one(F32)]


def attend_back_kernel(dims, heads_ref, grads_ref, log_ref, delta_ref, packed, *scratch):
    for b in range(packed.shape[0]):
        for _ in attend_back(dims, b, heads_ref, grads_ref, log_ref, delta_ref, packed.at[b], scratch):
            pass


def norm_back(rows, gain, gradient):
    q = row_norm(rows)
    n = rows * q
    u = gradient * gain
    return q * (u - n * jnp.mean(u * n, axis=-1, keepdims=True)), jnp.sum(gradient * n, axis=0, keepdims=True)


def weight_grad_kernel(left_ref, right_ref, out_ref):
    out_ref[...] = dot_nn(left_ref[...], right_ref[...]).astype(BF)


def weight_grad(left, right, width=256):
    rows, tokens = left.shape
    cols = right.shape[1]
    return call(
        weight_grad_kernel,
        shape_of((rows, cols), BF),
        [pl.BlockSpec((rows, tokens), lambda n: (0, 0)), pl.BlockSpec((tokens, width), lambda n: (0, n))],
        pl.BlockSpec((rows, width), lambda n: (0, n)),
        [],
        2 * rows * tokens * cols,
        2 * (rows * tokens + tokens * cols + rows * cols),
        grid=(cols // width,),
    )(left, right)


def project_back(dims, b, gains_ref, tables_ref, proj_ref, qkv, head_gain_grad_ref):
    nz, head_dim, widths = dims
    part_cols = nz * sum(widths)
    width = 256
    mask = head_mask(width, head_dim)
    cos = jnp.concatenate([tables_ref[0]] * (width // 128), axis=1)
    sin = jnp.concatenate([tables_ref[1]] * (width // 128), axis=1)
    for start in range(0, part_cols, width):
        cols = slice(b * part_cols + start, b * part_cols + start + width)
        rotated = qkv[:, cols].astype(F32)
        gradient = rotated * cos - partner(rotated, head_dim) * sin
        proj = proj_ref[:, start : start + width]
        scale = lax.rsqrt(head_sum(proj * proj, mask) * (1.0 / head_dim) + EPSILON)
        n = proj * scale
        u = gradient * head_gain(gains_ref, start, width)
        head_gain_grad_ref[:, cols] = jnp.sum(gradient * n, axis=0, keepdims=True)
        back = scale * (u - n * (head_sum(u * n, mask) * (1.0 / head_dim)))
        if start >= nz * widths[0]:
            back = jnp.where(key_lanes(back.shape, head_dim), back, rotated)
        qkv[:, cols] = back.astype(BF)


def input_back(x_ref, middle_grad_ref, gains_ref, qkv, weight, input_grad_ref, gain_grad_ref):
    normed_grad = dot_nt(qkv[...], weight[...])
    part, gain_sum = norm_back(x_ref[...].astype(F32), model_gain(gains_ref, 0), normed_grad)
    gain_grad_ref[...] = gain_sum
    input_grad_ref[...] = (middle_grad_ref[...] + part).astype(BF)


def post_kernel(dims, x_ref, middle_grad_ref, gains_ref, tables_ref, proj_ref, grads_ref, weight_ref, *refs):
    input_grad_ref, qkv, gain_grad_ref, head_gain_grad_ref = refs
    nz, _, widths = dims
    qkv[...] = grads_ref[...]
    for b in range(qkv.shape[1] // (nz * sum(widths))):
        part_cols = nz * sum(widths)
        part = proj_ref.at[:, pl.ds(b * part_cols, part_cols)]
        project_back(dims, b, gains_ref, tables_ref, part, qkv, head_gain_grad_ref)
    input_back(x_ref, middle_grad_ref, gains_ref, qkv, weight_ref, input_grad_ref, gain_grad_ref)


class Reduce:
    def __init__(self, links, fetch, me, z, x_first, away, kept, first, second, inward, across, out):
        self.links, self.fetch, self.me, self.z = links, fetch, me, z
        self.away, self.kept, self.out = away, kept, out
        self.bits = (2, 4) if x_first else (4, 2)
        order = (1, 3, 0, 2) if x_first else (2, 3, 0, 1)
        self.slots = {r: (away if i < 2 else kept, i % 2) for i, r in enumerate(order)}
        self.arrived, self.second, self.inward, self.across = first, second, inward, across
        self.outer, self.inner = (z == 0) | (z == 3), (z == 1) | (z == 2)
        self.one = links.copy(away, first, {"fsdp": me ^ self.bits[0]})
        self.two = links.copy(kept.at[1], second, {"fsdp": me ^ self.bits[1]})
        self.three = links.copy(kept.at[0], inward, {"seq": z ^ 1})
        self.four = links.copy(kept.at[0], across, {"seq": z ^ 3})
        self.five = links.copy(kept.at[1], out, {"seq": z ^ 1})
        self.here = fetch.copy(kept.at[1], out)
        self.load = fetch.copy(first, away)

    def put(self, r, cols, values):
        ref, i = self.slots[r]
        ref[i, :, cols] = values

    def rows_of(self):
        rows = self.kept.shape[1]
        step = 32 if rows % 32 == 0 else 16
        return rows // step, step

    def by_rows(self, work):
        count, step = self.rows_of()

        def body(i, _):
            work(pl.ds(pl.multiple_of(i * step, step), step))
            return 0

        lax.fori_loop(0, count, body, 0)

    def begin(self):
        self.one.start()

    def load_one(self):
        self.one.wait_recv()
        self.one.wait_send()
        self.load.start()

    def fold_one(self):
        self.load.wait()

        def work(rows):
            for i in range(2):
                self.kept[i, rows] = self.kept[i, rows] + self.away[i, rows]

        self.by_rows(work)
        self.two.start()

    def fold_two(self):
        self.two.wait_recv()

        def work(rows):
            self.kept[0, rows] = self.kept[0, rows] + self.second[rows]

        self.by_rows(work)

        @pl.when(self.outer)
        def _():
            self.three.start()

    def fold_three(self):
        @pl.when(self.inner)
        def _():
            self.three.wait_recv()

            def work(rows):
                self.kept[0, rows] = self.kept[0, rows] + self.inward[rows]

            self.by_rows(work)
            self.four.start()

    def fold_four(self):
        self.two.wait_send()

        @pl.when(self.inner)
        def _():
            self.four.wait_recv()

            def work(rows):
                self.kept[1, rows] = self.kept[0, rows] + self.across[rows]

            self.by_rows(work)
            self.five.start()
            self.here.start()

    def end(self):
        @pl.when(self.inner)
        def _():
            self.four.wait_send()
            self.five.wait_send()
            self.here.wait()

        @pl.when(self.outer)
        def _():
            self.three.wait_send()
            self.five.wait_recv()


def each(reduces, step):
    if step == "fold_one":
        each(reduces, "load_one")
    for reduce in reduces:
        getattr(reduce, step)()


class Total:
    def __init__(self, links, me, z, sums, arrived):
        self.sums, self.arrived = sums, arrived
        peers = [{"fsdp": me ^ 1}, {"fsdp": me ^ 2}, {"fsdp": me ^ 4}, {"seq": z ^ 1}, {"seq": z ^ 2}]
        self.copies = [links.copy(sums.at[i], arrived.at[i], peer) for i, peer in enumerate(peers)]

    def begin(self, at):
        self.copies[at].start()

    def fold(self, at):
        self.copies[at].wait_recv()
        self.sums[at + 1] = self.sums[at] + self.arrived[at]

    def end(self):
        for copy in self.copies:
            copy.wait_send()


EARLY = (
    ("wide4", "matmul"), ("wide4", "begin"), ("down1", "matmul"), ("down0", "matmul"), ("wide0", "matmul"),
    ("out", "matmul"), ("wide1", "matmul"), ("out", "begin"), ("wide4", "fold_one"), ("down0", "begin"),
    ("wide0", "begin"),
)
MIDDLE = (
    ("keys", 0, 0), ("keys", 0, 1), ("keys", 0, 2), ("wide4", "fold_two"), ("keys", 0, 3), ("keys", 0, 4),
    ("keys", 0, 5), ("keys", 0, 6), ("keys", 0, 7), ("wide5", "matmul"), ("wide2", "matmul"), ("wide4", "fold_three"),
    ("down0", "fold_one"), ("wide1", "begin"), ("keys", 1, 0), ("wide5", "begin"), ("keys", 1, 1),
    ("down0", "fold_two"), ("out", "fold_one"), ("keys", 1, 2), ("keys", 1, 3), ("keys", 1, 4), ("keys", 1, 5),
    ("keys", 1, 6), ("keys", 1, 7), ("wide0", "fold_one"), ("wide5", "fold_one"), ("wide3", "matmul"),
    ("wide1", "fold_one"), ("project", 0), ("out", "fold_two"), ("wide4", "fold_four"), ("down1", "begin"),
    ("wide2", "begin"), ("wide5", "fold_two"), ("down0", "fold_three"), ("wide1", "fold_two"), ("project", 1),
)
LATE = (
    ("out", "fold_three"), ("input",), ("down0", "fold_four"), ("wide5", "fold_three"), ("down1", "fold_one"),
    ("wide1", "fold_three"), ("out", "fold_four"), ("wide0", "fold_two"), ("total", 0), ("wide2", "fold_one"),
    ("wide5", "fold_four"), ("down1", "fold_two"), ("total", 1), ("last1", "matmul"), ("wide3", "begin"),
    ("wide0", "fold_three"), ("wide1", "fold_four"), ("total", 2), ("wide2", "fold_two"), ("down1", "fold_three"),
    ("last0", "matmul"), ("wide0", "fold_four"), ("wide3", "fold_one"), ("wide2", "fold_three"), ("last1", "begin"),
    ("down1", "fold_four"), ("last0", "begin"), ("wide3", "fold_two"), ("wide3", "fold_three"), ("last1", "fold_one"),
    ("wide2", "fold_four"), ("last0", "fold_one"), ("total", 3), ("last1", "fold_two"), ("wide3", "fold_four"),
    ("last0", "fold_two"), ("last0", "fold_three"), ("last1", "fold_three"), ("total", 4), ("last0", "fold_four"),
    ("last1", "fold_four"),
)


GATES = ("gate0x", "gate1y", "gate2x", "gate3y", "gate4x", "gate5y")
UPS = ("up0x", "up1y", "up2x", "up3y", "up4x", "up5y")


def backward_kernel(dims, gains_ref, tables_ref, delta_own, feed_gain_ref, heads_hbm, log_hbm, grad_low, low_own, *refs):
    nz, head_dim, widths, attend_dims, names = dims
    given, refs = refs[:12], refs[12:]
    x_hbm, middle_grad_hbm, proj_hbm, hidden_hbm, dy_hbm, normed_two_hbm = given[:6]
    gate_hbm, up_hbm, mixed_hbm, normed_hbm, first_hbm, second_hbm = given[6:]
    input_grad_ref, totals_ref = refs[:2]
    n = len(names)
    finals, refs = dict(zip(names, refs[2 : 2 + n])), refs[2 + n :]
    firsts, refs = dict(zip(names, refs[:n])), refs[n:]
    low_hbm, refs = refs[0], refs[1:]
    aways, refs = dict(zip(names, refs[:n])), refs[n:]
    kepts, refs = dict(zip(names, refs[:n])), refs[n:]
    seconds, refs = dict(zip(names, refs[:n])), refs[n:]
    inwards, refs = dict(zip(names, refs[:n])), refs[n:]
    acrosses, refs = dict(zip(names, refs[:n])), refs[n:]
    grads, delta, qkv, other_qkv, normed_two, normed, sums, sum_arrived, gain_grad, head_gain_grad = refs[:10]
    heads_ref, log_ref, low_ref, sems, send_sems, recv_sems = refs[10:]
    z, me = lax.axis_index("seq"), lax.axis_index("fsdp")
    chip, core = lax.div(me, 2), lax.rem(me, 2)
    links, fetch = Links(send_sems, recv_sems), Fetch(sems)
    low_load = fetch.start(low_own, low_ref)
    head_loads = [fetch.start(heads_hbm, heads_ref), fetch.start(log_hbm, log_ref)]
    enter(me, z, nz, True)
    tokens = grad_low.shape[0]
    seq_len, block_cols = heads_ref.shape
    part_cols = nz * sum(widths)
    parts = qkv.shape[1] // part_cols
    late = []

    def copy_here(source, target):
        copy = fetch.start(source, target)
        late.append(copy)
        return copy

    my_rows = pl.ds(pl.multiple_of(z * tokens, tokens), tokens)
    arrivals = []
    for b in range(parts):
        arrived = []
        for j in range(nz):
            owner = z ^ j
            from_cols = pl.ds(pl.multiple_of((owner * parts + b) * widths[0], widths[0]), widths[0])
            pairs = [(grad_low.at[:, from_cols], grads.at[my_rows, pl.ds(b * widths[0], widths[0])])]
            if b == 0:
                pairs.append((delta_own.at[pl.ds(pl.multiple_of(owner * 8, 8), 8)], delta.at[:, my_rows]))
            for source, target in pairs:
                if j == 0:
                    copy_here(source, target)
                else:
                    arrived.append(links.start(source, target, {"seq": owner}))
        arrivals.append(arrived)
    low_load.wait()
    low_arrival = both_cores(links, copy_here, me, low_ref, low_hbm, 0)
    reduces = {}
    for name in names:
        reduces[name] = Reduce(
            links, fetch, me, z, name[-1] == "x", aways[name], kepts[name], firsts[name], seconds[name], inwards[name],
            acrosses[name], finals[name],
        )
    down = [[reduces[f"down{c}{way}"] for way in "xy"] for c in range(2)]
    wide_names = GATES + UPS
    wide = [[reduces[name] for name in wide_names[i : i + 2]] for i in range(0, len(wide_names), 2)]
    out = [reduces["outx"], reduces["outy"]]
    last = [[reduces[f"last{b}{way}"] for way in "xy"] for b in range(parts)]
    total = Total(links, me, z, sums, sum_arrived)
    part_cols_of = lambda b: pl.ds(b * part_cols, part_cols)
    qkv_links = [
        links.copy(qkv.at[:, part_cols_of(b)], other_qkv.at[:, part_cols_of(b)], {"fsdp": me ^ 1}) for b in range(parts)
    ]
    chips = 4
    step = 256
    half = down[0][0].kept.shape[1]
    shard = wide[0][0].kept.shape[1]
    both = 2 * tokens
    model = low_ref.shape[1]

    def my_blocks(source, target, rows):
        copies = []
        for r in range(chips):
            owner = (chip ^ r) * 2 + core
            copies.append(fetch.start(source.at[pl.ds(pl.multiple_of(owner * rows, rows), rows)], target.at[pl.ds(r * rows, rows)]))
        return copies

    def wide_grads(places, left, right):
        width = right.shape[2]
        chunks = [
            (source, (first + c) * width, unit, c * width)
            for source, first, unit in places
            for c in range(unit.kept.shape[2] // width)
        ]
        count = len(chunks)
        loads = [
            fetch.copy(source.at[:, pl.ds(at, width)], right.at[c % 2]) for c, (source, at, _, _) in enumerate(chunks)
        ]
        loads[0].start()
        loads[1].start()
        for c in range(count):
            loads[c].wait()
            _, _, unit, base = chunks[c]

            def block(k, _):
                here = pl.ds(pl.multiple_of(k * step, step), step)
                to = pl.ds(pl.multiple_of(base + k * step, step), step)
                got = dot_nn(left[...], right[c % 2, :, here]).astype(BF)
                for r in range(chips):
                    unit.put(r, to, got[r * shard : (r + 1) * shard])
                return 0

            lax.fori_loop(0, width // step, block, 0)
            if c + 2 < count:
                loads[c + 2].start()

    ready = {"two": my_blocks(normed_two_hbm, normed_two, shard), "one": my_blocks(normed_hbm, normed, shard)}

    def ready_now(name):
        wait_all(ready.pop(name, ()))

    wide_part = wide[0][0].kept.shape[2]

    def wide_matmul(i, right):
        ready_now("two")
        places = []
        for at in (2 * i, 2 * i + 1):
            source = gate_hbm if at < len(GATES) else up_hbm
            places.append((source, at % len(GATES), wide[i][at % 2]))
        wide_grads(places, normed_two, right)

    def out_matmul(mixed, low):
        cols = out[0].kept.shape[2]
        for start in range(0, low.shape[1], step):
            got = dot_nn(mixed[...], low[:, start : start + step]).astype(BF)
            for r in range(chips):
                out[start // cols].put(r, slice(start % cols, start % cols + step), got[r * shard : (r + 1) * shard])

    def down_matmul(c, hidden, dy):
        cols = down[0][0].kept.shape[2]

        def block(i, _):
            to = pl.ds(pl.multiple_of(i * step, step), step)
            here = pl.ds(pl.multiple_of(c * cols + i * step, step), step)
            for r in range(chips):
                got = dot_nn(hidden[2 * r * half : 2 * (r + 1) * half], dy[:, here]).astype(BF)
                for side in range(2):
                    down[c][side].put(r, to, got[side * half : (side + 1) * half])
            return 0

        lax.fori_loop(0, cols // step, block, 0)

    def last_matmul(b):
        ready_now("one")
        mine = normed[:, pl.ds(pl.multiple_of(core * tokens, tokens), tokens)]
        theirs = normed[:, pl.ds(pl.multiple_of((1 - core) * tokens, tokens), tokens)]
        qkv_links[b].wait()
        cols = last[b][0].kept.shape[2]
        for start in range(0, part_cols, step):
            here = slice(b * part_cols + start, b * part_cols + start + step)
            got = (dot_nn(mine, qkv[:, here]) + dot_nn(theirs, other_qkv[:, here])).astype(BF)
            for r in range(chips):
                last[b][start // cols].put(r, slice(start % cols, start % cols + step), got[r * shard : (r + 1) * shard])

    pairs = {"out": out}
    pairs |= {f"down{c}": down[c] for c in range(2)}
    pairs |= {f"wide{i}": pair for i, pair in enumerate(wide)}
    pairs |= {f"last{b}": last[b] for b in range(parts)}
    right_shape = pltpu.VMEM((2, both, wide_part), BF)

    def sum_step(name, what):
        if what != "matmul":
            each(pairs[name], what)
        elif name[:4] == "last":
            last_matmul(int(name[4]))
        else:
            pl.run_scoped(functools.partial(wide_matmul, int(name[4])), right_shape)

    def early(hidden, dy, right, mixed, low):
        ready["down"] = my_blocks(hidden_hbm, hidden, 2 * half) + [fetch.start(dy_hbm, dy)]
        ready["out"] = my_blocks(mixed_hbm, mixed, shard)
        for name, what in EARLY:
            if what != "matmul":
                each(pairs[name], what)
            elif name[:4] == "down":
                ready_now("down")
                down_matmul(int(name[4]), hidden, dy)
            elif name == "out":
                low_arrival.wait_recv()
                wait_all(late)
                del late[:]
                ready["out"].append(fetch.start(low_hbm, low))
                ready_now("out")
                out_matmul(mixed, low)
            else:
                wide_matmul(int(name[4]), right)

    pl.run_scoped(
        early,
        pltpu.VMEM((2 * chips * half, both), BF),
        pltpu.VMEM((both, model), BF),
        right_shape,
        pltpu.VMEM((chips * shard, both), BF),
        pltpu.VMEM((both, model), BF),
    )

    wait_all(head_loads)
    heads = log_ref.shape[0]
    group = heads // parts
    first_back = links.reserve(parts * 2 * nz)
    own_back = fetch.used
    fetch.used += parts * 2

    def back_copies(b, packed):
        for i, width in enumerate(widths):
            base = b * part_cols + i * nz * widths[0]
            target = qkv.at[:, pl.ds(pl.multiple_of(base + z * width, width), width)]
            for j in range(nz):
                owner = z ^ j
                rows = pl.ds(pl.multiple_of(owner * tokens, tokens), tokens)
                source = packed.at[b, rows, pl.ds(i * widths[0], width)]
                if j == 0:
                    yield j, pltpu.make_async_copy(source, target, sems.at[own_back + 2 * b + i])
                else:
                    yield j, links.copy(source, target, {"seq": owner}, at=first_back + (2 * b + i) * nz + j)

    def middle(packed, delta_rows, *scratch):
        blocks = {}

        def keys_step(b, at):
            if at == 0:
                for copy in arrivals[b]:
                    copy.wait_recv()
                if b == 0:
                    for h in range(heads):
                        delta_rows[h] = jnp.broadcast_to(delta[h : h + 1], (8, seq_len))
                blocks[b] = attend_back(attend_dims, b, heads_ref, grads, log_ref, delta_rows, packed.at[b], scratch)
            next(blocks[b])
            if (at + 1) * attend_dims[0] == seq_len:
                for _, copy in back_copies(b, packed):
                    copy.start()

        def project_step(b):
            for j, copy in back_copies(b, packed):
                if j == 0:
                    copy.wait()
                else:
                    copy.wait_recv()

            def inner(proj):
                fetch.start(proj_hbm.at[:, part_cols_of(b)], proj).wait()
                project_back((nz, head_dim, widths), b, gains_ref, tables_ref, proj, qkv, head_gain_grad)

            pl.run_scoped(inner, pltpu.VMEM((tokens, part_cols), F32))
            qkv_links[b].start()

        for token in MIDDLE:
            if token[0] == "keys":
                keys_step(*token[1:])
            elif token[0] == "project":
                project_step(token[1])
            else:
                sum_step(*token)
        for b in range(parts):
            for j, copy in back_copies(b, packed):
                if j:
                    copy.wait_send()

    pl.run_scoped(
        middle,
        pltpu.VMEM((parts, seq_len, sum(widths)), BF),
        pltpu.VMEM((heads, 8, seq_len), F32),
        *attend_back_scratch(group, seq_len, head_dim),
    )

    def input_step(weight, x, middle_grad):
        copies = [fetch.start(x_hbm, x), fetch.start(middle_grad_hbm, middle_grad)]
        section = part_cols // 2
        for b in range(parts):
            for i, source in enumerate((first_hbm, second_hbm)):
                to = pl.ds(b * part_cols + i * section, section)
                copies.append(fetch.start(source.at[:, pl.ds(b * section, section)], weight.at[:, to]))
        wait_all(copies)
        input_back(x, middle_grad, gains_ref, qkv, weight, input_grad_ref, gain_grad)
        row = jnp.concatenate([gain_grad[...], head_gain_grad[...], feed_gain_ref[...]], axis=1)
        sums[0] = jnp.broadcast_to(row, sums.shape[1:])

    for token in LATE:
        if token[0] == "input":
            pl.run_scoped(
                input_step,
                pltpu.VMEM((model, parts * part_cols), BF),
                pltpu.VMEM((tokens, model), BF),
                pltpu.VMEM((tokens, model), F32),
            )
            total.begin(0)
        elif token[0] == "total":
            total.fold(token[1])
            if token[1] < 4:
                total.begin(token[1] + 1)
        else:
            sum_step(*token)
    totals_ref[...] = sums[5]
    total.end()
    for name in names:
        reduces[name].end()
    links.wait_sends()


def finish_kernel(dims, *refs):
    names, nz, head_dim = dims
    n = len(names)
    output_in, input_grad_in = refs[:2]
    shards, refs = dict(zip(names, refs[2 : 2 + n])), refs[2 + n :]
    output, input_grad, q_out, k_out, v_out, out_out, gate_out, up_out, down_out = refs[:9]
    slots, refs = dict(zip(names, refs[9 : 9 + n])), refs[9 + n :]
    passing, q, k, v, out, gate, up, down, load_sems, store_sems = refs
    fetch, store = Fetch(load_sems), Fetch(store_sems)
    order = GATES + UPS + tuple(name for name in names if name not in GATES + UPS)
    loads = {name: fetch.start(shards[name], slots[name]) for name in order}
    moves = [fetch.start(source, passing.at[i]) for i, source in enumerate((output_in, input_grad_in))]
    stores = []

    def place(name, target, row, col):
        loads[name].wait()
        rows, cols = slots[name].shape
        target[row : row + rows, col : col + cols] = slots[name][...].astype(F32)

    cols = slots["gate0x"].shape[1]
    for target, done, pieces in (
        (gate, gate_out, GATES),
        (up, up_out, UPS),
    ):
        for i, name in enumerate(pieces):
            place(name, target, 0, i * cols)
        stores.append(store.start(target, done))
    rows, cols = slots["down0x"].shape
    for c in range(2):
        for i, way in enumerate("xy"):
            place(f"down{c}{way}", down, i * rows, c * cols)
    stores.append(store.start(down, down_out))
    cols = slots["outx"].shape[1]
    for i, way in enumerate("xy"):
        place("out" + way, out, 0, i * cols)
    stores.append(store.start(out, out_out))
    parts = 2
    width = q.shape[1] // (nz * parts)
    for b in range(parts):
        loads[f"last{b}x"].wait()
        for i in range(nz):
            to = (i * parts + b) * width
            q[:, to : to + width] = slots[f"last{b}x"][:, i * width : (i + 1) * width].astype(F32)
    stores.append(store.start(q, q_out))
    for b in range(parts):
        loads[f"last{b}y"].wait()
    for i, target in enumerate((k, v)):
        pieces = [
            slots[f"last{b}y"][:, (2 * at + i) * head_dim : (2 * at + i + 1) * head_dim]
            for at in range(nz)
            for b in range(parts)
        ]
        target[...] = jnp.concatenate(pieces, axis=1).astype(F32)
    stores += [store.start(k, k_out), store.start(v, v_out)]
    for i, target in enumerate((output, input_grad)):
        moves[i].wait()
        stores.append(store.start(passing.at[i], target))
    wait_all(stores)


def add(a, b):
    return (a.astype(F32) + b.astype(F32)).astype(a.dtype)


def sum_line(values):
    size = lax.axis_size("seq")
    if size != 4:
        return lax.psum(values, "seq")
    z = lax.axis_index("seq")
    inner = add(values, lax.ppermute(values, "seq", [(0, 1), (3, 2)]))
    total = add(inner, lax.ppermute(inner, "seq", [(1, 2), (2, 1)]))
    outer = lax.ppermute(total, "seq", [(1, 0), (2, 3)])
    return jnp.where((z == 1) | (z == 2), total, outer)


def per_device(
    inputs,
    positions,
    cotangent,
    query_weight,
    key_weight,
    value_weight,
    out_weight,
    attention_gain,
    query_gain,
    key_gain,
    feedforward_gain,
    gate_weight,
    up_weight,
    down_weight,
):
    seqs, tokens, model = inputs.shape
    assert seqs == 1
    fsdp, nz = lax.axis_size("fsdp"), lax.axis_size("seq")
    me, z = lax.axis_index("fsdp"), lax.axis_index("seq")
    plane = fsdp == 8 and nz == 4
    both = 2 * tokens if plane else tokens
    x = inputs.reshape(tokens, model)
    dy = cotangent.reshape(tokens, model)
    head_dim = query_gain.shape[0] * fsdp
    q_cols, k_cols, v_cols = query_weight.shape[1], key_weight.shape[1], value_weight.shape[1]
    heads, kv_heads = q_cols // head_dim // nz, k_cols // head_dim // nz
    hidden_cols = gate_weight.shape[1]
    seq_len = tokens * nz

    group, parts = heads // kv_heads, kv_heads
    widths = (group * head_dim, 2 * head_dim)
    part_cols = nz * sum(widths)
    assert parts == 2

    section = nz * widths[0]
    assert model == 2 * section and part_cols == 2 * section
    half_out = model // 2
    first_cols = 2 * section + half_out
    if plane:
        given = [query_weight, key_weight, value_weight, out_weight, gate_weight, up_weight, down_weight]
        given += [query_gain[None], key_gain[None], attention_gain[None], feedforward_gain[None]]
    else:
        shard_rows = query_weight.shape[0]
        q = query_weight.reshape(shard_rows, nz, parts, widths[0])
        kv = jnp.stack([v.reshape(shard_rows, nz, parts, head_dim) for v in (key_weight, value_weight)], axis=3)
        first, second = (
            jnp.concatenate([v[:, :, b].reshape(shard_rows, section) for b in range(parts)] + [rest], axis=1)
            for v, rest in ((q, out_weight[:, :half_out]), (kv, out_weight[:, half_out:]))
        )
        gather = functools.partial(lax.all_gather, axis_name="fsdp", axis=0, tiled=True)
        first_full, second_full, gate_full = gather(first), gather(second), gather(gate_weight)
        up_full, down_full = gather(up_weight), gather(down_weight)
        key_row = jnp.concatenate([gather(key_gain), jnp.zeros((head_dim,), BF)])
        gain_rows = [gather(attention_gain).reshape(2, section), jnp.tile(gather(query_gain), nz * group)[None]]
        gain_rows += [jnp.tile(key_row, nz)[None], gather(feedforward_gain).reshape(2, section)]
        gain_rows = jnp.concatenate(gain_rows + [jnp.zeros((10, section), BF)]).astype(F32)
        given = [first_full, second_full, gain_rows, gate_full, up_full, down_full]

    half_dim = head_dim // 2
    freqs = ROPE_BASE ** (-(jnp.arange(128) % half_dim).astype(F32) / half_dim)

    rows_model = lambda kind: shape_of((tokens, model), kind)
    width = 512
    blocks = hidden_cols // width
    sizes = (blocks - 6,) + (1,) * 6
    block_cols = parts * sum(widths)
    mixed_cols = heads * head_dim
    attend_flops = 2 * heads * seq_len * seq_len * head_dim
    proj_flops = 2 * tokens * model * parts * part_cols
    outs = [
        shape_of((16, section), F32),
        shape_of((2, tokens, 128), F32),
        shape_of((1, model), F32),
        shape_of((8 * nz, tokens), F32),
        shape_of((seq_len, block_cols), BF),
        shape_of((heads, 8, seq_len), F32),
        rows_model(BF),
        rows_model(F32),
        rows_model(BF),
        shape_of((tokens, q_cols), BF),
        shape_of((tokens, parts * part_cols), F32),
        shape_of((model, both), BF),
        shape_of((q_cols, both), BF),
        shape_of((model, both), BF),
        shape_of((hidden_cols, both), BF),
        shape_of((both, hidden_cols), BF),
        shape_of((both, hidden_cols), BF),
        shape_of((both, model), BF),
    ]
    n_links = parts * 3 * (nz - 1)
    first_rows = model
    if plane:
        outs += [shape_of((model, first_cols), BF)] * 2
        outs += [shape_of((model, hidden_cols), BF)] * 2 + [shape_of((hidden_cols, model), BF)]
        n_links += (8 + 2 * len(sizes)) * 7 + 4
        first_rows += 8 * 16
    many = lambda count: pltpu.VMEM((count, seq_len, head_dim), BF)
    one = pltpu.VMEM((seq_len, head_dim), BF)
    got = call(
        functools.partial(forward_kernel, (nz, plane, head_dim, widths, min(256, seq_len), width, sizes)),
        outs,
        [VMEM] * 4 + ([ANY] * 7 + [VMEM] * 4 if plane else [ANY] * 2 + [VMEM] + [ANY] * 3),
        [VMEM] * 4 + [ANY] * (len(outs) - 4),
        [
            pltpu.VMEM((first_rows, first_cols), BF),
            pltpu.VMEM((model, first_cols), BF),
            pltpu.VMEM((q_cols, model), BF),
            pltpu.VMEM((tokens, model), BF),
            pltpu.VMEM((3, model, tokens), BF),
            pltpu.VMEM((tokens, parts * part_cols), F32),
            pltpu.VMEM((tokens, parts * part_cols), BF),
            many(group),
            one,
            one,
            many(group),
            pltpu.VMEM((parts, seq_len, widths[0]), BF),
            pltpu.VMEM((tokens, q_cols), BF),
            pltpu.VMEM((seq_len, block_cols), BF),
            pltpu.VMEM((heads, 8, seq_len), F32),
            pltpu.VMEM((tokens, model), BF),
            pltpu.VMEM((tokens, model), BF),
            pltpu.VMEM((tokens, q_cols), BF),
            pltpu.VMEM((2, model, width), BF),
            pltpu.VMEM((2, model, width), BF),
            pltpu.VMEM((2, width, model), BF),
            pltpu.VMEM((tokens, model), F32),
            pltpu.VMEM((tokens, model), F32),
            pltpu.VMEM((tokens, model), F32),
            pltpu.VMEM((2, width, tokens), BF),
            pltpu.VMEM((2, tokens, width), BF),
            pltpu.VMEM((2, tokens, width), BF),
            pltpu.SemaphoreType.DMA((64,)),
            pltpu.SemaphoreType.DMA((2, 3)),
            pltpu.SemaphoreType.DMA((2, 3)),
            pltpu.SemaphoreType.DMA((n_links,)),
            pltpu.SemaphoreType.DMA((n_links,)),
            pltpu.SemaphoreType.DMA((2, 3)),
            pltpu.SemaphoreType.DMA((blocks, 3)),
        ]
        + [pltpu.VMEM(w.shape, BF) for w in (gate_weight, up_weight, down_weight) if plane]
        + [pltpu.VMEM((query_weight.shape[0] + extra, 2 * section), BF) for extra in (16, 0) if plane]
        + [pltpu.VMEM(key_weight.shape, BF) for _ in range(2) if plane],
        proj_flops + 4 * attend_flops + 12 * tokens * model * hidden_cols,
        100 * 2**20,
        collective=1,
    )(x, dy, positions.reshape(1, tokens), freqs[None], *given)
    gains, tables, feed_gain_part, delta = got[:4]
    head_rows, logs, output, middle_grad, middle_low, mixed_grad = got[4:10]
    proj, normed_t, mixed_t, normed_two_t, hidden_t, gate_grad, up_grad, dy_both = got[10:18]
    if plane:
        first_full, second_full = got[18:20]

    attend_dims = (min(256, seq_len), min(1024, seq_len))
    attend_scratch = attend_back_scratch(group, seq_len, head_dim)
    if plane:
        down_rows, down_cols = down_weight.shape
        blocks = {f"down{c}{way}": (down_rows // 2, down_cols // 2) for c in range(2) for way in "xy"}
        blocks |= {name: (gate_weight.shape[0], hidden_cols // len(GATES)) for name in GATES + UPS}
        blocks |= {"out" + way: (out_weight.shape[0], model // 2) for way in "xy"}
        blocks |= {f"last{b}{way}": (query_weight.shape[0], part_cols // 2) for b in range(parts) for way in "xy"}
        names = tuple(blocks)
        pairs = [(2,) + shape for shape in blocks.values()]
        total_cols = model + parts * part_cols + model
        n_links = 3 * (nz - 1) + 2 * parts * nz + 1 + parts + 5 * len(names) + 5
        n_copies = 80 + 2 * len(names)
        got = call(
            functools.partial(backward_kernel, (nz, head_dim, widths, attend_dims, names)),
            [rows_model(BF), shape_of((8, total_cols), F32)]
            + [shape_of(shape, BF) for shape in blocks.values()]
            + [shape_of(shape, BF) for shape in pairs]
            + [shape_of((both, model), BF)],
            [VMEM] * 4 + [ANY] * 16,
            [VMEM] * 2 + [ANY] * (2 * len(names) + 1),
            [pltpu.VMEM(shape, BF) for shape in pairs] * 2
            + [pltpu.VMEM(shape, BF) for shape in blocks.values()] * 3
            + [
                pltpu.VMEM((seq_len, mixed_cols), BF),
                pltpu.VMEM((8, seq_len), F32),
                pltpu.VMEM((tokens, parts * part_cols), BF),
                pltpu.VMEM((tokens, parts * part_cols), BF),
                pltpu.VMEM((model // 2, both), BF),
                pltpu.VMEM((model // 2, both), BF),
                pltpu.VMEM((6, 8, total_cols), F32),
                pltpu.VMEM((5, 8, total_cols), F32),
                pltpu.VMEM((1, model), F32),
                pltpu.VMEM((1, parts * part_cols), F32),
                pltpu.VMEM((seq_len, block_cols), BF),
                pltpu.VMEM((heads, 8, seq_len), F32),
                pltpu.VMEM((tokens, model), BF),
                pltpu.SemaphoreType.DMA((n_copies,)),
                pltpu.SemaphoreType.DMA((n_links,)),
                pltpu.SemaphoreType.DMA((n_links,)),
            ],
            10 * attend_flops + 2 * tokens * model * (3 * hidden_cols + 3 * (q_cols + k_cols)),
            100 * 2**20,
            collective=3,
        )(
            gains, tables, delta, feed_gain_part, head_rows, logs, mixed_grad, middle_low, x, middle_grad, proj,
            hidden_t, dy_both, normed_two_t, gate_grad, up_grad, mixed_t, normed_t, first_full, second_full,
        )
        input_grad, totals = got[:2]
        slots = [pltpu.VMEM(shape, BF) for shape in blocks.values()]
        out_shapes = [w.shape for w in (query_weight, key_weight, value_weight, out_weight, gate_weight, up_weight, down_weight)]
        output, input_grad, q_shard, k_shard, v_shard, out_shard, gate_shard, up_shard, down_shard = call(
            functools.partial(finish_kernel, (names, nz, head_dim)),
            [rows_model(BF)] * 2 + [shape_of(shape, F32) for shape in out_shapes],
            [ANY] * (2 + len(names)),
            [ANY] * 9,
            slots
            + [pltpu.VMEM((2, tokens, model), BF)]
            + [pltpu.VMEM(shape, F32) for shape in out_shapes]
            + [pltpu.SemaphoreType.DMA((2 + len(names),)), pltpu.SemaphoreType.DMA((9,))],
            0,
            18 * 2**20,
        )(output, input_grad, *got[2 : 2 + len(names)])
        totals = totals[0]
    else:
        exchange = functools.partial(lax.all_to_all, axis_name="seq", tiled=True)
        grad_rows = exchange(mixed_grad, split_axis=1, concat_axis=0)
        delta_rows = exchange(delta, split_axis=0, concat_axis=1)
        packed = call(
            functools.partial(attend_back_kernel, attend_dims),
            shape_of((parts, seq_len, sum(widths)), BF),
            [VMEM] * 4,
            VMEM,
            attend_scratch,
            10 * attend_flops,
            20 * 2**20,
        )(head_rows, grad_rows, logs, jnp.broadcast_to(delta_rows[:heads, None], (heads, 8, seq_len)))
        pieces = [piece for b in range(parts) for piece in (packed[b, :, : widths[0]], packed[b, :, widths[0] :])]
        qkv = jnp.concatenate([exchange(piece, split_axis=0, concat_axis=1) for piece in pieces], axis=1)
        weight = jnp.concatenate(
            [full[:, b * section : (b + 1) * section] for b in range(parts) for full in (first_full, second_full)], axis=1
        )
        input_grad, qkv, gain_part, head_gain_part = call(
            functools.partial(post_kernel, (nz, head_dim, widths)),
            [
                rows_model(BF),
                shape_of((tokens, parts * part_cols), BF),
                shape_of((1, model), F32),
                shape_of((1, parts * part_cols), F32),
            ],
            [VMEM] * 7,
            [VMEM] * 4,
            [],
            proj_flops,
            14 * 2**20,
        )(x, middle_grad, gains, tables, proj, qkv, weight)

        def reduce(left, right):
            return sum_line(lax.psum_scatter(weight_grad(left, right), "fsdp", scatter_dimension=0, tiled=True)).astype(F32)

        down_shard, gate_shard = reduce(hidden_t, dy), reduce(normed_two_t, gate_grad)
        up_shard, out_shard = reduce(normed_two_t, up_grad), reduce(mixed_t, middle_low)
        qkv_shard = reduce(normed_t, qkv)
        part_shards = [
            (qkv_shard[:, b * part_cols : b * part_cols + section], qkv_shard[:, b * part_cols + section : (b + 1) * part_cols])
            for b in range(parts)
        ]
        q_shard = jnp.stack([q.reshape(shard_rows, nz, widths[0]) for q, _ in part_shards], axis=2).reshape(shard_rows, -1)
        kv_shard = jnp.stack([kv.reshape(shard_rows, nz, 2, head_dim) for _, kv in part_shards], axis=2)
        k_shard, v_shard = (kv_shard[:, :, :, i].reshape(shard_rows, -1) for i in range(2))
        totals = lax.psum(jnp.concatenate([gain_part, head_gain_part, feed_gain_part], axis=1)[0], ("seq", "fsdp"))

    head_totals = totals[model : model + parts * part_cols].reshape(parts, part_cols)
    q_total = head_totals[:, : nz * widths[0]].reshape(-1, head_dim).sum(axis=0)
    k_total = head_totals[:, nz * widths[0] :].reshape(-1, 2, head_dim)[:, 0].sum(axis=0)

    def share(values):
        own = jnp.arange(fsdp)[:, None] == me
        return jnp.sum(jnp.where(own, values.reshape(fsdp, -1), 0.0), axis=0)

    return (
        output.reshape(inputs.shape),
        input_grad.reshape(inputs.shape),
        q_shard,
        k_shard,
        v_shard,
        out_shard,
        share(totals[:model]),
        share(q_total),
        share(k_total),
        share(totals[model + parts * part_cols :]),
        gate_shard,
        up_shard,
        down_shard,
    )


def solution(mesh):
    tokens, rows, row = P("fsdp", "seq", None), P("fsdp", None), P("fsdp")
    in_specs = (tokens, P("fsdp", "seq"), tokens) + (rows,) * 4 + (row,) * 4 + (rows,) * 3
    out_specs = (tokens, tokens) + (rows,) * 4 + (row,) * 4 + (rows,) * 3
    return jax.shard_map(per_device, mesh=mesh, in_specs=in_specs, out_specs=out_specs, check_vma=False)
```

```python
import functools

import jax
import jax.numpy as jnp
from jax import lax
from jax.experimental import pallas as pl
from jax.experimental.pallas import tpu as pltpu
from jax.sharding import PartitionSpec as P

EPSILON = 1e-05
ROPE_BASE = 1000000.0
LOG2E = 1.4426950408889634
BF = jnp.bfloat16
F32 = jnp.float32
VMEM = pl.BlockSpec(memory_space=pltpu.VMEM)
SMEM = pl.BlockSpec(memory_space=pltpu.SMEM)
ANY = pl.BlockSpec(memory_space=pl.ANY)
VMEM_BYTES = 62 * 2**20


def dot_nn(a, b):
    return lax.dot_general(a, b, (((1,), (0,)), ((), ())), preferred_element_type=F32)


def dot_nt(a, b):
    return lax.dot_general(a, b, (((1,), (1,)), ((), ())), preferred_element_type=F32)


def dot_tn(a, b):
    return lax.dot_general(a, b, (((0,), (0,)), ((), ())), preferred_element_type=F32)


def shape_of(shape, dtype):
    return jax.ShapeDtypeStruct(shape, dtype)


def call(kernel, outs, in_specs, out_specs, scratch, flops, moved, collective=None, **more):
    params = {} if collective is None else {"collective_id": collective, "has_side_effects": True}
    return pl.pallas_call(
        kernel,
        out_shape=outs,
        in_specs=in_specs,
        out_specs=out_specs,
        scratch_shapes=scratch,
        compiler_params=pltpu.CompilerParams(vmem_limit_bytes=VMEM_BYTES, **params),
        cost_estimate=pl.CostEstimate(flops=flops, bytes_accessed=moved, transcendentals=0),
        **more,
    )


def row_norm(values):
    return lax.rsqrt(jnp.mean(values * values, axis=-1, keepdims=True) + EPSILON)


class Fetch:
    def __init__(self, sems):
        self.sems, self.used = sems, 0

    def copy(self, source, target):
        self.used += 1
        return pltpu.make_async_copy(source, target, self.sems.at[self.used - 1])

    def start(self, source, target):
        copy = self.copy(source, target)
        copy.start()
        return copy


def wait_all(copies):
    for copy in copies:
        copy.wait()


def head_mask(width, head_dim):
    rows = lax.broadcasted_iota(jnp.int32, (width, width), 0) // head_dim
    cols = lax.broadcasted_iota(jnp.int32, (width, width), 1) // head_dim
    return (rows == cols).astype(BF)


def head_sum(values, mask):
    high = values.astype(BF)
    rest = (values - high.astype(F32)).astype(BF)
    return dot_nn(high, mask) + dot_nn(rest, mask)


def head_gain(gains, start, width):
    section = gains.shape[1]
    row, first = (2, start) if start < section else (3, start - section)
    return gains[row : row + 1, first : first + width]


def model_gain(gains, row):
    return jnp.concatenate([gains[row : row + 1, :], gains[row + 1 : row + 2, :]], axis=1)


def key_lanes(shape, head_dim):
    return lax.broadcasted_iota(jnp.int32, shape, 1) % (2 * head_dim) < head_dim


def partner(values, head_dim):
    half = head_dim // 2
    width = values.shape[-1]
    lane = lax.broadcasted_iota(jnp.int32, values.shape, 1)
    after = pltpu.roll(values, width - half, 1)
    before = pltpu.roll(values, half, 1)
    return jnp.where(lane % head_dim < half, after, before)


class Links:
    def __init__(self, send_sems, recv_sems):
        self.sems, self.used, self.started = (send_sems, recv_sems), 0, []

    def reserve(self, count):
        self.used += count
        return self.used - count

    def copy(self, source, target, device, at=None):
        at = self.reserve(1) if at is None else at
        return pltpu.make_async_remote_copy(
            src_ref=source,
            dst_ref=target,
            send_sem=self.sems[0].at[at],
            recv_sem=self.sems[1].at[at],
            device_id=device,
            device_id_type=pl.DeviceIdType.MESH,
        )

    def plan(self, source, target, device):
        self.started.append(self.copy(source, target, device))
        return self.started[-1]

    def start(self, source, target, device):
        copy = self.plan(source, target, device)
        copy.start()
        return copy

    def wait_sends(self):
        for copy in self.started:
            copy.wait_send()


def enter(me, z, nz, plane):
    barrier = pltpu.get_barrier_semaphore()
    peers = [{"seq": z ^ j} for j in range(1, nz)]
    if plane:
        peers += [{"fsdp": me ^ bit} for bit in (1, 2, 4)]
    for peer in peers:
        pl.semaphore_signal(barrier, inc=1, device_id=peer, device_id_type=pl.DeviceIdType.MESH)
    pl.semaphore_wait(barrier, len(peers))


class Gather:
    def __init__(self, links, me, own, whole, x_first, stride=None, base=0):
        self.links, self.me, self.own, self.whole = links, me, own, whole
        self.rows = own.shape[0]
        self.stride, self.base = self.rows if stride is None else stride, base
        near, other = (2, 4) if x_first else (4, 2)
        self.first, self.second = self.pass_on(0, near), self.pass_on(0, other)
        self.far = self.pass_on(near, other)
        self.to_core = [self.pass_on(b, 1) for b in (0, near, other, near + other)]

    def block(self, b):
        return self.whole.at[pl.ds(pl.multiple_of((self.me ^ b) * self.stride + self.base, 16), self.rows)]

    def pass_on(self, b, bit):
        source = self.own if b == 0 else self.block(b)
        return self.links.plan(source, self.block(b), {"fsdp": self.me ^ bit})

    def begin(self):
        for copy in (self.first, self.second, self.to_core[0]):
            copy.start()

    def forward_first(self):
        self.first.wait_recv()
        self.far.start()
        self.to_core[1].start()

    def forward_second(self):
        self.second.wait_recv()
        self.to_core[2].start()

    def forward_far(self):
        self.far.wait_recv()
        self.to_core[3].start()

    def end(self):
        for copy in self.to_core:
            copy.wait_recv()


def begin(gathers):
    for gather in gathers:
        gather.begin()


def forward_first(gathers):
    for gather in gathers:
        gather.forward_first()
    for gather in gathers:
        gather.forward_second()


def forward_far(gathers):
    for gather in gathers:
        gather.forward_far()


def end(gathers):
    for gather in gathers:
        gather.end()


def rotation(position_ref, freq_ref, head_dim):
    tokens = position_ref.shape[1]
    at = jnp.broadcast_to(position_ref[...].astype(F32), (8, tokens)).T[:, 0:1]
    angles = at * freq_ref[...]
    lane = lax.broadcasted_iota(jnp.int32, (1, 128), 1)
    return jnp.cos(angles), jnp.sin(angles) * jnp.where(lane % head_dim < head_dim // 2, -1.0, 1.0)


def forward_kernel(dims, x_ref, dy_ref, position_ref, freq_ref, *refs):
    nz, plane, head_dim, widths, rows, width, groups = dims
    n_in = 11 if plane else 6
    given, refs = refs[:n_in], refs[n_in:]
    gains_ref, tables_ref, gain_grad_ref, delta_ref = refs[:4]
    heads_hbm, log_hbm, output_hbm, middle_grad_hbm, middle_low_hbm, grad_low_hbm = refs[4:10]
    refs = refs[10:]
    proj_hbm, normed_t_hbm, mixed_t_hbm, normed_two_hbm, hidden_hbm, gate_grad_hbm, up_grad_hbm, dy_hbm = refs[:8]
    refs = refs[8:]
    if plane:
        first_hbm, second_hbm, gate_hbm, up_hbm, down_hbm = refs[:5]
        refs = refs[5:]
    else:
        gate_hbm, up_hbm, down_hbm = given[3:]
    w_first, w_second, w_out, normed, transposed, proj, qkv, queries, keys, values, full, mix, mixed = refs[:13]
    heads_ref, log_ref, output_slot, low_slot, grad_low, refs = *refs[13:18], refs[:13] + refs[18:]
    w_gate, w_up, w_down, middle, total, back, hidden_slot, gate_slot, up_slot = refs[13:22]
    local_sems, weight_sems, slot_sems, send_sems, recv_sems, slot_sends, block_recvs = refs[22:29]
    own_slots = refs[29:]
    z, me = lax.axis_index("seq"), lax.axis_index("fsdp")
    model = w_second.shape[0]
    hidden_cols = gate_hbm.shape[1]
    tokens = x_ref.shape[0]
    enter(me, z, nz, plane)
    links = Links(send_sems, recv_sems)
    local = []
    to_core = []
    core = lax.rem(me, 2) if plane else 0
    place = pl.ds(pl.multiple_of(core * tokens, tokens), tokens)
    sibling = {"fsdp": me ^ 1}

    def copy_here(source, target):
        copy = pltpu.make_async_copy(source, target, local_sems.at[len(local)])
        copy.start()
        local.append(copy)
        return copy

    def share(source, target):
        copy_here(source, target)
        if plane:
            to_core.append(links.start(source, target, sibling))

    part_cols = nz * sum(widths)
    section = nz * widths[0]
    parts = qkv.shape[1] // part_cols
    if plane:
        own_q, own_k, own_v, own_out, own_gate, own_up, own_down = given[:7]
        own_first, own_second, own_keys, own_values = own_slots[3:]
        packing = [copy_here(own_k, own_keys), copy_here(own_v, own_values)]
        for at in range(nz * parts):
            to = pl.ds(at % parts * section + at // parts * widths[0], widths[0])
            source = own_q.at[:, pl.ds(at * widths[0], widths[0])]
            packing.append(copy_here(source, own_first.at[pl.ds(0, own_q.shape[0]), to]))
        lane = lax.broadcasted_iota(jnp.int32, (8, section), 1)
        head_rows = []
        for gain, period in zip(given[7:9], (head_dim, 2 * head_dim)):
            size = gain.shape[1]
            row = jnp.zeros((1, section), F32)
            for i in range(size):
                row = jnp.where(lane[:1] % period == me * size + i, gain[:, i : i + 1].astype(F32), row)
            head_rows.append(row)
        model_rows = []
        for gain in given[9:]:
            size = gain.shape[1]
            tiled = jnp.concatenate([gain[...].astype(F32)] * (section // size), axis=1)
            for row in range(2):
                model_rows.append(jnp.where((row * section + lane[:1]) // size == me, tiled, 0.0))
        rows_16 = model_rows[:2] + head_rows + model_rows[2:] + [jnp.zeros((10, section), F32)]
        own_first[own_q.shape[0] :, :section] = jnp.concatenate(rows_16, axis=0).astype(BF)
        wait_all(packing)
        pieces = []
        for b in range(parts):
            for at in range(nz):
                cols = slice((at * parts + b) * head_dim, (at * parts + b + 1) * head_dim)
                pieces += [own_keys[:, cols], own_values[:, cols]]
        own_second[...] = jnp.concatenate(pieces, axis=1)
        half = own_down.shape[0] // 2
        shard = own_q.shape[0]
        stride = own_first.shape[0]

        def columns(pairs, start, size):
            cols = pl.ds(start, size)
            return [Gather(links, me, own.at[:, cols], whole.at[:, cols], x_first) for own, whole, x_first in pairs]

        by_part = [columns(((own_first, w_first, True), (own_second, w_second, False)), 0, section)]
        later = pl.ds(section, section)
        by_part.append(
            [
                Gather(links, me, own_first.at[pl.ds(0, shard), later], w_first.at[:, later], True, stride),
                Gather(links, me, own_second.at[:, later], w_second.at[:, later], False),
            ]
        )
        out_half = own_out.shape[1] // 2
        to = pl.ds(2 * section, out_half)
        outward = [
            Gather(links, me, own_out.at[:, pl.ds(0, out_half)], w_first.at[:, to], True, stride),
            Gather(links, me, own_out.at[:, pl.ds(out_half, out_half)], w_second.at[:, to], False),
        ]
        begin(by_part[0])
        here = [copy_here(gather.own, gather.block(0)) for gather in by_part[0] + by_part[1] + outward]
        own_places = [(own_gate, own_slots[0], gate_hbm), (own_up, own_slots[1], up_hbm), (own_down, own_slots[2], down_hbm)]
        own_loads = [copy_here(own, slot) for own, slot, _ in own_places]
        down = [
            Gather(links, me, own_down.at[pl.ds(side * half, half)], down_hbm, side == 0, 2 * half, side * half)
            for side in range(2)
        ]
        wide, at = [], 0
        for count in groups:
            wide.append(columns(((own_gate, gate_hbm, True), (own_up, up_hbm, False)), at * width, count * width))
            at += count
    else:
        here = [copy_here(given[0], w_first), copy_here(given[1], w_second)]
    x = x_ref[...].astype(F32)
    unit = x * row_norm(x)
    cosine, sine = rotation(position_ref, freq_ref, head_dim)
    tables_ref[0] = cosine
    tables_ref[1] = sine
    if plane:
        forward_first(by_part[0])
        begin(by_part[1])
        begin(outward)
        forward_far(by_part[0])
        end(by_part[0])
        wait_all(here + own_loads)
        own_stores = []
        for own, slot, whole in own_places:
            count = own.shape[0]
            own_stores.append(copy_here(slot, whole.at[pl.ds(pl.multiple_of(me * count, count), count)]))
        gains = sum(w_first[s * stride + shard : (s + 1) * stride, :section].astype(F32) for s in range(8))
    else:
        stride = shard = model
        wait_all(here)
        gains = given[2][:, :section].astype(F32)
    gains_ref[...] = gains
    normed[...] = (unit * model_gain(gains, 0)).astype(BF)
    chunk = 256
    mask = head_mask(chunk, head_dim)
    cos = jnp.concatenate([tables_ref[0]] * (chunk // 128), axis=1)
    sin = jnp.concatenate([tables_ref[1]] * (chunk // 128), axis=1)
    out_half = model // 2
    my_rows = pl.ds(pl.multiple_of(z * tokens, tokens), tokens)
    arrivals = []
    for b in range(parts):
        if plane and b == 1:
            forward_first(by_part[1])
            begin(down)
            forward_far(by_part[1])
            end(by_part[1])
        for start in range(0, part_cols, chunk):
            at = b * section + start % section
            cols = slice(at, at + chunk)
            if start >= section:
                weight = w_second[:, cols]
            elif stride == shard:
                weight = w_first[:, cols]
            else:
                weight = jnp.concatenate([w_first[s * stride : s * stride + shard, cols] for s in range(8)], axis=0)
            got = dot_nn(normed[...], weight)
            here_cols = slice(b * part_cols + start, b * part_cols + start + chunk)
            proj[:, here_cols] = got
            scale = lax.rsqrt(head_sum(got * got, mask) * (1.0 / head_dim) + EPSILON)
            head = got * scale * head_gain(gains_ref, start, chunk)
            head = head * cos + partner(head, head_dim) * sin
            if start >= nz * widths[0]:
                head = jnp.where(key_lanes(head.shape, head_dim), head, got)
            qkv[:, here_cols] = head.astype(BF)
        arrived = []
        for j in range(nz):
            owner = z ^ j
            for i, size in enumerate(widths):
                base = b * part_cols + i * nz * widths[0]
                source = qkv.at[:, pl.ds(pl.multiple_of(base + owner * size, size), size)]
                target = heads_ref.at[my_rows, pl.ds(b * sum(widths) + i * widths[0], size)]
                if j == 0:
                    arrived.append(copy_here(source, target))
                else:
                    arrived.append(links.start(source, target, {"seq": owner}))
        arrivals.append(arrived)
    copy_here(proj, proj_hbm)
    transposed[0] = normed[...].T
    share(transposed.at[0], normed_t_hbm.at[:, place])
    share(dy_ref, dy_hbm.at[place])
    if plane:
        forward_first(outward)
        begin(wide[0])
    group, seq_len, _ = queries.shape
    factor = head_dim**-0.5 * LOG2E
    arriving, here_mixed = [], []
    for b in range(parts):
        for i, copy in enumerate(arrivals[b]):
            if i < 2:
                copy.wait()
            else:
                copy.wait_recv()
        first = b * sum(widths)
        for g in range(group):
            queries[g] = heads_ref[:, first + g * head_dim : first + (g + 1) * head_dim]
        first += widths[0]
        keys[...] = heads_ref[:, first : first + head_dim]
        values[...] = heads_ref[:, first + head_dim : first + 2 * head_dim]
        for r in range(seq_len // rows):
            span = slice(r * rows, (r + 1) * rows)
            reach = (r + 1) * rows

            def one_head(g, _):
                scores = dot_nt(queries[g, span], keys[:reach]) * factor
                row = lax.broadcasted_iota(jnp.int32, scores.shape, 0) + r * rows
                col = lax.broadcasted_iota(jnp.int32, scores.shape, 1)
                probs = jnp.exp2(jnp.where(row >= col, scores, -1e30))
                total = jnp.sum(probs, axis=1, keepdims=True)
                full[g, span] = (dot_nn(probs.astype(BF), values[:reach]) * (1.0 / total)).astype(BF)
                log_ref[b * group + g, :, span] = jnp.broadcast_to(jnp.log2(total), (rows, 128)).T[0:8]
                return 0

            lax.fori_loop(0, group, one_head, 0)
        mix[b] = jnp.concatenate([full[g] for g in range(group)], axis=1)
        for j in range(nz):
            owner = z ^ j
            source = mix.at[b, pl.ds(pl.multiple_of(owner * tokens, tokens), tokens)]
            to = pl.multiple_of((z * parts + b) * widths[0], widths[0])
            target = mixed.at[:, pl.ds(to, widths[0])]
            if j == 0:
                here_mixed.append(copy_here(source, target))
            else:
                arriving.append(links.start(source, target, {"seq": owner}))
        if plane and b == 0:
            forward_far(outward)
            forward_first(down)
            end(outward)
            for s in range(8):
                copy_here(w_first.at[pl.ds(s * stride, shard)], first_hbm.at[pl.ds(s * shard, shard)])
            copy_here(w_second, second_hbm)
            forward_first(wide[0])
            begin(wide[1])
            begin(wide[2])
        if b == 0:
            out_copies = [
                copy_here(
                    w_first.at[pl.ds(s * stride, shard), pl.ds(2 * section, out_half)],
                    w_out.at[pl.ds(s * shard, shard), pl.ds(0, out_half)],
                )
                for s in range(model // shard)
            ]
            out_copies.append(copy_here(w_second.at[:, pl.ds(2 * section, out_half)], w_out.at[:, pl.ds(out_half, out_half)]))
    if plane:
        forward_far(down)
        end(down)
        wait_all(own_stores)
        forward_far(wide[0])
    for copy in arriving:
        copy.wait_recv()
    wait_all(here_mixed + out_copies)

    copy_here(heads_ref, heads_hbm)
    copy_here(log_ref, log_hbm)

    gain = model_gain(gains_ref, 4)
    middle[...] = dot_nn(mixed[...], w_out[...])

    def by_rows(work):
        step = 128

        def body(i, _):
            work(pl.ds(pl.multiple_of(i * step, step), step))
            return 0

        lax.fori_loop(0, tokens // step, body, 0)

    def middle_norm(rows):
        middle_rows = x_ref[rows, :].astype(F32) + middle[rows, :]
        middle[rows, :] = middle_rows
        total[rows, :] = middle_rows
        normed[rows, :] = (middle_rows * row_norm(middle_rows) * gain).astype(BF)
        back[rows, :] = jnp.zeros(middle_rows.shape, F32)

    by_rows(middle_norm)
    normed_rows = normed[...]
    transposed[1] = normed_rows.T
    share(transposed.at[1], normed_two_hbm.at[:, place])
    transposed[2] = mixed[...].T
    share(transposed.at[2], mixed_t_hbm.at[:, place])

    def slot_places(f):
        here = pl.ds(pl.multiple_of(f * width, width), width)
        return (
            (hidden_slot, hidden_hbm.at[here, place]),
            (gate_slot, gate_grad_hbm.at[place, here]),
            (up_slot, up_grad_hbm.at[place, here]),
        )

    def slot_copies(slot, f):
        return [
            pltpu.make_async_copy(s.at[slot], target, slot_sems.at[slot, i]) for i, (s, target) in enumerate(slot_places(f))
        ]

    def slot_links(slot, f):
        if not plane:
            return []
        return [
            pltpu.make_async_remote_copy(
                src_ref=s.at[slot],
                dst_ref=target,
                send_sem=slot_sends.at[slot, i],
                recv_sem=block_recvs.at[f, i],
                device_id=sibling,
                device_id_type=pl.DeviceIdType.MESH,
            )
            for i, (s, target) in enumerate(slot_places(f))
        ]

    def wait_slot(slot, f):
        wait_all(slot_copies(slot, f))
        for copy in slot_links(slot, f):
            copy.wait_send()

    def weight_copies(f):
        here = pl.ds(pl.multiple_of(f * width, width), width)
        slot = lax.rem(f, 2)
        pairs = ((gate_hbm.at[:, here], w_gate), (up_hbm.at[:, here], w_up), (down_hbm.at[here], w_down))
        return [
            pltpu.make_async_copy(source, target.at[slot], weight_sems.at[slot, i])
            for i, (source, target) in enumerate(pairs)
        ]

    blocks = hidden_cols // width
    firsts = [sum(groups[:g]) for g in range(len(groups))]

    ahead = [0, 0, firsts[min(1, len(firsts) - 1)] - 1] + firsts[2:]

    def arrive(f):
        for g in range(1, len(groups)):

            @pl.when(f == ahead[g])
            def _():
                forward_first(wide[g])
                if g + 2 < len(groups):
                    begin(wide[g + 2])

        for g in range(len(groups)):

            @pl.when(f == firsts[g])
            def _():
                if g:
                    forward_far(wide[g])
                end(wide[g])

    def one_block(f, _):
        slot = lax.rem(f, 2)
        if plane:
            arrive(f)

        def fetch(block):
            for copy in weight_copies(block):
                copy.start()

        in_first = f < (firsts[1] if plane else blocks)
        pl.when((f == 0) | ~in_first)(lambda: fetch(f))
        pl.when(in_first & (f + 1 < (firsts[1] if plane else blocks)))(lambda: fetch(f + 1))
        wait_all(weight_copies(f))

        @pl.when(f >= 2)
        def _():
            wait_slot(slot, f - 2)

        gate = dot_nn(normed[...], w_gate[slot])
        up = dot_nn(normed[...], w_up[slot])
        hidden_grad = dot_nt(dy_ref[...], w_down[slot])
        s = 1.0 / (1.0 + jnp.exp(-gate))
        silu = gate * s
        hidden = (silu * up).astype(BF)
        gate_grad = (hidden_grad * up * (s * (1.0 + gate * (1.0 - s)))).astype(BF)
        up_grad = (hidden_grad * silu).astype(BF)
        hidden_slot[slot] = hidden.T
        gate_slot[slot] = gate_grad
        up_slot[slot] = up_grad
        for copy in slot_copies(slot, f) + slot_links(slot, f):
            copy.start()
        total[...] = total[...] + dot_nn(hidden, w_down[slot])
        back[...] = back[...] + (dot_nt(gate_grad, w_gate[slot]) + dot_nt(up_grad, w_up[slot]))
        return 0

    lax.fori_loop(0, blocks, one_block, 0)
    gain_grad_ref[...] = jnp.zeros(gain_grad_ref.shape, F32)

    def middle_back(rows):
        part, gain_sum = norm_back(middle[rows, :], gain, back[rows, :])
        gain_grad_ref[...] = gain_grad_ref[...] + gain_sum
        middle_grad = dy_ref[rows, :].astype(F32) + part
        back[rows, :] = middle_grad
        low_slot[rows, :] = middle_grad.astype(BF)

    by_rows(middle_back)
    copy_here(low_slot, middle_low_hbm)
    grad_low[...] = dot_nt(low_slot[...], w_out[...]).astype(BF)
    copy_here(grad_low, grad_low_hbm)
    copy_here(back, middle_grad_hbm)
    heads = mixed.shape[1] // head_dim // nz
    row = lax.broadcasted_iota(jnp.int32, (8 * nz, mixed.shape[1]), 0)
    col = lax.broadcasted_iota(jnp.int32, (8 * nz, mixed.shape[1]), 1)
    pick = ((col // head_dim == (row // 8) * heads + row % 8) & (row % 8 < heads)).astype(BF)

    def head_products(rows):
        product = grad_low[rows, :].astype(F32) * mixed[rows, :].astype(F32)
        high = product.astype(BF)
        delta_ref[:, rows] = dot_nt(pick, high) + dot_nt(pick, (product - high.astype(F32)).astype(BF))
        output_slot[rows, :] = total[rows, :].astype(BF)

    by_rows(head_products)
    copy_here(output_slot, output_hbm)
    for f in (blocks - 2, blocks - 1):
        wait_slot(f % 2, f)
    if plane:
        for f in range(blocks):
            for copy in slot_links(f % 2, f):
                copy.wait_recv()
        for copy in to_core:
            copy.wait_recv()
        links.wait_sends()
    done = here + out_copies + here_mixed + [c for arrived in arrivals for c in arrived[:2]]
    if plane:
        done += packing + own_loads + own_stores
    for copy in local:
        if not any(copy is other for other in done):
            copy.wait()


def both_cores(links, copy_here, me, source, target, axis):
    size = source.shape[axis]
    here = pl.ds(pl.multiple_of(lax.rem(me, 2) * size, size), size)
    place = target.at[here] if axis == 0 else target.at[:, here]
    copy_here(source, place)
    return links.start(source, place, {"fsdp": me ^ 1})


def attend_back(dims, b, heads_ref, grads_ref, log_ref, delta_ref, packed, scratch):
    rows, chunk = dims
    queries, keys, values, grad, q_grad, k_grad, v_grad = scratch
    group, seq_len, head_dim = queries.shape
    first = b * (group + 2) * head_dim
    for g in range(group):
        queries[g] = heads_ref[:, first + g * head_dim : first + (g + 1) * head_dim]
        at = (b * group + g) * head_dim
        grad[g] = grads_ref[:, at : at + head_dim]
        q_grad[g] = jnp.zeros((seq_len, head_dim), F32)
    first += group * head_dim
    keys[...] = heads_ref[:, first : first + head_dim]
    values[...] = heads_ref[:, first + head_dim : first + 2 * head_dim]
    factor = head_dim**-0.5
    scale = factor * LOG2E
    for at in range(seq_len // rows):
        span = slice(at * rows, (at + 1) * rows)
        key, value = keys[span], values[span]
        k_grad[span] = jnp.zeros((rows, head_dim), F32)
        v_grad[span] = jnp.zeros((rows, head_dim), F32)

        def one_head(g, _):
            key_total = jnp.zeros((rows, head_dim), F32)
            value_total = jnp.zeros((rows, head_dim), F32)
            for start in range(at * rows, seq_len, chunk):
                part = slice(start, min(start + chunk, seq_len))
                query, out_grad = queries[g, part], grad[g, part]
                scores = dot_nt(key, query) * scale - log_ref[b * group + g, 0:1, part]
                if start == at * rows:
                    key_at = lax.broadcasted_iota(jnp.int32, scores.shape, 0) + at * rows
                    query_at = lax.broadcasted_iota(jnp.int32, scores.shape, 1) + start
                    scores = jnp.where(query_at >= key_at, scores, -1e30)
                probs = jnp.exp2(scores)
                prob_grad = dot_nt(value, out_grad)
                score_grad = (probs * (prob_grad - delta_ref[b * group + g, 0:1, part])).astype(BF)
                value_total = value_total + dot_nn(probs.astype(BF), out_grad)
                key_total = key_total + dot_nn(score_grad, query)
                q_grad[g, part] = q_grad[g, part] + dot_tn(score_grad, key)
            k_grad[span] = k_grad[span] + key_total
            v_grad[span] = v_grad[span] + value_total
            return 0

        lax.fori_loop(0, group, one_head, 0)
        parts = [(q_grad[g, span] * factor).astype(BF) for g in range(group)]
        parts += [(k_grad[span] * factor).astype(BF), v_grad[span].astype(BF)]
        packed[span] = jnp.concatenate(parts, axis=1)
        yield at


def attend_back_scratch(group, seq_len, head_dim):
    many = lambda kind: pltpu.VMEM((group, seq_len, head_dim), kind)
    one = lambda kind: pltpu.VMEM((seq_len, head_dim), kind)
    return [many(BF), one(BF), one(BF), many(BF), many(F32), one(F32), one(F32)]


def attend_back_kernel(dims, heads_ref, grads_ref, log_ref, delta_ref, packed, *scratch):
    for b in range(packed.shape[0]):
        for _ in attend_back(dims, b, heads_ref, grads_ref, log_ref, delta_ref, packed.at[b], scratch):
            pass


def norm_back(rows, gain, gradient):
    q = row_norm(rows)
    n = rows * q
    u = gradient * gain
    return q * (u - n * jnp.mean(u * n, axis=-1, keepdims=True)), jnp.sum(gradient * n, axis=0, keepdims=True)


def weight_grad_kernel(left_ref, right_ref, out_ref):
    out_ref[...] = dot_nn(left_ref[...], right_ref[...]).astype(BF)


def weight_grad(left, right, width=256):
    rows, tokens = left.shape
    cols = right.shape[1]
    return call(
        weight_grad_kernel,
        shape_of((rows, cols), BF),
        [pl.BlockSpec((rows, tokens), lambda n: (0, 0)), pl.BlockSpec((tokens, width), lambda n: (0, n))],
        pl.BlockSpec((rows, width), lambda n: (0, n)),
        [],
        2 * rows * tokens * cols,
        2 * (rows * tokens + tokens * cols + rows * cols),
        grid=(cols // width,),
    )(left, right)


def project_back(dims, b, gains_ref, tables_ref, proj_ref, qkv, head_gain_grad_ref):
    nz, head_dim, widths = dims
    part_cols = nz * sum(widths)
    width = 256
    mask = head_mask(width, head_dim)
    cos = jnp.concatenate([tables_ref[0]] * (width // 128), axis=1)
    sin = jnp.concatenate([tables_ref[1]] * (width // 128), axis=1)
    for start in range(0, part_cols, width):
        cols = slice(b * part_cols + start, b * part_cols + start + width)
        rotated = qkv[:, cols].astype(F32)
        gradient = rotated * cos - partner(rotated, head_dim) * sin
        proj = proj_ref[:, start : start + width]
        scale = lax.rsqrt(head_sum(proj * proj, mask) * (1.0 / head_dim) + EPSILON)
        n = proj * scale
        u = gradient * head_gain(gains_ref, start, width)
        head_gain_grad_ref[:, cols] = jnp.sum(gradient * n, axis=0, keepdims=True)
        back = scale * (u - n * (head_sum(u * n, mask) * (1.0 / head_dim)))
        if start >= nz * widths[0]:
            back = jnp.where(key_lanes(back.shape, head_dim), back, rotated)
        qkv[:, cols] = back.astype(BF)


def input_back(x_ref, middle_grad_ref, gains_ref, qkv, weight, input_grad_ref, gain_grad_ref):
    normed_grad = dot_nt(qkv[...], weight[...])
    part, gain_sum = norm_back(x_ref[...].astype(F32), model_gain(gains_ref, 0), normed_grad)
    gain_grad_ref[...] = gain_sum
    input_grad_ref[...] = (middle_grad_ref[...] + part).astype(BF)


def post_kernel(dims, x_ref, middle_grad_ref, gains_ref, tables_ref, proj_ref, grads_ref, weight_ref, *refs):
    input_grad_ref, qkv, gain_grad_ref, head_gain_grad_ref = refs
    nz, _, widths = dims
    qkv[...] = grads_ref[...]
    for b in range(qkv.shape[1] // (nz * sum(widths))):
        part_cols = nz * sum(widths)
        part = proj_ref.at[:, pl.ds(b * part_cols, part_cols)]
        project_back(dims, b, gains_ref, tables_ref, part, qkv, head_gain_grad_ref)
    input_back(x_ref, middle_grad_ref, gains_ref, qkv, weight_ref, input_grad_ref, gain_grad_ref)


class Reduce:
    def __init__(self, links, fetch, me, z, x_first, away, kept, first, second, inward, across, out):
        self.links, self.fetch, self.me, self.z = links, fetch, me, z
        self.away, self.kept, self.out = away, kept, out
        self.bits = (2, 4) if x_first else (4, 2)
        order = (1, 3, 0, 2) if x_first else (2, 3, 0, 1)
        self.slots = {r: (away if i < 2 else kept, i % 2) for i, r in enumerate(order)}
        self.arrived, self.second, self.inward, self.across = first, second, inward, across
        self.outer, self.inner = (z == 0) | (z == 3), (z == 1) | (z == 2)
        self.one = links.copy(away, first, {"fsdp": me ^ self.bits[0]})
        self.two = links.copy(kept.at[1], second, {"fsdp": me ^ self.bits[1]})
        self.three = links.copy(kept.at[0], inward, {"seq": z ^ 1})
        self.four = links.copy(kept.at[0], across, {"seq": z ^ 3})
        self.five = links.copy(kept.at[1], out, {"seq": z ^ 1})
        self.here = fetch.copy(kept.at[1], out)
        self.load = fetch.copy(first, away)

    def put(self, r, cols, values):
        ref, i = self.slots[r]
        ref[i, :, cols] = values

    def rows_of(self):
        rows = self.kept.shape[1]
        step = 32 if rows % 32 == 0 else 16
        return rows // step, step

    def by_rows(self, work):
        count, step = self.rows_of()

        def body(i, _):
            work(pl.ds(pl.multiple_of(i * step, step), step))
            return 0

        lax.fori_loop(0, count, body, 0)

    def begin(self):
        self.one.start()

    def load_one(self):
        self.one.wait_recv()
        self.one.wait_send()
        self.load.start()

    def fold_one(self):
        self.load.wait()

        def work(rows):
            for i in range(2):
                self.kept[i, rows] = self.kept[i, rows] + self.away[i, rows]

        self.by_rows(work)
        self.two.start()

    def fold_two(self):
        self.two.wait_recv()

        def work(rows):
            self.kept[0, rows] = self.kept[0, rows] + self.second[rows]

        self.by_rows(work)

        @pl.when(self.outer)
        def _():
            self.three.start()

    def fold_three(self):
        @pl.when(self.inner)
        def _():
            self.three.wait_recv()

            def work(rows):
                self.kept[0, rows] = self.kept[0, rows] + self.inward[rows]

            self.by_rows(work)
            self.four.start()

    def fold_four(self):
        self.two.wait_send()

        @pl.when(self.inner)
        def _():
            self.four.wait_recv()

            def work(rows):
                self.kept[1, rows] = self.kept[0, rows] + self.across[rows]

            self.by_rows(work)
            self.five.start()
            self.here.start()

    def end(self):
        @pl.when(self.inner)
        def _():
            self.four.wait_send()
            self.five.wait_send()
            self.here.wait()

        @pl.when(self.outer)
        def _():
            self.three.wait_send()
            self.five.wait_recv()


def each(reduces, step):
    if step == "fold_one":
        each(reduces, "load_one")
    for reduce in reduces:
        getattr(reduce, step)()


class Total:
    def __init__(self, links, me, z, sums, arrived):
        self.sums, self.arrived = sums, arrived
        peers = [{"fsdp": me ^ 1}, {"fsdp": me ^ 2}, {"fsdp": me ^ 4}, {"seq": z ^ 1}, {"seq": z ^ 2}]
        self.copies = [links.copy(sums.at[i], arrived.at[i], peer) for i, peer in enumerate(peers)]

    def begin(self, at):
        self.copies[at].start()

    def fold(self, at):
        self.copies[at].wait_recv()
        self.sums[at + 1] = self.sums[at] + self.arrived[at]

    def end(self):
        for copy in self.copies:
            copy.wait_send()


EARLY = (
    ("wide4", "matmul"), ("wide4", "begin"), ("down1", "matmul"), ("down0", "matmul"), ("wide0", "matmul"),
    ("out", "matmul"), ("wide1", "matmul"), ("out", "begin"), ("wide4", "fold_one"), ("down0", "begin"),
    ("wide0", "begin"),
)
MIDDLE = (
    ("keys", 0, 0), ("keys", 0, 1), ("keys", 0, 2), ("wide4", "fold_two"), ("keys", 0, 3), ("keys", 0, 4),
    ("keys", 0, 5), ("keys", 0, 6), ("keys", 0, 7), ("wide5", "matmul"), ("wide2", "matmul"), ("wide4", "fold_three"),
    ("down0", "fold_one"), ("wide1", "begin"), ("keys", 1, 0), ("wide5", "begin"), ("keys", 1, 1),
    ("down0", "fold_two"), ("out", "fold_one"), ("keys", 1, 2), ("keys", 1, 3), ("keys", 1, 4), ("keys", 1, 5),
    ("keys", 1, 6), ("keys", 1, 7), ("wide0", "fold_one"), ("wide5", "fold_one"), ("wide3", "matmul"),
    ("wide1", "fold_one"), ("project", 0), ("out", "fold_two"), ("wide4", "fold_four"), ("down1", "begin"),
    ("wide2", "begin"), ("wide5", "fold_two"), ("down0", "fold_three"), ("wide1", "fold_two"), ("project", 1),
)
LATE = (
    ("out", "fold_three"), ("input",), ("down0", "fold_four"), ("wide5", "fold_three"), ("down1", "fold_one"),
    ("wide1", "fold_three"), ("out", "fold_four"), ("wide0", "fold_two"), ("total", 0), ("wide2", "fold_one"),
    ("wide5", "fold_four"), ("down1", "fold_two"), ("total", 1), ("last1", "matmul"), ("wide3", "begin"),
    ("wide0", "fold_three"), ("wide1", "fold_four"), ("total", 2), ("wide2", "fold_two"), ("down1", "fold_three"),
    ("last0", "matmul"), ("wide0", "fold_four"), ("wide3", "fold_one"), ("wide2", "fold_three"), ("last1", "begin"),
    ("down1", "fold_four"), ("last0", "begin"), ("wide3", "fold_two"), ("wide3", "fold_three"), ("last1", "fold_one"),
    ("wide2", "fold_four"), ("last0", "fold_one"), ("total", 3), ("last1", "fold_two"), ("wide3", "fold_four"),
    ("last0", "fold_two"), ("last0", "fold_three"), ("last1", "fold_three"), ("total", 4), ("last0", "fold_four"),
    ("last1", "fold_four"),
)


GATES = ("gate0x", "gate1y", "gate2x", "gate3y", "gate4x", "gate5y")
UPS = ("up0x", "up1y", "up2x", "up3y", "up4x", "up5y")


def backward_kernel(dims, gains_hbm, tables_hbm, delta_own, feed_gain_hbm, heads_hbm, log_hbm, grad_low, low_own, *refs):
    nz, head_dim, widths, attend_dims, names = dims
    given, refs = refs[:12], refs[12:]
    x_hbm, middle_grad_hbm, proj_hbm, hidden_hbm, dy_hbm, normed_two_hbm = given[:6]
    gate_hbm, up_hbm, mixed_hbm, normed_hbm, first_hbm, second_hbm = given[6:]
    input_grad_ref, totals_ref = refs[:2]
    n = len(names)
    finals, refs = dict(zip(names, refs[2 : 2 + n])), refs[2 + n :]
    firsts, refs = dict(zip(names, refs[:n])), refs[n:]
    low_hbm, refs = refs[0], refs[1:]
    aways, refs = dict(zip(names, refs[:n])), refs[n:]
    kepts, refs = dict(zip(names, refs[:n])), refs[n:]
    seconds, refs = dict(zip(names, refs[:n])), refs[n:]
    inwards, refs = dict(zip(names, refs[:n])), refs[n:]
    acrosses, refs = dict(zip(names, refs[:n])), refs[n:]
    grads, delta, qkv, other_qkv, normed_two, normed, sums, sum_arrived, gain_grad, head_gain_grad = refs[:10]
    heads_ref, log_ref, low_ref, gains_ref, tables_ref, feed_gain_ref, sems, send_sems, recv_sems = refs[10:]
    z, me = lax.axis_index("seq"), lax.axis_index("fsdp")
    chip, core = lax.div(me, 2), lax.rem(me, 2)
    links, fetch = Links(send_sems, recv_sems), Fetch(sems)
    enter(me, z, nz, True)
    low_load = fetch.start(low_own, low_ref)
    head_loads = [
        fetch.start(source, target)
        for source, target in (
            (heads_hbm, heads_ref),
            (log_hbm, log_ref),
            (gains_hbm, gains_ref),
            (tables_hbm, tables_ref),
            (feed_gain_hbm, feed_gain_ref),
        )
    ]
    tokens = grad_low.shape[0]
    seq_len, block_cols = heads_ref.shape
    part_cols = nz * sum(widths)
    parts = qkv.shape[1] // part_cols
    late = []

    def copy_here(source, target):
        copy = fetch.start(source, target)
        late.append(copy)
        return copy

    my_rows = pl.ds(pl.multiple_of(z * tokens, tokens), tokens)
    arrivals = []
    for b in range(parts):
        arrived = []
        for j in range(nz):
            owner = z ^ j
            from_cols = pl.ds(pl.multiple_of((owner * parts + b) * widths[0], widths[0]), widths[0])
            pairs = [(grad_low.at[:, from_cols], grads.at[my_rows, pl.ds(b * widths[0], widths[0])])]
            if b == 0:
                pairs.append((delta_own.at[pl.ds(pl.multiple_of(owner * 8, 8), 8)], delta.at[:, my_rows]))
            for source, target in pairs:
                if j == 0:
                    copy_here(source, target)
                else:
                    arrived.append(links.start(source, target, {"seq": owner}))
        arrivals.append(arrived)
    low_load.wait()
    low_arrival = both_cores(links, copy_here, me, low_ref, low_hbm, 0)
    reduces = {}
    for name in names:
        reduces[name] = Reduce(
            links, fetch, me, z, name[-1] == "x", aways[name], kepts[name], firsts[name], seconds[name], inwards[name],
            acrosses[name], finals[name],
        )
    down = [[reduces[f"down{c}{way}"] for way in "xy"] for c in range(2)]
    wide_names = GATES + UPS
    wide = [[reduces[name] for name in wide_names[i : i + 2]] for i in range(0, len(wide_names), 2)]
    out = [reduces["outx"], reduces["outy"]]
    last = [[reduces[f"last{b}{way}"] for way in "xy"] for b in range(parts)]
    total = Total(links, me, z, sums, sum_arrived)
    part_cols_of = lambda b: pl.ds(b * part_cols, part_cols)
    qkv_links = [
        links.copy(qkv.at[:, part_cols_of(b)], other_qkv.at[:, part_cols_of(b)], {"fsdp": me ^ 1}) for b in range(parts)
    ]
    chips = 4
    step = 256
    half = down[0][0].kept.shape[1]
    shard = wide[0][0].kept.shape[1]
    both = 2 * tokens
    model = low_ref.shape[1]

    def my_blocks(source, target, rows):
        copies = []
        for r in range(chips):
            owner = (chip ^ r) * 2 + core
            copies.append(fetch.start(source.at[pl.ds(pl.multiple_of(owner * rows, rows), rows)], target.at[pl.ds(r * rows, rows)]))
        return copies

    def wide_grads(places, left, right):
        width = right.shape[2]
        chunks = [
            (source, (first + c) * width, unit, c * width)
            for source, first, unit in places
            for c in range(unit.kept.shape[2] // width)
        ]
        count = len(chunks)
        loads = [
            fetch.copy(source.at[:, pl.ds(at, width)], right.at[c % 2]) for c, (source, at, _, _) in enumerate(chunks)
        ]
        loads[0].start()
        loads[1].start()
        for c in range(count):
            loads[c].wait()
            _, _, unit, base = chunks[c]

            def block(k, _):
                here = pl.ds(pl.multiple_of(k * step, step), step)
                to = pl.ds(pl.multiple_of(base + k * step, step), step)
                got = dot_nn(left[...], right[c % 2, :, here]).astype(BF)
                for r in range(chips):
                    unit.put(r, to, got[r * shard : (r + 1) * shard])
                return 0

            lax.fori_loop(0, width // step, block, 0)
            if c + 2 < count:
                loads[c + 2].start()

    ready = {"two": my_blocks(normed_two_hbm, normed_two, shard), "one": my_blocks(normed_hbm, normed, shard)}

    def ready_now(name):
        wait_all(ready.pop(name, ()))

    wide_part = wide[0][0].kept.shape[2]

    def wide_matmul(i, right):
        ready_now("two")
        places = []
        for at in (2 * i, 2 * i + 1):
            source = gate_hbm if at < len(GATES) else up_hbm
            places.append((source, at % len(GATES), wide[i][at % 2]))
        wide_grads(places, normed_two, right)

    def out_matmul(mixed, low):
        cols = out[0].kept.shape[2]
        for start in range(0, low.shape[1], step):
            got = dot_nn(mixed[...], low[:, start : start + step]).astype(BF)
            for r in range(chips):
                out[start // cols].put(r, slice(start % cols, start % cols + step), got[r * shard : (r + 1) * shard])

    def down_matmul(c, hidden, dy):
        cols = down[0][0].kept.shape[2]

        def block(i, _):
            to = pl.ds(pl.multiple_of(i * step, step), step)
            here = pl.ds(pl.multiple_of(c * cols + i * step, step), step)
            for r in range(chips):
                got = dot_nn(hidden[2 * r * half : 2 * (r + 1) * half], dy[:, here]).astype(BF)
                for side in range(2):
                    down[c][side].put(r, to, got[side * half : (side + 1) * half])
            return 0

        lax.fori_loop(0, cols // step, block, 0)

    def last_matmul(b):
        ready_now("one")
        mine = normed[:, pl.ds(pl.multiple_of(core * tokens, tokens), tokens)]
        theirs = normed[:, pl.ds(pl.multiple_of((1 - core) * tokens, tokens), tokens)]
        qkv_links[b].wait()
        cols = last[b][0].kept.shape[2]
        for start in range(0, part_cols, step):
            here = slice(b * part_cols + start, b * part_cols + start + step)
            got = (dot_nn(mine, qkv[:, here]) + dot_nn(theirs, other_qkv[:, here])).astype(BF)
            for r in range(chips):
                last[b][start // cols].put(r, slice(start % cols, start % cols + step), got[r * shard : (r + 1) * shard])

    pairs = {"out": out}
    pairs |= {f"down{c}": down[c] for c in range(2)}
    pairs |= {f"wide{i}": pair for i, pair in enumerate(wide)}
    pairs |= {f"last{b}": last[b] for b in range(parts)}
    right_shape = pltpu.VMEM((2, both, wide_part), BF)

    def sum_step(name, what):
        if what != "matmul":
            each(pairs[name], what)
        elif name[:4] == "last":
            last_matmul(int(name[4]))
        else:
            pl.run_scoped(functools.partial(wide_matmul, int(name[4])), right_shape)

    def early(hidden, dy, right, mixed, low):
        ready["down"] = my_blocks(hidden_hbm, hidden, 2 * half) + [fetch.start(dy_hbm, dy)]
        ready["out"] = my_blocks(mixed_hbm, mixed, shard)
        for name, what in EARLY:
            if what != "matmul":
                each(pairs[name], what)
            elif name[:4] == "down":
                ready_now("down")
                down_matmul(int(name[4]), hidden, dy)
            elif name == "out":
                low_arrival.wait_recv()
                wait_all(late)
                del late[:]
                ready["out"].append(fetch.start(low_hbm, low))
                ready_now("out")
                out_matmul(mixed, low)
            else:
                wide_matmul(int(name[4]), right)

    pl.run_scoped(
        early,
        pltpu.VMEM((2 * chips * half, both), BF),
        pltpu.VMEM((both, model), BF),
        right_shape,
        pltpu.VMEM((chips * shard, both), BF),
        pltpu.VMEM((both, model), BF),
    )

    wait_all(head_loads)
    heads = log_ref.shape[0]
    group = heads // parts
    first_back = links.reserve(parts * 2 * nz)
    own_back = fetch.used
    fetch.used += parts * 2

    def back_copies(b, packed):
        for i, width in enumerate(widths):
            base = b * part_cols + i * nz * widths[0]
            target = qkv.at[:, pl.ds(pl.multiple_of(base + z * width, width), width)]
            for j in range(nz):
                owner = z ^ j
                rows = pl.ds(pl.multiple_of(owner * tokens, tokens), tokens)
                source = packed.at[b, rows, pl.ds(i * widths[0], width)]
                if j == 0:
                    yield j, pltpu.make_async_copy(source, target, sems.at[own_back + 2 * b + i])
                else:
                    yield j, links.copy(source, target, {"seq": owner}, at=first_back + (2 * b + i) * nz + j)

    def middle(packed, delta_rows, *scratch):
        blocks = {}

        def keys_step(b, at):
            if at == 0:
                for copy in arrivals[b]:
                    copy.wait_recv()
                if b == 0:
                    for h in range(heads):
                        delta_rows[h] = jnp.broadcast_to(delta[h : h + 1], (8, seq_len))
                blocks[b] = attend_back(attend_dims, b, heads_ref, grads, log_ref, delta_rows, packed.at[b], scratch)
            next(blocks[b])
            if (at + 1) * attend_dims[0] == seq_len:
                for _, copy in back_copies(b, packed):
                    copy.start()

        def project_step(b):
            for j, copy in back_copies(b, packed):
                if j == 0:
                    copy.wait()
                else:
                    copy.wait_recv()

            def inner(proj):
                fetch.start(proj_hbm.at[:, part_cols_of(b)], proj).wait()
                project_back((nz, head_dim, widths), b, gains_ref, tables_ref, proj, qkv, head_gain_grad)

            pl.run_scoped(inner, pltpu.VMEM((tokens, part_cols), F32))
            qkv_links[b].start()

        for token in MIDDLE:
            if token[0] == "keys":
                keys_step(*token[1:])
            elif token[0] == "project":
                project_step(token[1])
            else:
                sum_step(*token)
        for b in range(parts):
            for j, copy in back_copies(b, packed):
                if j:
                    copy.wait_send()

    pl.run_scoped(
        middle,
        pltpu.VMEM((parts, seq_len, sum(widths)), BF),
        pltpu.VMEM((heads, 8, seq_len), F32),
        *attend_back_scratch(group, seq_len, head_dim),
    )

    def input_step(weight, x, middle_grad):
        copies = [fetch.start(x_hbm, x), fetch.start(middle_grad_hbm, middle_grad)]
        section = part_cols // 2
        for b in range(parts):
            for i, source in enumerate((first_hbm, second_hbm)):
                to = pl.ds(b * part_cols + i * section, section)
                copies.append(fetch.start(source.at[:, pl.ds(b * section, section)], weight.at[:, to]))
        wait_all(copies)
        input_back(x, middle_grad, gains_ref, qkv, weight, input_grad_ref, gain_grad)
        row = jnp.concatenate([gain_grad[...], head_gain_grad[...], feed_gain_ref[...]], axis=1)
        sums[0] = jnp.broadcast_to(row, sums.shape[1:])

    for token in LATE:
        if token[0] == "input":
            pl.run_scoped(
                input_step,
                pltpu.VMEM((model, parts * part_cols), BF),
                pltpu.VMEM((tokens, model), BF),
                pltpu.VMEM((tokens, model), F32),
            )
            total.begin(0)
        elif token[0] == "total":
            total.fold(token[1])
            if token[1] < 4:
                total.begin(token[1] + 1)
        else:
            sum_step(*token)
    totals_ref[...] = sums[5]
    total.end()
    for name in names:
        reduces[name].end()
    links.wait_sends()


def finish_kernel(dims, *refs):
    names, nz, head_dim = dims
    n = len(names)
    totals_hbm, refs = refs[0], refs[1:]
    output_in, input_grad_in = refs[:2]
    shards, refs = dict(zip(names, refs[2 : 2 + n])), refs[2 + n :]
    output, input_grad, q_out, k_out, v_out, out_out, gate_out, up_out, down_out = refs[:9]
    gain_outs, refs = refs[9:13], refs[13:]
    slots, refs = dict(zip(names, refs[:n])), refs[n:]
    passing, q, k, v, out, gate, up, down, totals_ref, load_sems, store_sems = refs
    fetch, store = Fetch(load_sems), Fetch(store_sems)
    order = GATES + UPS + tuple(name for name in names if name not in GATES + UPS)
    loads = {name: fetch.start(shards[name], slots[name]) for name in order}
    totals_load = fetch.start(totals_hbm, totals_ref)
    moves = [fetch.start(source, passing.at[i]) for i, source in enumerate((output_in, input_grad_in))]
    stores = []

    def place(name, target, row, col):
        loads[name].wait()
        rows, cols = slots[name].shape
        target[row : row + rows, col : col + cols] = slots[name][...].astype(F32)

    cols = slots["gate0x"].shape[1]
    for target, done, pieces in (
        (gate, gate_out, GATES),
        (up, up_out, UPS),
    ):
        for i, name in enumerate(pieces):
            place(name, target, 0, i * cols)
        stores.append(store.start(target, done))
    rows, cols = slots["down0x"].shape
    for c in range(2):
        for i, way in enumerate("xy"):
            place(f"down{c}{way}", down, i * rows, c * cols)
    stores.append(store.start(down, down_out))
    cols = slots["outx"].shape[1]
    for i, way in enumerate("xy"):
        place("out" + way, out, 0, i * cols)
    stores.append(store.start(out, out_out))
    parts = 2
    width = q.shape[1] // (nz * parts)
    for b in range(parts):
        loads[f"last{b}x"].wait()
        for i in range(nz):
            to = (i * parts + b) * width
            q[:, to : to + width] = slots[f"last{b}x"][:, i * width : (i + 1) * width].astype(F32)
    stores.append(store.start(q, q_out))
    for b in range(parts):
        loads[f"last{b}y"].wait()
    for i, target in enumerate((k, v)):
        pieces = [
            slots[f"last{b}y"][:, (2 * at + i) * head_dim : (2 * at + i + 1) * head_dim]
            for at in range(nz)
            for b in range(parts)
        ]
        target[...] = jnp.concatenate(pieces, axis=1).astype(F32)
    stores += [store.start(k, k_out), store.start(v, v_out)]
    totals_load.wait()
    me = lax.axis_index("fsdp")
    model = down_out.shape[1]
    section = model // 2
    share = gain_outs[0].shape[1]
    for ref, base in ((gain_outs[0], 0), (gain_outs[3], model + 4 * section)):
        ref[...] = totals_ref[0:1, pl.ds(pl.multiple_of(base + me * share, share), share)]
    for ref, shift, period in ((gain_outs[1], 0, head_dim), (gain_outs[2], section, 2 * head_dim)):
        share = ref.shape[1]
        row = sum(
            totals_ref[0:1, model + part * 2 * section + shift + at : model + part * 2 * section + shift + at + head_dim]
            for part in range(2)
            for at in range(0, section, period)
        )
        row = jnp.concatenate([row] * (128 // head_dim), axis=1)
        ref[...] = pltpu.roll(row, 128 - me * share, 1)[:, :share]
    for i, target in enumerate((output, input_grad)):
        moves[i].wait()
        stores.append(store.start(passing.at[i], target))
    wait_all(stores)


def add(a, b):
    return (a.astype(F32) + b.astype(F32)).astype(a.dtype)


def sum_line(values):
    size = lax.axis_size("seq")
    if size != 4:
        return lax.psum(values, "seq")
    z = lax.axis_index("seq")
    inner = add(values, lax.ppermute(values, "seq", [(0, 1), (3, 2)]))
    total = add(inner, lax.ppermute(inner, "seq", [(1, 2), (2, 1)]))
    outer = lax.ppermute(total, "seq", [(1, 0), (2, 3)])
    return jnp.where((z == 1) | (z == 2), total, outer)


def per_device(
    inputs,
    positions,
    cotangent,
    query_weight,
    key_weight,
    value_weight,
    out_weight,
    attention_gain,
    query_gain,
    key_gain,
    feedforward_gain,
    gate_weight,
    up_weight,
    down_weight,
):
    seqs, tokens, model = inputs.shape
    assert seqs == 1
    fsdp, nz = lax.axis_size("fsdp"), lax.axis_size("seq")
    me, z = lax.axis_index("fsdp"), lax.axis_index("seq")
    plane = fsdp == 8 and nz == 4
    both = 2 * tokens if plane else tokens
    x = inputs.reshape(tokens, model)
    dy = cotangent.reshape(tokens, model)
    head_dim = query_gain.shape[0] * fsdp
    q_cols, k_cols, v_cols = query_weight.shape[1], key_weight.shape[1], value_weight.shape[1]
    heads, kv_heads = q_cols // head_dim // nz, k_cols // head_dim // nz
    hidden_cols = gate_weight.shape[1]
    seq_len = tokens * nz

    group, parts = heads // kv_heads, kv_heads
    widths = (group * head_dim, 2 * head_dim)
    part_cols = nz * sum(widths)
    assert parts == 2

    section = nz * widths[0]
    assert model == 2 * section and part_cols == 2 * section
    half_out = model // 2
    first_cols = 2 * section + half_out
    if plane:
        given = [query_weight, key_weight, value_weight, out_weight, gate_weight, up_weight, down_weight]
        given += [query_gain[None], key_gain[None], attention_gain[None], feedforward_gain[None]]
    else:
        shard_rows = query_weight.shape[0]
        q = query_weight.reshape(shard_rows, nz, parts, widths[0])
        kv = jnp.stack([v.reshape(shard_rows, nz, parts, head_dim) for v in (key_weight, value_weight)], axis=3)
        first, second = (
            jnp.concatenate([v[:, :, b].reshape(shard_rows, section) for b in range(parts)] + [rest], axis=1)
            for v, rest in ((q, out_weight[:, :half_out]), (kv, out_weight[:, half_out:]))
        )
        gather = functools.partial(lax.all_gather, axis_name="fsdp", axis=0, tiled=True)
        first_full, second_full, gate_full = gather(first), gather(second), gather(gate_weight)
        up_full, down_full = gather(up_weight), gather(down_weight)
        key_row = jnp.concatenate([gather(key_gain), jnp.zeros((head_dim,), BF)])
        gain_rows = [gather(attention_gain).reshape(2, section), jnp.tile(gather(query_gain), nz * group)[None]]
        gain_rows += [jnp.tile(key_row, nz)[None], gather(feedforward_gain).reshape(2, section)]
        gain_rows = jnp.concatenate(gain_rows + [jnp.zeros((10, section), BF)]).astype(F32)
        given = [first_full, second_full, gain_rows, gate_full, up_full, down_full]

    half_dim = head_dim // 2
    freqs = ROPE_BASE ** (-(jnp.arange(128) % half_dim).astype(F32) / half_dim)

    rows_model = lambda kind: shape_of((tokens, model), kind)
    width = 512
    blocks = hidden_cols // width
    sizes = (blocks - 6,) + (1,) * 6
    block_cols = parts * sum(widths)
    mixed_cols = heads * head_dim
    attend_flops = 2 * heads * seq_len * seq_len * head_dim
    proj_flops = 2 * tokens * model * parts * part_cols
    outs = [
        shape_of((16, section), F32),
        shape_of((2, tokens, 128), F32),
        shape_of((1, model), F32),
        shape_of((8 * nz, tokens), F32),
        shape_of((seq_len, block_cols), BF),
        shape_of((heads, 8, seq_len), F32),
        rows_model(BF),
        rows_model(F32),
        rows_model(BF),
        shape_of((tokens, q_cols), BF),
        shape_of((tokens, parts * part_cols), F32),
        shape_of((model, both), BF),
        shape_of((q_cols, both), BF),
        shape_of((model, both), BF),
        shape_of((hidden_cols, both), BF),
        shape_of((both, hidden_cols), BF),
        shape_of((both, hidden_cols), BF),
        shape_of((both, model), BF),
    ]
    n_links = parts * 3 * (nz - 1)
    first_rows = model
    if plane:
        outs += [shape_of((model, first_cols), BF)] * 2
        outs += [shape_of((model, hidden_cols), BF)] * 2 + [shape_of((hidden_cols, model), BF)]
        n_links += (8 + 2 * len(sizes)) * 7 + 4
        first_rows += 8 * 16
    many = lambda count: pltpu.VMEM((count, seq_len, head_dim), BF)
    one = pltpu.VMEM((seq_len, head_dim), BF)
    got = call(
        functools.partial(forward_kernel, (nz, plane, head_dim, widths, min(256, seq_len), width, sizes)),
        outs,
        [VMEM] * 4 + ([ANY] * 7 + [VMEM] * 4 if plane else [ANY] * 2 + [VMEM] + [ANY] * 3),
        [VMEM] * 4 + [ANY] * (len(outs) - 4),
        [
            pltpu.VMEM((first_rows, first_cols), BF),
            pltpu.VMEM((model, first_cols), BF),
            pltpu.VMEM((q_cols, model), BF),
            pltpu.VMEM((tokens, model), BF),
            pltpu.VMEM((3, model, tokens), BF),
            pltpu.VMEM((tokens, parts * part_cols), F32),
            pltpu.VMEM((tokens, parts * part_cols), BF),
            many(group),
            one,
            one,
            many(group),
            pltpu.VMEM((parts, seq_len, widths[0]), BF),
            pltpu.VMEM((tokens, q_cols), BF),
            pltpu.VMEM((seq_len, block_cols), BF),
            pltpu.VMEM((heads, 8, seq_len), F32),
            pltpu.VMEM((tokens, model), BF),
            pltpu.VMEM((tokens, model), BF),
            pltpu.VMEM((tokens, q_cols), BF),
            pltpu.VMEM((2, model, width), BF),
            pltpu.VMEM((2, model, width), BF),
            pltpu.VMEM((2, width, model), BF),
            pltpu.VMEM((tokens, model), F32),
            pltpu.VMEM((tokens, model), F32),
            pltpu.VMEM((tokens, model), F32),
            pltpu.VMEM((2, width, tokens), BF),
            pltpu.VMEM((2, tokens, width), BF),
            pltpu.VMEM((2, tokens, width), BF),
            pltpu.SemaphoreType.DMA((64,)),
            pltpu.SemaphoreType.DMA((2, 3)),
            pltpu.SemaphoreType.DMA((2, 3)),
            pltpu.SemaphoreType.DMA((n_links,)),
            pltpu.SemaphoreType.DMA((n_links,)),
            pltpu.SemaphoreType.DMA((2, 3)),
            pltpu.SemaphoreType.DMA((blocks, 3)),
        ]
        + [pltpu.VMEM(w.shape, BF) for w in (gate_weight, up_weight, down_weight) if plane]
        + [pltpu.VMEM((query_weight.shape[0] + extra, 2 * section), BF) for extra in (16, 0) if plane]
        + [pltpu.VMEM(key_weight.shape, BF) for _ in range(2) if plane],
        proj_flops + 4 * attend_flops + 12 * tokens * model * hidden_cols,
        100 * 2**20,
        collective=1,
    )(x, dy, positions.reshape(1, tokens), freqs[None], *given)
    gains, tables, feed_gain_part, delta = got[:4]
    head_rows, logs, output, middle_grad, middle_low, mixed_grad = got[4:10]
    proj, normed_t, mixed_t, normed_two_t, hidden_t, gate_grad, up_grad, dy_both = got[10:18]
    if plane:
        first_full, second_full = got[18:20]

    attend_dims = (min(256, seq_len), min(1024, seq_len))
    attend_scratch = attend_back_scratch(group, seq_len, head_dim)
    if plane:
        down_rows, down_cols = down_weight.shape
        blocks = {f"down{c}{way}": (down_rows // 2, down_cols // 2) for c in range(2) for way in "xy"}
        blocks |= {name: (gate_weight.shape[0], hidden_cols // len(GATES)) for name in GATES + UPS}
        blocks |= {"out" + way: (out_weight.shape[0], model // 2) for way in "xy"}
        blocks |= {f"last{b}{way}": (query_weight.shape[0], part_cols // 2) for b in range(parts) for way in "xy"}
        names = tuple(blocks)
        pairs = [(2,) + shape for shape in blocks.values()]
        total_cols = model + parts * part_cols + model
        n_links = 3 * (nz - 1) + 2 * parts * nz + 1 + parts + 5 * len(names) + 5
        n_copies = 80 + 2 * len(names)
        got = call(
            functools.partial(backward_kernel, (nz, head_dim, widths, attend_dims, names)),
            [rows_model(BF), shape_of((8, total_cols), F32)]
            + [shape_of(shape, BF) for shape in blocks.values()]
            + [shape_of(shape, BF) for shape in pairs]
            + [shape_of((both, model), BF)],
            [ANY] * 20,
            [VMEM] * 2 + [ANY] * (2 * len(names) + 1),
            [pltpu.VMEM(shape, BF) for shape in pairs] * 2
            + [pltpu.VMEM(shape, BF) for shape in blocks.values()] * 3
            + [
                pltpu.VMEM((seq_len, mixed_cols), BF),
                pltpu.VMEM((8, seq_len), F32),
                pltpu.VMEM((tokens, parts * part_cols), BF),
                pltpu.VMEM((tokens, parts * part_cols), BF),
                pltpu.VMEM((model // 2, both), BF),
                pltpu.VMEM((model // 2, both), BF),
                pltpu.VMEM((6, 8, total_cols), F32),
                pltpu.VMEM((5, 8, total_cols), F32),
                pltpu.VMEM((1, model), F32),
                pltpu.VMEM((1, parts * part_cols), F32),
                pltpu.VMEM((seq_len, block_cols), BF),
                pltpu.VMEM((heads, 8, seq_len), F32),
                pltpu.VMEM((tokens, model), BF),
                pltpu.VMEM(gains.shape, F32),
                pltpu.VMEM(tables.shape, F32),
                pltpu.VMEM((1, model), F32),
                pltpu.SemaphoreType.DMA((n_copies,)),
                pltpu.SemaphoreType.DMA((n_links,)),
                pltpu.SemaphoreType.DMA((n_links,)),
            ],
            10 * attend_flops + 2 * tokens * model * (3 * hidden_cols + 3 * (q_cols + k_cols)),
            100 * 2**20,
            collective=3,
        )(
            gains, tables, delta, feed_gain_part, head_rows, logs, mixed_grad, middle_low, x, middle_grad, proj,
            hidden_t, dy_both, normed_two_t, gate_grad, up_grad, mixed_t, normed_t, first_full, second_full,
        )
        input_grad, totals = got[:2]
        slots = [pltpu.VMEM(shape, BF) for shape in blocks.values()]
        out_shapes = [w.shape for w in (query_weight, key_weight, value_weight, out_weight, gate_weight, up_weight, down_weight)]
        gain_shapes = [(1, g.shape[0]) for g in (attention_gain, query_gain, key_gain, feedforward_gain)]
        *results, attention_total, q_total, k_total, feed_total = call(
            functools.partial(finish_kernel, (names, nz, head_dim)),
            [rows_model(BF)] * 2 + [shape_of(shape, F32) for shape in out_shapes + gain_shapes],
            [ANY] * (3 + len(names)),
            [ANY] * 9 + [VMEM] * 4,
            slots
            + [pltpu.VMEM((2, tokens, model), BF)]
            + [pltpu.VMEM(shape, F32) for shape in out_shapes]
            + [pltpu.VMEM(totals.shape, F32)]
            + [pltpu.SemaphoreType.DMA((3 + len(names),)), pltpu.SemaphoreType.DMA((9,))],
            0,
            18 * 2**20,
        )(totals, output, input_grad, *got[2 : 2 + len(names)])
        output, input_grad, q_shard, k_shard, v_shard, out_shard, gate_shard, up_shard, down_shard = results
    else:
        exchange = functools.partial(lax.all_to_all, axis_name="seq", tiled=True)
        grad_rows = exchange(mixed_grad, split_axis=1, concat_axis=0)
        delta_rows = exchange(delta, split_axis=0, concat_axis=1)
        packed = call(
            functools.partial(attend_back_kernel, attend_dims),
            shape_of((parts, seq_len, sum(widths)), BF),
            [VMEM] * 4,
            VMEM,
            attend_scratch,
            10 * attend_flops,
            20 * 2**20,
        )(head_rows, grad_rows, logs, jnp.broadcast_to(delta_rows[:heads, None], (heads, 8, seq_len)))
        pieces = [piece for b in range(parts) for piece in (packed[b, :, : widths[0]], packed[b, :, widths[0] :])]
        qkv = jnp.concatenate([exchange(piece, split_axis=0, concat_axis=1) for piece in pieces], axis=1)
        weight = jnp.concatenate(
            [full[:, b * section : (b + 1) * section] for b in range(parts) for full in (first_full, second_full)], axis=1
        )
        input_grad, qkv, gain_part, head_gain_part = call(
            functools.partial(post_kernel, (nz, head_dim, widths)),
            [
                rows_model(BF),
                shape_of((tokens, parts * part_cols), BF),
                shape_of((1, model), F32),
                shape_of((1, parts * part_cols), F32),
            ],
            [VMEM] * 7,
            [VMEM] * 4,
            [],
            proj_flops,
            14 * 2**20,
        )(x, middle_grad, gains, tables, proj, qkv, weight)

        def reduce(left, right):
            return sum_line(lax.psum_scatter(weight_grad(left, right), "fsdp", scatter_dimension=0, tiled=True)).astype(F32)

        down_shard, gate_shard = reduce(hidden_t, dy), reduce(normed_two_t, gate_grad)
        up_shard, out_shard = reduce(normed_two_t, up_grad), reduce(mixed_t, middle_low)
        qkv_shard = reduce(normed_t, qkv)
        part_shards = [
            (qkv_shard[:, b * part_cols : b * part_cols + section], qkv_shard[:, b * part_cols + section : (b + 1) * part_cols])
            for b in range(parts)
        ]
        q_shard = jnp.stack([q.reshape(shard_rows, nz, widths[0]) for q, _ in part_shards], axis=2).reshape(shard_rows, -1)
        kv_shard = jnp.stack([kv.reshape(shard_rows, nz, 2, head_dim) for _, kv in part_shards], axis=2)
        k_shard, v_shard = (kv_shard[:, :, :, i].reshape(shard_rows, -1) for i in range(2))
        totals = lax.psum(jnp.concatenate([gain_part, head_gain_part, feed_gain_part], axis=1)[0], ("seq", "fsdp"))

        head_totals = totals[model : model + parts * part_cols].reshape(parts, part_cols)
        q_total = head_totals[:, : nz * widths[0]].reshape(-1, head_dim).sum(axis=0)
        k_total = head_totals[:, nz * widths[0] :].reshape(-1, 2, head_dim)[:, 0].sum(axis=0)

        def share(values):
            own = jnp.arange(fsdp)[:, None] == me
            return jnp.sum(jnp.where(own, values.reshape(fsdp, -1), 0.0), axis=0)
        attention_total, feed_total = share(totals[:model]), share(totals[model + parts * part_cols :])
        q_total, k_total = share(q_total), share(k_total)

    return (
        output.reshape(inputs.shape),
        input_grad.reshape(inputs.shape),
        q_shard,
        k_shard,
        v_shard,
        out_shard,
        attention_total.reshape(-1),
        q_total.reshape(-1),
        k_total.reshape(-1),
        feed_total.reshape(-1),
        gate_shard,
        up_shard,
        down_shard,
    )


def solution(mesh):
    tokens, rows, row = P("fsdp", "seq", None), P("fsdp", None), P("fsdp")
    in_specs = (tokens, P("fsdp", "seq"), tokens) + (rows,) * 4 + (row,) * 4 + (rows,) * 3
    out_specs = (tokens, tokens) + (rows,) * 4 + (row,) * 4 + (rows,) * 3
    return jax.shard_map(per_device, mesh=mesh, in_specs=in_specs, out_specs=out_specs, check_vma=False)
```

```python
import functools

import jax
import jax.numpy as jnp
from jax import lax
from jax.experimental import pallas as pl
from jax.experimental.pallas import tpu as pltpu
from jax.sharding import PartitionSpec as P

EPSILON = 1e-05
ROPE_BASE = 1000000.0
LOG2E = 1.4426950408889634
BF = jnp.bfloat16
F32 = jnp.float32
VMEM = pl.BlockSpec(memory_space=pltpu.VMEM)
SMEM = pl.BlockSpec(memory_space=pltpu.SMEM)
ANY = pl.BlockSpec(memory_space=pl.ANY)
VMEM_BYTES = 62 * 2**20


def dot_nn(a, b):
    return lax.dot_general(a, b, (((1,), (0,)), ((), ())), preferred_element_type=F32)


def dot_nt(a, b):
    return lax.dot_general(a, b, (((1,), (1,)), ((), ())), preferred_element_type=F32)


def dot_tn(a, b):
    return lax.dot_general(a, b, (((0,), (0,)), ((), ())), preferred_element_type=F32)


def shape_of(shape, dtype):
    return jax.ShapeDtypeStruct(shape, dtype)


def call(kernel, outs, in_specs, out_specs, scratch, flops, moved, collective=None, **more):
    params = {} if collective is None else {"collective_id": collective, "has_side_effects": True}
    return pl.pallas_call(
        kernel,
        out_shape=outs,
        in_specs=in_specs,
        out_specs=out_specs,
        scratch_shapes=scratch,
        compiler_params=pltpu.CompilerParams(vmem_limit_bytes=VMEM_BYTES, **params),
        cost_estimate=pl.CostEstimate(flops=flops, bytes_accessed=moved, transcendentals=0),
        **more,
    )


def row_norm(values):
    return lax.rsqrt(jnp.mean(values * values, axis=-1, keepdims=True) + EPSILON)


class Fetch:
    def __init__(self, sems):
        self.sems, self.used = sems, 0

    def copy(self, source, target):
        self.used += 1
        return pltpu.make_async_copy(source, target, self.sems.at[self.used - 1])

    def start(self, source, target):
        copy = self.copy(source, target)
        copy.start()
        return copy


def wait_all(copies):
    for copy in copies:
        copy.wait()


def head_mask(width, head_dim):
    rows = lax.broadcasted_iota(jnp.int32, (width, width), 0) // head_dim
    cols = lax.broadcasted_iota(jnp.int32, (width, width), 1) // head_dim
    return (rows == cols).astype(BF)


def head_sum(values, mask):
    high = values.astype(BF)
    rest = (values - high.astype(F32)).astype(BF)
    return dot_nn(high, mask) + dot_nn(rest, mask)


def head_gain(gains, start, width):
    section = gains.shape[1]
    row, first = (2, start) if start < section else (3, start - section)
    return gains[row : row + 1, first : first + width]


def model_gain(gains, row):
    return jnp.concatenate([gains[row : row + 1, :], gains[row + 1 : row + 2, :]], axis=1)


def key_lanes(shape, head_dim):
    return lax.broadcasted_iota(jnp.int32, shape, 1) % (2 * head_dim) < head_dim


def partner(values, head_dim):
    half = head_dim // 2
    width = values.shape[-1]
    lane = lax.broadcasted_iota(jnp.int32, values.shape, 1)
    after = pltpu.roll(values, width - half, 1)
    before = pltpu.roll(values, half, 1)
    return jnp.where(lane % head_dim < half, after, before)


class Links:
    def __init__(self, send_sems, recv_sems):
        self.sems, self.used, self.started = (send_sems, recv_sems), 0, []

    def reserve(self, count):
        self.used += count
        return self.used - count

    def copy(self, source, target, device, at=None):
        at = self.reserve(1) if at is None else at
        return pltpu.make_async_remote_copy(
            src_ref=source,
            dst_ref=target,
            send_sem=self.sems[0].at[at],
            recv_sem=self.sems[1].at[at],
            device_id=device,
            device_id_type=pl.DeviceIdType.MESH,
        )

    def plan(self, source, target, device):
        self.started.append(self.copy(source, target, device))
        return self.started[-1]

    def start(self, source, target, device):
        copy = self.plan(source, target, device)
        copy.start()
        return copy

    def wait_sends(self):
        for copy in self.started:
            copy.wait_send()


def enter(me, z, nz, plane):
    barrier = pltpu.get_barrier_semaphore()
    peers = [{"seq": z ^ j} for j in range(1, nz)]
    if plane:
        peers += [{"fsdp": me ^ bit} for bit in (1, 2, 4)]
    for peer in peers:
        pl.semaphore_signal(barrier, inc=1, device_id=peer, device_id_type=pl.DeviceIdType.MESH)
    pl.semaphore_wait(barrier, len(peers))


class Gather:
    def __init__(self, links, me, own, whole, x_first, stride=None, base=0):
        self.links, self.me, self.own, self.whole = links, me, own, whole
        self.rows = own.shape[0]
        self.stride, self.base = self.rows if stride is None else stride, base
        near, other = (2, 4) if x_first else (4, 2)
        self.first, self.second = self.pass_on(0, near), self.pass_on(0, other)
        self.far = self.pass_on(near, other)
        self.to_core = [self.pass_on(b, 1) for b in (0, near, other, near + other)]

    def block(self, b):
        return self.whole.at[pl.ds(pl.multiple_of((self.me ^ b) * self.stride + self.base, 16), self.rows)]

    def pass_on(self, b, bit):
        source = self.own if b == 0 else self.block(b)
        return self.links.plan(source, self.block(b), {"fsdp": self.me ^ bit})

    def begin(self):
        for copy in (self.first, self.second, self.to_core[0]):
            copy.start()

    def forward_first(self):
        self.first.wait_recv()
        self.far.start()
        self.to_core[1].start()

    def forward_second(self):
        self.second.wait_recv()
        self.to_core[2].start()

    def forward_far(self):
        self.far.wait_recv()
        self.to_core[3].start()

    def end(self):
        for copy in self.to_core:
            copy.wait_recv()


def begin(gathers):
    for gather in gathers:
        gather.begin()


def forward_first(gathers):
    for gather in gathers:
        gather.forward_first()
    for gather in gathers:
        gather.forward_second()


def forward_far(gathers):
    for gather in gathers:
        gather.forward_far()


def end(gathers):
    for gather in gathers:
        gather.end()


def rotation(position_ref, freq_ref, head_dim):
    tokens = position_ref.shape[1]
    at = jnp.broadcast_to(position_ref[...].astype(F32), (8, tokens)).T[:, 0:1]
    angles = at * freq_ref[...]
    lane = lax.broadcasted_iota(jnp.int32, (1, 128), 1)
    return jnp.cos(angles), jnp.sin(angles) * jnp.where(lane % head_dim < head_dim // 2, -1.0, 1.0)


def forward_kernel(dims, x_ref, dy_ref, position_ref, freq_ref, *refs):
    nz, plane, head_dim, widths, rows, width, groups = dims
    n_in = 11 if plane else 6
    given, refs = refs[:n_in], refs[n_in:]
    gains_ref, tables_ref, gain_grad_ref, delta_ref = refs[:4]
    heads_hbm, log_hbm, output_hbm, middle_grad_hbm, middle_low_hbm, grad_low_hbm = refs[4:10]
    refs = refs[10:]
    proj_hbm, normed_t_hbm, mixed_t_hbm, normed_two_hbm, hidden_hbm, gate_grad_hbm, up_grad_hbm, dy_hbm = refs[:8]
    refs = refs[8:]
    if plane:
        first_hbm, second_hbm, gate_hbm, up_hbm, down_hbm = refs[:5]
        refs = refs[5:]
    else:
        gate_hbm, up_hbm, down_hbm = given[3:]
    w_first, w_second, w_out, normed, transposed, proj, qkv, queries, keys, values, full, mix, mixed = refs[:13]
    heads_ref, log_ref, output_slot, low_slot, grad_low, refs = *refs[13:18], refs[:13] + refs[18:]
    w_gate, w_up, w_down, middle, total, back, hidden_slot, gate_slot, up_slot = refs[13:22]
    local_sems, weight_sems, slot_sems, send_sems, recv_sems, slot_sends, block_recvs = refs[22:29]
    own_slots = refs[29:]
    z, me = lax.axis_index("seq"), lax.axis_index("fsdp")
    model = w_second.shape[0]
    hidden_cols = gate_hbm.shape[1]
    tokens = x_ref.shape[0]
    enter(me, z, nz, plane)
    links = Links(send_sems, recv_sems)
    local = []
    to_core = []
    core = lax.rem(me, 2) if plane else 0
    place = pl.ds(pl.multiple_of(core * tokens, tokens), tokens)
    sibling = {"fsdp": me ^ 1}

    def copy_here(source, target):
        copy = pltpu.make_async_copy(source, target, local_sems.at[len(local)])
        copy.start()
        local.append(copy)
        return copy

    def share(source, target):
        copy_here(source, target)
        if plane:
            to_core.append(links.start(source, target, sibling))

    part_cols = nz * sum(widths)
    section = nz * widths[0]
    parts = qkv.shape[1] // part_cols
    if plane:
        own_q, own_k, own_v, own_out, own_gate, own_up, own_down = given[:7]
        own_first, own_second, own_keys, own_values = own_slots[3:]
        packing = [copy_here(own_k, own_keys), copy_here(own_v, own_values)]
        for at in range(nz * parts):
            to = pl.ds(at % parts * section + at // parts * widths[0], widths[0])
            source = own_q.at[:, pl.ds(at * widths[0], widths[0])]
            packing.append(copy_here(source, own_first.at[pl.ds(0, own_q.shape[0]), to]))
        lane = lax.broadcasted_iota(jnp.int32, (8, section), 1)
        head_rows = []
        for gain, period in zip(given[7:9], (head_dim, 2 * head_dim)):
            size = gain.shape[1]
            row = jnp.zeros((1, section), F32)
            for i in range(size):
                row = jnp.where(lane[:1] % period == me * size + i, gain[:, i : i + 1].astype(F32), row)
            head_rows.append(row)
        model_rows = []
        for gain in given[9:]:
            size = gain.shape[1]
            tiled = jnp.concatenate([gain[...].astype(F32)] * (section // size), axis=1)
            for row in range(2):
                model_rows.append(jnp.where((row * section + lane[:1]) // size == me, tiled, 0.0))
        rows_16 = model_rows[:2] + head_rows + model_rows[2:] + [jnp.zeros((10, section), F32)]
        own_first[own_q.shape[0] :, :section] = jnp.concatenate(rows_16, axis=0).astype(BF)
        wait_all(packing)
        pieces = []
        for b in range(parts):
            for at in range(nz):
                cols = slice((at * parts + b) * head_dim, (at * parts + b + 1) * head_dim)
                pieces += [own_keys[:, cols], own_values[:, cols]]
        own_second[...] = jnp.concatenate(pieces, axis=1)
        half = own_down.shape[0] // 2
        shard = own_q.shape[0]
        stride = own_first.shape[0]

        def columns(pairs, start, size):
            cols = pl.ds(start, size)
            return [Gather(links, me, own.at[:, cols], whole.at[:, cols], x_first) for own, whole, x_first in pairs]

        by_part = [columns(((own_first, w_first, True), (own_second, w_second, False)), 0, section)]
        later = pl.ds(section, section)
        by_part.append(
            [
                Gather(links, me, own_first.at[pl.ds(0, shard), later], w_first.at[:, later], True, stride),
                Gather(links, me, own_second.at[:, later], w_second.at[:, later], False),
            ]
        )
        out_half = own_out.shape[1] // 2
        to = pl.ds(2 * section, out_half)
        outward = [
            Gather(links, me, own_out.at[:, pl.ds(0, out_half)], w_first.at[:, to], True, stride),
            Gather(links, me, own_out.at[:, pl.ds(out_half, out_half)], w_second.at[:, to], False),
        ]
        begin(by_part[0])
        here = [copy_here(gather.own, gather.block(0)) for gather in by_part[0] + by_part[1] + outward]
        own_places = [(own_gate, own_slots[0], gate_hbm), (own_up, own_slots[1], up_hbm), (own_down, own_slots[2], down_hbm)]
        own_loads = [copy_here(own, slot) for own, slot, _ in own_places]
        down = [
            Gather(links, me, own_down.at[pl.ds(side * half, half)], down_hbm, side == 0, 2 * half, side * half)
            for side in range(2)
        ]
        wide, at = [], 0
        for count in groups:
            wide.append(columns(((own_gate, gate_hbm, True), (own_up, up_hbm, False)), at * width, count * width))
            at += count
    else:
        here = [copy_here(given[0], w_first), copy_here(given[1], w_second)]
    x = x_ref[...].astype(F32)
    unit = x * row_norm(x)
    cosine, sine = rotation(position_ref, freq_ref, head_dim)
    tables_ref[0] = cosine
    tables_ref[1] = sine
    if plane:
        forward_first(by_part[0])
        begin(by_part[1])
        begin(outward)
        forward_far(by_part[0])
        end(by_part[0])
        wait_all(here + own_loads)
        own_stores = []
        for own, slot, whole in own_places:
            count = own.shape[0]
            own_stores.append(copy_here(slot, whole.at[pl.ds(pl.multiple_of(me * count, count), count)]))
        gains = sum(w_first[s * stride + shard : (s + 1) * stride, :section].astype(F32) for s in range(8))
    else:
        stride = shard = model
        wait_all(here)
        gains = given[2][:, :section].astype(F32)
    gains_ref[...] = gains
    normed[...] = (unit * model_gain(gains, 0)).astype(BF)
    chunk = 256
    mask = head_mask(chunk, head_dim)
    cos = jnp.concatenate([tables_ref[0]] * (chunk // 128), axis=1)
    sin = jnp.concatenate([tables_ref[1]] * (chunk // 128), axis=1)
    out_half = model // 2
    my_rows = pl.ds(pl.multiple_of(z * tokens, tokens), tokens)
    arrivals = []
    for b in range(parts):
        if plane and b == 1:
            forward_first(by_part[1])
            begin(down)
            forward_far(by_part[1])
            end(by_part[1])
        for start in range(0, part_cols, chunk):
            at = b * section + start % section
            cols = slice(at, at + chunk)
            if start >= section:
                weight = w_second[:, cols]
            elif stride == shard:
                weight = w_first[:, cols]
            else:
                weight = jnp.concatenate([w_first[s * stride : s * stride + shard, cols] for s in range(8)], axis=0)
            got = dot_nn(normed[...], weight)
            here_cols = slice(b * part_cols + start, b * part_cols + start + chunk)
            proj[:, here_cols] = got
            scale = lax.rsqrt(head_sum(got * got, mask) * (1.0 / head_dim) + EPSILON)
            head = got * scale * head_gain(gains_ref, start, chunk)
            head = head * cos + partner(head, head_dim) * sin
            if start >= nz * widths[0]:
                head = jnp.where(key_lanes(head.shape, head_dim), head, got)
            qkv[:, here_cols] = head.astype(BF)
        arrived = []
        for j in range(nz):
            owner = z ^ j
            for i, size in enumerate(widths):
                base = b * part_cols + i * nz * widths[0]
                source = qkv.at[:, pl.ds(pl.multiple_of(base + owner * size, size), size)]
                target = heads_ref.at[my_rows, pl.ds(b * sum(widths) + i * widths[0], size)]
                if j == 0:
                    arrived.append(copy_here(source, target))
                else:
                    arrived.append(links.start(source, target, {"seq": owner}))
        arrivals.append(arrived)
    copy_here(proj, proj_hbm)
    transposed[0] = normed[...].T
    share(transposed.at[0], normed_t_hbm.at[:, place])
    share(dy_ref, dy_hbm.at[place])
    if plane:
        forward_first(outward)
        begin(wide[0])
    group, seq_len, _ = queries.shape
    factor = head_dim**-0.5 * LOG2E
    arriving, here_mixed = [], []
    for b in range(parts):
        for i, copy in enumerate(arrivals[b]):
            if i < 2:
                copy.wait()
            else:
                copy.wait_recv()
        first = b * sum(widths)
        for g in range(group):
            queries[g] = heads_ref[:, first + g * head_dim : first + (g + 1) * head_dim]
        first += widths[0]
        keys[...] = heads_ref[:, first : first + head_dim]
        values[...] = heads_ref[:, first + head_dim : first + 2 * head_dim]
        for r in range(seq_len // rows):
            span = slice(r * rows, (r + 1) * rows)
            reach = (r + 1) * rows

            def one_head(g, _):
                scores = dot_nt(queries[g, span], keys[:reach]) * factor
                row = lax.broadcasted_iota(jnp.int32, scores.shape, 0) + r * rows
                col = lax.broadcasted_iota(jnp.int32, scores.shape, 1)
                probs = jnp.exp2(jnp.where(row >= col, scores, -1e30))
                total = jnp.sum(probs, axis=1, keepdims=True)
                full[g, span] = (dot_nn(probs.astype(BF), values[:reach]) * (1.0 / total)).astype(BF)
                log_ref[b * group + g, :, span] = jnp.broadcast_to(jnp.log2(total), (rows, 128)).T[0:8]
                return 0

            lax.fori_loop(0, group, one_head, 0)
        mix[b] = jnp.concatenate([full[g] for g in range(group)], axis=1)
        for j in range(nz):
            owner = z ^ j
            source = mix.at[b, pl.ds(pl.multiple_of(owner * tokens, tokens), tokens)]
            to = pl.multiple_of((z * parts + b) * widths[0], widths[0])
            target = mixed.at[:, pl.ds(to, widths[0])]
            if j == 0:
                here_mixed.append(copy_here(source, target))
            else:
                arriving.append(links.start(source, target, {"seq": owner}))
        if plane and b == 0:
            forward_far(outward)
            forward_first(down)
            end(outward)
            for s in range(8):
                copy_here(w_first.at[pl.ds(s * stride, shard)], first_hbm.at[pl.ds(s * shard, shard)])
            copy_here(w_second, second_hbm)
        if b == 0:
            out_copies = [
                copy_here(
                    w_first.at[pl.ds(s * stride, shard), pl.ds(2 * section, out_half)],
                    w_out.at[pl.ds(s * shard, shard), pl.ds(0, out_half)],
                )
                for s in range(model // shard)
            ]
            out_copies.append(copy_here(w_second.at[:, pl.ds(2 * section, out_half)], w_out.at[:, pl.ds(out_half, out_half)]))
    if plane:
        forward_first(wide[0])
        begin(wide[1])
        begin(wide[2])
        forward_far(down)
        end(down)
        wait_all(own_stores)
    for copy in arriving:
        copy.wait_recv()
    wait_all(here_mixed + out_copies)

    copy_here(heads_ref, heads_hbm)
    copy_here(log_ref, log_hbm)

    gain = model_gain(gains_ref, 4)
    middle[...] = dot_nn(mixed[...], w_out[...])

    def by_rows(work):
        step = 128

        def body(i, _):
            work(pl.ds(pl.multiple_of(i * step, step), step))
            return 0

        lax.fori_loop(0, tokens // step, body, 0)

    def middle_norm(rows):
        middle_rows = x_ref[rows, :].astype(F32) + middle[rows, :]
        middle[rows, :] = middle_rows
        total[rows, :] = middle_rows
        normed[rows, :] = (middle_rows * row_norm(middle_rows) * gain).astype(BF)
        back[rows, :] = jnp.zeros(middle_rows.shape, F32)

    by_rows(middle_norm)
    normed_rows = normed[...]
    transposed[1] = normed_rows.T
    share(transposed.at[1], normed_two_hbm.at[:, place])
    transposed[2] = mixed[...].T
    share(transposed.at[2], mixed_t_hbm.at[:, place])

    def slot_places(f):
        here = pl.ds(pl.multiple_of(f * width, width), width)
        return (
            (hidden_slot, hidden_hbm.at[here, place]),
            (gate_slot, gate_grad_hbm.at[place, here]),
            (up_slot, up_grad_hbm.at[place, here]),
        )

    def slot_copies(slot, f):
        return [
            pltpu.make_async_copy(s.at[slot], target, slot_sems.at[slot, i]) for i, (s, target) in enumerate(slot_places(f))
        ]

    def slot_links(slot, f):
        if not plane:
            return []
        return [
            pltpu.make_async_remote_copy(
                src_ref=s.at[slot],
                dst_ref=target,
                send_sem=slot_sends.at[slot, i],
                recv_sem=block_recvs.at[f, i],
                device_id=sibling,
                device_id_type=pl.DeviceIdType.MESH,
            )
            for i, (s, target) in enumerate(slot_places(f))
        ]

    def wait_slot(slot, f):
        wait_all(slot_copies(slot, f))
        for copy in slot_links(slot, f):
            copy.wait_send()

    def weight_copies(f):
        here = pl.ds(pl.multiple_of(f * width, width), width)
        slot = lax.rem(f, 2)
        pairs = ((gate_hbm.at[:, here], w_gate), (up_hbm.at[:, here], w_up), (down_hbm.at[here], w_down))
        return [
            pltpu.make_async_copy(source, target.at[slot], weight_sems.at[slot, i])
            for i, (source, target) in enumerate(pairs)
        ]

    blocks = hidden_cols // width
    firsts = [sum(groups[:g]) for g in range(len(groups))]

    ahead = [0, 0, firsts[min(1, len(firsts) - 1)] - 1] + firsts[2:]

    def arrive(f):
        for g in range(1, len(groups)):

            @pl.when(f == ahead[g])
            def _():
                forward_first(wide[g])
                if g + 2 < len(groups):
                    begin(wide[g + 2])

        for g in range(len(groups)):

            @pl.when(f == firsts[g])
            def _():
                if g:
                    forward_far(wide[g])
                end(wide[g])

    def one_block(f, _):
        slot = lax.rem(f, 2)
        if plane:
            arrive(f)

        def fetch(block):
            for copy in weight_copies(block):
                copy.start()

        in_first = f < (firsts[1] if plane else blocks)
        pl.when((f == 0) | ~in_first)(lambda: fetch(f))
        pl.when(in_first & (f + 1 < (firsts[1] if plane else blocks)))(lambda: fetch(f + 1))
        wait_all(weight_copies(f))

        @pl.when(f >= 2)
        def _():
            wait_slot(slot, f - 2)

        gate = dot_nn(normed[...], w_gate[slot])
        up = dot_nn(normed[...], w_up[slot])
        hidden_grad = dot_nt(dy_ref[...], w_down[slot])
        s = 1.0 / (1.0 + jnp.exp(-gate))
        silu = gate * s
        hidden = (silu * up).astype(BF)
        gate_grad = (hidden_grad * up * (s * (1.0 + gate * (1.0 - s)))).astype(BF)
        up_grad = (hidden_grad * silu).astype(BF)
        hidden_slot[slot] = hidden.T
        gate_slot[slot] = gate_grad
        up_slot[slot] = up_grad
        for copy in slot_copies(slot, f) + slot_links(slot, f):
            copy.start()
        total[...] = total[...] + dot_nn(hidden, w_down[slot])
        back[...] = back[...] + (dot_nt(gate_grad, w_gate[slot]) + dot_nt(up_grad, w_up[slot]))
        return 0

    if plane:
        forward_far(wide[0])
    lax.fori_loop(0, blocks, one_block, 0)
    gain_grad_ref[...] = jnp.zeros(gain_grad_ref.shape, F32)

    def middle_back(rows):
        part, gain_sum = norm_back(middle[rows, :], gain, back[rows, :])
        gain_grad_ref[...] = gain_grad_ref[...] + gain_sum
        middle_grad = dy_ref[rows, :].astype(F32) + part
        back[rows, :] = middle_grad
        low_slot[rows, :] = middle_grad.astype(BF)

    by_rows(middle_back)
    copy_here(low_slot, middle_low_hbm)
    grad_low[...] = dot_nt(low_slot[...], w_out[...]).astype(BF)
    copy_here(grad_low, grad_low_hbm)
    copy_here(back, middle_grad_hbm)
    heads = mixed.shape[1] // head_dim // nz
    row = lax.broadcasted_iota(jnp.int32, (8 * nz, mixed.shape[1]), 0)
    col = lax.broadcasted_iota(jnp.int32, (8 * nz, mixed.shape[1]), 1)
    pick = ((col // head_dim == (row // 8) * heads + row % 8) & (row % 8 < heads)).astype(BF)

    def head_products(rows):
        product = grad_low[rows, :].astype(F32) * mixed[rows, :].astype(F32)
        high = product.astype(BF)
        delta_ref[:, rows] = dot_nt(pick, high) + dot_nt(pick, (product - high.astype(F32)).astype(BF))
        output_slot[rows, :] = total[rows, :].astype(BF)

    by_rows(head_products)
    copy_here(output_slot, output_hbm)
    for f in (blocks - 2, blocks - 1):
        wait_slot(f % 2, f)
    if plane:
        for f in range(blocks):
            for copy in slot_links(f % 2, f):
                copy.wait_recv()
        for copy in to_core:
            copy.wait_recv()
        links.wait_sends()
    done = here + out_copies + here_mixed + [c for arrived in arrivals for c in arrived[:2]]
    if plane:
        done += packing + own_loads + own_stores
    for copy in local:
        if not any(copy is other for other in done):
            copy.wait()


def both_cores(links, copy_here, me, source, target, axis):
    size = source.shape[axis]
    here = pl.ds(pl.multiple_of(lax.rem(me, 2) * size, size), size)
    place = target.at[here] if axis == 0 else target.at[:, here]
    copy_here(source, place)
    return links.start(source, place, {"fsdp": me ^ 1})


def attend_back(dims, b, heads_ref, grads_ref, log_ref, delta_ref, packed, scratch):
    rows, chunk = dims
    queries, keys, values, grad, q_grad, k_grad, v_grad = scratch
    group, seq_len, head_dim = queries.shape
    first = b * (group + 2) * head_dim
    for g in range(group):
        queries[g] = heads_ref[:, first + g * head_dim : first + (g + 1) * head_dim]
        at = (b * group + g) * head_dim
        grad[g] = grads_ref[:, at : at + head_dim]
        q_grad[g] = jnp.zeros((seq_len, head_dim), F32)
    first += group * head_dim
    keys[...] = heads_ref[:, first : first + head_dim]
    values[...] = heads_ref[:, first + head_dim : first + 2 * head_dim]
    factor = head_dim**-0.5
    scale = factor * LOG2E
    for at in range(seq_len // rows):
        span = slice(at * rows, (at + 1) * rows)
        key, value = keys[span], values[span]
        k_grad[span] = jnp.zeros((rows, head_dim), F32)
        v_grad[span] = jnp.zeros((rows, head_dim), F32)

        def one_head(g, _):
            key_total = jnp.zeros((rows, head_dim), F32)
            value_total = jnp.zeros((rows, head_dim), F32)
            for start in range(at * rows, seq_len, chunk):
                part = slice(start, min(start + chunk, seq_len))
                query, out_grad = queries[g, part], grad[g, part]
                scores = dot_nt(key, query) * scale - log_ref[b * group + g, 0:1, part]
                if start == at * rows:
                    key_at = lax.broadcasted_iota(jnp.int32, scores.shape, 0) + at * rows
                    query_at = lax.broadcasted_iota(jnp.int32, scores.shape, 1) + start
                    scores = jnp.where(query_at >= key_at, scores, -1e30)
                probs = jnp.exp2(scores)
                prob_grad = dot_nt(value, out_grad)
                score_grad = (probs * (prob_grad - delta_ref[b * group + g, 0:1, part])).astype(BF)
                value_total = value_total + dot_nn(probs.astype(BF), out_grad)
                key_total = key_total + dot_nn(score_grad, query)
                q_grad[g, part] = q_grad[g, part] + dot_tn(score_grad, key)
            k_grad[span] = k_grad[span] + key_total
            v_grad[span] = v_grad[span] + value_total
            return 0

        lax.fori_loop(0, group, one_head, 0)
        parts = [(q_grad[g, span] * factor).astype(BF) for g in range(group)]
        parts += [(k_grad[span] * factor).astype(BF), v_grad[span].astype(BF)]
        packed[span] = jnp.concatenate(parts, axis=1)
        yield at


def attend_back_scratch(group, seq_len, head_dim):
    many = lambda kind: pltpu.VMEM((group, seq_len, head_dim), kind)
    one = lambda kind: pltpu.VMEM((seq_len, head_dim), kind)
    return [many(BF), one(BF), one(BF), many(BF), many(F32), one(F32), one(F32)]


def attend_back_kernel(dims, heads_ref, grads_ref, log_ref, delta_ref, packed, *scratch):
    for b in range(packed.shape[0]):
        for _ in attend_back(dims, b, heads_ref, grads_ref, log_ref, delta_ref, packed.at[b], scratch):
            pass


def norm_back(rows, gain, gradient):
    q = row_norm(rows)
    n = rows * q
    u = gradient * gain
    return q * (u - n * jnp.mean(u * n, axis=-1, keepdims=True)), jnp.sum(gradient * n, axis=0, keepdims=True)


def weight_grad_kernel(left_ref, right_ref, out_ref):
    out_ref[...] = dot_nn(left_ref[...], right_ref[...]).astype(BF)


def weight_grad(left, right, width=256):
    rows, tokens = left.shape
    cols = right.shape[1]
    return call(
        weight_grad_kernel,
        shape_of((rows, cols), BF),
        [pl.BlockSpec((rows, tokens), lambda n: (0, 0)), pl.BlockSpec((tokens, width), lambda n: (0, n))],
        pl.BlockSpec((rows, width), lambda n: (0, n)),
        [],
        2 * rows * tokens * cols,
        2 * (rows * tokens + tokens * cols + rows * cols),
        grid=(cols // width,),
    )(left, right)


def project_back(dims, b, gains_ref, tables_ref, proj_ref, qkv, head_gain_grad_ref):
    nz, head_dim, widths = dims
    part_cols = nz * sum(widths)
    width = 256
    mask = head_mask(width, head_dim)
    cos = jnp.concatenate([tables_ref[0]] * (width // 128), axis=1)
    sin = jnp.concatenate([tables_ref[1]] * (width // 128), axis=1)
    for start in range(0, part_cols, width):
        cols = slice(b * part_cols + start, b * part_cols + start + width)
        rotated = qkv[:, cols].astype(F32)
        gradient = rotated * cos - partner(rotated, head_dim) * sin
        proj = proj_ref[:, start : start + width]
        scale = lax.rsqrt(head_sum(proj * proj, mask) * (1.0 / head_dim) + EPSILON)
        n = proj * scale
        u = gradient * head_gain(gains_ref, start, width)
        head_gain_grad_ref[:, cols] = jnp.sum(gradient * n, axis=0, keepdims=True)
        back = scale * (u - n * (head_sum(u * n, mask) * (1.0 / head_dim)))
        if start >= nz * widths[0]:
            back = jnp.where(key_lanes(back.shape, head_dim), back, rotated)
        qkv[:, cols] = back.astype(BF)


def input_back(x_ref, middle_grad_ref, gains_ref, qkv, weight, input_grad_ref, gain_grad_ref):
    normed_grad = dot_nt(qkv[...], weight[...])
    part, gain_sum = norm_back(x_ref[...].astype(F32), model_gain(gains_ref, 0), normed_grad)
    gain_grad_ref[...] = gain_sum
    input_grad_ref[...] = (middle_grad_ref[...] + part).astype(BF)


def post_kernel(dims, x_ref, middle_grad_ref, gains_ref, tables_ref, proj_ref, grads_ref, weight_ref, *refs):
    input_grad_ref, qkv, gain_grad_ref, head_gain_grad_ref = refs
    nz, _, widths = dims
    qkv[...] = grads_ref[...]
    for b in range(qkv.shape[1] // (nz * sum(widths))):
        part_cols = nz * sum(widths)
        part = proj_ref.at[:, pl.ds(b * part_cols, part_cols)]
        project_back(dims, b, gains_ref, tables_ref, part, qkv, head_gain_grad_ref)
    input_back(x_ref, middle_grad_ref, gains_ref, qkv, weight_ref, input_grad_ref, gain_grad_ref)


class Reduce:
    def __init__(self, links, fetch, me, z, x_first, away, kept, first, second, inward, across, out):
        self.links, self.fetch, self.me, self.z = links, fetch, me, z
        self.away, self.kept, self.out = away, kept, out
        self.bits = (2, 4) if x_first else (4, 2)
        order = (1, 3, 0, 2) if x_first else (2, 3, 0, 1)
        self.slots = {r: (away if i < 2 else kept, i % 2) for i, r in enumerate(order)}
        self.arrived, self.second, self.inward, self.across = first, second, inward, across
        self.outer, self.inner = (z == 0) | (z == 3), (z == 1) | (z == 2)
        self.one = links.copy(away, first, {"fsdp": me ^ self.bits[0]})
        self.two = links.copy(kept.at[1], second, {"fsdp": me ^ self.bits[1]})
        self.three = links.copy(kept.at[0], inward, {"seq": z ^ 1})
        self.four = links.copy(kept.at[0], across, {"seq": z ^ 3})
        self.five = links.copy(kept.at[1], out, {"seq": z ^ 1})
        self.here = fetch.copy(kept.at[1], out)
        self.load = fetch.copy(first, away)

    def put(self, r, cols, values):
        ref, i = self.slots[r]
        ref[i, :, cols] = values

    def rows_of(self):
        rows = self.kept.shape[1]
        step = 32 if rows % 32 == 0 else 16
        return rows // step, step

    def by_rows(self, work):
        count, step = self.rows_of()

        def body(i, _):
            work(pl.ds(pl.multiple_of(i * step, step), step))
            return 0

        lax.fori_loop(0, count, body, 0)

    def begin(self):
        self.one.start()

    def load_one(self):
        self.one.wait_recv()
        self.one.wait_send()
        self.load.start()

    def fold_one(self):
        self.load.wait()

        def work(rows):
            for i in range(2):
                self.kept[i, rows] = self.kept[i, rows] + self.away[i, rows]

        self.by_rows(work)
        self.two.start()

    def fold_two(self):
        self.two.wait_recv()

        def work(rows):
            self.kept[0, rows] = self.kept[0, rows] + self.second[rows]

        self.by_rows(work)

        @pl.when(self.outer)
        def _():
            self.three.start()

    def fold_three(self):
        @pl.when(self.inner)
        def _():
            self.three.wait_recv()

            def work(rows):
                self.kept[0, rows] = self.kept[0, rows] + self.inward[rows]

            self.by_rows(work)
            self.four.start()

    def fold_four(self):
        self.two.wait_send()

        @pl.when(self.inner)
        def _():
            self.four.wait_recv()

            def work(rows):
                self.kept[1, rows] = self.kept[0, rows] + self.across[rows]

            self.by_rows(work)
            self.five.start()
            self.here.start()

    def end(self):
        @pl.when(self.inner)
        def _():
            self.four.wait_send()
            self.five.wait_send()
            self.here.wait()

        @pl.when(self.outer)
        def _():
            self.three.wait_send()
            self.five.wait_recv()


def each(reduces, step):
    if step == "fold_one":
        each(reduces, "load_one")
    for reduce in reduces:
        getattr(reduce, step)()


class Total:
    def __init__(self, links, me, z, sums, arrived):
        self.sums, self.arrived = sums, arrived
        peers = [{"fsdp": me ^ 1}, {"fsdp": me ^ 2}, {"fsdp": me ^ 4}, {"seq": z ^ 1}, {"seq": z ^ 2}]
        self.copies = [links.copy(sums.at[i], arrived.at[i], peer) for i, peer in enumerate(peers)]

    def begin(self, at):
        self.copies[at].start()

    def fold(self, at):
        self.copies[at].wait_recv()
        self.sums[at + 1] = self.sums[at] + self.arrived[at]

    def end(self):
        for copy in self.copies:
            copy.wait_send()


EARLY = (
    ("wide4", "matmul"), ("wide4", "begin"), ("down1", "matmul"), ("down0", "matmul"), ("wide0", "matmul"),
    ("out", "matmul"), ("wide1", "matmul"), ("out", "begin"), ("wide4", "fold_one"), ("down0", "begin"),
    ("wide0", "begin"),
)
MIDDLE = (
    ("keys", 0, 0), ("keys", 0, 1), ("keys", 0, 2), ("wide4", "fold_two"), ("keys", 0, 3), ("keys", 0, 4),
    ("keys", 0, 5), ("keys", 0, 6), ("keys", 0, 7), ("wide5", "matmul"), ("wide2", "matmul"), ("wide4", "fold_three"),
    ("down0", "fold_one"), ("wide1", "begin"), ("keys", 1, 0), ("wide5", "begin"), ("keys", 1, 1),
    ("down0", "fold_two"), ("out", "fold_one"), ("keys", 1, 2), ("keys", 1, 3), ("keys", 1, 4), ("keys", 1, 5),
    ("keys", 1, 6), ("keys", 1, 7), ("wide0", "fold_one"), ("wide5", "fold_one"), ("wide3", "matmul"),
    ("wide1", "fold_one"), ("project", 0), ("out", "fold_two"), ("wide4", "fold_four"), ("down1", "begin"),
    ("wide2", "begin"), ("wide5", "fold_two"), ("down0", "fold_three"), ("wide1", "fold_two"), ("project", 1),
)
LATE = (
    ("out", "fold_three"), ("input",), ("down0", "fold_four"), ("wide5", "fold_three"), ("down1", "fold_one"),
    ("wide1", "fold_three"), ("out", "fold_four"), ("wide0", "fold_two"), ("total", 0), ("wide2", "fold_one"),
    ("wide5", "fold_four"), ("down1", "fold_two"), ("total", 1), ("last1", "matmul"), ("wide3", "begin"),
    ("wide0", "fold_three"), ("wide1", "fold_four"), ("total", 2), ("wide2", "fold_two"), ("down1", "fold_three"),
    ("last0", "matmul"), ("wide0", "fold_four"), ("wide3", "fold_one"), ("wide2", "fold_three"), ("last1", "begin"),
    ("down1", "fold_four"), ("last0", "begin"), ("wide3", "fold_two"), ("wide3", "fold_three"), ("last1", "fold_one"),
    ("wide2", "fold_four"), ("last0", "fold_one"), ("total", 3), ("last1", "fold_two"), ("wide3", "fold_four"),
    ("last0", "fold_two"), ("last0", "fold_three"), ("last1", "fold_three"), ("total", 4), ("last0", "fold_four"),
    ("last1", "fold_four"),
)


GATES = ("gate0x", "gate1y", "gate2x", "gate3y", "gate4x", "gate5y")
UPS = ("up0x", "up1y", "up2x", "up3y", "up4x", "up5y")


def backward_kernel(dims, gains_hbm, tables_hbm, delta_own, feed_gain_hbm, heads_hbm, log_hbm, grad_low, low_own, *refs):
    nz, head_dim, widths, attend_dims, names = dims
    given, refs = refs[:12], refs[12:]
    x_hbm, middle_grad_hbm, proj_hbm, hidden_hbm, dy_hbm, normed_two_hbm = given[:6]
    gate_hbm, up_hbm, mixed_hbm, normed_hbm, first_hbm, second_hbm = given[6:]
    input_grad_ref, totals_ref = refs[:2]
    n = len(names)
    finals, refs = dict(zip(names, refs[2 : 2 + n])), refs[2 + n :]
    firsts, refs = dict(zip(names, refs[:n])), refs[n:]
    low_hbm, refs = refs[0], refs[1:]
    aways, refs = dict(zip(names, refs[:n])), refs[n:]
    kepts, refs = dict(zip(names, refs[:n])), refs[n:]
    seconds, refs = dict(zip(names, refs[:n])), refs[n:]
    inwards, refs = dict(zip(names, refs[:n])), refs[n:]
    acrosses, refs = dict(zip(names, refs[:n])), refs[n:]
    grads, delta, qkv, other_qkv, normed_two, normed, sums, sum_arrived, gain_grad, head_gain_grad = refs[:10]
    heads_ref, log_ref, low_ref, gains_ref, tables_ref, feed_gain_ref, sems, send_sems, recv_sems = refs[10:]
    z, me = lax.axis_index("seq"), lax.axis_index("fsdp")
    chip, core = lax.div(me, 2), lax.rem(me, 2)
    links, fetch = Links(send_sems, recv_sems), Fetch(sems)
    enter(me, z, nz, True)
    low_load = fetch.start(low_own, low_ref)
    head_loads = [
        fetch.start(source, target)
        for source, target in (
            (heads_hbm, heads_ref),
            (log_hbm, log_ref),
            (gains_hbm, gains_ref),
            (tables_hbm, tables_ref),
            (feed_gain_hbm, feed_gain_ref),
        )
    ]
    tokens = grad_low.shape[0]
    seq_len, block_cols = heads_ref.shape
    part_cols = nz * sum(widths)
    parts = qkv.shape[1] // part_cols
    late = []

    def copy_here(source, target):
        copy = fetch.start(source, target)
        late.append(copy)
        return copy

    my_rows = pl.ds(pl.multiple_of(z * tokens, tokens), tokens)
    arrivals = []
    for b in range(parts):
        arrived = []
        for j in range(nz):
            owner = z ^ j
            from_cols = pl.ds(pl.multiple_of((owner * parts + b) * widths[0], widths[0]), widths[0])
            pairs = [(grad_low.at[:, from_cols], grads.at[my_rows, pl.ds(b * widths[0], widths[0])])]
            if b == 0:
                pairs.append((delta_own.at[pl.ds(pl.multiple_of(owner * 8, 8), 8)], delta.at[:, my_rows]))
            for source, target in pairs:
                if j == 0:
                    copy_here(source, target)
                else:
                    arrived.append(links.start(source, target, {"seq": owner}))
        arrivals.append(arrived)
    low_load.wait()
    low_arrival = both_cores(links, copy_here, me, low_ref, low_hbm, 0)
    reduces = {}
    for name in names:
        reduces[name] = Reduce(
            links, fetch, me, z, name[-1] == "x", aways[name], kepts[name], firsts[name], seconds[name], inwards[name],
            acrosses[name], finals[name],
        )
    down = [[reduces[f"down{c}{way}"] for way in "xy"] for c in range(2)]
    wide_names = GATES + UPS
    wide = [[reduces[name] for name in wide_names[i : i + 2]] for i in range(0, len(wide_names), 2)]
    out = [reduces["outx"], reduces["outy"]]
    last = [[reduces[f"last{b}{way}"] for way in "xy"] for b in range(parts)]
    total = Total(links, me, z, sums, sum_arrived)
    part_cols_of = lambda b: pl.ds(b * part_cols, part_cols)
    qkv_links = [
        links.copy(qkv.at[:, part_cols_of(b)], other_qkv.at[:, part_cols_of(b)], {"fsdp": me ^ 1}) for b in range(parts)
    ]
    chips = 4
    step = 256
    half = down[0][0].kept.shape[1]
    shard = wide[0][0].kept.shape[1]
    both = 2 * tokens
    model = low_ref.shape[1]

    def my_blocks(source, target, rows):
        copies = []
        for r in range(chips):
            owner = (chip ^ r) * 2 + core
            copies.append(fetch.start(source.at[pl.ds(pl.multiple_of(owner * rows, rows), rows)], target.at[pl.ds(r * rows, rows)]))
        return copies

    def wide_grads(places, left, right):
        width = right.shape[2]
        chunks = [
            (source, (first + c) * width, unit, c * width)
            for source, first, unit in places
            for c in range(unit.kept.shape[2] // width)
        ]
        count = len(chunks)
        loads = [
            fetch.copy(source.at[:, pl.ds(at, width)], right.at[c % 2]) for c, (source, at, _, _) in enumerate(chunks)
        ]
        loads[0].start()
        loads[1].start()
        for c in range(count):
            loads[c].wait()
            _, _, unit, base = chunks[c]

            def block(k, _):
                here = pl.ds(pl.multiple_of(k * step, step), step)
                to = pl.ds(pl.multiple_of(base + k * step, step), step)
                got = dot_nn(left[...], right[c % 2, :, here]).astype(BF)
                for r in range(chips):
                    unit.put(r, to, got[r * shard : (r + 1) * shard])
                return 0

            lax.fori_loop(0, width // step, block, 0)
            if c + 2 < count:
                loads[c + 2].start()

    ready = {"two": my_blocks(normed_two_hbm, normed_two, shard), "one": my_blocks(normed_hbm, normed, shard)}

    def ready_now(name):
        wait_all(ready.pop(name, ()))

    wide_part = wide[0][0].kept.shape[2]

    def wide_matmul(i, right):
        ready_now("two")
        places = []
        for at in (2 * i, 2 * i + 1):
            source = gate_hbm if at < len(GATES) else up_hbm
            places.append((source, at % len(GATES), wide[i][at % 2]))
        wide_grads(places, normed_two, right)

    def out_matmul(mixed, low):
        cols = out[0].kept.shape[2]
        for start in range(0, low.shape[1], step):
            got = dot_nn(mixed[...], low[:, start : start + step]).astype(BF)
            for r in range(chips):
                out[start // cols].put(r, slice(start % cols, start % cols + step), got[r * shard : (r + 1) * shard])

    def down_matmul(c, hidden, dy):
        cols = down[0][0].kept.shape[2]

        def block(i, _):
            to = pl.ds(pl.multiple_of(i * step, step), step)
            here = pl.ds(pl.multiple_of(c * cols + i * step, step), step)
            for r in range(chips):
                got = dot_nn(hidden[2 * r * half : 2 * (r + 1) * half], dy[:, here]).astype(BF)
                for side in range(2):
                    down[c][side].put(r, to, got[side * half : (side + 1) * half])
            return 0

        lax.fori_loop(0, cols // step, block, 0)

    def last_matmul(b):
        ready_now("one")
        mine = normed[:, pl.ds(pl.multiple_of(core * tokens, tokens), tokens)]
        theirs = normed[:, pl.ds(pl.multiple_of((1 - core) * tokens, tokens), tokens)]
        qkv_links[b].wait()
        cols = last[b][0].kept.shape[2]
        for start in range(0, part_cols, step):
            here = slice(b * part_cols + start, b * part_cols + start + step)
            got = (dot_nn(mine, qkv[:, here]) + dot_nn(theirs, other_qkv[:, here])).astype(BF)
            for r in range(chips):
                last[b][start // cols].put(r, slice(start % cols, start % cols + step), got[r * shard : (r + 1) * shard])

    pairs = {"out": out}
    pairs |= {f"down{c}": down[c] for c in range(2)}
    pairs |= {f"wide{i}": pair for i, pair in enumerate(wide)}
    pairs |= {f"last{b}": last[b] for b in range(parts)}
    right_shape = pltpu.VMEM((2, both, wide_part), BF)

    def sum_step(name, what):
        if what != "matmul":
            each(pairs[name], what)
        elif name[:4] == "last":
            last_matmul(int(name[4]))
        else:
            pl.run_scoped(functools.partial(wide_matmul, int(name[4])), right_shape)

    def early(hidden, dy, right, mixed, low):
        ready["down"] = my_blocks(hidden_hbm, hidden, 2 * half) + [fetch.start(dy_hbm, dy)]
        ready["out"] = my_blocks(mixed_hbm, mixed, shard)
        for name, what in EARLY:
            if what != "matmul":
                each(pairs[name], what)
            elif name[:4] == "down":
                ready_now("down")
                down_matmul(int(name[4]), hidden, dy)
            elif name == "out":
                low_arrival.wait_recv()
                wait_all(late)
                del late[:]
                ready["out"].append(fetch.start(low_hbm, low))
                ready_now("out")
                out_matmul(mixed, low)
            else:
                wide_matmul(int(name[4]), right)

    pl.run_scoped(
        early,
        pltpu.VMEM((2 * chips * half, both), BF),
        pltpu.VMEM((both, model), BF),
        right_shape,
        pltpu.VMEM((chips * shard, both), BF),
        pltpu.VMEM((both, model), BF),
    )

    wait_all(head_loads)
    heads = log_ref.shape[0]
    group = heads // parts
    first_back = links.reserve(parts * 2 * nz)
    own_back = fetch.used
    fetch.used += parts * 2

    def back_copies(b, packed):
        for i, width in enumerate(widths):
            base = b * part_cols + i * nz * widths[0]
            target = qkv.at[:, pl.ds(pl.multiple_of(base + z * width, width), width)]
            for j in range(nz):
                owner = z ^ j
                rows = pl.ds(pl.multiple_of(owner * tokens, tokens), tokens)
                source = packed.at[b, rows, pl.ds(i * widths[0], width)]
                if j == 0:
                    yield j, pltpu.make_async_copy(source, target, sems.at[own_back + 2 * b + i])
                else:
                    yield j, links.copy(source, target, {"seq": owner}, at=first_back + (2 * b + i) * nz + j)

    def middle(packed, delta_rows, *scratch):
        blocks = {}

        def keys_step(b, at):
            if at == 0:
                for copy in arrivals[b]:
                    copy.wait_recv()
                if b == 0:
                    for h in range(heads):
                        delta_rows[h] = jnp.broadcast_to(delta[h : h + 1], (8, seq_len))
                blocks[b] = attend_back(attend_dims, b, heads_ref, grads, log_ref, delta_rows, packed.at[b], scratch)
            next(blocks[b])
            if (at + 1) * attend_dims[0] == seq_len:
                for _, copy in back_copies(b, packed):
                    copy.start()

        def project_step(b):
            for j, copy in back_copies(b, packed):
                if j == 0:
                    copy.wait()
                else:
                    copy.wait_recv()

            def inner(proj):
                fetch.start(proj_hbm.at[:, part_cols_of(b)], proj).wait()
                project_back((nz, head_dim, widths), b, gains_ref, tables_ref, proj, qkv, head_gain_grad)

            pl.run_scoped(inner, pltpu.VMEM((tokens, part_cols), F32))
            qkv_links[b].start()

        for token in MIDDLE:
            if token[0] == "keys":
                keys_step(*token[1:])
            elif token[0] == "project":
                project_step(token[1])
            else:
                sum_step(*token)
        for b in range(parts):
            for j, copy in back_copies(b, packed):
                if j:
                    copy.wait_send()

    pl.run_scoped(
        middle,
        pltpu.VMEM((parts, seq_len, sum(widths)), BF),
        pltpu.VMEM((heads, 8, seq_len), F32),
        *attend_back_scratch(group, seq_len, head_dim),
    )

    def input_step(weight, x, middle_grad):
        copies = [fetch.start(x_hbm, x), fetch.start(middle_grad_hbm, middle_grad)]
        section = part_cols // 2
        for b in range(parts):
            for i, source in enumerate((first_hbm, second_hbm)):
                to = pl.ds(b * part_cols + i * section, section)
                copies.append(fetch.start(source.at[:, pl.ds(b * section, section)], weight.at[:, to]))
        wait_all(copies)
        input_back(x, middle_grad, gains_ref, qkv, weight, input_grad_ref, gain_grad)
        row = jnp.concatenate([gain_grad[...], head_gain_grad[...], feed_gain_ref[...]], axis=1)
        sums[0] = jnp.broadcast_to(row, sums.shape[1:])

    for token in LATE:
        if token[0] == "input":
            pl.run_scoped(
                input_step,
                pltpu.VMEM((model, parts * part_cols), BF),
                pltpu.VMEM((tokens, model), BF),
                pltpu.VMEM((tokens, model), F32),
            )
            total.begin(0)
        elif token[0] == "total":
            total.fold(token[1])
            if token[1] < 4:
                total.begin(token[1] + 1)
        else:
            sum_step(*token)
    totals_ref[...] = sums[5]
    total.end()
    for name in names:
        reduces[name].end()
    links.wait_sends()


def finish_kernel(dims, *refs):
    names, nz, head_dim = dims
    n = len(names)
    totals_hbm, refs = refs[0], refs[1:]
    output_in, input_grad_in = refs[:2]
    shards, refs = dict(zip(names, refs[2 : 2 + n])), refs[2 + n :]
    output, input_grad, q_out, k_out, v_out, out_out, gate_out, up_out, down_out = refs[:9]
    gain_outs, refs = refs[9:13], refs[13:]
    slots, refs = dict(zip(names, refs[:n])), refs[n:]
    passing, q, k, v, out, gate, up, down, totals_ref, load_sems, store_sems = refs
    fetch, store = Fetch(load_sems), Fetch(store_sems)
    order = GATES + UPS + tuple(name for name in names if name not in GATES + UPS)
    loads = {name: fetch.start(shards[name], slots[name]) for name in order}
    totals_load = fetch.start(totals_hbm, totals_ref)
    moves = [fetch.start(source, passing.at[i]) for i, source in enumerate((output_in, input_grad_in))]
    stores = []

    def place(name, target, row, col):
        loads[name].wait()
        rows, cols = slots[name].shape
        target[row : row + rows, col : col + cols] = slots[name][...].astype(F32)

    cols = slots["gate0x"].shape[1]
    for target, done, pieces in (
        (gate, gate_out, GATES),
        (up, up_out, UPS),
    ):
        for i, name in enumerate(pieces):
            place(name, target, 0, i * cols)
        stores.append(store.start(target, done))
    rows, cols = slots["down0x"].shape
    for c in range(2):
        for i, way in enumerate("xy"):
            place(f"down{c}{way}", down, i * rows, c * cols)
    stores.append(store.start(down, down_out))
    cols = slots["outx"].shape[1]
    for i, way in enumerate("xy"):
        place("out" + way, out, 0, i * cols)
    stores.append(store.start(out, out_out))
    parts = 2
    width = q.shape[1] // (nz * parts)
    for b in range(parts):
        loads[f"last{b}x"].wait()
        for i in range(nz):
            to = (i * parts + b) * width
            q[:, to : to + width] = slots[f"last{b}x"][:, i * width : (i + 1) * width].astype(F32)
    stores.append(store.start(q, q_out))
    for b in range(parts):
        loads[f"last{b}y"].wait()
    for i, target in enumerate((k, v)):
        pieces = [
            slots[f"last{b}y"][:, (2 * at + i) * head_dim : (2 * at + i + 1) * head_dim]
            for at in range(nz)
            for b in range(parts)
        ]
        target[...] = jnp.concatenate(pieces, axis=1).astype(F32)
    stores += [store.start(k, k_out), store.start(v, v_out)]
    totals_load.wait()
    me = lax.axis_index("fsdp")
    model = down_out.shape[1]
    section = model // 2
    share = gain_outs[0].shape[1]
    for ref, base in ((gain_outs[0], 0), (gain_outs[3], model + 4 * section)):
        ref[...] = totals_ref[0:1, pl.ds(pl.multiple_of(base + me * share, share), share)]
    for ref, shift, period in ((gain_outs[1], 0, head_dim), (gain_outs[2], section, 2 * head_dim)):
        share = ref.shape[1]
        row = sum(
            totals_ref[0:1, model + part * 2 * section + shift + at : model + part * 2 * section + shift + at + head_dim]
            for part in range(2)
            for at in range(0, section, period)
        )
        row = jnp.concatenate([row] * (128 // head_dim), axis=1)
        ref[...] = pltpu.roll(row, 128 - me * share, 1)[:, :share]
    for i, target in enumerate((output, input_grad)):
        moves[i].wait()
        stores.append(store.start(passing.at[i], target))
    wait_all(stores)


def add(a, b):
    return (a.astype(F32) + b.astype(F32)).astype(a.dtype)


def sum_line(values):
    size = lax.axis_size("seq")
    if size != 4:
        return lax.psum(values, "seq")
    z = lax.axis_index("seq")
    inner = add(values, lax.ppermute(values, "seq", [(0, 1), (3, 2)]))
    total = add(inner, lax.ppermute(inner, "seq", [(1, 2), (2, 1)]))
    outer = lax.ppermute(total, "seq", [(1, 0), (2, 3)])
    return jnp.where((z == 1) | (z == 2), total, outer)


def per_device(
    inputs,
    positions,
    cotangent,
    query_weight,
    key_weight,
    value_weight,
    out_weight,
    attention_gain,
    query_gain,
    key_gain,
    feedforward_gain,
    gate_weight,
    up_weight,
    down_weight,
):
    seqs, tokens, model = inputs.shape
    assert seqs == 1
    fsdp, nz = lax.axis_size("fsdp"), lax.axis_size("seq")
    me, z = lax.axis_index("fsdp"), lax.axis_index("seq")
    plane = fsdp == 8 and nz == 4
    both = 2 * tokens if plane else tokens
    x = inputs.reshape(tokens, model)
    dy = cotangent.reshape(tokens, model)
    head_dim = query_gain.shape[0] * fsdp
    q_cols, k_cols, v_cols = query_weight.shape[1], key_weight.shape[1], value_weight.shape[1]
    heads, kv_heads = q_cols // head_dim // nz, k_cols // head_dim // nz
    hidden_cols = gate_weight.shape[1]
    seq_len = tokens * nz

    group, parts = heads // kv_heads, kv_heads
    widths = (group * head_dim, 2 * head_dim)
    part_cols = nz * sum(widths)
    assert parts == 2

    section = nz * widths[0]
    assert model == 2 * section and part_cols == 2 * section
    half_out = model // 2
    first_cols = 2 * section + half_out
    if plane:
        given = [query_weight, key_weight, value_weight, out_weight, gate_weight, up_weight, down_weight]
        given += [query_gain[None], key_gain[None], attention_gain[None], feedforward_gain[None]]
    else:
        shard_rows = query_weight.shape[0]
        q = query_weight.reshape(shard_rows, nz, parts, widths[0])
        kv = jnp.stack([v.reshape(shard_rows, nz, parts, head_dim) for v in (key_weight, value_weight)], axis=3)
        first, second = (
            jnp.concatenate([v[:, :, b].reshape(shard_rows, section) for b in range(parts)] + [rest], axis=1)
            for v, rest in ((q, out_weight[:, :half_out]), (kv, out_weight[:, half_out:]))
        )
        gather = functools.partial(lax.all_gather, axis_name="fsdp", axis=0, tiled=True)
        first_full, second_full, gate_full = gather(first), gather(second), gather(gate_weight)
        up_full, down_full = gather(up_weight), gather(down_weight)
        key_row = jnp.concatenate([gather(key_gain), jnp.zeros((head_dim,), BF)])
        gain_rows = [gather(attention_gain).reshape(2, section), jnp.tile(gather(query_gain), nz * group)[None]]
        gain_rows += [jnp.tile(key_row, nz)[None], gather(feedforward_gain).reshape(2, section)]
        gain_rows = jnp.concatenate(gain_rows + [jnp.zeros((10, section), BF)]).astype(F32)
        given = [first_full, second_full, gain_rows, gate_full, up_full, down_full]

    half_dim = head_dim // 2
    freqs = ROPE_BASE ** (-(jnp.arange(128) % half_dim).astype(F32) / half_dim)

    rows_model = lambda kind: shape_of((tokens, model), kind)
    width = 512
    blocks = hidden_cols // width
    sizes = (blocks - 6,) + (1,) * 6
    block_cols = parts * sum(widths)
    mixed_cols = heads * head_dim
    attend_flops = 2 * heads * seq_len * seq_len * head_dim
    proj_flops = 2 * tokens * model * parts * part_cols
    outs = [
        shape_of((16, section), F32),
        shape_of((2, tokens, 128), F32),
        shape_of((1, model), F32),
        shape_of((8 * nz, tokens), F32),
        shape_of((seq_len, block_cols), BF),
        shape_of((heads, 8, seq_len), F32),
        rows_model(BF),
        rows_model(F32),
        rows_model(BF),
        shape_of((tokens, q_cols), BF),
        shape_of((tokens, parts * part_cols), F32),
        shape_of((model, both), BF),
        shape_of((q_cols, both), BF),
        shape_of((model, both), BF),
        shape_of((hidden_cols, both), BF),
        shape_of((both, hidden_cols), BF),
        shape_of((both, hidden_cols), BF),
        shape_of((both, model), BF),
    ]
    n_links = parts * 3 * (nz - 1)
    first_rows = model
    if plane:
        outs += [shape_of((model, first_cols), BF)] * 2
        outs += [shape_of((model, hidden_cols), BF)] * 2 + [shape_of((hidden_cols, model), BF)]
        n_links += (8 + 2 * len(sizes)) * 7 + 4
        first_rows += 8 * 16
    many = lambda count: pltpu.VMEM((count, seq_len, head_dim), BF)
    one = pltpu.VMEM((seq_len, head_dim), BF)
    got = call(
        functools.partial(forward_kernel, (nz, plane, head_dim, widths, min(256, seq_len), width, sizes)),
        outs,
        [VMEM] * 4 + ([ANY] * 7 + [VMEM] * 4 if plane else [ANY] * 2 + [VMEM] + [ANY] * 3),
        [VMEM] * 4 + [ANY] * (len(outs) - 4),
        [
            pltpu.VMEM((first_rows, first_cols), BF),
            pltpu.VMEM((model, first_cols), BF),
            pltpu.VMEM((q_cols, model), BF),
            pltpu.VMEM((tokens, model), BF),
            pltpu.VMEM((3, model, tokens), BF),
            pltpu.VMEM((tokens, parts * part_cols), F32),
            pltpu.VMEM((tokens, parts * part_cols), BF),
            many(group),
            one,
            one,
            many(group),
            pltpu.VMEM((parts, seq_len, widths[0]), BF),
            pltpu.VMEM((tokens, q_cols), BF),
            pltpu.VMEM((seq_len, block_cols), BF),
            pltpu.VMEM((heads, 8, seq_len), F32),
            pltpu.VMEM((tokens, model), BF),
            pltpu.VMEM((tokens, model), BF),
            pltpu.VMEM((tokens, q_cols), BF),
            pltpu.VMEM((2, model, width), BF),
            pltpu.VMEM((2, model, width), BF),
            pltpu.VMEM((2, width, model), BF),
            pltpu.VMEM((tokens, model), F32),
            pltpu.VMEM((tokens, model), F32),
            pltpu.VMEM((tokens, model), F32),
            pltpu.VMEM((2, width, tokens), BF),
            pltpu.VMEM((2, tokens, width), BF),
            pltpu.VMEM((2, tokens, width), BF),
            pltpu.SemaphoreType.DMA((64,)),
            pltpu.SemaphoreType.DMA((2, 3)),
            pltpu.SemaphoreType.DMA((2, 3)),
            pltpu.SemaphoreType.DMA((n_links,)),
            pltpu.SemaphoreType.DMA((n_links,)),
            pltpu.SemaphoreType.DMA((2, 3)),
            pltpu.SemaphoreType.DMA((blocks, 3)),
        ]
        + [pltpu.VMEM(w.shape, BF) for w in (gate_weight, up_weight, down_weight) if plane]
        + [pltpu.VMEM((query_weight.shape[0] + extra, 2 * section), BF) for extra in (16, 0) if plane]
        + [pltpu.VMEM(key_weight.shape, BF) for _ in range(2) if plane],
        proj_flops + 4 * attend_flops + 12 * tokens * model * hidden_cols,
        100 * 2**20,
        collective=1,
    )(x, dy, positions.reshape(1, tokens), freqs[None], *given)
    gains, tables, feed_gain_part, delta = got[:4]
    head_rows, logs, output, middle_grad, middle_low, mixed_grad = got[4:10]
    proj, normed_t, mixed_t, normed_two_t, hidden_t, gate_grad, up_grad, dy_both = got[10:18]
    if plane:
        first_full, second_full = got[18:20]

    attend_dims = (min(256, seq_len), min(1024, seq_len))
    attend_scratch = attend_back_scratch(group, seq_len, head_dim)
    if plane:
        down_rows, down_cols = down_weight.shape
        blocks = {f"down{c}{way}": (down_rows // 2, down_cols // 2) for c in range(2) for way in "xy"}
        blocks |= {name: (gate_weight.shape[0], hidden_cols // len(GATES)) for name in GATES + UPS}
        blocks |= {"out" + way: (out_weight.shape[0], model // 2) for way in "xy"}
        blocks |= {f"last{b}{way}": (query_weight.shape[0], part_cols // 2) for b in range(parts) for way in "xy"}
        names = tuple(blocks)
        pairs = [(2,) + shape for shape in blocks.values()]
        total_cols = model + parts * part_cols + model
        n_links = 3 * (nz - 1) + 2 * parts * nz + 1 + parts + 5 * len(names) + 5
        n_copies = 80 + 2 * len(names)
        got = call(
            functools.partial(backward_kernel, (nz, head_dim, widths, attend_dims, names)),
            [rows_model(BF), shape_of((8, total_cols), F32)]
            + [shape_of(shape, BF) for shape in blocks.values()]
            + [shape_of(shape, BF) for shape in pairs]
            + [shape_of((both, model), BF)],
            [ANY] * 20,
            [VMEM] * 2 + [ANY] * (2 * len(names) + 1),
            [pltpu.VMEM(shape, BF) for shape in pairs] * 2
            + [pltpu.VMEM(shape, BF) for shape in blocks.values()] * 3
            + [
                pltpu.VMEM((seq_len, mixed_cols), BF),
                pltpu.VMEM((8, seq_len), F32),
                pltpu.VMEM((tokens, parts * part_cols), BF),
                pltpu.VMEM((tokens, parts * part_cols), BF),
                pltpu.VMEM((model // 2, both), BF),
                pltpu.VMEM((model // 2, both), BF),
                pltpu.VMEM((6, 8, total_cols), F32),
                pltpu.VMEM((5, 8, total_cols), F32),
                pltpu.VMEM((1, model), F32),
                pltpu.VMEM((1, parts * part_cols), F32),
                pltpu.VMEM((seq_len, block_cols), BF),
                pltpu.VMEM((heads, 8, seq_len), F32),
                pltpu.VMEM((tokens, model), BF),
                pltpu.VMEM(gains.shape, F32),
                pltpu.VMEM(tables.shape, F32),
                pltpu.VMEM((1, model), F32),
                pltpu.SemaphoreType.DMA((n_copies,)),
                pltpu.SemaphoreType.DMA((n_links,)),
                pltpu.SemaphoreType.DMA((n_links,)),
            ],
            10 * attend_flops + 2 * tokens * model * (3 * hidden_cols + 3 * (q_cols + k_cols)),
            100 * 2**20,
            collective=3,
        )(
            gains, tables, delta, feed_gain_part, head_rows, logs, mixed_grad, middle_low, x, middle_grad, proj,
            hidden_t, dy_both, normed_two_t, gate_grad, up_grad, mixed_t, normed_t, first_full, second_full,
        )
        input_grad, totals = got[:2]
        slots = [pltpu.VMEM(shape, BF) for shape in blocks.values()]
        out_shapes = [w.shape for w in (query_weight, key_weight, value_weight, out_weight, gate_weight, up_weight, down_weight)]
        gain_shapes = [(1, g.shape[0]) for g in (attention_gain, query_gain, key_gain, feedforward_gain)]
        *results, attention_total, q_total, k_total, feed_total = call(
            functools.partial(finish_kernel, (names, nz, head_dim)),
            [rows_model(BF)] * 2 + [shape_of(shape, F32) for shape in out_shapes + gain_shapes],
            [ANY] * (3 + len(names)),
            [ANY] * 9 + [VMEM] * 4,
            slots
            + [pltpu.VMEM((2, tokens, model), BF)]
            + [pltpu.VMEM(shape, F32) for shape in out_shapes]
            + [pltpu.VMEM(totals.shape, F32)]
            + [pltpu.SemaphoreType.DMA((3 + len(names),)), pltpu.SemaphoreType.DMA((9,))],
            0,
            18 * 2**20,
        )(totals, output, input_grad, *got[2 : 2 + len(names)])
        output, input_grad, q_shard, k_shard, v_shard, out_shard, gate_shard, up_shard, down_shard = results
    else:
        exchange = functools.partial(lax.all_to_all, axis_name="seq", tiled=True)
        grad_rows = exchange(mixed_grad, split_axis=1, concat_axis=0)
        delta_rows = exchange(delta, split_axis=0, concat_axis=1)
        packed = call(
            functools.partial(attend_back_kernel, attend_dims),
            shape_of((parts, seq_len, sum(widths)), BF),
            [VMEM] * 4,
            VMEM,
            attend_scratch,
            10 * attend_flops,
            20 * 2**20,
        )(head_rows, grad_rows, logs, jnp.broadcast_to(delta_rows[:heads, None], (heads, 8, seq_len)))
        pieces = [piece for b in range(parts) for piece in (packed[b, :, : widths[0]], packed[b, :, widths[0] :])]
        qkv = jnp.concatenate([exchange(piece, split_axis=0, concat_axis=1) for piece in pieces], axis=1)
        weight = jnp.concatenate(
            [full[:, b * section : (b + 1) * section] for b in range(parts) for full in (first_full, second_full)], axis=1
        )
        input_grad, qkv, gain_part, head_gain_part = call(
            functools.partial(post_kernel, (nz, head_dim, widths)),
            [
                rows_model(BF),
                shape_of((tokens, parts * part_cols), BF),
                shape_of((1, model), F32),
                shape_of((1, parts * part_cols), F32),
            ],
            [VMEM] * 7,
            [VMEM] * 4,
            [],
            proj_flops,
            14 * 2**20,
        )(x, middle_grad, gains, tables, proj, qkv, weight)

        def reduce(left, right):
            return sum_line(lax.psum_scatter(weight_grad(left, right), "fsdp", scatter_dimension=0, tiled=True)).astype(F32)

        down_shard, gate_shard = reduce(hidden_t, dy), reduce(normed_two_t, gate_grad)
        up_shard, out_shard = reduce(normed_two_t, up_grad), reduce(mixed_t, middle_low)
        qkv_shard = reduce(normed_t, qkv)
        part_shards = [
            (qkv_shard[:, b * part_cols : b * part_cols + section], qkv_shard[:, b * part_cols + section : (b + 1) * part_cols])
            for b in range(parts)
        ]
        q_shard = jnp.stack([q.reshape(shard_rows, nz, widths[0]) for q, _ in part_shards], axis=2).reshape(shard_rows, -1)
        kv_shard = jnp.stack([kv.reshape(shard_rows, nz, 2, head_dim) for _, kv in part_shards], axis=2)
        k_shard, v_shard = (kv_shard[:, :, :, i].reshape(shard_rows, -1) for i in range(2))
        totals = lax.psum(jnp.concatenate([gain_part, head_gain_part, feed_gain_part], axis=1)[0], ("seq", "fsdp"))

        head_totals = totals[model : model + parts * part_cols].reshape(parts, part_cols)
        q_total = head_totals[:, : nz * widths[0]].reshape(-1, head_dim).sum(axis=0)
        k_total = head_totals[:, nz * widths[0] :].reshape(-1, 2, head_dim)[:, 0].sum(axis=0)

        def share(values):
            own = jnp.arange(fsdp)[:, None] == me
            return jnp.sum(jnp.where(own, values.reshape(fsdp, -1), 0.0), axis=0)
        attention_total, feed_total = share(totals[:model]), share(totals[model + parts * part_cols :])
        q_total, k_total = share(q_total), share(k_total)

    return (
        output.reshape(inputs.shape),
        input_grad.reshape(inputs.shape),
        q_shard,
        k_shard,
        v_shard,
        out_shard,
        attention_total.reshape(-1),
        q_total.reshape(-1),
        k_total.reshape(-1),
        feed_total.reshape(-1),
        gate_shard,
        up_shard,
        down_shard,
    )


def solution(mesh):
    tokens, rows, row = P("fsdp", "seq", None), P("fsdp", None), P("fsdp")
    in_specs = (tokens, P("fsdp", "seq"), tokens) + (rows,) * 4 + (row,) * 4 + (rows,) * 3
    out_specs = (tokens, tokens) + (rows,) * 4 + (row,) * 4 + (rows,) * 3
    return jax.shard_map(per_device, mesh=mesh, in_specs=in_specs, out_specs=out_specs, check_vma=False)
```
